32 devices in a mesh: tm: 8 (over y, x, core), space: 4 (over z).
Axes of the slice: x: 2, y: 2, z: 4, core: 2. Of those that a mesh axis runs over, the one named last changes fastest.
Arguments:
- frames_in: bfloat16 [64, 32, 64, 256], P('tm', 'space'), may hold values from -6 to 6
- cotangent: bfloat16 [64, 32, 64, 256], P('tm', 'space'), may hold values from -6 to 6
- spatial: bfloat16 [3, 3, 256, 256], replicated, may hold values from -0.125 to 0.125
- temporal: bfloat16 [3, 256, 256], replicated, may hold values from -0.375 to 0.375
- norm_gain: float32 [256], replicated, may hold values from 0.5 to 2
- norm_shift: float32 [256], replicated, may hold values from -3 to 3
- clip_frames: int32 [2], replicated, may hold values from 8 to 48, as said below
- dilation: int32 [2], replicated, may hold values from 1 to 8, as said below
Outputs:
- out_frames: bfloat16 [64, 32, 64, 256], P('tm', 'space')
- in_grad: bfloat16 [64, 32, 64, 256], P('tm', 'space')
- spatial_grad: float32 [3, 3, 256, 256], replicated
- temporal_grad: float32 [3, 256, 256], replicated
The draws below stay inside these ranges and needn't reach their ends.
Inputs may be any that keep to these rules, and one draw needn't show every extreme that they name: `clip_frames`: the two clips are packed in order from slot 0 and fill at least 56 and at most 64 slots together; one of them has exactly 48 frames. One of the two clips has dilation 8.
All inputs are finite; a program needn't handle non-finite values.
Results may differ from the reference program's by a relative error of at most 0.0055.
Values may be sent and summed in bfloat16 or wider, within the bound.
No kernel may reach another device: no remote copies, remote signals or barrier semaphores. Data moves between devices by JAX's collectives and lax.ppermute only.
A program may use at most 128 MiB of HBM per device.

```python
import math
import jax
import jax.numpy as jnp
from jax import lax

C = 256
GROUPS = 32
H = 32
W = 64
DMAX = 8
FS = 8
SLOTS = 64


def draw_clip_frames(key, part):
    key = jax.random.fold_in(key, 7)
    short_key, coin_key = jax.random.split(key)
    lowest = SLOTS // 8
    longest = SLOTS - lowest - FS
    shorter = jax.random.randint(short_key, (), lowest, lowest + FS + 1)
    coin_flip = jax.random.randint(coin_key, (), 0, 2)
    longer = jnp.int32(longest)
    return jnp.where(coin_flip == 0, jnp.stack([longer, shorter]), jnp.stack([shorter, longer])).astype(jnp.int32)


def draw_dilation(key, part):
    key = jax.random.fold_in(key, 13)
    coin_key, second_key = jax.random.split(key)
    second = jax.random.randint(second_key, (), 1, DMAX + 1)
    coin_flip = jax.random.randint(coin_key, (), 0, 2)
    widest = jnp.int32(DMAX)
    return jnp.where(coin_flip == 0, jnp.stack([widest, second]), jnp.stack([second, widest])).astype(jnp.int32)


def levels(stream_key, shape, shards, least, largest):
    level, own = 1.0, jax.random.fold_in(stream_key, 6)
    for position, blocks in shards:
        steps = jnp.exp(jax.random.uniform(jax.random.fold_in(own, position), (blocks,), jnp.float32, least / len(shards), largest / len(shards)))
        level = level * jnp.repeat(steps, shape[position] // blocks).reshape([-1 if axis == position else 1 for axis in range(len(shape))])
    return level


def scatter_about(own_key, dims, width, reach, cuts=(), kind=jnp.bfloat16):
    gain = levels(own_key, dims, cuts, -0.22, 0.18) if cuts else 1.0
    values = jax.random.normal(own_key, dims, jnp.float32) * width * gain
    return jnp.minimum(jnp.maximum(values, -reach), reach).astype(kind)


def setup_inputs(seed: int = 0) -> dict:
    arg_keys = jax.random.split(jax.random.key(seed), 9)
    frames_in = scatter_about(arg_keys[0], (SLOTS, H, W, C), 1.0, 6.0, ((0, 8), (1, 4)))
    cotangent = scatter_about(arg_keys[1], (SLOTS, H, W, C), 1.0, 6.0, ((0, 8), (1, 4)))
    spatial = scatter_about(arg_keys[2], (3, 3, C, C), (9 * C) ** -0.5, 0.125)
    temporal = scatter_about(arg_keys[3], (3, C, C), C ** -0.5, 0.375)
    norm_gain = jnp.clip(jnp.exp(jax.random.uniform(arg_keys[4], (C,), jnp.float32, math.log(0.5), math.log(2.0))), 0.5, 2.0)
    norm_shift = scatter_about(arg_keys[5], (C,), 0.5, 3.0, (), jnp.float32)
    clip_frames = draw_clip_frames(jax.random.fold_in(arg_keys[8], 71), 0)
    dilation = draw_dilation(jax.random.fold_in(arg_keys[8], 71), 0)
    return dict(frames_in=frames_in, cotangent=cotangent, spatial=spatial, temporal=temporal, norm_gain=norm_gain, norm_shift=norm_shift, clip_frames=clip_frames, dilation=dilation)


NORM_EPS = 1e-05

def slot_tables(frame_ids, clip_frames):
    filled = clip_frames[0] + clip_frames[1]
    usable = (frame_ids >= 0) & (frame_ids < filled)
    clip_ids = (frame_ids >= clip_frames[0]).astype(jnp.int32)
    return (usable, clip_ids)

def shifted_pieces(source, first_frame, out_first, frame_count, clip_frames, dilation, direction):
    frame_ids = out_first + jnp.arange(frame_count, dtype=jnp.int32)
    usable, clip_ids = slot_tables(frame_ids, clip_frames)
    results = []
    for tap_index in range(3):
        combined = jnp.zeros((frame_count,) + source.shape[1:], source.dtype)
        for which_clip in range(2):
            offset_val = direction * (tap_index - 1) * dilation[which_clip]
            target_ok, target_clip = slot_tables(frame_ids + offset_val, clip_frames)
            keep_mask = usable & target_ok & (clip_ids == which_clip) & (target_clip == which_clip)
            start_row = (out_first + offset_val - first_frame).astype(jnp.int32)
            shifted = lax.dynamic_slice_in_dim(source, start_row, frame_count, 0)
            combined = jnp.where(keep_mask[:, None, None], shifted, combined)
        results.append(combined)
    return results

def time_forward(act_src, first_frame, out_first, frame_count, clip_frames, dilation, temporal):
    pieces = shifted_pieces(act_src, first_frame, out_first, frame_count, clip_frames, dilation, 1)
    summed = jnp.zeros(pieces[0].shape, jnp.float32)
    for tap_index in range(3):
        summed = summed + jnp.dot(pieces[tap_index], temporal[tap_index], preferred_element_type=jnp.float32)
    return summed.astype(jnp.bfloat16)

def time_backward(act_src, grad_src, first_frame, out_first, frame_count, clip_frames, dilation, temporal):
    pieces_act = shifted_pieces(act_src, first_frame, out_first, frame_count, clip_frames, dilation, 1)
    pieces_grad = shifted_pieces(grad_src, first_frame, out_first, frame_count, clip_frames, dilation, -1)
    channels = grad_src.shape[-1]
    own_grad = lax.dynamic_slice_in_dim(grad_src, out_first - first_frame, frame_count, 0)
    flat_grad = own_grad.reshape(-1, channels)
    back_sum = jnp.zeros(pieces_grad[0].shape, jnp.float32)
    weight_terms = []
    for tap_index in range(3):
        back_sum = back_sum + lax.dot_general(pieces_grad[tap_index], temporal[tap_index], (((2,), (1,)), ((), ())), preferred_element_type=jnp.float32)
        weight_terms.append(lax.dot_general(pieces_act[tap_index].reshape(-1, channels), flat_grad, (((0,), (0,)), ((), ())), preferred_element_type=jnp.float32))
    return (back_sum.astype(jnp.bfloat16), jnp.stack(weight_terms))

def widen(padded):
    return jnp.pad(padded, ((0, 0), (0, 0), (1, 1), (0, 0)))

def spatial_forward(padded, spatial):
    row_count = padded.shape[1] - 2
    col_count = padded.shape[2]
    wide = widen(padded)
    summed = jnp.zeros((padded.shape[0], row_count, col_count, spatial.shape[3]), jnp.float32)
    for offset_row in range(3):
        for offset_col in range(3):
            window = wide[:, offset_row:offset_row + row_count, offset_col:offset_col + col_count, :]
            summed = summed + jnp.dot(window, spatial[offset_row, offset_col], preferred_element_type=jnp.float32)
    return summed

def spatial_backward(padded, spatial):
    row_count = padded.shape[1] - 2
    col_count = padded.shape[2]
    wide = widen(padded)
    summed = jnp.zeros((padded.shape[0], row_count, col_count, spatial.shape[2]), jnp.float32)
    for offset_row in range(3):
        for offset_col in range(3):
            window = wide[:, 2 - offset_row:2 - offset_row + row_count, 2 - offset_col:2 - offset_col + col_count, :]
            summed = summed + lax.dot_general(window, spatial[offset_row, offset_col], (((3,), (1,)), ((), ())), preferred_element_type=jnp.float32)
    return summed

def weight_grad(padded, grad_conv):
    row_count = padded.shape[1] - 2
    col_count = padded.shape[2]
    channels = grad_conv.shape[-1]
    wide = widen(padded)
    flat_grad = grad_conv.reshape(-1, channels)
    outer_rows = []
    for offset_row in range(3):
        inner_cols = []
        for offset_col in range(3):
            window = wide[:, offset_row:offset_row + row_count, offset_col:offset_col + col_count, :]
            inner_cols.append(lax.dot_general(window.reshape(-1, window.shape[-1]), flat_grad, (((0,), (0,)), ((), ())), preferred_element_type=jnp.float32))
        outer_rows.append(jnp.stack(inner_cols))
    return jnp.stack(outer_rows)

def group_fold(values):
    return values.reshape(values.shape[0], GROUPS, -1).sum(axis=2)

def spread_groups(values, group_size):
    return jnp.repeat(values, group_size, axis=-1)[:, None, None, :]

def normalize(conv_out, sum_first, sum_second, norm_gain, norm_shift, entries):
    group_size = conv_out.shape[-1] // GROUPS
    mean_val = sum_first / entries
    variance = sum_second / entries - mean_val * mean_val
    inv_std = lax.rsqrt(variance + NORM_EPS)
    inv_wide = spread_groups(inv_std, group_size)
    normed = (conv_out - spread_groups(mean_val, group_size)) * inv_wide
    shaped = normed * norm_gain + norm_shift
    return (normed, shaped, inv_wide)

def gradient_normed(grad_act, shaped, norm_gain):
    sigmoid_val = jax.nn.sigmoid(shaped)
    return grad_act.astype(jnp.float32) * sigmoid_val * (1.0 + shaped * (1.0 - sigmoid_val)) * norm_gain

def norm_backward(grad_normed, normed, inv_wide, mean_first, mean_second):
    group_size = grad_normed.shape[-1] // GROUPS
    result = inv_wide * (grad_normed - spread_groups(mean_first, group_size) - normed * spread_groups(mean_second, group_size))
    return result.astype(jnp.bfloat16)

def reference(frames_in, cotangent, spatial, temporal, norm_gain, norm_shift, clip_frames, dilation):
    slot_count, height, col_count, channels = frames_in.shape
    entries = height * col_count * (channels // GROUPS)
    row_pad = ((0, 0), (1, 1), (0, 0), (0, 0))

    def frame_norm(frame):
        padded = jnp.pad(frame[None], row_pad)
        conv_out = spatial_forward(padded, spatial)
        sums_first = group_fold(lax.optimization_barrier(jnp.sum(conv_out, axis=(1, 2))))
        sums_second = group_fold(lax.optimization_barrier(jnp.sum(conv_out * conv_out, axis=(1, 2))))
        normed, shaped, inv_wide = normalize(conv_out, sums_first, sums_second, norm_gain, norm_shift, entries)
        return (padded, normed, shaped, inv_wide)

    def front(frame):
        padded, normed, shaped, inv_wide = frame_norm(frame)
        return jax.nn.silu(shaped)[0].astype(jnp.bfloat16)
    silu_frames = lax.map(front, frames_in)
    usable, clip_ids = slot_tables(jnp.arange(slot_count, dtype=jnp.int32), clip_frames)
    activation = jnp.where(usable[:, None, None, None], silu_frames, jnp.zeros_like(silu_frames))
    activation = activation.reshape(slot_count, height * col_count, channels)
    grad_rows = cotangent.reshape(slot_count, height * col_count, channels)
    pad_spec = ((DMAX, DMAX), (0, 0), (0, 0))
    act_src = jnp.pad(activation, pad_spec)
    grad_src = jnp.pad(grad_rows, pad_spec)
    temporal_out = time_forward(act_src, -DMAX, 0, slot_count, clip_frames, dilation, temporal)
    grad_act, temporal_grad = time_backward(act_src, grad_src, -DMAX, 0, slot_count, clip_frames, dilation, temporal)
    out_frames = (frames_in.astype(jnp.float32) + temporal_out.reshape(frames_in.shape).astype(jnp.float32)).astype(jnp.bfloat16)
    grad_act = grad_act.reshape(frames_in.shape)

    def back(carry, items):
        frame, grad_frame, cot_frame = items
        padded, normed, shaped, inv_wide = frame_norm(frame)
        grad_normed = gradient_normed(grad_frame[None], shaped, norm_gain)
        mean_first = group_fold(lax.optimization_barrier(jnp.sum(grad_normed, axis=(1, 2)))) / entries
        mean_second = group_fold(lax.optimization_barrier(jnp.sum(grad_normed * normed, axis=(1, 2)))) / entries
        grad_conv = norm_backward(grad_normed, normed, inv_wide, mean_first, mean_second)
        conv_pad = jnp.pad(grad_conv, row_pad)
        in_frame = (cot_frame[None].astype(jnp.float32) + spatial_backward(conv_pad, spatial)).astype(jnp.bfloat16)
        return (carry + weight_grad(padded, grad_conv), in_frame[0])
    spatial_grad, in_grad = lax.scan(back, jnp.zeros(spatial.shape, jnp.float32), (frames_in, grad_act, cotangent))
    return (out_frames, in_grad, spatial_grad, temporal_grad)
```

```python
import functools

import jax
import jax.numpy as jnp
from jax import lax
from jax.experimental import pallas as pl
from jax.experimental.pallas import tpu as pltpu
from jax.sharding import PartitionSpec as P

GROUPS = 32
NORM_EPS = 1e-05
BF16 = jnp.bfloat16
F32 = jnp.float32
VMEM_LIMIT = 48 * 2**20


def params():
    return pltpu.CompilerParams(
        vmem_limit_bytes=VMEM_LIMIT, dimension_semantics=("arbitrary",)
    )


def cost(flops, moved, exps=0):
    return pl.CostEstimate(flops=int(flops), bytes_accessed=int(moved), transcendentals=int(exps))


def dot(a, b):
    return jnp.dot(a, b, preferred_element_type=F32)


def dot_rows(a, b):
    return lax.dot_general(a, b, (((0,), (0,)), ((), ())), preferred_element_type=F32)


def group_total(row, group_size):
    channels = row.shape[-1]
    lane = lax.broadcasted_iota(jnp.int32, row.shape, 1)
    step = 1
    while step < group_size:
        up = pltpu.roll(row, channels - step, axis=1)
        down = pltpu.roll(row, step, axis=1)
        row = row + jnp.where((lane & step) == 0, up, down)
        step *= 2
    return row


def frame_stats(part_refs, entries, group_size):
    total = part_refs[0][0]
    for ref in part_refs[1:]:
        total = total + ref[0]
    return group_total(total, group_size) / entries


def mean_and_inv(part_refs, entries, group_size):
    both = frame_stats(part_refs, entries, group_size)
    mean = both[0:1]
    inv = lax.rsqrt(both[1:2] - mean * mean + NORM_EPS)
    return mean, inv


def column_sums(first, second, out_ref):
    out_ref[0, 0:1, :] = jnp.sum(first, axis=0, keepdims=True)
    out_ref[0, 1:2, :] = jnp.sum(second, axis=0, keepdims=True)


def with_halo(above_ref, mid, below_ref):
    width, channels = above_ref.shape[-2:]
    return jnp.concatenate(
        [above_ref[...].reshape(width, channels), mid, below_ref[...].reshape(width, channels)],
        axis=0,
    )


def from_left(y, width):
    col = lax.broadcasted_iota(jnp.int32, y.shape, 0) & (width - 1)
    return jnp.where(col == 0, 0.0, pltpu.roll(y, 1, axis=0))


def from_right(y, width):
    col = lax.broadcasted_iota(jnp.int32, y.shape, 0) & (width - 1)
    return jnp.where(col == width - 1, 0.0, pltpu.roll(y, y.shape[0] - 1, axis=0))


def conv_kernel(x_ref, above_ref, below_ref, w_ref, out_ref, sums_ref):
    _, rows, width, channels = x_ref.shape
    pixels = rows * width
    padded = with_halo(above_ref, x_ref[...].reshape(pixels, channels), below_ref)
    lhs = jnp.concatenate([padded[i * width : i * width + pixels] for i in range(3)], axis=1)
    y = [dot(lhs, w_ref[:, j].reshape(3 * channels, channels)) for j in range(3)]
    out = y[1] + from_left(y[0], width) + from_right(y[2], width)
    out_ref[0] = out
    column_sums(out, out * out, sums_ref)


def act_kernel(n, entries, group_size, info_ref, *refs):
    parts, (conv_ref, gain_ref, shift_ref, act_ref) = refs[:n], refs[n:]
    mean, inv = mean_and_inv(parts, entries, group_size)
    shaped = (conv_ref[0] - mean) * inv * gain_ref[...] + shift_ref[...]
    used = info_ref[pl.program_id(0), 6] > 0
    act_ref[0] = jnp.where(used, shaped * jax.nn.sigmoid(shaped), 0.0).astype(BF16)


def gather_taps(info_ref, own_up, nxt, mid, own_dn, prv, cat_ref, up_slot):
    frame = pl.program_id(0)
    channels = mid.shape[-1]
    dn_slot = 2 - up_slot

    def put(slot, ref):
        cat_ref[:, slot * channels : (slot + 1) * channels] = ref[0]

    def clear(slot):
        cat_ref[:, slot * channels : (slot + 1) * channels] = jnp.zeros(
            (cat_ref.shape[0], channels), cat_ref.dtype
        )

    for slot, which, own, other in ((up_slot, info_ref[frame, 2], own_up, nxt), (dn_slot, info_ref[frame, 5], own_dn, prv)):
        pl.when(which == 1)(functools.partial(put, slot, own))
        pl.when(which == 2)(functools.partial(put, slot, other))
        pl.when(which == 0)(functools.partial(clear, slot))
    used = info_ref[frame, 6]
    pl.when(used == 1)(functools.partial(put, 1, mid))
    pl.when(used == 0)(functools.partial(clear, 1))


def grad_act_kernel(
    n, entries, group_size, info_ref, own_up, nxt, mid, own_dn, prv, tw_ref, conv_ref, gain_ref, shift_ref, *rest
):
    parts, (gn_ref, sums_ref, cat_ref) = rest[:n], rest[n:]
    gather_taps(info_ref, own_up, nxt, mid, own_dn, prv, cat_ref, 0)
    grad_act = dot(cat_ref[...], tw_ref[...]).astype(BF16).astype(F32)
    mean, inv = mean_and_inv(parts, entries, group_size)
    normed = (conv_ref[0] - mean) * inv
    shaped = normed * gain_ref[...] + shift_ref[...]
    sig = jax.nn.sigmoid(shaped)
    gn = grad_act * sig * (1.0 + shaped * (1.0 - sig)) * gain_ref[...]
    gn_ref[0] = gn
    column_sums(gn, gn * normed, sums_ref)


def temporal_grad_kernel(info_ref, own_up, nxt, mid, own_dn, prv, act_ref, out_ref, cat_ref):
    channels = act_ref.shape[-1]
    gather_taps(info_ref, own_up, nxt, mid, own_dn, prv, cat_ref, 0)
    part = dot_rows(act_ref[0], cat_ref[...])

    @pl.when(pl.program_id(0) == 0)
    def _():
        out_ref[...] = jnp.zeros_like(out_ref)

    for k in range(3):
        out_ref[k] += part[:, k * channels : (k + 1) * channels]


def weight_grad_kernel(
    n, entries, group_size, x_ref, above_ref, below_ref, conv_ref, gn_ref, *refs
):
    parts, grad_parts, (g_ref, first_ref, last_ref, out_ref) = refs[:n], refs[n : 2 * n], refs[2 * n :]
    _, rows, width, channels = x_ref.shape
    pixels = rows * width
    mean, inv = mean_and_inv(parts, entries, group_size)
    means = frame_stats(grad_parts, entries, group_size)
    normed = (conv_ref[0] - mean) * inv
    grad = (inv * (gn_ref[0] - means[0:1] - normed * means[1:2])).astype(BF16)
    g_ref[0] = grad
    first_ref[0] = grad[:width]
    last_ref[0] = grad[pixels - width :]
    wide = grad.astype(F32)
    moved = jnp.concatenate(
        [from_right(wide, width).astype(BF16), grad, from_left(wide, width).astype(BF16)], axis=1
    )
    padded = with_halo(above_ref, x_ref[...].reshape(pixels, channels), below_ref)

    @pl.when(pl.program_id(0) == 0)
    def _():
        out_ref[...] = jnp.zeros_like(out_ref)

    for i in range(3):
        part = dot_rows(padded[i * width : i * width + pixels], moved)
        for j in range(3):
            out_ref[i, j] += part[:, j * channels : (j + 1) * channels]


def conv_back_kernel(g_ref, above_ref, below_ref, cot_ref, w_ref, out_ref):
    _, rows, width, channels = cot_ref.shape
    pixels = rows * width
    padded = with_halo(above_ref, g_ref[0], below_ref)
    lhs = jnp.concatenate([padded[(2 - i) * width : (2 - i) * width + pixels] for i in range(3)], axis=1)
    z = [dot(lhs, w_ref[j]) for j in range(3)]
    out = z[1] + from_right(z[0], width) + from_left(z[2], width)
    out = out + cot_ref[...].reshape(pixels, channels).astype(F32)
    out_ref[...] = out.astype(BF16).reshape(out_ref.shape)


def out_kernel(info_ref, own_up, nxt, mid, own_dn, prv, tw_ref, x_ref, out_ref, cat_ref):
    gather_taps(info_ref, own_up, nxt, mid, own_dn, prv, cat_ref, 2)
    _, rows, width, channels = x_ref.shape
    temporal_out = dot(cat_ref[...], tw_ref[...]).astype(BF16).astype(F32)
    out = x_ref[...].reshape(rows * width, channels).astype(F32) + temporal_out
    out_ref[...] = out.astype(BF16).reshape(out_ref.shape)


def neighbours(axis, low, high):
    size = lax.axis_size(axis)
    up = [(i, i + 1) for i in range(size - 1)]
    down = [(j, i) for i, j in up]
    return lax.ppermute(high, axis, up), lax.ppermute(low, axis, down)


def spread_parts(part, axis):
    size = lax.axis_size(axis)
    return [part] + [
        lax.ppermute(part, axis, [(i, (i + s) % size) for i in range(size)]) for s in range(1, size)
    ]


def halve(x, axis, bit):
    size = lax.axis_size(axis)
    mine = (lax.axis_index(axis) >> bit) & 1
    half = x.shape[0] // 2
    send = lax.dynamic_slice_in_dim(x, (1 - mine) * half, half, 0).astype(BF16)
    keep = lax.dynamic_slice_in_dim(x, mine * half, half, 0)
    got = lax.ppermute(send, axis, [(i, i ^ (1 << bit)) for i in range(size)])
    return keep + got.astype(F32)


def double(x, axis, bit):
    size = lax.axis_size(axis)
    mine = (lax.axis_index(axis) >> bit) & 1
    got = lax.ppermute(x, axis, [(i, i ^ (1 << bit)) for i in range(size)])
    return jnp.concatenate([jnp.where(mine == 1, got, x), jnp.where(mine == 1, x, got)], axis=0)


def sum_everywhere(x):
    bits = [("tm", b) for b in range(1, lax.axis_size("tm").bit_length() - 1)]
    deep = [("space", b) for b in range(lax.axis_size("space").bit_length() - 1)]
    x = halve(x, "tm", 0)
    half = x.shape[0] // 2
    orders = [bits + deep, bits[::-1] + deep]
    pieces = [x[:half], x[half:]]
    for step in range(len(orders[0])):
        pieces = [halve(p, *order[step]) for p, order in zip(pieces, orders)]
    pieces = [p.astype(BF16) for p in pieces]
    for step in range(len(orders[0]) - 1, -1, -1):
        pieces = [double(p, *order[step]) for p, order in zip(pieces, orders)]
    return double(jnp.concatenate(pieces, axis=0), "tm", 0)


def slot_info(frames, clip_frames, dilation):
    first = lax.axis_index("tm") * frames
    local = jnp.arange(frames, dtype=jnp.int32)
    ids = first + local
    filled = clip_frames[0] + clip_frames[1]

    def clip_of(f):
        return (f >= clip_frames[0]).astype(jnp.int32)

    used = (ids >= 0) & (ids < filled)
    d = jnp.where(clip_of(ids) == 0, dilation[0], dilation[1])

    def live(g):
        return used & (g >= 0) & (g < filled) & (clip_of(g) == clip_of(ids))

    up, dn = local + d, local - d
    up_which = jnp.where(live(ids + d), jnp.where(up < frames, 1, 2), 0)
    dn_which = jnp.where(live(ids - d), jnp.where(dn >= 0, 1, 2), 0)
    last = frames - 1
    columns = [
        jnp.clip(up, 0, last),
        jnp.clip(up - frames, 0, last),
        up_which,
        jnp.clip(dn, 0, last),
        jnp.clip(dn + frames, 0, last),
        dn_which,
        used.astype(jnp.int32),
    ]
    return jnp.stack(columns, axis=1).astype(jnp.int32)


def per_device(frames_in, cotangent, spatial, temporal, norm_gain, norm_shift, clip_frames, dilation):
    frames, rows, width, channels = frames_in.shape
    pixels = rows * width
    n = lax.axis_size("space")
    group_size = channels // GROUPS
    entries = float(rows * n * width * group_size)
    gain, shift = norm_gain[None], norm_shift[None]
    info = slot_info(frames, clip_frames, dilation)
    big = frames * pixels * channels

    x_spec = pl.BlockSpec((1, rows, width, channels), lambda f, *_: (f, 0, 0, 0))
    edge_spec = pl.BlockSpec((1, 1, width, channels), lambda f, *_: (f, 0, 0, 0))
    row_spec = pl.BlockSpec((1, width, channels), lambda f, *_: (f, 0, 0))
    px_spec = pl.BlockSpec((1, pixels, channels), lambda f, *_: (f, 0, 0))
    sum_spec = pl.BlockSpec((1, 2, channels), lambda f, *_: (f, 0, 0))
    chan_spec = pl.BlockSpec((1, channels), lambda f, *_: (0, 0))

    def whole(*dims):
        return pl.BlockSpec(dims, lambda f, *_: (0,) * len(dims))

    def picked(column):
        return pl.BlockSpec((1, pixels, channels), lambda f, info: (info[f, column], 0, 0))

    taps = [picked(0), picked(1), px_spec, picked(3), picked(4)]
    cat = pltpu.VMEM((pixels, 3 * channels), BF16)
    shape = jax.ShapeDtypeStruct

    above, below = neighbours("space", frames_in[:, :1], frames_in[:, rows - 1 :])
    cot = cotangent.reshape(frames, pixels, channels)
    cot_prev, cot_next = neighbours("tm", cot, cot)

    conv_out, sums = pl.pallas_call(
        conv_kernel,
        grid=(frames,),
        in_specs=[x_spec, edge_spec, edge_spec, whole(3, 3, channels, channels)],
        out_specs=[px_spec, sum_spec],
        out_shape=[shape((frames, pixels, channels), F32), shape((frames, 2, channels), F32)],
        compiler_params=params(),
        cost_estimate=cost(18 * big * channels, 6 * big),
        name="conv_forward",
    )(frames_in, above, below, spatial)
    parts = spread_parts(sums, "space")

    act = pl.pallas_call(
        functools.partial(act_kernel, n, entries, group_size),
        grid_spec=pltpu.PrefetchScalarGridSpec(
            num_scalar_prefetch=1,
            grid=(frames,),
            in_specs=[sum_spec] * n + [px_spec, chan_spec, chan_spec],
            out_specs=px_spec,
        ),
        out_shape=shape((frames, pixels, channels), BF16),
        compiler_params=params(),
        cost_estimate=cost(10 * big, 6 * big, 2 * big),
        name="activation",
    )(info, *parts, conv_out, gain, shift)
    act_prev, act_next = neighbours("tm", act, act)

    grad_normed, grad_sums = pl.pallas_call(
        functools.partial(grad_act_kernel, n, entries, group_size),
        grid_spec=pltpu.PrefetchScalarGridSpec(
            num_scalar_prefetch=1,
            grid=(frames,),
            in_specs=taps + [whole(3 * channels, channels), px_spec, chan_spec, chan_spec] + [sum_spec] * n,
            out_specs=[px_spec, sum_spec],
            scratch_shapes=[cat],
        ),
        out_shape=[shape((frames, pixels, channels), F32), shape((frames, 2, channels), F32)],
        compiler_params=params(),
        cost_estimate=cost(6 * big * channels, 16 * big, 2 * big),
        name="grad_activation",
    )(
        info, cot, cot_next, cot, cot, cot_prev,
        temporal.transpose(0, 2, 1).reshape(3 * channels, channels), conv_out, gain, shift, *parts,
    )
    grad_parts = spread_parts(grad_sums, "space")

    temporal_part = pl.pallas_call(
        temporal_grad_kernel,
        grid_spec=pltpu.PrefetchScalarGridSpec(
            num_scalar_prefetch=1,
            grid=(frames,),
            in_specs=taps + [px_spec],
            out_specs=whole(3, channels, channels),
            scratch_shapes=[cat],
        ),
        out_shape=shape((3, channels, channels), F32),
        compiler_params=params(),
        cost_estimate=cost(6 * big * channels, 8 * big),
        name="temporal_grad",
    )(info, cot, cot_next, cot, cot, cot_prev, act)

    grad_conv, first_rows, last_rows, spatial_part = pl.pallas_call(
        functools.partial(weight_grad_kernel, n, entries, group_size),
        grid=(frames,),
        in_specs=[x_spec, edge_spec, edge_spec, px_spec, px_spec] + [sum_spec] * (2 * n),
        out_specs=[px_spec, row_spec, row_spec, whole(3, 3, channels, channels)],
        out_shape=[
            shape((frames, pixels, channels), BF16),
            shape((frames, width, channels), BF16),
            shape((frames, width, channels), BF16),
            shape((3, 3, channels, channels), F32),
        ],
        compiler_params=params(),
        cost_estimate=cost(18 * big * channels, 12 * big),
        name="weight_grad",
    )(frames_in, above, below, conv_out, grad_normed, *parts, *grad_parts)

    grad_above, grad_below = neighbours("space", first_rows, last_rows)
    back_weights = spatial.transpose(1, 0, 3, 2).reshape(3, 3 * channels, channels)
    in_grad = pl.pallas_call(
        conv_back_kernel,
        grid=(frames,),
        in_specs=[px_spec, row_spec, row_spec, x_spec, whole(3, 3 * channels, channels)],
        out_specs=x_spec,
        out_shape=shape(frames_in.shape, BF16),
        compiler_params=params(),
        cost_estimate=cost(18 * big * channels, 6 * big),
        name="conv_backward",
    )(grad_conv, grad_above, grad_below, cotangent, back_weights)

    out_frames = pl.pallas_call(
        out_kernel,
        grid_spec=pltpu.PrefetchScalarGridSpec(
            num_scalar_prefetch=1,
            grid=(frames,),
            in_specs=taps + [whole(3 * channels, channels), x_spec],
            out_specs=x_spec,
            scratch_shapes=[cat],
        ),
        out_shape=shape(frames_in.shape, BF16),
        compiler_params=params(),
        cost_estimate=cost(6 * big * channels, 10 * big),
        name="temporal_forward",
    )(info, act, act_next, act, act, act_prev, temporal.reshape(3 * channels, channels), frames_in)

    stacked = jnp.concatenate([spatial_part.reshape(-1, channels), temporal_part.reshape(-1, channels)], axis=0)
    total = sum_everywhere(stacked).astype(F32)
    split = 9 * channels
    spatial_grad = total[:split].reshape(spatial.shape)
    temporal_grad = total[split:].reshape(temporal.shape)
    return (out_frames, in_grad, spatial_grad, temporal_grad)


def solution(mesh):
    tiles = P("tm", "space", None, None)
    return jax.shard_map(
        per_device,
        mesh=mesh,
        in_specs=(tiles, tiles, P(), P(), P(), P(), P(), P()),
        out_specs=(tiles, tiles, P(), P()),
        check_vma=False,
    )
```

```python
import functools

import jax
import jax.numpy as jnp
from jax import lax
from jax.experimental import pallas as pl
from jax.experimental.pallas import tpu as pltpu
from jax.sharding import PartitionSpec as P

GROUPS = 32
NORM_EPS = 1e-05
BF16 = jnp.bfloat16
F32 = jnp.float32
VMEM_LIMIT = 24 * 2**20


def params():
    return pltpu.CompilerParams(
        vmem_limit_bytes=VMEM_LIMIT, dimension_semantics=("arbitrary",)
    )


def light():
    return pl.CostEstimate(flops=1000, bytes_accessed=1000, transcendentals=0)


def dot(a, b):
    return jnp.dot(a, b, preferred_element_type=F32)


def dot_rows(a, b):
    return lax.dot_general(a, b, (((0,), (0,)), ((), ())), preferred_element_type=F32)


def group_total(row, group_size):
    channels = row.shape[-1]
    lane = lax.broadcasted_iota(jnp.int32, row.shape, 1)
    step = 1
    while step < group_size:
        up = pltpu.roll(row, channels - step, axis=1)
        down = pltpu.roll(row, step, axis=1)
        row = row + jnp.where((lane & step) == 0, up, down)
        step *= 2
    return row


def frame_stats(part_refs, b, entries, group_size):
    total = part_refs[0][b]
    for ref in part_refs[1:]:
        total = total + ref[b]
    return group_total(total, group_size) / entries


def sigmoid(x):
    return 0.5 * jnp.tanh(0.5 * x) + 0.5


def mean_and_inv(part_refs, b, entries, group_size):
    both = frame_stats(part_refs, b, entries, group_size)
    mean = both[0:1]
    inv = lax.rsqrt(both[1:2] - mean * mean + NORM_EPS)
    return mean, inv


def column_sums(first, second, out_ref, b=0):
    out_ref[b, 0:1, :] = jnp.sum(first, axis=0, keepdims=True)
    out_ref[b, 1:2, :] = jnp.sum(second, axis=0, keepdims=True)


def with_halo(above_ref, mid, below_ref):
    width, channels = above_ref.shape[-2:]
    return jnp.concatenate(
        [above_ref[...].reshape(width, channels), mid, below_ref[...].reshape(width, channels)],
        axis=0,
    )


def from_left(y, width):
    col = lax.broadcasted_iota(jnp.int32, y.shape, 0) & (width - 1)
    return jnp.where(col == 0, 0.0, pltpu.roll(y, 1, axis=0))


def from_right(y, width):
    col = lax.broadcasted_iota(jnp.int32, y.shape, 0) & (width - 1)
    return jnp.where(col == width - 1, 0.0, pltpu.roll(y, y.shape[0] - 1, axis=0))


def slot_sources(clip_ref, dil_ref, first, local, frames):
    slot = first + local
    start1 = clip_ref[0]
    filled = start1 + clip_ref[1]
    in_first = slot < start1
    d = jnp.where(in_first, dil_ref[0], dil_ref[1])
    low = jnp.where(in_first, 0, start1)
    high = jnp.where(in_first, start1, filled)
    used = slot < filled
    later, earlier = local + d, local - d
    later_live = used & (slot + d < high)
    earlier_live = used & (slot - d >= low)
    later_which = jnp.where(later_live, jnp.where(later < frames, 1, 2), 0)
    earlier_which = jnp.where(earlier_live, jnp.where(earlier >= 0, 1, 2), 0)
    return (later, later_which), (earlier, earlier_which), used


def conv_kernel(x_ref, above_ref, below_ref, w_ref, out_ref, sums_ref):
    _, rows, width, channels = x_ref.shape
    pixels = rows * width
    padded = with_halo(above_ref, x_ref[...].reshape(pixels, channels), below_ref)
    lhs = jnp.concatenate([padded[i * width : i * width + pixels] for i in range(3)], axis=1)
    y = [dot(lhs, w_ref[:, j].reshape(3 * channels, channels)) for j in range(3)]
    out = y[1] + from_left(y[0], width) + from_right(y[2], width)
    out_ref[0] = out
    column_sums(out, out * out, sums_ref)


def act_kernel(n, entries, group_size, first_ref, clip_ref, dil_ref, *refs):
    parts, (conv_ref, gain_ref, shift_ref, act_ref, normed_ref, slope_ref) = refs[:n], refs[n:]
    step = conv_ref.shape[0]
    for b in range(step):
        mean, inv = mean_and_inv(parts, b, entries, group_size)
        normed = (conv_ref[b] - mean) * inv
        shaped = normed * gain_ref[...] + shift_ref[...]
        sig = sigmoid(shaped)
        slot = first_ref[0] + pl.program_id(0) * step + b
        used = slot < clip_ref[0] + clip_ref[1]
        act_ref[b] = jnp.where(used, shaped * sig, 0.0).astype(BF16)
        normed_ref[b] = normed
        slope_ref[b] = sig * (1.0 + shaped * (1.0 - sig)) * gain_ref[...]


def transpose_kernel(x_ref, above_ref, below_ref, out_ref):
    step, rows, width, channels = x_ref.shape
    pixels = rows * width
    for b in range(step):
        padded = with_halo(above_ref.at[b], x_ref[b].reshape(pixels, channels), below_ref.at[b])
        for i in range(3):
            out_ref[i, :, b * pixels : (b + 1) * pixels] = padded[i * width : i * width + pixels].T


def gather_taps(frames, scalars, own_up, nxt_a, nxt_b, mid, own_dn, prv_a, prv_b, cat_ref, up_slot):
    first_ref, clip_ref, dil_ref = scalars
    later, earlier, used = slot_sources(clip_ref, dil_ref, first_ref[0], pl.program_id(0), frames)
    channels = mid.shape[-1]
    half = frames // 2

    def put(slot, ref):
        cat_ref[:, slot * channels : (slot + 1) * channels] = ref[0]

    def clear(slot):
        cat_ref[:, slot * channels : (slot + 1) * channels] = jnp.zeros(
            (cat_ref.shape[0], channels), cat_ref.dtype
        )

    for slot, (index, which), own, low, high, shift in (
        (up_slot, later, own_up, nxt_a, nxt_b, -frames),
        (2 - up_slot, earlier, own_dn, prv_a, prv_b, frames),
    ):
        in_low = index + shift < half
        pl.when(which == 1)(functools.partial(put, slot, own))
        pl.when((which == 2) & in_low)(functools.partial(put, slot, low))
        pl.when((which == 2) & jnp.logical_not(in_low))(functools.partial(put, slot, high))
        pl.when(which == 0)(functools.partial(clear, slot))
    pl.when(used)(functools.partial(put, 1, mid))
    pl.when(jnp.logical_not(used))(functools.partial(clear, 1))


def grad_act_kernel(frames, *refs):
    scalars, taps = refs[:3], refs[3:10]
    tw_ref, normed_ref, slope_ref, gn_ref, sums_ref, cat_ref = refs[10:]
    gather_taps(frames, scalars, *taps, cat_ref, 0)
    grad_act = dot(cat_ref[...], tw_ref[...]).astype(BF16).astype(F32)
    gn = grad_act * slope_ref[0]
    gn_ref[0] = gn
    column_sums(gn, gn * normed_ref[0], sums_ref)


def temporal_grad_kernel(frames, *refs):
    scalars, taps = refs[:3], refs[3:10]
    act_ref, out_ref, cat_ref = refs[10:]
    channels = act_ref.shape[-1]
    gather_taps(frames, scalars, *taps, cat_ref, 0)
    part = dot_rows(act_ref[0], cat_ref[...])

    @pl.when(pl.program_id(0) == 0)
    def _():
        out_ref[...] = jnp.zeros_like(out_ref)

    for k in range(3):
        out_ref[k] += part[:, k * channels : (k + 1) * channels]


def weight_grad_kernel(n, entries, group_size, core_ref, xt_ref, normed_ref, gn_ref, temporal_ref, *refs):
    parts, grad_parts = refs[:n], refs[n : 2 * n]
    g_ref, first_ref, last_ref, send_ref, keep_ref, moved_ref, acc_ref = refs[2 * n :]
    step, pixels, channels = normed_ref.shape
    width = first_ref.shape[1]
    for b in range(step):
        _, inv = mean_and_inv(parts, b, entries, group_size)
        means = frame_stats(grad_parts, b, entries, group_size)
        wide = inv * (gn_ref[b] - means[0:1] - normed_ref[b] * means[1:2])
        grad = wide.astype(BF16)
        g_ref[b] = grad
        first_ref[b] = grad[:width]
        last_ref[b] = grad[pixels - width :]
        here = slice(b * pixels, (b + 1) * pixels)
        moved_ref[here, :channels] = from_right(wide, width).astype(BF16)
        moved_ref[here, channels : 2 * channels] = grad
        moved_ref[here, 2 * channels :] = from_left(wide, width).astype(BF16)

    at = pl.program_id(0)
    for i in range(3):
        part = dot(xt_ref[i], moved_ref[...])

        @pl.when(at == 0)
        def _():
            acc_ref[i] = part

        @pl.when(at > 0)
        def _():
            acc_ref[i] += part

    @pl.when(at == pl.num_programs(0) - 1)
    def _():
        half = channels // 2
        kept = pl.multiple_of(core_ref[0] * half, half)
        sent = pl.multiple_of((1 - core_ref[0]) * half, half)
        for i in range(3):
            for j in range(3):
                lanes = slice(j * channels, (j + 1) * channels)
                keep_ref[3 * i + j] = acc_ref[i, pl.ds(kept, half), lanes]
                send_ref[3 * i + j] = acc_ref[i, pl.ds(sent, half), lanes].astype(BF16)
        for k in range(3):
            keep_ref[9 + k] = temporal_ref[k, pl.ds(kept, half), :]
            send_ref[9 + k] = temporal_ref[k, pl.ds(sent, half), :].astype(BF16)


def conv_back_kernel(g_ref, above_ref, below_ref, cot_ref, w_ref, out_ref):
    _, rows, width, channels = cot_ref.shape
    pixels = rows * width
    padded = with_halo(above_ref, g_ref[0], below_ref)
    lhs = jnp.concatenate([padded[(2 - i) * width : (2 - i) * width + pixels] for i in range(3)], axis=1)
    z = [dot(lhs, w_ref[j]) for j in range(3)]
    out = z[1] + from_right(z[0], width) + from_left(z[2], width)
    out = out + cot_ref[...].reshape(pixels, channels).astype(F32)
    out_ref[...] = out.astype(BF16).reshape(out_ref.shape)


def out_kernel(frames, *refs):
    scalars, taps = refs[:3], refs[3:10]
    tw_ref, x_ref, out_ref, cat_ref = refs[10:]
    gather_taps(frames, scalars, *taps, cat_ref, 2)
    _, rows, width, channels = x_ref.shape
    temporal_out = dot(cat_ref[...], tw_ref[...]).astype(BF16).astype(F32)
    out = x_ref[...].reshape(rows * width, channels).astype(F32) + temporal_out
    out_ref[...] = out.astype(BF16).reshape(out_ref.shape)


def neighbours(axis, low, high):
    size = lax.axis_size(axis)
    up = [(i, i + 1) for i in range(size - 1)]
    down = [(j, i) for i, j in up]
    return lax.ppermute(high, axis, up), lax.ppermute(low, axis, down)


def frame_neighbours(x):
    size, frames = lax.axis_size("tm"), x.shape[0]
    low, high = x[: frames // 2], x[frames // 2 :]
    prev_low, next_low = neighbours("tm", low, low)
    if size != 8:
        prev_high, next_high = neighbours("tm", high, high)
        return (prev_low, prev_high), (next_low, next_high)
    relayed = lax.ppermute(high, "tm", [(3, 7), (4, 0)])
    me = lax.axis_index("tm")
    up = [(i, i + 1) for i in range(7) if i != 3] + [(7, 4)]
    down = [(i + 1, i) for i in range(7) if i != 3] + [(0, 3)]
    prev_high = lax.ppermute(jnp.where(me == 7, relayed, high), "tm", up)
    next_high = lax.ppermute(jnp.where(me == 0, relayed, high), "tm", down)
    return (prev_low, prev_high), (next_low, next_high)


def spread_parts(part, axis):
    size = lax.axis_size(axis)
    return [part] + [
        lax.ppermute(part, axis, [(i, (i + s) % size) for i in range(size)]) for s in range(1, size)
    ]


def scatter_sum(x, axis, me, count, pairs):
    block = x.shape[1] // count

    def take(k):
        return lax.dynamic_slice_in_dim(x, k * block, block, 1)

    total = take(me)
    got = [lax.ppermute(take(me ^ s).astype(BF16), axis, pairs(s)) for s in range(1, count)]
    for g in got:
        total = total + g.astype(F32)
    return total


def gather_blocks(x, axis, me, count, pairs):
    out = jnp.zeros((count,) + x.shape, x.dtype)
    got = [(me, x)] + [(me ^ s, lax.ppermute(x, axis, pairs(s))) for s in range(1, count)]
    for k, g in got:
        out = lax.dynamic_update_index_in_dim(out, g, k, 0)
    return out


def sum_everywhere(send, keep):
    tm, n = lax.axis_size("tm"), lax.axis_size("space")
    chips = tm // 2
    me = lax.axis_index("tm")
    core, chip, deep = me & 1, me >> 1, lax.axis_index("space")
    other_core = [(i, i ^ 1) for i in range(tm)]

    def in_plane(s):
        return [(i, i ^ (2 * s)) for i in range(tm)]

    def in_line(s):
        return [(i, i ^ s) for i in range(n)]

    x = keep + lax.ppermute(send, "tm", other_core).astype(F32)
    x = scatter_sum(x, "tm", chip, chips, in_plane)
    x = scatter_sum(x, "space", deep, n, in_line).astype(BF16)
    x = gather_blocks(x, "space", deep, n, in_line)
    x = gather_blocks(x, "tm", chip, chips, in_plane)
    got = lax.ppermute(x, "tm", other_core)
    both = jnp.stack([jnp.where(core == 0, x, got), jnp.where(core == 0, got, x)])
    tiles, channels = send.shape[0], send.shape[2]
    return both.transpose(3, 0, 1, 2, 4, 5).reshape(tiles, channels, channels).astype(F32)


def per_device(frames_in, cotangent, spatial, temporal, norm_gain, norm_shift, clip_frames, dilation):
    frames, rows, width, channels = frames_in.shape
    pixels = rows * width
    n = lax.axis_size("space")
    group_size = channels // GROUPS
    entries = float(rows * n * width * group_size)
    gain, shift = norm_gain[None], norm_shift[None]
    me = lax.axis_index("tm").astype(jnp.int32)
    scalars = ((me * frames)[None], clip_frames, dilation)
    half = frames // 2

    def per_frame(*dims, step=1):
        return pl.BlockSpec((step,) + dims, lambda f, *_: (f,) + (0,) * len(dims))

    def whole(*dims):
        return pl.BlockSpec(dims, lambda f, *_: (0,) * len(dims))

    x_spec, px_spec = per_frame(rows, width, channels), per_frame(pixels, channels)
    edge_spec, row_spec = per_frame(1, width, channels), per_frame(width, channels)
    sum_spec = per_frame(2, channels)
    chan_spec = whole(1, channels)

    def tap(side, which, low, count, offset):
        def index(f, first_ref, clip_ref, dil_ref):
            found = slot_sources(clip_ref, dil_ref, first_ref[0], f, frames)[side][0]
            return (jnp.clip(found + offset - low, 0, count - 1), 0, 0)

        return pl.BlockSpec((1, pixels, channels), index)

    taps = [
        tap(0, 1, 0, frames, 0), tap(0, 2, 0, half, -frames), tap(0, 2, half, half, -frames),
        px_spec,
        tap(1, 1, 0, frames, 0), tap(1, 2, 0, half, frames), tap(1, 2, half, half, frames),
    ]
    cat = pltpu.VMEM((pixels, 3 * channels), BF16)
    shape = jax.ShapeDtypeStruct

    def call(kernel, name, grid, in_specs, out_specs, out_shape, prefetch=0, scratch=()):
        return pl.pallas_call(
            kernel,
            grid_spec=pltpu.PrefetchScalarGridSpec(
                num_scalar_prefetch=prefetch,
                grid=(grid,),
                in_specs=in_specs,
                out_specs=out_specs,
                scratch_shapes=list(scratch),
            ),
            out_shape=out_shape,
            compiler_params=params(),
            cost_estimate=light(),
            name=name,
        )

    def around(mid, prev, nxt):
        return (mid, *nxt, mid, mid, *prev)

    above, below = neighbours("space", frames_in[:, :1], frames_in[:, rows - 1 :])
    cot = cotangent.reshape(frames, pixels, channels)
    cot_taps = around(cot, *frame_neighbours(cot))

    conv_out, sums = call(
        conv_kernel, "conv_forward", frames,
        [x_spec, edge_spec, edge_spec, whole(3, 3, channels, channels)],
        [px_spec, sum_spec],
        [shape((frames, pixels, channels), F32), shape((frames, 2, channels), F32)],
    )(frames_in, above, below, spatial)
    parts = spread_parts(sums, "space")

    pair_px, pair_sum = per_frame(pixels, channels, step=2), per_frame(2, channels, step=2)
    act, normed, slope = call(
        functools.partial(act_kernel, n, entries, group_size), "activation", frames // 2,
        [pair_sum] * n + [pair_px, chan_spec, chan_spec],
        [pair_px] * 3,
        [shape((frames, pixels, channels), t) for t in (BF16, F32, F32)],
        prefetch=3,
    )(*scalars, *parts, conv_out, gain, shift)
    act_taps = around(act, *frame_neighbours(act))

    pair_edge = per_frame(1, width, channels, step=2)
    x_turned = call(
        transpose_kernel, "turn_windows", frames // 2,
        [per_frame(rows, width, channels, step=2), pair_edge, pair_edge],
        pl.BlockSpec((3, channels, 2 * pixels), lambda f, *_: (0, 0, f)),
        shape((3, channels, frames * pixels), BF16),
    )(frames_in, above, below)

    grad_normed, grad_sums = call(
        functools.partial(grad_act_kernel, frames), "grad_activation", frames,
        taps + [whole(3 * channels, channels), px_spec, px_spec],
        [px_spec, sum_spec],
        [shape((frames, pixels, channels), F32), shape((frames, 2, channels), F32)],
        prefetch=3, scratch=[cat],
    )(*scalars, *cot_taps, temporal.transpose(0, 2, 1).reshape(3 * channels, channels), normed, slope)
    grad_parts = spread_parts(grad_sums, "space")

    temporal_part = call(
        functools.partial(temporal_grad_kernel, frames), "temporal_grad", frames,
        taps + [px_spec], whole(3, channels, channels), shape((3, channels, channels), F32),
        prefetch=3, scratch=[cat],
    )(*scalars, *cot_taps, act)

    halves = (12, channels // 2, channels)
    grad_conv, first_rows, last_rows, send, keep = call(
        functools.partial(weight_grad_kernel, n, entries, group_size), "weight_grad", frames // 2,
        [pl.BlockSpec((3, channels, 2 * pixels), lambda f, *_: (0, 0, f)), pair_px, pair_px, whole(3, channels, channels)]
        + [pair_sum] * (2 * n),
        [pair_px, per_frame(width, channels, step=2), per_frame(width, channels, step=2), whole(*halves), whole(*halves)],
        [
            shape((frames, pixels, channels), BF16),
            shape((frames, width, channels), BF16),
            shape((frames, width, channels), BF16),
            shape(halves, BF16),
            shape(halves, F32),
        ],
        prefetch=1,
        scratch=[pltpu.VMEM((2 * pixels, 3 * channels), BF16), pltpu.VMEM((3, channels, 3 * channels), F32)],
    )((me & 1)[None], x_turned, normed, grad_normed, temporal_part, *parts, *grad_parts)

    total = sum_everywhere(send, keep)

    grad_above, grad_below = neighbours("space", first_rows, last_rows)
    back_weights = spatial.transpose(1, 0, 3, 2).reshape(3, 3 * channels, channels)
    in_grad = call(
        conv_back_kernel, "conv_backward", frames,
        [px_spec, row_spec, row_spec, x_spec, whole(3, 3 * channels, channels)],
        x_spec, shape(frames_in.shape, BF16),
    )(grad_conv, grad_above, grad_below, cotangent, back_weights)

    out_frames = call(
        functools.partial(out_kernel, frames), "temporal_forward", frames,
        taps + [whole(3 * channels, channels), x_spec], x_spec, shape(frames_in.shape, BF16),
        prefetch=3, scratch=[cat],
    )(*scalars, *act_taps, temporal.reshape(3 * channels, channels), frames_in)

    return (out_frames, in_grad, total[:9].reshape(spatial.shape), total[9:])


def solution(mesh):
    tiles = P("tm", "space", None, None)
    return jax.shard_map(
        per_device,
        mesh=mesh,
        in_specs=(tiles, tiles, P(), P(), P(), P(), P(), P()),
        out_specs=(tiles, tiles, P(), P()),
        check_vma=False,
    )
```

```python
import functools

import jax
import jax.numpy as jnp
from jax import lax
from jax.experimental import pallas as pl
from jax.experimental.pallas import tpu as pltpu
from jax.sharding import PartitionSpec as P

GROUPS = 32
NORM_EPS = 1e-05
BF16 = jnp.bfloat16
F32 = jnp.float32
VMEM_LIMIT = 20 * 2**20


def call(kernel, name, operands, out_shape, flops=0, moved=0, scratch=()):
    vmem = pl.BlockSpec(memory_space=pltpu.VMEM)
    smem = pl.BlockSpec(memory_space=pltpu.SMEM)
    return pl.pallas_call(
        kernel,
        in_specs=[smem if x.dtype == jnp.int32 else vmem for x in operands],
        out_specs=jax.tree.map(lambda _: vmem, out_shape),
        out_shape=out_shape,
        scratch_shapes=list(scratch),
        compiler_params=pltpu.CompilerParams(vmem_limit_bytes=VMEM_LIMIT),
        cost_estimate=pl.CostEstimate(flops=int(flops), bytes_accessed=int(moved), transcendentals=0),
        name=name,
    )(*operands)


def dot(a, b):
    return jnp.dot(a, b, preferred_element_type=F32)


def dot_rows(a, b):
    return lax.dot_general(a, b, (((0,), (0,)), ((), ())), preferred_element_type=F32)


def group_total(row, group_size):
    channels = row.shape[-1]
    lane = lax.broadcasted_iota(jnp.int32, row.shape, 1)
    step = 1
    while step < group_size:
        up = pltpu.roll(row, channels - step, axis=1)
        down = pltpu.roll(row, step, axis=1)
        row = row + jnp.where((lane & step) == 0, up, down)
        step *= 2
    return row


def frame_stats(part_refs, f, entries, group_size):
    total = part_refs[0][f]
    for ref in part_refs[1:]:
        total = total + ref[f]
    return group_total(total, group_size) / entries


def sigmoid(x):
    return 0.5 * jnp.tanh(0.5 * x) + 0.5


def mean_and_inv(part_refs, f, entries, group_size):
    both = frame_stats(part_refs, f, entries, group_size)
    mean = both[0:1]
    inv = lax.rsqrt(both[1:2] - mean * mean + NORM_EPS)
    return mean, inv


def column_sums(first, second):
    return jnp.concatenate(
        [jnp.sum(first, axis=0, keepdims=True), jnp.sum(second, axis=0, keepdims=True)], axis=0
    )


def put_windows(above, mid, below, lhs_ref, at, order):
    width, (pixels, channels) = above.shape[0], mid.shape
    first, mid_at, last = (slice(k * channels, (k + 1) * channels) for k in order)
    lhs_ref[at : at + width, first] = above
    lhs_ref[at + width : at + pixels, first] = mid[: pixels - width]
    lhs_ref[at : at + pixels, mid_at] = mid
    lhs_ref[at : at + pixels - width, last] = mid[width:]
    lhs_ref[at + pixels - width : at + pixels, last] = below


def from_left(y, width):
    col = lax.broadcasted_iota(jnp.int32, y.shape, 0) & (width - 1)
    return jnp.where(col == 0, 0.0, pltpu.roll(y, 1, axis=0))


def from_right(y, width):
    col = lax.broadcasted_iota(jnp.int32, y.shape, 0) & (width - 1)
    return jnp.where(col == width - 1, 0.0, pltpu.roll(y, y.shape[0] - 1, axis=0))


def slot_sources(clip_ref, dil_ref, local, frames):
    slot = lax.axis_index("tm") * frames + local
    start1 = clip_ref[0]
    filled = start1 + clip_ref[1]
    in_first = slot < start1
    d = jnp.where(in_first, dil_ref[0], dil_ref[1])
    low = jnp.where(in_first, 0, start1)
    high = jnp.where(in_first, start1, filled)
    used = slot < filled
    later, earlier = local + d, local - d
    later_live = used & (slot + d < high)
    earlier_live = used & (slot - d >= low)
    later_which = jnp.where(later_live, jnp.where(later < frames, 1, 2), 0)
    earlier_which = jnp.where(earlier_live, jnp.where(earlier >= 0, 1, 2), 0)
    return (later, later_which), (earlier, earlier_which), used


def gather_taps(clip_ref, dil_ref, local, own, nxt, prv, corner, cat_ref, at, up_slot):
    frames, pixels, channels = own.shape
    later, earlier, used = slot_sources(clip_ref, dil_ref, local, frames)
    me, half = lax.axis_index("tm"), frames // 2

    def put(slot, ref, index):
        cat_ref[pl.ds(at, pixels), slot * channels : (slot + 1) * channels] = ref[index]

    def clear(slot):
        cat_ref[pl.ds(at, pixels), slot * channels : (slot + 1) * channels] = jnp.zeros((pixels, channels), BF16)

    for slot, (index, which), other, shift, turn in (
        (up_slot, later, nxt, -frames, 3),
        (2 - up_slot, earlier, prv, frames, 4),
    ):
        beyond = which == 2
        there = jnp.clip(index + shift, 0, frames - 1)
        pl.when(which == 1)(functools.partial(put, slot, own, jnp.clip(index, 0, frames - 1)))
        pl.when(which == 0)(functools.partial(clear, slot))
        if corner:
            by_corner = beyond & (me == turn)
            low, high = by_corner & (there < half), by_corner & (there >= half)
            pl.when(low)(functools.partial(put, slot, corner[0], jnp.minimum(there, half - 1)))
            pl.when(high)(functools.partial(put, slot, corner[1], jnp.maximum(there - half, 0)))
            beyond = beyond & (me != turn)
        pl.when(beyond)(functools.partial(put, slot, other, there))
    pl.when(used)(functools.partial(put, 1, own, local))
    pl.when(jnp.logical_not(used))(functools.partial(clear, 1))


def loop(count, body):
    def step(k, carry):
        body(k)
        return carry

    lax.fori_loop(0, count, step, 0)


def conv_kernel(x_ref, above_ref, below_ref, w_ref, out_ref, sums_ref, lhs_ref):
    frames, rows, width, channels = x_ref.shape
    pixels = rows * width

    def body(pair):
        for b in range(2):
            f = 2 * pair + b
            mid = x_ref[f].reshape(pixels, channels)
            put_windows(above_ref[f, 0], mid, below_ref[f, 0], lhs_ref, b * pixels, (0, 1, 2))
        lhs = lhs_ref[...]
        y = [dot(lhs, w_ref[:, j].reshape(3 * channels, channels)) for j in range(3)]
        out = y[1] + from_left(y[0], width) + from_right(y[2], width)
        for b in range(2):
            one = out[b * pixels : (b + 1) * pixels]
            out_ref[2 * pair + b] = one
            sums_ref[2 * pair + b] = column_sums(one, one * one)

    loop(frames // 2, body)


def act_kernel(n, entries, group_size, clip_ref, *refs):
    parts, (conv_ref, gain_ref, shift_ref, act_ref, normed_ref, slope_ref) = refs[:n], refs[n:]
    frames = conv_ref.shape[0]
    first = lax.axis_index("tm") * frames
    filled = clip_ref[0] + clip_ref[1]

    def body(f):
        mean, inv = mean_and_inv(parts, f, entries, group_size)
        normed = (conv_ref[f] - mean) * inv
        shaped = normed * gain_ref[...] + shift_ref[...]
        sig = sigmoid(shaped)
        act_ref[f] = jnp.where(first + f < filled, shaped * sig, 0.0).astype(BF16)
        normed_ref[f] = normed.astype(BF16)
        slope_ref[f] = (sig * (1.0 + shaped * (1.0 - sig)) * gain_ref[...]).astype(BF16)

    loop(frames, body)


def turn_kernel(x_ref, above_ref, below_ref, act_ref, xt_ref, at_ref, lhs_ref):
    frames, rows, width, channels = x_ref.shape
    pixels = rows * width

    def body(f):
        mid = x_ref[f].reshape(pixels, channels)
        put_windows(above_ref[f, 0], mid, below_ref[f, 0], lhs_ref, 0, (0, 1, 2))
        lanes = pl.ds(pl.multiple_of(f * pixels, pixels), pixels)
        for i in range(3):
            block = slice(i * channels, (i + 1) * channels)
            xt_ref[block, lanes] = lhs_ref[:, block].T
        at_ref[:, lanes] = act_ref[f].T

    loop(frames, body)


def grad_act_kernel(corners, clip_ref, dil_ref, own, nxt, prv, *refs):
    corner, (tw_ref, normed_ref, slope_ref, ga_ref, cat_ref, sums_ref) = refs[:corners], refs[corners:]
    frames, pixels, _ = own.shape

    def body(pair):
        rows = pl.ds(pl.multiple_of(2 * pair * pixels, 2 * pixels), 2 * pixels)
        for b in range(2):
            at = pl.multiple_of((2 * pair + b) * pixels, pixels)
            gather_taps(clip_ref, dil_ref, 2 * pair + b, own, nxt, prv, corner, cat_ref, at, 0)
        grad_act = dot(cat_ref[rows], tw_ref[...]).astype(BF16)
        for b in range(2):
            f = 2 * pair + b
            one = grad_act[b * pixels : (b + 1) * pixels]
            ga_ref[f] = one
            gn = one.astype(F32) * slope_ref[f].astype(F32)
            sums_ref[f] = column_sums(gn, gn * normed_ref[f].astype(F32))

    loop(frames // 2, body)


def temporal_grad_kernel(at_ref, cat_ref, out_ref):
    out_ref[...] = dot(at_ref[...], cat_ref[...])


def weight_grad_kernel(n, entries, group_size, xt_ref, normed_ref, slope_ref, ga_ref, temporal_ref, *refs):
    parts, grad_parts = refs[:n], refs[n : 2 * n]
    g_ref, first_ref, last_ref, send_ref, keep_ref, moved_ref, acc_ref = refs[2 * n :]
    frames, pixels, channels = normed_ref.shape
    width = first_ref.shape[2]

    def body(f):
        _, inv = mean_and_inv(parts, f, entries, group_size)
        means = frame_stats(grad_parts, f, entries, group_size)
        gn = ga_ref[f].astype(F32) * slope_ref[f].astype(F32)
        wide = inv * (gn - means[0:1] - normed_ref[f].astype(F32) * means[1:2])
        grad = wide.astype(BF16)
        g_ref[f] = grad
        first_ref[f, 0] = grad[:width]
        last_ref[f, 0] = grad[pixels - width :]
        here = pl.ds(pl.multiple_of(f * pixels, pixels), pixels)
        moved_ref[here, :channels] = from_right(wide, width).astype(BF16)
        moved_ref[here, channels : 2 * channels] = grad
        moved_ref[here, 2 * channels :] = from_left(wide, width).astype(BF16)

    loop(frames, body)
    for j in range(3):
        lanes = slice(j * channels, (j + 1) * channels)
        acc_ref[: 3 * channels, lanes] = dot(xt_ref[...], moved_ref[:, lanes])
    acc_ref[3 * channels :, :] = temporal_ref[...]

    chips, depth, block, _ = keep_ref.shape
    half = chips * depth * block
    core = lax.axis_index("tm") & 1

    def hand_out(kept, sent):
        for p in range(chips):
            for z in range(depth):
                at = (p * depth + z) * block
                keep_ref[p, z] = acc_ref[kept + at : kept + at + block]
                send_ref[p, z] = acc_ref[sent + at : sent + at + block].astype(BF16)

    pl.when(core == 0)(functools.partial(hand_out, 0, half))
    pl.when(core == 1)(functools.partial(hand_out, half, 0))


def conv_back_kernel(g_ref, above_ref, below_ref, cot_ref, w_ref, out_ref, lhs_ref):
    frames, rows, width, channels = cot_ref.shape
    pixels = rows * width

    def body(pair):
        for b in range(2):
            f = 2 * pair + b
            put_windows(above_ref[f, 0], g_ref[f], below_ref[f, 0], lhs_ref, b * pixels, (2, 1, 0))
        lhs = lhs_ref[...]
        z = [dot(lhs, w_ref[j]) for j in range(3)]
        out = z[1] + from_right(z[0], width) + from_left(z[2], width)
        for b in range(2):
            one = out[b * pixels : (b + 1) * pixels].reshape(rows, width, channels)
            out_ref[2 * pair + b] = (one + cot_ref[2 * pair + b].astype(F32)).astype(BF16)

    loop(frames // 2, body)


def out_kernel(corners, clip_ref, dil_ref, own, nxt, prv, *refs):
    corner, (tw_ref, x_ref, out_ref, cat_ref) = refs[:corners], refs[corners:]
    frames, rows, width, channels = x_ref.shape
    pixels = rows * width

    def body(pair):
        for b in range(2):
            gather_taps(clip_ref, dil_ref, 2 * pair + b, own, nxt, prv, corner, cat_ref, b * pixels, 2)
        temporal_out = dot(cat_ref[...], tw_ref[...]).astype(BF16).astype(F32)
        for b in range(2):
            one = temporal_out[b * pixels : (b + 1) * pixels].reshape(rows, width, channels)
            out_ref[2 * pair + b] = (x_ref[2 * pair + b].astype(F32) + one).astype(BF16)

    loop(frames // 2, body)


def core_sum_kernel(keep_ref, got_ref, own_ref, *send_refs):
    chip = lax.axis_index("tm") >> 1
    own_ref[...] = keep_ref[chip] + got_ref[chip].astype(F32)
    for s, ref in enumerate(send_refs, 1):
        ref[...] = (keep_ref[chip ^ s] + got_ref[chip ^ s].astype(F32)).astype(BF16)


def sum_kernel(count, own_ref, *refs):
    total = own_ref[...]
    for ref in refs[:count]:
        total = total + ref[...].astype(F32)
    refs[count][...] = total.astype(BF16)


def sum_split_kernel(count, own_ref, *refs):
    got, (mine_ref, *send_refs) = refs[:count], refs[count:]
    deep = lax.axis_index("space")

    def block(k):
        total = own_ref[k]
        for ref in got:
            total = total + ref[k].astype(F32)
        return total

    mine_ref[...] = block(deep)
    for s, ref in enumerate(send_refs, 1):
        ref[...] = block(deep ^ s).astype(BF16)


def place_kernel(axis, shift, *refs):
    me = lax.axis_index(axis) >> shift
    for s, ref in enumerate(refs[:-1]):
        refs[-1][me ^ s] = ref[...]


def finish_kernel(mine_ref, got_ref, spatial_ref, temporal_ref):
    chips, depth, block, _ = mine_ref.shape
    channels = spatial_ref.shape[-1]

    def write(pair):
        for c in range(2):
            for p in range(chips):
                for z in range(depth):
                    row = ((c * chips + p) * depth + z) * block
                    values = pair[c][p, z].astype(F32)
                    i, at = row // channels, row % channels
                    for k in range(3):
                        lanes = values[:, k * channels : (k + 1) * channels]
                        if i < 3:
                            spatial_ref[i, k, at : at + block] = lanes
                        else:
                            temporal_ref[k, at : at + block] = lanes

    core = lax.axis_index("tm") & 1
    pl.when(core == 0)(functools.partial(write, (mine_ref, got_ref)))
    pl.when(core == 1)(functools.partial(write, (got_ref, mine_ref)))


def neighbours(axis, low, high):
    size = lax.axis_size(axis)
    up = [(i, i + 1) for i in range(size - 1)]
    down = [(j, i) for i, j in up]
    return lax.ppermute(high, axis, up), lax.ppermute(low, axis, down)


def frame_neighbours(x):
    size, frames = lax.axis_size("tm"), x.shape[0]
    if size != 8:
        prev, nxt = neighbours("tm", x, x)
        return [nxt, prev]
    near = [i for i in range(7) if i != 3]
    prev = lax.ppermute(x, "tm", [(i, i + 1) for i in near])
    nxt = lax.ppermute(x, "tm", [(i + 1, i) for i in near])
    high = lax.ppermute(x[frames // 2 :], "tm", [(3, 7), (4, 0)])
    low = lax.ppermute(x[: frames // 2], "tm", [(3, 4), (4, 3)])
    high = lax.ppermute(high, "tm", [(7, 4), (0, 3)])
    return [nxt, prev, low, high]


def spread_parts(part, axis):
    size = lax.axis_size(axis)
    return [part] + [
        lax.ppermute(part, axis, [(i, (i + s) % size) for i in range(size)]) for s in range(1, size)
    ]


def per_device(frames_in, cotangent, spatial, temporal, norm_gain, norm_shift, clip_frames, dilation):
    frames, rows, width, channels = frames_in.shape
    pixels = rows * width
    n, tm = lax.axis_size("space"), lax.axis_size("tm")
    chips = tm // 2
    group_size = channels // GROUPS
    entries = float(rows * n * width * group_size)
    gain, shift = norm_gain[None], norm_shift[None]
    big = frames * pixels * channels
    shape = jax.ShapeDtypeStruct
    per_px = (frames, pixels, channels)
    windows = pltpu.VMEM((2 * pixels, 3 * channels), BF16)

    above, below = neighbours("space", frames_in[:, :1], frames_in[:, rows - 1 :])
    cot = cotangent.reshape(per_px)
    cot_around = frame_neighbours(cot)
    corners = len(cot_around) - 2

    conv_out, sums = call(
        conv_kernel, "conv_forward", [frames_in, above, below, spatial],
        [shape(per_px, F32), shape((frames, 2, channels), F32)],
        18 * big * channels, 8 * big, [windows],
    )
    parts = spread_parts(sums, "space")
    act, normed, slope = call(
        functools.partial(act_kernel, n, entries, group_size), "activation",
        [clip_frames, *parts, conv_out, gain, shift],
        [shape(per_px, BF16)] * 3, 10 * big, 10 * big,
    )
    act_around = frame_neighbours(act)
    x_turned, act_turned = call(
        turn_kernel, "turned", [frames_in, above, below, act],
        [shape((3 * channels, frames * pixels), BF16), shape((channels, frames * pixels), BF16)],
        0, 12 * big, [pltpu.VMEM((pixels, 3 * channels), BF16)],
    )

    grad_act, cot_cat, grad_sums = call(
        functools.partial(grad_act_kernel, corners), "grad_activation",
        [clip_frames, dilation, cot, *cot_around, temporal.transpose(0, 2, 1).reshape(3 * channels, channels), normed, slope],
        [shape(per_px, BF16), shape((frames * pixels, 3 * channels), BF16), shape((frames, 2, channels), F32)],
        6 * big * channels, 16 * big,
    )
    grad_parts = spread_parts(grad_sums, "space")
    temporal_part = call(
        temporal_grad_kernel, "temporal_grad", [act_turned, cot_cat],
        shape((channels, 3 * channels), F32), 6 * big * channels, 8 * big,
    )

    block = 2 * channels // (chips * n)
    lanes = 3 * channels
    grad_conv, first_rows, last_rows, send, keep = call(
        functools.partial(weight_grad_kernel, n, entries, group_size), "weight_grad",
        [x_turned, normed, slope, grad_act, temporal_part, *parts, *grad_parts],
        [shape(per_px, BF16)] + [shape((frames, 1, width, channels), BF16)] * 2
        + [shape((chips, n, block, lanes), BF16), shape((chips, n, block, lanes), F32)],
        18 * big * channels, 12 * big,
        [pltpu.VMEM((frames * pixels, lanes), BF16), pltpu.VMEM((4 * channels, lanes), F32)],
    )

    def other_chip(s):
        return [(i, i ^ (2 * s)) for i in range(tm)]

    def other_plane(s):
        return [(i, i ^ s) for i in range(n)]

    other_core = [(i, i ^ 1) for i in range(tm)]
    got = lax.ppermute(send, "tm", other_core)
    own, *sends = call(
        core_sum_kernel, "core_sum", [keep, got],
        [shape((n, block, lanes), F32)] + [shape((n, block, lanes), BF16)] * (chips - 1), 0, 4 * big,
    )
    gots = [lax.ppermute(x, "tm", other_chip(s)) for s, x in enumerate(sends, 1)]

    out_frames = call(
        functools.partial(out_kernel, corners), "temporal_forward",
        [clip_frames, dilation, act, *act_around, temporal.reshape(3 * channels, channels), frames_in],
        shape(frames_in.shape, BF16), 6 * big * channels, 10 * big, [windows],
    )
    own, out_frames = lax.optimization_barrier((own, out_frames))

    own, *sends = call(
        functools.partial(sum_split_kernel, chips - 1), "plane_sum", [own, *gots],
        [shape((block, lanes), F32)] + [shape((block, lanes), BF16)] * (n - 1), 0, big,
    )
    gots = [lax.ppermute(x, "space", other_plane(s)) for s, x in enumerate(sends, 1)]
    own = call(
        functools.partial(sum_kernel, n - 1), "line_sum", [own, *gots], shape((block, lanes), BF16), 0, big
    )
    gots = [lax.ppermute(own, "space", other_plane(s)) for s in range(1, n)]
    own = call(
        functools.partial(place_kernel, "space", 0), "line_place", [own, *gots], shape((n, block, lanes), BF16), 0, big
    )
    gots = [lax.ppermute(own, "tm", other_chip(s)) for s in range(1, chips)]

    grad_above, grad_below = neighbours("space", first_rows, last_rows)
    back_weights = spatial.transpose(1, 0, 3, 2).reshape(3, 3 * channels, channels)
    in_grad = call(
        conv_back_kernel, "conv_backward", [grad_conv, grad_above, grad_below, cotangent, back_weights],
        shape(frames_in.shape, BF16), 18 * big * channels, 8 * big, [windows],
    )
    own, in_grad = lax.optimization_barrier((own, in_grad))

    own = call(
        functools.partial(place_kernel, "tm", 1), "plane_place", [own, *gots], shape((chips, n, block, lanes), BF16), 0, big
    )
    got = lax.ppermute(own, "tm", other_core)
    spatial_grad, temporal_grad = call(
        finish_kernel, "finish", [own, got], [shape(spatial.shape, F32), shape(temporal.shape, F32)], 0, 4 * big
    )
    return (out_frames, in_grad, spatial_grad, temporal_grad)


def solution(mesh):
    tiles = P("tm", "space", None, None)
    return jax.shard_map(
        per_device,
        mesh=mesh,
        in_specs=(tiles, tiles, P(), P(), P(), P(), P(), P()),
        out_specs=(tiles, tiles, P(), P()),
        check_vma=False,
    )
```

```python
import functools

import jax
import jax.numpy as jnp
from jax import lax
from jax.experimental import pallas as pl
from jax.experimental.pallas import tpu as pltpu
from jax.sharding import PartitionSpec as P

GROUPS = 32
NORM_EPS = 1e-05
BF16 = jnp.bfloat16
F32 = jnp.float32
MIB = 2**20


def call(kernel, name, operands, out_shape, flops=0, moved=0, scratch=(), grant=14):
    vmem = pl.BlockSpec(memory_space=pltpu.VMEM)
    smem = pl.BlockSpec(memory_space=pltpu.SMEM)
    return pl.pallas_call(
        kernel,
        in_specs=[smem if x.dtype == jnp.int32 else vmem for x in operands],
        out_specs=jax.tree.map(lambda _: vmem, out_shape),
        out_shape=out_shape,
        scratch_shapes=list(scratch),
        compiler_params=pltpu.CompilerParams(vmem_limit_bytes=grant * MIB),
        cost_estimate=pl.CostEstimate(flops=int(flops), bytes_accessed=int(moved), transcendentals=0),
        name=name,
    )(*operands)


def dot(a, b):
    return jnp.dot(a, b, preferred_element_type=F32)


def dot_rows(a, b):
    return lax.dot_general(a, b, (((0,), (0,)), ((), ())), preferred_element_type=F32)


def group_total(row, group_size):
    channels = row.shape[-1]
    lane = lax.broadcasted_iota(jnp.int32, row.shape, 1)
    step = 1
    while step < group_size:
        up = pltpu.roll(row, channels - step, axis=1)
        down = pltpu.roll(row, step, axis=1)
        row = row + jnp.where((lane & step) == 0, up, down)
        step *= 2
    return row


def frame_stats(part_refs, f, entries, group_size):
    total = part_refs[0][f]
    for ref in part_refs[1:]:
        total = total + ref[f]
    return group_total(total, group_size) / entries


def sigmoid(x):
    return 0.5 * jnp.tanh(0.5 * x) + 0.5


def mean_and_inv(part_refs, f, entries, group_size):
    both = frame_stats(part_refs, f, entries, group_size)
    mean = both[0:1]
    inv = lax.rsqrt(both[1:2] - mean * mean + NORM_EPS)
    return mean, inv


def column_sums(first, second):
    return jnp.concatenate(
        [jnp.sum(first, axis=0, keepdims=True), jnp.sum(second, axis=0, keepdims=True)], axis=0
    )


def put_windows(above, mid, below, lhs_ref, at, order):
    width, (pixels, channels) = above.shape[0], mid.shape
    first, mid_at, last = (slice(k * channels, (k + 1) * channels) for k in order)
    lhs_ref[at : at + width, first] = above
    lhs_ref[at + width : at + pixels, first] = mid[: pixels - width]
    lhs_ref[at : at + pixels, mid_at] = mid
    lhs_ref[at : at + pixels - width, last] = mid[width:]
    lhs_ref[at + pixels - width : at + pixels, last] = below


def from_left(y, width):
    col = lax.broadcasted_iota(jnp.int32, y.shape, 0) & (width - 1)
    return jnp.where(col == 0, 0.0, pltpu.roll(y, 1, axis=0))


def from_right(y, width):
    col = lax.broadcasted_iota(jnp.int32, y.shape, 0) & (width - 1)
    return jnp.where(col == width - 1, 0.0, pltpu.roll(y, y.shape[0] - 1, axis=0))


def slot_sources(clip_ref, dil_ref, local, frames):
    slot = lax.axis_index("tm") * frames + local
    start1 = clip_ref[0]
    filled = start1 + clip_ref[1]
    in_first = slot < start1
    d = jnp.where(in_first, dil_ref[0], dil_ref[1])
    low = jnp.where(in_first, 0, start1)
    high = jnp.where(in_first, start1, filled)
    used = slot < filled
    later, earlier = local + d, local - d
    later_live = used & (slot + d < high)
    earlier_live = used & (slot - d >= low)
    later_which = jnp.where(later_live, jnp.where(later < frames, 1, 2), 0)
    earlier_which = jnp.where(earlier_live, jnp.where(earlier >= 0, 1, 2), 0)
    return (later, later_which), (earlier, earlier_which), used


def gather_taps(clip_ref, dil_ref, local, own, nxt, prv, corner, cat_ref, at, up_slot):
    frames, pixels, channels = own.shape
    later, earlier, used = slot_sources(clip_ref, dil_ref, local, frames)
    me, half = lax.axis_index("tm"), frames // 2

    def put(slot, ref, index):
        cat_ref[pl.ds(at, pixels), slot * channels : (slot + 1) * channels] = ref[index]

    def clear(slot):
        cat_ref[pl.ds(at, pixels), slot * channels : (slot + 1) * channels] = jnp.zeros((pixels, channels), BF16)

    for slot, (index, which), other, shift, turn in (
        (up_slot, later, nxt, -frames, 3),
        (2 - up_slot, earlier, prv, frames, 4),
    ):
        beyond = which == 2
        there = jnp.clip(index + shift, 0, frames - 1)
        pl.when(which == 1)(functools.partial(put, slot, own, jnp.clip(index, 0, frames - 1)))
        pl.when(which == 0)(functools.partial(clear, slot))
        if corner:
            by_corner = beyond & (me == turn)
            low, high = by_corner & (there < half), by_corner & (there >= half)
            pl.when(low)(functools.partial(put, slot, corner[0], jnp.minimum(there, half - 1)))
            pl.when(high)(functools.partial(put, slot, corner[1], jnp.maximum(there - half, 0)))
            beyond = beyond & (me != turn)
        pl.when(beyond)(functools.partial(put, slot, other, there))
    pl.when(used)(functools.partial(put, 1, own, local))
    pl.when(jnp.logical_not(used))(functools.partial(clear, 1))


def loop(count, body):
    def step(k, carry):
        body(k)
        return carry

    lax.fori_loop(0, count, step, 0)


def conv_kernel(x_ref, above_ref, below_ref, w_ref, out_ref, sums_ref, lhs_ref):
    frames, rows, width, channels = x_ref.shape
    pixels = rows * width

    def body(pair):
        for b in range(2):
            f = 2 * pair + b
            mid = x_ref[f].reshape(pixels, channels)
            put_windows(above_ref[f, 0], mid, below_ref[f, 0], lhs_ref, b * pixels, (0, 1, 2))
        lhs = lhs_ref[...]
        y = [dot(lhs, w_ref[:, j].reshape(3 * channels, channels)) for j in range(3)]
        out = y[1] + from_left(y[0], width) + from_right(y[2], width)
        for b in range(2):
            one = out[b * pixels : (b + 1) * pixels]
            out_ref[2 * pair + b] = one
            sums_ref[2 * pair + b] = column_sums(one, one * one)

    loop(frames // 2, body)


def act_kernel(n, entries, group_size, clip_ref, *refs):
    parts, (conv_ref, gain_ref, shift_ref, act_ref, normed_ref, slope_ref) = refs[:n], refs[n:]
    frames = conv_ref.shape[0]
    first = lax.axis_index("tm") * frames
    filled = clip_ref[0] + clip_ref[1]

    def body(f):
        mean, inv = mean_and_inv(parts, f, entries, group_size)
        normed = (conv_ref[f] - mean) * inv
        shaped = normed * gain_ref[...] + shift_ref[...]
        sig = sigmoid(shaped)
        act_ref[f] = jnp.where(first + f < filled, shaped * sig, 0.0).astype(BF16)
        normed_ref[f] = normed.astype(BF16)
        slope_ref[f] = (sig * (1.0 + shaped * (1.0 - sig)) * gain_ref[...]).astype(BF16)

    loop(frames, body)


def turn_kernel(x_ref, above_ref, below_ref, xt_ref, lhs_ref):
    frames, rows, width, channels = x_ref.shape
    pixels = rows * width

    def body(f):
        mid = x_ref[f].reshape(pixels, channels)
        put_windows(above_ref[f, 0], mid, below_ref[f, 0], lhs_ref, 0, (0, 1, 2))
        lanes = pl.ds(pl.multiple_of(f * pixels, pixels), pixels)
        for i in range(3):
            block = slice(i * channels, (i + 1) * channels)
            xt_ref[block, lanes] = lhs_ref[:, block].T

    loop(frames, body)


def grad_act_kernel(corners, clip_ref, dil_ref, own, nxt, prv, *refs):
    corner, (tw_ref, normed_ref, slope_ref, ga_ref, cat_ref, sums_ref) = refs[:corners], refs[corners:]
    frames, pixels, _ = own.shape

    def body(pair):
        rows = pl.ds(pl.multiple_of(2 * pair * pixels, 2 * pixels), 2 * pixels)
        for b in range(2):
            at = pl.multiple_of((2 * pair + b) * pixels, pixels)
            gather_taps(clip_ref, dil_ref, 2 * pair + b, own, nxt, prv, corner, cat_ref, at, 0)
        grad_act = dot(cat_ref[rows], tw_ref[...]).astype(BF16)
        for b in range(2):
            f = 2 * pair + b
            one = grad_act[b * pixels : (b + 1) * pixels]
            ga_ref[f] = one
            gn = one.astype(F32) * slope_ref[f].astype(F32)
            sums_ref[f] = column_sums(gn, gn * normed_ref[f].astype(F32))

    loop(frames // 2, body)


def temporal_grad_kernel(act_ref, cat_ref, out_ref):
    frames, pixels, channels = act_ref.shape
    out_ref[...] = dot_rows(act_ref[...].reshape(frames * pixels, channels), cat_ref[...])


def norm_back_kernel(n, m, entries, group_size, normed_ref, slope_ref, ga_ref, *refs):
    parts, grad_parts = refs[:n], refs[n : n + m]
    g_ref, first_ref, last_ref, moved_ref = refs[n + m :]
    _, pixels, channels = normed_ref.shape
    width = first_ref.shape[2]

    def body(f):
        _, inv = mean_and_inv(parts, f, entries, group_size)
        means = frame_stats(grad_parts, f, entries, group_size)
        gn = ga_ref[f].astype(F32) * slope_ref[f].astype(F32)
        wide = inv * (gn - means[0:1] - normed_ref[f].astype(F32) * means[1:2])
        grad = wide.astype(BF16)
        g_ref[f] = grad
        first_ref[f, 0] = grad[:width]
        last_ref[f, 0] = grad[pixels - width :]
        here = pl.ds(pl.multiple_of(f * pixels, pixels), pixels)
        moved_ref[here, :channels] = from_right(wide, width).astype(BF16)
        moved_ref[here, channels : 2 * channels] = grad
        moved_ref[here, 2 * channels :] = from_left(wide, width).astype(BF16)

    loop(normed_ref.shape[0], body)


def weight_grad_kernel(xt_ref, moved_ref, temporal_ref, send_ref, keep_ref, acc_ref):
    channels = temporal_ref.shape[0]
    for j in range(3):
        lanes = slice(j * channels, (j + 1) * channels)
        acc_ref[: 3 * channels, lanes] = dot(xt_ref[...], moved_ref[:, lanes])
    acc_ref[3 * channels :, :] = temporal_ref[...]

    chips, depth, block, _ = keep_ref.shape
    half = chips * depth * block
    core = lax.axis_index("tm") & 1

    def hand_out(kept, sent):
        for p in range(chips):
            for z in range(depth):
                at = (p * depth + z) * block
                keep_ref[p, z] = acc_ref[kept + at : kept + at + block]
                send_ref[p, z] = acc_ref[sent + at : sent + at + block].astype(BF16)

    pl.when(core == 0)(functools.partial(hand_out, 0, half))
    pl.when(core == 1)(functools.partial(hand_out, half, 0))


def conv_back_kernel(g_ref, above_ref, below_ref, cot_ref, w_ref, out_ref, lhs_ref):
    frames, rows, width, channels = cot_ref.shape
    pixels = rows * width

    def body(pair):
        for b in range(2):
            f = 2 * pair + b
            put_windows(above_ref[f, 0], g_ref[f], below_ref[f, 0], lhs_ref, b * pixels, (2, 1, 0))
        lhs = lhs_ref[...]
        z = [dot(lhs, w_ref[j]) for j in range(3)]
        out = z[1] + from_right(z[0], width) + from_left(z[2], width)
        for b in range(2):
            one = out[b * pixels : (b + 1) * pixels].reshape(rows, width, channels)
            out_ref[2 * pair + b] = (one + cot_ref[2 * pair + b].astype(F32)).astype(BF16)

    loop(frames // 2, body)


def out_kernel(corners, clip_ref, dil_ref, own, nxt, prv, *refs):
    corner, (tw_ref, x_ref, out_ref, cat_ref) = refs[:corners], refs[corners:]
    frames, rows, width, channels = x_ref.shape
    pixels = rows * width

    def body(pair):
        for b in range(2):
            gather_taps(clip_ref, dil_ref, 2 * pair + b, own, nxt, prv, corner, cat_ref, b * pixels, 2)
        temporal_out = dot(cat_ref[...], tw_ref[...]).astype(BF16).astype(F32)
        for b in range(2):
            one = temporal_out[b * pixels : (b + 1) * pixels].reshape(rows, width, channels)
            out_ref[2 * pair + b] = (x_ref[2 * pair + b].astype(F32) + one).astype(BF16)

    loop(frames // 2, body)


def core_sum_kernel(keep_ref, got_ref, own_ref, *send_refs):
    chip = lax.axis_index("tm") >> 1
    own_ref[...] = keep_ref[chip] + got_ref[chip].astype(F32)
    for s, ref in enumerate(send_refs, 1):
        ref[...] = (keep_ref[chip ^ s] + got_ref[chip ^ s].astype(F32)).astype(BF16)


def sum_kernel(count, own_ref, *refs):
    total = own_ref[...]
    for ref in refs[:count]:
        total = total + ref[...].astype(F32)
    refs[count][...] = total.astype(BF16)


def sum_split_kernel(count, own_ref, *refs):
    got, (mine_ref, *send_refs) = refs[:count], refs[count:]
    deep = lax.axis_index("space")

    def block(k):
        total = own_ref[k]
        for ref in got:
            total = total + ref[k].astype(F32)
        return total

    mine_ref[...] = block(deep)
    for s, ref in enumerate(send_refs, 1):
        ref[...] = block(deep ^ s).astype(BF16)


def place_kernel(axis, shift, *refs):
    me = lax.axis_index(axis) >> shift
    for s, ref in enumerate(refs[:-1]):
        refs[-1][me ^ s] = ref[...]


def finish_kernel(mine_ref, got_ref, spatial_ref, temporal_ref):
    chips, depth, block, _ = mine_ref.shape
    channels = spatial_ref.shape[-1]

    def write(pair):
        for c in range(2):
            for p in range(chips):
                for z in range(depth):
                    row = ((c * chips + p) * depth + z) * block
                    values = pair[c][p, z].astype(F32)
                    i, at = row // channels, row % channels
                    for k in range(3):
                        lanes = values[:, k * channels : (k + 1) * channels]
                        if i < 3:
                            spatial_ref[i, k, at : at + block] = lanes
                        else:
                            temporal_ref[k, at : at + block] = lanes

    core = lax.axis_index("tm") & 1
    pl.when(core == 0)(functools.partial(write, (mine_ref, got_ref)))
    pl.when(core == 1)(functools.partial(write, (got_ref, mine_ref)))


def neighbours(axis, low, high):
    size = lax.axis_size(axis)
    up = [(i, i + 1) for i in range(size - 1)]
    down = [(j, i) for i, j in up]
    return lax.ppermute(high, axis, up), lax.ppermute(low, axis, down)


def near_frames(x, corner):
    pairs = [(i, i + 1) for i in range(lax.axis_size("tm") - 1) if corner or i != 3]
    return lax.ppermute(x, "tm", [(j, i) for i, j in pairs]), lax.ppermute(x, "tm", pairs)


def spread_sums(part, axis):
    size = lax.axis_size(axis)
    step, got = 1, None
    while step < size:
        if got is not None:
            part = part + got
        got = lax.ppermute(part, axis, [(i, i ^ step) for i in range(size)])
        step *= 2
    return [part, got]


def per_device(frames_in, cotangent, spatial, temporal, norm_gain, norm_shift, clip_frames, dilation):
    frames, rows, width, channels = frames_in.shape
    pixels = rows * width
    n, tm = lax.axis_size("space"), lax.axis_size("tm")
    chips = tm // 2
    group_size = channels // GROUPS
    entries = float(rows * n * width * group_size)
    gain, shift = norm_gain[None], norm_shift[None]
    big = frames * pixels * channels
    shape = jax.ShapeDtypeStruct
    per_px = (frames, pixels, channels)
    windows = pltpu.VMEM((2 * pixels, 3 * channels), BF16)

    first, last = frames_in[:, :1], frames_in[:, rows - 1 :]
    first, last, cot = lax.optimization_barrier((first, last, cotangent.reshape(per_px)))
    above, below = neighbours("space", first, last)
    by_corner = tm == 8
    cot_around = list(near_frames(cot, not by_corner))
    if by_corner:
        above, below, late = lax.optimization_barrier((above, below, cot))
        relayed = lax.ppermute(late[frames // 2 :], "tm", [(3, 7), (4, 0)])
        cot_around.append(lax.ppermute(late[: frames // 2], "tm", [(3, 4), (4, 3)]))

    conv_out, sums = call(
        conv_kernel, "conv_forward", [frames_in, above, below, spatial],
        [shape(per_px, F32), shape((frames, 2, channels), F32)],
        18 * big * channels, 8 * big, [windows], 18,
    )
    if by_corner:
        relayed, sums = lax.optimization_barrier((relayed, sums))
        cot_around.append(lax.ppermute(relayed, "tm", [(7, 4), (0, 3)]))
    corners = len(cot_around) - 2
    parts = spread_sums(sums, "space")
    x_turned = call(
        turn_kernel, "turned", [frames_in, above, below], shape((3 * channels, frames * pixels), BF16),
        0, 8 * big, [pltpu.VMEM((pixels, 3 * channels), BF16)],
    )
    act, normed, slope = call(
        functools.partial(act_kernel, len(parts), entries, group_size), "activation",
        [clip_frames, *parts, conv_out, gain, shift],
        [shape(per_px, BF16)] * 3, 10 * big, 10 * big,
    )
    act_sent, *cot_around[:2] = lax.optimization_barrier((act, *cot_around[:2]))
    act_around = near_frames(act_sent, True)

    grad_act, cot_cat, grad_sums = call(
        functools.partial(grad_act_kernel, corners), "grad_activation",
        [clip_frames, dilation, cot, *cot_around, temporal.transpose(0, 2, 1).reshape(3 * channels, channels), normed, slope],
        [shape(per_px, BF16), shape((frames * pixels, 3 * channels), BF16), shape((frames, 2, channels), F32)],
        6 * big * channels, 16 * big,
    )
    grad_parts = spread_sums(grad_sums, "space")
    temporal_part = call(
        temporal_grad_kernel, "temporal_grad", [act, cot_cat],
        shape((channels, 3 * channels), F32), 6 * big * channels, 8 * big,
    )
    lanes = 3 * channels
    grad_conv, first_rows, last_rows, moved = call(
        functools.partial(norm_back_kernel, len(parts), len(grad_parts), entries, group_size), "norm_backward",
        [normed, slope, grad_act, *parts, *grad_parts],
        [shape(per_px, BF16)] + [shape((frames, 1, width, channels), BF16)] * 2
        + [shape((frames * pixels, lanes), BF16)],
        0, 12 * big,
    )
    grad_above, grad_below = neighbours("space", first_rows, last_rows)
    block = 2 * channels // (chips * n)
    send, keep = call(
        weight_grad_kernel, "weight_grad", [x_turned, moved, temporal_part],
        [shape((chips, n, block, lanes), BF16), shape((chips, n, block, lanes), F32)],
        18 * big * channels, 12 * big, [pltpu.VMEM((4 * channels, lanes), F32)], 20,
    )

    def other_chip(s):
        return [(i, i ^ (2 * s)) for i in range(tm)]

    def other_plane(s):
        return [(i, i ^ s) for i in range(n)]

    other_core = [(i, i ^ 1) for i in range(tm)]
    got = lax.ppermute(send, "tm", other_core)
    own, *sends = call(
        core_sum_kernel, "core_sum", [keep, got],
        [shape((n, block, lanes), F32)] + [shape((n, block, lanes), BF16)] * (chips - 1), 0, 4 * big,
    )
    gots = [lax.ppermute(x, "tm", other_chip(s)) for s, x in enumerate(sends, 1)]

    back_weights = spatial.transpose(1, 0, 3, 2).reshape(3, 3 * channels, channels)
    in_grad = call(
        conv_back_kernel, "conv_backward", [grad_conv, grad_above, grad_below, cotangent, back_weights],
        shape(frames_in.shape, BF16), 18 * big * channels, 8 * big, [windows], 20,
    )
    own, in_grad = lax.optimization_barrier((own, in_grad))

    own, *sends = call(
        functools.partial(sum_split_kernel, chips - 1), "plane_sum", [own, *gots],
        [shape((block, lanes), F32)] + [shape((block, lanes), BF16)] * (n - 1), 0, big,
    )
    gots = [lax.ppermute(x, "space", other_plane(s)) for s, x in enumerate(sends, 1)]
    own = call(
        functools.partial(sum_kernel, n - 1), "line_sum", [own, *gots], shape((block, lanes), BF16), 0, big
    )
    gots = [lax.ppermute(own, "space", other_plane(s)) for s in range(1, n)]
    own = call(
        functools.partial(place_kernel, "space", 0), "line_place", [own, *gots], shape((n, block, lanes), BF16), 0, big
    )
    gots = [lax.ppermute(own, "tm", other_chip(s)) for s in range(1, chips)]

    out_frames = call(
        functools.partial(out_kernel, 0), "temporal_forward",
        [clip_frames, dilation, act, *act_around, temporal.reshape(3 * channels, channels), frames_in],
        shape(frames_in.shape, BF16), 6 * big * channels, 10 * big, [windows],
    )
    own, out_frames = lax.optimization_barrier((own, out_frames))

    own = call(
        functools.partial(place_kernel, "tm", 1), "plane_place", [own, *gots], shape((chips, n, block, lanes), BF16), 0, big
    )
    got = lax.ppermute(own, "tm", other_core)
    spatial_grad, temporal_grad = call(
        finish_kernel, "finish", [own, got], [shape(spatial.shape, F32), shape(temporal.shape, F32)], 0, 4 * big
    )
    return (out_frames, in_grad, spatial_grad, temporal_grad)


def solution(mesh):
    tiles = P("tm", "space", None, None)
    return jax.shard_map(
        per_device,
        mesh=mesh,
        in_specs=(tiles, tiles, P(), P(), P(), P(), P(), P()),
        out_specs=(tiles, tiles, P(), P()),
        check_vma=False,
    )
```

```python
import functools

import jax
import jax.numpy as jnp
from jax import lax
from jax.experimental import pallas as pl
from jax.experimental.pallas import tpu as pltpu
from jax.sharding import PartitionSpec as P

GROUPS = 32
NORM_EPS = 1e-05
BF16 = jnp.bfloat16
F32 = jnp.float32
MIB = 2**20


def call(kernel, name, operands, out_shape, flops=0, moved=0, scratch=(), grant=14):
    vmem = pl.BlockSpec(memory_space=pltpu.VMEM)
    smem = pl.BlockSpec(memory_space=pltpu.SMEM)
    return pl.pallas_call(
        kernel,
        in_specs=[smem if x.dtype == jnp.int32 else vmem for x in operands],
        out_specs=jax.tree.map(lambda _: vmem, out_shape),
        out_shape=out_shape,
        scratch_shapes=list(scratch),
        compiler_params=pltpu.CompilerParams(vmem_limit_bytes=grant * MIB),
        cost_estimate=pl.CostEstimate(flops=int(flops), bytes_accessed=int(moved), transcendentals=0),
        name=name,
    )(*operands)


def dot(a, b):
    return jnp.dot(a, b, preferred_element_type=F32)


def dot_rows(a, b):
    return lax.dot_general(a, b, (((0,), (0,)), ((), ())), preferred_element_type=F32)


def group_total(row, group_size):
    channels = row.shape[-1]
    lane = lax.broadcasted_iota(jnp.int32, row.shape, 1)
    step = 1
    while step < group_size:
        up = pltpu.roll(row, channels - step, axis=1)
        down = pltpu.roll(row, step, axis=1)
        row = row + jnp.where((lane & step) == 0, up, down)
        step *= 2
    return row


def frame_stats(part_refs, f, entries, group_size):
    total = part_refs[0][f]
    for ref in part_refs[1:]:
        total = total + ref[f]
    return group_total(total, group_size) / entries


def sigmoid(x):
    return 0.5 * jnp.tanh(0.5 * x) + 0.5


def mean_and_inv(part_refs, f, entries, group_size):
    both = frame_stats(part_refs, f, entries, group_size)
    mean = both[0:1]
    inv = lax.rsqrt(both[1:2] - mean * mean + NORM_EPS)
    return mean, inv


def column_sums(first, second):
    return jnp.concatenate(
        [jnp.sum(first, axis=0, keepdims=True), jnp.sum(second, axis=0, keepdims=True)], axis=0
    )


def put_windows(above, mid, below, lhs_ref, at, order):
    width, (pixels, channels) = above.shape[0], mid.shape
    first, mid_at, last = (slice(k * channels, (k + 1) * channels) for k in order)
    lhs_ref[at : at + width, first] = above
    lhs_ref[at + width : at + pixels, first] = mid[: pixels - width]
    lhs_ref[at : at + pixels, mid_at] = mid
    lhs_ref[at : at + pixels - width, last] = mid[width:]
    lhs_ref[at + pixels - width : at + pixels, last] = below


def from_left(y, width):
    col = lax.broadcasted_iota(jnp.int32, y.shape, 0) & (width - 1)
    return jnp.where(col == 0, 0.0, pltpu.roll(y, 1, axis=0))


def from_right(y, width):
    col = lax.broadcasted_iota(jnp.int32, y.shape, 0) & (width - 1)
    return jnp.where(col == width - 1, 0.0, pltpu.roll(y, y.shape[0] - 1, axis=0))


def slot_sources(clip_ref, dil_ref, local, frames):
    slot = lax.axis_index("tm") * frames + local
    start1 = clip_ref[0]
    filled = start1 + clip_ref[1]
    in_first = slot < start1
    d = jnp.where(in_first, dil_ref[0], dil_ref[1])
    low = jnp.where(in_first, 0, start1)
    high = jnp.where(in_first, start1, filled)
    used = slot < filled
    later, earlier = local + d, local - d
    later_live = used & (slot + d < high)
    earlier_live = used & (slot - d >= low)
    later_which = jnp.where(later_live, jnp.where(later < frames, 1, 2), 0)
    earlier_which = jnp.where(earlier_live, jnp.where(earlier >= 0, 1, 2), 0)
    return (later, later_which), (earlier, earlier_which), used


def gather_taps(clip_ref, dil_ref, local, own, nxt, prv, corner, cat_ref, at, up_slot):
    frames, pixels, channels = own.shape
    later, earlier, used = slot_sources(clip_ref, dil_ref, local, frames)
    me, half = lax.axis_index("tm"), frames // 2

    def put(slot, ref, index):
        cat_ref[pl.ds(at, pixels), slot * channels : (slot + 1) * channels] = ref[index]

    def clear(slot):
        cat_ref[pl.ds(at, pixels), slot * channels : (slot + 1) * channels] = jnp.zeros((pixels, channels), BF16)

    for slot, (index, which), other, shift, turn in (
        (up_slot, later, nxt, -frames, 3),
        (2 - up_slot, earlier, prv, frames, 4),
    ):
        beyond = which == 2
        there = jnp.clip(index + shift, 0, frames - 1)
        pl.when(which == 1)(functools.partial(put, slot, own, jnp.clip(index, 0, frames - 1)))
        pl.when(which == 0)(functools.partial(clear, slot))
        if corner:
            by_corner = beyond & (me == turn)
            low, high = by_corner & (there < half), by_corner & (there >= half)
            pl.when(low)(functools.partial(put, slot, corner[0], jnp.minimum(there, half - 1)))
            pl.when(high)(functools.partial(put, slot, corner[1], jnp.maximum(there - half, 0)))
            beyond = beyond & (me != turn)
        pl.when(beyond)(functools.partial(put, slot, other, there))
    pl.when(used)(functools.partial(put, 1, own, local))
    pl.when(jnp.logical_not(used))(functools.partial(clear, 1))


def loop(count, body):
    def step(k, carry):
        body(k)
        return carry

    lax.fori_loop(0, count, step, 0)


def conv_kernel(x_ref, above_ref, below_ref, w_ref, out_ref, sums_ref, lhs_ref):
    frames, rows, width, channels = x_ref.shape
    pixels = rows * width

    def body(pair):
        for b in range(2):
            f = 2 * pair + b
            mid = x_ref[f].reshape(pixels, channels)
            put_windows(above_ref[f, 0], mid, below_ref[f, 0], lhs_ref, b * pixels, (0, 1, 2))
        lhs = lhs_ref[...]
        y = [dot(lhs, w_ref[:, j].reshape(3 * channels, channels)) for j in range(3)]
        out = y[1] + from_left(y[0], width) + from_right(y[2], width)
        for b in range(2):
            one = out[b * pixels : (b + 1) * pixels]
            out_ref[2 * pair + b] = one
            sums_ref[2 * pair + b] = column_sums(one, one * one)

    loop(frames // 2, body)


def act_kernel(n, entries, group_size, clip_ref, *refs):
    parts, (conv_ref, gain_ref, shift_ref, act_ref, normed_ref, slope_ref) = refs[:n], refs[n:]
    frames = conv_ref.shape[0]
    first = lax.axis_index("tm") * frames
    filled = clip_ref[0] + clip_ref[1]

    def body(f):
        mean, inv = mean_and_inv(parts, f, entries, group_size)
        normed = (conv_ref[f] - mean) * inv
        shaped = normed * gain_ref[...] + shift_ref[...]
        sig = sigmoid(shaped)
        act_ref[f] = jnp.where(first + f < filled, shaped * sig, 0.0).astype(BF16)
        normed_ref[f] = normed.astype(BF16)
        slope_ref[f] = (sig * (1.0 + shaped * (1.0 - sig)) * gain_ref[...]).astype(BF16)

    loop(frames, body)


def turn_kernel(x_ref, above_ref, below_ref, xt_ref, lhs_ref):
    frames, rows, width, channels = x_ref.shape
    pixels = rows * width

    def body(f):
        mid = x_ref[f].reshape(pixels, channels)
        put_windows(above_ref[f, 0], mid, below_ref[f, 0], lhs_ref, 0, (0, 1, 2))
        lanes = pl.ds(pl.multiple_of(f * pixels, pixels), pixels)
        for i in range(3):
            block = slice(i * channels, (i + 1) * channels)
            xt_ref[block, lanes] = lhs_ref[:, block].T

    loop(frames, body)


def turn_weights_kernel(spatial_ref, temporal_ref, back_ref, out_ref):
    channels = spatial_ref.shape[-1]
    for i in range(3):
        rows = slice(i * channels, (i + 1) * channels)
        out_ref[rows] = temporal_ref[i].T
        for j in range(3):
            back_ref[j, rows] = spatial_ref[i, j].T


def grad_act_kernel(corners, clip_ref, dil_ref, own, nxt, prv, *refs):
    corner, (tw_ref, normed_ref, slope_ref, ga_ref, cat_ref, sums_ref) = refs[:corners], refs[corners:]
    frames, pixels, _ = own.shape

    def body(pair):
        rows = pl.ds(pl.multiple_of(2 * pair * pixels, 2 * pixels), 2 * pixels)
        for b in range(2):
            at = pl.multiple_of((2 * pair + b) * pixels, pixels)
            gather_taps(clip_ref, dil_ref, 2 * pair + b, own, nxt, prv, corner, cat_ref, at, 0)
        grad_act = dot(cat_ref[rows], tw_ref[...]).astype(BF16)
        for b in range(2):
            f = 2 * pair + b
            one = grad_act[b * pixels : (b + 1) * pixels]
            ga_ref[f] = one
            gn = one.astype(F32) * slope_ref[f].astype(F32)
            sums_ref[f] = column_sums(gn, gn * normed_ref[f].astype(F32))

    loop(frames // 2, body)


def temporal_grad_kernel(act_ref, cat_ref, out_ref):
    frames, pixels, channels = act_ref.shape
    out_ref[...] = dot_rows(act_ref[...].reshape(frames * pixels, channels), cat_ref[...])


def norm_back_kernel(n, m, entries, group_size, normed_ref, slope_ref, ga_ref, *refs):
    parts, grad_parts = refs[:n], refs[n : n + m]
    g_ref, first_ref, last_ref, moved_ref = refs[n + m :]
    _, pixels, channels = normed_ref.shape
    width = first_ref.shape[2]

    def body(f):
        _, inv = mean_and_inv(parts, f, entries, group_size)
        means = frame_stats(grad_parts, f, entries, group_size)
        gn = ga_ref[f].astype(F32) * slope_ref[f].astype(F32)
        wide = inv * (gn - means[0:1] - normed_ref[f].astype(F32) * means[1:2])
        grad = wide.astype(BF16)
        g_ref[f] = grad
        first_ref[f, 0] = grad[:width]
        last_ref[f, 0] = grad[pixels - width :]
        here = pl.ds(pl.multiple_of(f * pixels, pixels), pixels)
        moved_ref[here, :channels] = from_right(wide, width).astype(BF16)
        moved_ref[here, channels : 2 * channels] = grad
        moved_ref[here, 2 * channels :] = from_left(wide, width).astype(BF16)

    loop(normed_ref.shape[0], body)


def weight_grad_kernel(xt_ref, moved_ref, temporal_ref, send_ref, keep_ref, acc_ref):
    channels = temporal_ref.shape[0]
    for j in range(3):
        lanes = slice(j * channels, (j + 1) * channels)
        acc_ref[: 3 * channels, lanes] = dot(xt_ref[...], moved_ref[:, lanes])
    acc_ref[3 * channels :, :] = temporal_ref[...]

    chips, depth, block, _ = keep_ref.shape
    half = chips * depth * block
    core = lax.axis_index("tm") & 1

    def hand_out(kept, sent):
        for p in range(chips):
            for z in range(depth):
                at = (p * depth + z) * block
                keep_ref[p, z] = acc_ref[kept + at : kept + at + block]
                send_ref[p, z] = acc_ref[sent + at : sent + at + block].astype(BF16)

    pl.when(core == 0)(functools.partial(hand_out, 0, half))
    pl.when(core == 1)(functools.partial(hand_out, half, 0))


def conv_back_kernel(g_ref, above_ref, below_ref, cot_ref, w_ref, out_ref, lhs_ref):
    frames, rows, width, channels = cot_ref.shape
    pixels = rows * width

    def body(pair):
        for b in range(2):
            f = 2 * pair + b
            put_windows(above_ref[f, 0], g_ref[f], below_ref[f, 0], lhs_ref, b * pixels, (2, 1, 0))
        lhs = lhs_ref[...]
        z = [dot(lhs, w_ref[j]) for j in range(3)]
        out = z[1] + from_right(z[0], width) + from_left(z[2], width)
        for b in range(2):
            one = out[b * pixels : (b + 1) * pixels].reshape(rows, width, channels)
            out_ref[2 * pair + b] = (one + cot_ref[2 * pair + b].astype(F32)).astype(BF16)

    loop(frames // 2, body)


def out_kernel(corners, clip_ref, dil_ref, own, nxt, prv, *refs):
    corner, (tw_ref, x_ref, out_ref, cat_ref) = refs[:corners], refs[corners:]
    frames, rows, width, channels = x_ref.shape
    pixels = rows * width

    def body(pair):
        for b in range(2):
            gather_taps(clip_ref, dil_ref, 2 * pair + b, own, nxt, prv, corner, cat_ref, b * pixels, 2)
        temporal_out = dot(cat_ref[...], tw_ref[...]).astype(BF16).astype(F32)
        for b in range(2):
            one = temporal_out[b * pixels : (b + 1) * pixels].reshape(rows, width, channels)
            out_ref[2 * pair + b] = (x_ref[2 * pair + b].astype(F32) + one).astype(BF16)

    loop(frames // 2, body)


def core_sum_kernel(keep_ref, got_ref, own_ref, *send_refs):
    chip = lax.axis_index("tm") >> 1
    own_ref[...] = keep_ref[chip] + got_ref[chip].astype(F32)
    for s, ref in enumerate(send_refs, 1):
        ref[...] = (keep_ref[chip ^ s] + got_ref[chip ^ s].astype(F32)).astype(BF16)


def sum_kernel(count, own_ref, *refs):
    total = own_ref[...]
    for ref in refs[:count]:
        total = total + ref[...].astype(F32)
    refs[count][...] = total.astype(BF16)


def sum_split_kernel(count, own_ref, *refs):
    got, (mine_ref, *send_refs) = refs[:count], refs[count:]
    deep = lax.axis_index("space")

    def block(k):
        total = own_ref[k]
        for ref in got:
            total = total + ref[k].astype(F32)
        return total

    mine_ref[...] = block(deep)
    for s, ref in enumerate(send_refs, 1):
        ref[...] = block(deep ^ s).astype(BF16)


def place_kernel(axis, shift, *refs):
    me = lax.axis_index(axis) >> shift
    for s, ref in enumerate(refs[:-1]):
        refs[-1][me ^ s] = ref[...]


def finish_kernel(mine_ref, got_ref, spatial_ref, temporal_ref):
    chips, depth, block, _ = mine_ref.shape
    channels = spatial_ref.shape[-1]

    def write(pair):
        for c in range(2):
            for p in range(chips):
                for z in range(depth):
                    row = ((c * chips + p) * depth + z) * block
                    values = pair[c][p, z].astype(F32)
                    i, at = row // channels, row % channels
                    for k in range(3):
                        lanes = values[:, k * channels : (k + 1) * channels]
                        if i < 3:
                            spatial_ref[i, k, at : at + block] = lanes
                        else:
                            temporal_ref[k, at : at + block] = lanes

    core = lax.axis_index("tm") & 1
    pl.when(core == 0)(functools.partial(write, (mine_ref, got_ref)))
    pl.when(core == 1)(functools.partial(write, (got_ref, mine_ref)))


def neighbours(axis, low, high):
    size = lax.axis_size(axis)
    up = [(i, i + 1) for i in range(size - 1)]
    down = [(j, i) for i, j in up]
    return lax.ppermute(high, axis, up), lax.ppermute(low, axis, down)


def near_frames(x, corner):
    pairs = [(i, i + 1) for i in range(lax.axis_size("tm") - 1) if corner or i != 3]
    return lax.ppermute(x, "tm", [(j, i) for i, j in pairs]), lax.ppermute(x, "tm", pairs)


def spread_sums(part, axis):
    size = lax.axis_size(axis)
    step, got = 1, None
    while step < size:
        if got is not None:
            part = part + got
        got = lax.ppermute(part, axis, [(i, i ^ step) for i in range(size)])
        step *= 2
    return [part, got]


def per_device(frames_in, cotangent, spatial, temporal, norm_gain, norm_shift, clip_frames, dilation):
    frames, rows, width, channels = frames_in.shape
    pixels = rows * width
    n, tm = lax.axis_size("space"), lax.axis_size("tm")
    chips = tm // 2
    group_size = channels // GROUPS
    entries = float(rows * n * width * group_size)
    gain, shift = norm_gain[None], norm_shift[None]
    big = frames * pixels * channels
    shape = jax.ShapeDtypeStruct
    per_px = (frames, pixels, channels)
    windows = pltpu.VMEM((2 * pixels, 3 * channels), BF16)

    first, last = frames_in[:, :1], frames_in[:, rows - 1 :]
    first, last, cot = lax.optimization_barrier((first, last, cotangent.reshape(per_px)))
    above, below = neighbours("space", first, last)
    by_corner = tm == 8
    cot_around = list(near_frames(cot, not by_corner))

    conv_out, sums = call(
        conv_kernel, "conv_forward", [frames_in, above, below, spatial],
        [shape(per_px, F32), shape((frames, 2, channels), F32)],
        18 * big * channels, 8 * big, [windows], 18,
    )
    if by_corner:
        sums, late = lax.optimization_barrier((sums, cot))
        relayed = lax.ppermute(late[frames // 2 :], "tm", [(3, 7), (4, 0)])
        cot_around.append(lax.ppermute(late[: frames // 2], "tm", [(3, 4), (4, 3)]))
    parts = spread_sums(sums, "space")
    x_turned = call(
        turn_kernel, "turned", [frames_in, above, below], shape((3 * channels, frames * pixels), BF16),
        0, 8 * big, [pltpu.VMEM((pixels, 3 * channels), BF16)],
    )
    back_weights, back_taps = call(
        turn_weights_kernel, "turn_weights", [spatial, temporal],
        [shape((3, 3 * channels, channels), BF16), shape((3 * channels, channels), BF16)], 0, big,
    )
    x_turned, back_weights, back_taps, *parts = lax.optimization_barrier((x_turned, back_weights, back_taps, *parts))
    if by_corner:
        relayed, *parts = lax.optimization_barrier((relayed, *parts))
        cot_around.append(lax.ppermute(relayed, "tm", [(7, 4), (0, 3)]))
    corners = len(cot_around) - 2
    act, normed, slope = call(
        functools.partial(act_kernel, len(parts), entries, group_size), "activation",
        [clip_frames, *parts, conv_out, gain, shift],
        [shape(per_px, BF16)] * 3, 10 * big, 10 * big,
    )
    act_sent, *cot_around[:2] = lax.optimization_barrier((act, *cot_around[:2]))
    act_around = near_frames(act_sent, True)

    grad_act, cot_cat, grad_sums = call(
        functools.partial(grad_act_kernel, corners), "grad_activation",
        [clip_frames, dilation, cot, *cot_around, back_taps, normed, slope],
        [shape(per_px, BF16), shape((frames * pixels, 3 * channels), BF16), shape((frames, 2, channels), F32)],
        6 * big * channels, 16 * big,
    )
    grad_parts = spread_sums(grad_sums, "space")
    temporal_part = call(
        temporal_grad_kernel, "temporal_grad", [act, cot_cat],
        shape((channels, 3 * channels), F32), 6 * big * channels, 8 * big,
    )
    lanes = 3 * channels
    grad_conv, first_rows, last_rows, moved = call(
        functools.partial(norm_back_kernel, len(parts), len(grad_parts), entries, group_size), "norm_backward",
        [normed, slope, grad_act, *parts, *grad_parts],
        [shape(per_px, BF16)] + [shape((frames, 1, width, channels), BF16)] * 2
        + [shape((frames * pixels, lanes), BF16)],
        0, 12 * big,
    )
    grad_above, grad_below = neighbours("space", first_rows, last_rows)
    block = 2 * channels // (chips * n)
    send, keep = call(
        weight_grad_kernel, "weight_grad", [x_turned, moved, temporal_part],
        [shape((chips, n, block, lanes), BF16), shape((chips, n, block, lanes), F32)],
        18 * big * channels, 12 * big, [pltpu.VMEM((4 * channels, lanes), F32)], 20,
    )

    def other_chip(s):
        return [(i, i ^ (2 * s)) for i in range(tm)]

    def other_plane(s):
        return [(i, i ^ s) for i in range(n)]

    other_core = [(i, i ^ 1) for i in range(tm)]
    got = lax.ppermute(send, "tm", other_core)
    own, *sends = call(
        core_sum_kernel, "core_sum", [keep, got],
        [shape((n, block, lanes), F32)] + [shape((n, block, lanes), BF16)] * (chips - 1), 0, 4 * big,
    )
    gots = [lax.ppermute(x, "tm", other_chip(s)) for s, x in enumerate(sends, 1)]

    in_grad = call(
        conv_back_kernel, "conv_backward", [grad_conv, grad_above, grad_below, cotangent, back_weights],
        shape(frames_in.shape, BF16), 18 * big * channels, 8 * big, [windows], 20,
    )
    own, in_grad = lax.optimization_barrier((own, in_grad))

    own, *sends = call(
        functools.partial(sum_split_kernel, chips - 1), "plane_sum", [own, *gots],
        [shape((block, lanes), F32)] + [shape((block, lanes), BF16)] * (n - 1), 0, big,
    )
    gots = [lax.ppermute(x, "space", other_plane(s)) for s, x in enumerate(sends, 1)]
    own = call(
        functools.partial(sum_kernel, n - 1), "line_sum", [own, *gots], shape((block, lanes), BF16), 0, big
    )
    gots = [lax.ppermute(own, "space", other_plane(s)) for s in range(1, n)]
    own = call(
        functools.partial(place_kernel, "space", 0), "line_place", [own, *gots], shape((n, block, lanes), BF16), 0, big
    )
    gots = [lax.ppermute(own, "tm", other_chip(s)) for s in range(1, chips)]

    out_frames = call(
        functools.partial(out_kernel, 0), "temporal_forward",
        [clip_frames, dilation, act, *act_around, temporal.reshape(3 * channels, channels), frames_in],
        shape(frames_in.shape, BF16), 6 * big * channels, 10 * big, [windows],
    )
    own, out_frames = lax.optimization_barrier((own, out_frames))

    own = call(
        functools.partial(place_kernel, "tm", 1), "plane_place", [own, *gots], shape((chips, n, block, lanes), BF16), 0, big
    )
    got = lax.ppermute(own, "tm", other_core)
    spatial_grad, temporal_grad = call(
        finish_kernel, "finish", [own, got], [shape(spatial.shape, F32), shape(temporal.shape, F32)], 0, 4 * big
    )
    return (out_frames, in_grad, spatial_grad, temporal_grad)


def solution(mesh):
    tiles = P("tm", "space", None, None)
    return jax.shard_map(
        per_device,
        mesh=mesh,
        in_specs=(tiles, tiles, P(), P(), P(), P(), P(), P()),
        out_specs=(tiles, tiles, P(), P()),
        check_vma=False,
    )
```

```python
import functools

import jax
import jax.numpy as jnp
from jax import lax
from jax.experimental import pallas as pl
from jax.experimental.pallas import tpu as pltpu
from jax.sharding import PartitionSpec as P

GROUPS = 32
NORM_EPS = 1e-05
BF16 = jnp.bfloat16
F32 = jnp.float32
MIB = 2**20


def call(kernel, name, operands, out_shape, flops=0, moved=0, scratch=(), grant=14):
    vmem = pl.BlockSpec(memory_space=pltpu.VMEM)
    smem = pl.BlockSpec(memory_space=pltpu.SMEM)
    return pl.pallas_call(
        kernel,
        in_specs=[smem if x.dtype == jnp.int32 else vmem for x in operands],
        out_specs=jax.tree.map(lambda _: vmem, out_shape),
        out_shape=out_shape,
        scratch_shapes=list(scratch),
        compiler_params=pltpu.CompilerParams(vmem_limit_bytes=grant * MIB),
        cost_estimate=pl.CostEstimate(flops=int(flops), bytes_accessed=int(moved), transcendentals=0),
        name=name,
    )(*operands)


def dot(a, b):
    return jnp.dot(a, b, preferred_element_type=F32)


def dot_rows(a, b):
    return lax.dot_general(a, b, (((0,), (0,)), ((), ())), preferred_element_type=F32)


def group_total(row, group_size):
    channels = row.shape[-1]
    lane = lax.broadcasted_iota(jnp.int32, row.shape, 1)
    step = 1
    while step < group_size:
        up = pltpu.roll(row, channels - step, axis=1)
        down = pltpu.roll(row, step, axis=1)
        row = row + jnp.where((lane & step) == 0, up, down)
        step *= 2
    return row


def frame_stats(part_refs, f, entries, group_size):
    total = part_refs[0][f]
    for ref in part_refs[1:]:
        total = total + ref[f]
    return group_total(total, group_size) / entries


def mean_and_inv(part_refs, f, entries, group_size):
    both = frame_stats(part_refs, f, entries, group_size)
    mean = both[0:1]
    inv = lax.rsqrt(both[1:2] - mean * mean + NORM_EPS)
    return mean, inv


def column_sums(first, second):
    return jnp.concatenate(
        [jnp.sum(first, axis=0, keepdims=True), jnp.sum(second, axis=0, keepdims=True)], axis=0
    )


def put_windows(above, mid, below, lhs_ref, at, order):
    width, (pixels, channels) = above.shape[0], mid.shape
    first, mid_at, last = (slice(k * channels, (k + 1) * channels) for k in order)
    lhs_ref[at : at + width, first] = above
    lhs_ref[at + width : at + pixels, first] = mid[: pixels - width]
    lhs_ref[at : at + pixels, mid_at] = mid
    lhs_ref[at : at + pixels - width, last] = mid[width:]
    lhs_ref[at + pixels - width : at + pixels, last] = below


def from_left(y, width):
    col = lax.broadcasted_iota(jnp.int32, y.shape, 0) & (width - 1)
    return jnp.where(col == 0, 0.0, pltpu.roll(y, 1, axis=0))


def from_right(y, width):
    col = lax.broadcasted_iota(jnp.int32, y.shape, 0) & (width - 1)
    return jnp.where(col == width - 1, 0.0, pltpu.roll(y, y.shape[0] - 1, axis=0))


def slot_sources(clip_ref, dil_ref, local, frames):
    slot = lax.axis_index("tm") * frames + local
    start1 = clip_ref[0]
    filled = start1 + clip_ref[1]
    in_first = slot < start1
    d = jnp.where(in_first, dil_ref[0], dil_ref[1])
    low = jnp.where(in_first, 0, start1)
    high = jnp.where(in_first, start1, filled)
    used = slot < filled
    later, earlier = local + d, local - d
    later_live = used & (slot + d < high)
    earlier_live = used & (slot - d >= low)
    later_which = jnp.where(later_live, jnp.where(later < frames, 1, 2), 0)
    earlier_which = jnp.where(earlier_live, jnp.where(earlier >= 0, 1, 2), 0)
    return (later, later_which), (earlier, earlier_which), used


def gather_taps(clip_ref, dil_ref, local, own, nxt, prv, cat_ref, at, up_slot):
    frames, pixels, channels = own.shape
    later, earlier, used = slot_sources(clip_ref, dil_ref, local, frames)

    def put(slot, ref, index):
        cat_ref[pl.ds(at, pixels), slot * channels : (slot + 1) * channels] = ref[index]

    def clear(slot):
        cat_ref[pl.ds(at, pixels), slot * channels : (slot + 1) * channels] = jnp.zeros((pixels, channels), BF16)

    for slot, (index, which), other, shift in (
        (up_slot, later, nxt, -frames),
        (2 - up_slot, earlier, prv, frames),
    ):
        pl.when(which == 0)(functools.partial(clear, slot))
        pl.when(which == 1)(functools.partial(put, slot, own, jnp.clip(index, 0, frames - 1)))
        pl.when(which == 2)(functools.partial(put, slot, other, jnp.clip(index + shift, 0, frames - 1)))
    pl.when(used)(functools.partial(put, 1, own, local))
    pl.when(jnp.logical_not(used))(functools.partial(clear, 1))


def loop(count, body):
    def step(k, carry):
        body(k)
        return carry

    lax.fori_loop(0, count, step, 0)


def conv_kernel(x_ref, above_ref, below_ref, w_ref, out_ref, sums_ref, lhs_ref):
    frames, rows, width, channels = x_ref.shape
    pixels = rows * width

    def body(pair):
        for b in range(2):
            f = 2 * pair + b
            mid = x_ref[f].reshape(pixels, channels)
            put_windows(above_ref[f, 0], mid, below_ref[f, 0], lhs_ref, b * pixels, (0, 1, 2))
        lhs = lhs_ref[...]
        y = [dot(lhs, w_ref[:, j].reshape(3 * channels, channels)) for j in range(3)]
        out = y[1] + from_left(y[0], width) + from_right(y[2], width)
        for b in range(2):
            one = out[b * pixels : (b + 1) * pixels]
            out_ref[2 * pair + b] = one
            sums_ref[2 * pair + b] = column_sums(one, one * one)

    loop(frames // 2, body)


def act_kernel(n, entries, group_size, clip_ref, *refs):
    parts, (conv_ref, gain_ref, shift_ref, act_ref, normed_ref, slope_ref) = refs[:n], refs[n:]
    frames = conv_ref.shape[0]
    first = lax.axis_index("tm") * frames
    filled = clip_ref[0] + clip_ref[1]
    half_gain, half_shift = 0.5 * gain_ref[...], 0.5 * shift_ref[...]

    def body(f):
        mean, inv = mean_and_inv(parts, f, entries, group_size)
        normed = (conv_ref[f] - mean) * inv
        h = normed * half_gain + half_shift
        t = jnp.tanh(h)
        rise = 1.0 + t
        act_ref[f] = jnp.where(first + f < filled, h * rise, 0.0).astype(BF16)
        normed_ref[f] = normed.astype(BF16)
        slope_ref[f] = (rise * (1.0 + h * (1.0 - t)) * half_gain).astype(BF16)

    loop(frames, body)


def turn_kernel(x_ref, above_ref, below_ref, xt_ref, lhs_ref):
    frames, rows, width, channels = x_ref.shape
    pixels = rows * width

    def body(f):
        mid = x_ref[f].reshape(pixels, channels)
        put_windows(above_ref[f, 0], mid, below_ref[f, 0], lhs_ref, 0, (0, 1, 2))
        lanes = pl.ds(pl.multiple_of(f * pixels, pixels), pixels)
        for i in range(3):
            block = slice(i * channels, (i + 1) * channels)
            xt_ref[block, lanes] = lhs_ref[:, block].T

    loop(frames, body)


def turn_weights_kernel(spatial_ref, temporal_ref, back_ref, out_ref):
    channels = spatial_ref.shape[-1]
    for i in range(3):
        rows = slice(i * channels, (i + 1) * channels)
        out_ref[rows] = temporal_ref[i].T
        for j in range(3):
            back_ref[j, rows] = spatial_ref[i, j].T


def grad_act_kernel(
    clip_ref, dil_ref, own, nxt, prv, tw_ref, normed_ref, slope_ref, ga_ref, cat_ref, sums_ref
):
    frames, pixels, _ = own.shape

    def body(pair):
        rows = pl.ds(pl.multiple_of(2 * pair * pixels, 2 * pixels), 2 * pixels)
        for b in range(2):
            at = pl.multiple_of((2 * pair + b) * pixels, pixels)
            gather_taps(clip_ref, dil_ref, 2 * pair + b, own, nxt, prv, cat_ref, at, 0)
        grad_act = dot(cat_ref[rows], tw_ref[...]).astype(BF16)
        for b in range(2):
            f = 2 * pair + b
            one = grad_act[b * pixels : (b + 1) * pixels]
            ga_ref[f] = one
            gn = one.astype(F32) * slope_ref[f].astype(F32)
            sums_ref[f] = column_sums(gn, gn * normed_ref[f].astype(F32))

    loop(frames // 2, body)


def temporal_grad_kernel(act_ref, cat_ref, out_ref):
    frames, pixels, channels = act_ref.shape
    out_ref[...] = dot_rows(act_ref[...].reshape(frames * pixels, channels), cat_ref[...])


def norm_back_kernel(n, m, entries, group_size, normed_ref, slope_ref, ga_ref, *refs):
    parts, grad_parts = refs[:n], refs[n : n + m]
    g_ref, first_ref, last_ref, moved_ref = refs[n + m :]
    _, pixels, channels = normed_ref.shape
    width = first_ref.shape[2]

    def body(f):
        _, inv = mean_and_inv(parts, f, entries, group_size)
        means = frame_stats(grad_parts, f, entries, group_size)
        gn = ga_ref[f].astype(F32) * slope_ref[f].astype(F32)
        wide = inv * (gn - means[0:1] - normed_ref[f].astype(F32) * means[1:2])
        grad = wide.astype(BF16)
        g_ref[f] = grad
        first_ref[f, 0] = grad[:width]
        last_ref[f, 0] = grad[pixels - width :]
        here = pl.ds(pl.multiple_of(f * pixels, pixels), pixels)
        moved_ref[here, :channels] = from_right(wide, width).astype(BF16)
        moved_ref[here, channels : 2 * channels] = grad
        moved_ref[here, 2 * channels :] = from_left(wide, width).astype(BF16)

    loop(normed_ref.shape[0], body)


def weight_part_kernel(xt_ref, moved_ref, out_ref):
    out_ref[...] = dot(xt_ref[...], moved_ref[:, : out_ref.shape[1]])


def weight_grad_kernel(xt_ref, moved_ref, part_ref, temporal_ref, send_ref, keep_ref, acc_ref):
    channels = temporal_ref.shape[0]
    done = part_ref.shape[1]
    acc_ref[: 3 * channels, done:] = dot(xt_ref[...], moved_ref[:, done:])
    acc_ref[: 3 * channels, :done] = part_ref[...]
    acc_ref[3 * channels :, :] = temporal_ref[...]

    chips, depth, block, _ = keep_ref.shape
    half = chips * depth * block
    core = lax.axis_index("tm") & 1

    def hand_out(kept, sent):
        for p in range(chips):
            for z in range(depth):
                at = (p * depth + z) * block
                keep_ref[p, z] = acc_ref[kept + at : kept + at + block]
                send_ref[p, z] = acc_ref[sent + at : sent + at + block].astype(BF16)

    pl.when(core == 0)(functools.partial(hand_out, 0, half))
    pl.when(core == 1)(functools.partial(hand_out, half, 0))


def conv_back_kernel(g_ref, above_ref, below_ref, cot_ref, w_ref, out_ref, lhs_ref):
    frames, rows, width, channels = cot_ref.shape
    pixels = rows * width

    def body(pair):
        for b in range(2):
            f = 2 * pair + b
            put_windows(above_ref[f, 0], g_ref[f], below_ref[f, 0], lhs_ref, b * pixels, (2, 1, 0))
        lhs = lhs_ref[...]
        z = [dot(lhs, w_ref[j]) for j in range(3)]
        out = z[1] + from_right(z[0], width) + from_left(z[2], width)
        for b in range(2):
            one = out[b * pixels : (b + 1) * pixels].reshape(rows, width, channels)
            out_ref[2 * pair + b] = (one + cot_ref[2 * pair + b].astype(F32)).astype(BF16)

    loop(frames // 2, body)


def out_kernel(clip_ref, dil_ref, own, nxt, prv, tw_ref, x_ref, out_ref, cat_ref):
    frames, rows, width, channels = x_ref.shape
    pixels = rows * width

    def body(pair):
        for b in range(2):
            gather_taps(clip_ref, dil_ref, 2 * pair + b, own, nxt, prv, cat_ref, b * pixels, 2)
        temporal_out = dot(cat_ref[...], tw_ref[...]).astype(BF16).astype(F32)
        for b in range(2):
            one = temporal_out[b * pixels : (b + 1) * pixels].reshape(rows, width, channels)
            out_ref[2 * pair + b] = (x_ref[2 * pair + b].astype(F32) + one).astype(BF16)

    loop(frames // 2, body)


def core_sum_kernel(keep_ref, got_ref, own_ref, *send_refs):
    chip = lax.axis_index("tm") >> 1
    own_ref[...] = keep_ref[chip] + got_ref[chip].astype(F32)
    for s, ref in enumerate(send_refs, 1):
        ref[...] = (keep_ref[chip ^ s] + got_ref[chip ^ s].astype(F32)).astype(BF16)


def sum_kernel(count, own_ref, *refs):
    total = own_ref[...]
    for ref in refs[:count]:
        total = total + ref[...].astype(F32)
    refs[count][...] = total.astype(BF16)


def sum_split_kernel(count, own_ref, *refs):
    got, (mine_ref, *send_refs) = refs[:count], refs[count:]
    deep = lax.axis_index("space")

    def block(k):
        total = own_ref[k]
        for ref in got:
            total = total + ref[k].astype(F32)
        return total

    mine_ref[...] = block(deep)
    for s, ref in enumerate(send_refs, 1):
        ref[...] = block(deep ^ s).astype(BF16)


def place_kernel(axis, shift, *refs):
    me = lax.axis_index(axis) >> shift
    for s, ref in enumerate(refs[:-1]):
        refs[-1][me ^ s] = ref[...]


def finish_kernel(mine_ref, got_ref, spatial_ref, temporal_ref):
    chips, depth, block, _ = mine_ref.shape
    channels = spatial_ref.shape[-1]

    def write(pair):
        for c in range(2):
            for p in range(chips):
                for z in range(depth):
                    row = ((c * chips + p) * depth + z) * block
                    values = pair[c][p, z].astype(F32)
                    i, at = row // channels, row % channels
                    for k in range(3):
                        lanes = values[:, k * channels : (k + 1) * channels]
                        if i < 3:
                            spatial_ref[i, k, at : at + block] = lanes
                        else:
                            temporal_ref[k, at : at + block] = lanes

    core = lax.axis_index("tm") & 1
    pl.when(core == 0)(functools.partial(write, (mine_ref, got_ref)))
    pl.when(core == 1)(functools.partial(write, (got_ref, mine_ref)))


def neighbours(axis, low, high):
    size = lax.axis_size(axis)
    up = [(i, i + 1) for i in range(size - 1)]
    down = [(j, i) for i, j in up]
    return lax.ppermute(high, axis, up), lax.ppermute(low, axis, down)


def spread_sums(part, axis):
    size = lax.axis_size(axis)
    step, got = 1, None
    while step < size:
        if got is not None:
            part = part + got
        got = lax.ppermute(part, axis, [(i, i ^ step) for i in range(size)])
        step *= 2
    return [part, got]


def per_device(frames_in, cotangent, spatial, temporal, norm_gain, norm_shift, clip_frames, dilation):
    frames, rows, width, channels = frames_in.shape
    pixels = rows * width
    n, tm = lax.axis_size("space"), lax.axis_size("tm")
    chips = tm // 2
    group_size = channels // GROUPS
    entries = float(rows * n * width * group_size)
    gain, shift = norm_gain[None], norm_shift[None]
    big = frames * pixels * channels
    shape = jax.ShapeDtypeStruct
    per_px = (frames, pixels, channels)
    windows = pltpu.VMEM((2 * pixels, 3 * channels), BF16)

    cot = cotangent.reshape(per_px)
    cot_prev, cot_next = neighbours("tm", cot, cot)
    above, below = neighbours("space", frames_in[:, :1], frames_in[:, rows - 1 :])

    back_weights, back_taps = call(
        turn_weights_kernel, "turn_weights", [spatial, temporal],
        [shape((3, 3 * channels, channels), BF16), shape((3 * channels, channels), BF16)], 0, big,
    )
    above, back_weights, back_taps = lax.optimization_barrier((above, back_weights, back_taps))
    conv_out, sums = call(
        conv_kernel, "conv_forward", [frames_in, above, below, spatial],
        [shape(per_px, F32), shape((frames, 2, channels), F32)],
        18 * big * channels, 8 * big, [windows], 18,
    )
    parts = spread_sums(sums, "space")
    x_turned = call(
        turn_kernel, "turned", [frames_in, above, below], shape((3 * channels, frames * pixels), BF16),
        0, 8 * big, [pltpu.VMEM((pixels, 3 * channels), BF16)],
    )
    x_turned, *parts = lax.optimization_barrier((x_turned, *parts))
    act, normed, slope = call(
        functools.partial(act_kernel, len(parts), entries, group_size), "activation",
        [clip_frames, *parts, conv_out, gain, shift],
        [shape(per_px, BF16)] * 3, 10 * big, 10 * big,
    )
    act_sent, cot_prev, cot_next = lax.optimization_barrier((act, cot_prev, cot_next))
    act_prev, act_next = neighbours("tm", act_sent, act_sent)

    grad_act, cot_cat, grad_sums = call(
        grad_act_kernel, "grad_activation",
        [clip_frames, dilation, cot, cot_next, cot_prev, back_taps, normed, slope],
        [shape(per_px, BF16), shape((frames * pixels, 3 * channels), BF16), shape((frames, 2, channels), F32)],
        6 * big * channels, 16 * big,
    )
    grad_parts = spread_sums(grad_sums, "space")
    temporal_part = call(
        temporal_grad_kernel, "temporal_grad", [act, cot_cat],
        shape((channels, 3 * channels), F32), 6 * big * channels, 8 * big,
    )
    lanes = 3 * channels
    grad_conv, first_rows, last_rows, moved = call(
        functools.partial(norm_back_kernel, len(parts), len(grad_parts), entries, group_size), "norm_backward",
        [normed, slope, grad_act, *parts, *grad_parts],
        [shape(per_px, BF16)] + [shape((frames, 1, width, channels), BF16)] * 2
        + [shape((frames * pixels, lanes), BF16)],
        0, 12 * big,
    )
    grad_above, grad_below = neighbours("space", first_rows, last_rows)
    part = call(
        weight_part_kernel, "weight_part", [x_turned, moved], shape((lanes, 2 * channels), F32),
        12 * big * channels, 8 * big,
    )
    moved, grad_above, grad_below = lax.optimization_barrier((moved, grad_above, grad_below))
    block = 2 * channels // (chips * n)
    send, keep = call(
        weight_grad_kernel, "weight_grad", [x_turned, moved, part, temporal_part],
        [shape((chips, n, block, lanes), BF16), shape((chips, n, block, lanes), F32)],
        6 * big * channels, 8 * big, [pltpu.VMEM((4 * channels, lanes), F32)], 20,
    )

    def other_chip(s):
        return [(i, i ^ (2 * s)) for i in range(tm)]

    def other_plane(s):
        return [(i, i ^ s) for i in range(n)]

    other_core = [(i, i ^ 1) for i in range(tm)]
    got = lax.ppermute(send, "tm", other_core)
    own, *sends = call(
        core_sum_kernel, "core_sum", [keep, got],
        [shape((n, block, lanes), F32)] + [shape((n, block, lanes), BF16)] * (chips - 1), 0, 4 * big,
    )
    gots = [lax.ppermute(x, "tm", other_chip(s)) for s, x in enumerate(sends, 1)]

    in_grad = call(
        conv_back_kernel, "conv_backward", [grad_conv, grad_above, grad_below, cotangent, back_weights],
        shape(frames_in.shape, BF16), 18 * big * channels, 8 * big, [windows], 20,
    )
    own, in_grad = lax.optimization_barrier((own, in_grad))

    own, *sends = call(
        functools.partial(sum_split_kernel, chips - 1), "plane_sum", [own, *gots],
        [shape((block, lanes), F32)] + [shape((block, lanes), BF16)] * (n - 1), 0, big,
    )
    gots = [lax.ppermute(x, "space", other_plane(s)) for s, x in enumerate(sends, 1)]
    own = call(
        functools.partial(sum_kernel, n - 1), "line_sum", [own, *gots], shape((block, lanes), BF16), 0, big
    )
    gots = [lax.ppermute(own, "space", other_plane(s)) for s in range(1, n)]
    own = call(
        functools.partial(place_kernel, "space", 0), "line_place", [own, *gots], shape((n, block, lanes), BF16), 0, big
    )
    gots = [lax.ppermute(own, "tm", other_chip(s)) for s in range(1, chips)]

    out_frames = call(
        out_kernel, "temporal_forward",
        [clip_frames, dilation, act, act_next, act_prev, temporal.reshape(3 * channels, channels), frames_in],
        shape(frames_in.shape, BF16), 6 * big * channels, 10 * big, [windows],
    )
    own, out_frames = lax.optimization_barrier((own, out_frames))

    own = call(
        functools.partial(place_kernel, "tm", 1), "plane_place", [own, *gots], shape((chips, n, block, lanes), BF16), 0, big
    )
    got = lax.ppermute(own, "tm", other_core)
    spatial_grad, temporal_grad = call(
        finish_kernel, "finish", [own, got], [shape(spatial.shape, F32), shape(temporal.shape, F32)], 0, 4 * big
    )
    return (out_frames, in_grad, spatial_grad, temporal_grad)


def solution(mesh):
    tiles = P("tm", "space", None, None)
    return jax.shard_map(
        per_device,
        mesh=mesh,
        in_specs=(tiles, tiles, P(), P(), P(), P(), P(), P()),
        out_specs=(tiles, tiles, P(), P()),
        check_vma=False,
    )
```

```python
import functools

import jax
import jax.numpy as jnp
from jax import lax
from jax.experimental import pallas as pl
from jax.experimental.pallas import tpu as pltpu
from jax.sharding import PartitionSpec as P

GROUPS = 32
NORM_EPS = 1e-05
BF16 = jnp.bfloat16
F32 = jnp.float32
MIB = 2**20


def call(kernel, name, operands, out_shape, flops=0, moved=0, scratch=(), grant=14):
    vmem = pl.BlockSpec(memory_space=pltpu.VMEM)
    smem = pl.BlockSpec(memory_space=pltpu.SMEM)
    return pl.pallas_call(
        kernel,
        in_specs=[smem if x.dtype == jnp.int32 else vmem for x in operands],
        out_specs=jax.tree.map(lambda _: vmem, out_shape),
        out_shape=out_shape,
        scratch_shapes=list(scratch),
        compiler_params=pltpu.CompilerParams(vmem_limit_bytes=grant * MIB),
        cost_estimate=pl.CostEstimate(flops=int(flops), bytes_accessed=int(moved), transcendentals=0),
        name=name,
    )(*operands)


def dot(a, b):
    return jnp.dot(a, b, preferred_element_type=F32)


def dot_rows(a, b):
    return lax.dot_general(a, b, (((0,), (0,)), ((), ())), preferred_element_type=F32)


def group_total(row, group_size):
    channels = row.shape[-1]
    lane = lax.broadcasted_iota(jnp.int32, row.shape, 1)
    step = 1
    while step < group_size:
        up = pltpu.roll(row, channels - step, axis=1)
        down = pltpu.roll(row, step, axis=1)
        row = row + jnp.where((lane & step) == 0, up, down)
        step *= 2
    return row


def frame_stats(part_refs, f, entries, group_size):
    total = part_refs[0][f]
    for ref in part_refs[1:]:
        total = total + ref[f]
    return group_total(total, group_size) / entries


def mean_and_inv(part_refs, f, entries, group_size):
    both = frame_stats(part_refs, f, entries, group_size)
    mean = both[0:1]
    inv = lax.rsqrt(both[1:2] - mean * mean + NORM_EPS)
    return mean, inv


def column_sums(first, second):
    return jnp.concatenate(
        [jnp.sum(first, axis=0, keepdims=True), jnp.sum(second, axis=0, keepdims=True)], axis=0
    )


def put_windows(above, mid, below, lhs_ref, at, order):
    width, (pixels, channels) = above.shape[0], mid.shape
    first, mid_at, last = (slice(k * channels, (k + 1) * channels) for k in order)
    lhs_ref[at : at + width, first] = above
    lhs_ref[at + width : at + pixels, first] = mid[: pixels - width]
    lhs_ref[at : at + pixels, mid_at] = mid
    lhs_ref[at : at + pixels - width, last] = mid[width:]
    lhs_ref[at + pixels - width : at + pixels, last] = below


def from_left(y, width):
    col = lax.broadcasted_iota(jnp.int32, y.shape, 0) & (width - 1)
    return jnp.where(col == 0, 0.0, pltpu.roll(y, 1, axis=0))


def from_right(y, width):
    col = lax.broadcasted_iota(jnp.int32, y.shape, 0) & (width - 1)
    return jnp.where(col == width - 1, 0.0, pltpu.roll(y, y.shape[0] - 1, axis=0))


def slot_sources(clip_ref, dil_ref, local, frames):
    slot = lax.axis_index("tm") * frames + local
    start1 = clip_ref[0]
    filled = start1 + clip_ref[1]
    in_first = slot < start1
    d = jnp.where(in_first, dil_ref[0], dil_ref[1])
    low = jnp.where(in_first, 0, start1)
    high = jnp.where(in_first, start1, filled)
    used = slot < filled
    later, earlier = local + d, local - d
    later_live = used & (slot + d < high)
    earlier_live = used & (slot - d >= low)
    later_which = jnp.where(later_live, jnp.where(later < frames, 1, 2), 0)
    earlier_which = jnp.where(earlier_live, jnp.where(earlier >= 0, 1, 2), 0)
    return (later, later_which), (earlier, earlier_which), used


def gather_taps(clip_ref, dil_ref, local, own, nxt, prv, cat_ref, at, up_slot):
    frames, pixels, channels = own.shape
    later, earlier, used = slot_sources(clip_ref, dil_ref, local, frames)

    def put(slot, ref, index):
        cat_ref[pl.ds(at, pixels), slot * channels : (slot + 1) * channels] = ref[index]

    def clear(slot):
        cat_ref[pl.ds(at, pixels), slot * channels : (slot + 1) * channels] = jnp.zeros((pixels, channels), BF16)

    for slot, (index, which), other, shift in (
        (up_slot, later, nxt, -frames),
        (2 - up_slot, earlier, prv, frames),
    ):
        pl.when(which == 0)(functools.partial(clear, slot))
        pl.when(which == 1)(functools.partial(put, slot, own, jnp.clip(index, 0, frames - 1)))
        pl.when(which == 2)(functools.partial(put, slot, other, jnp.clip(index + shift, 0, frames - 1)))
    pl.when(used)(functools.partial(put, 1, own, local))
    pl.when(jnp.logical_not(used))(functools.partial(clear, 1))


def loop(count, body):
    def step(k, carry):
        body(k)
        return carry

    lax.fori_loop(0, count, step, 0)


def conv_kernel(x_ref, above_ref, below_ref, w_ref, out_ref, sums_ref, lhs_ref):
    frames, rows, width, channels = x_ref.shape
    pixels = rows * width

    def body(pair):
        for b in range(2):
            f = 2 * pair + b
            mid = x_ref[f].reshape(pixels, channels)
            put_windows(above_ref[f, 0], mid, below_ref[f, 0], lhs_ref, b * pixels, (0, 1, 2))
        lhs = lhs_ref[...]
        y = [dot(lhs, w_ref[:, j].reshape(3 * channels, channels)) for j in range(3)]
        out = y[1] + from_left(y[0], width) + from_right(y[2], width)
        for b in range(2):
            one = out[b * pixels : (b + 1) * pixels]
            out_ref[2 * pair + b] = one
            sums_ref[2 * pair + b] = column_sums(one, one * one)

    loop(frames // 2, body)


def act_kernel(n, entries, group_size, clip_ref, *refs):
    parts, refs = refs[:n], refs[n:]
    conv_ref, gain_ref, shift_ref, act_ref, normed_ref, slope_ref, first_ref, last_ref = refs
    frames, pixels, _ = conv_ref.shape
    width = first_ref.shape[2]
    first = lax.axis_index("tm") * frames
    top, bottom = slice(0, width), slice(pixels - width, pixels)
    filled = clip_ref[0] + clip_ref[1]
    half_gain, half_shift = 0.5 * gain_ref[...], 0.5 * shift_ref[...]

    def body(f):
        mean, inv = mean_and_inv(parts, f, entries, group_size)
        normed = (conv_ref[f] - mean) * inv
        h = normed * half_gain + half_shift
        t = jnp.tanh(h)
        rise = 1.0 + t
        act_ref[f] = jnp.where(first + f < filled, h * rise, 0.0).astype(BF16)
        for k, (ref, value) in enumerate(((normed_ref, normed), (slope_ref, rise * (1.0 + h * (1.0 - t)) * half_gain))):
            value = value.astype(BF16)
            ref[f] = value
            first_ref[f, k] = value[top]
            last_ref[f, k] = value[bottom]

    loop(frames, body)


def turn_kernel(x_ref, above_ref, below_ref, xt_ref, lhs_ref):
    frames, rows, width, channels = x_ref.shape
    pixels = rows * width

    def body(f):
        mid = x_ref[f].reshape(pixels, channels)
        put_windows(above_ref[f, 0], mid, below_ref[f, 0], lhs_ref, 0, (0, 1, 2))
        lanes = pl.ds(pl.multiple_of(f * pixels, pixels), pixels)
        for i in range(3):
            block = slice(i * channels, (i + 1) * channels)
            xt_ref[block, lanes] = lhs_ref[:, block].T

    loop(frames, body)


def turn_weights_kernel(spatial_ref, temporal_ref, back_ref, out_ref):
    channels = spatial_ref.shape[-1]
    for i in range(3):
        rows = slice(i * channels, (i + 1) * channels)
        out_ref[rows] = temporal_ref[i].T
        for j in range(3):
            back_ref[j, rows] = spatial_ref[i, j].T


def grad_act_kernel(
    clip_ref, dil_ref, own, nxt, prv, tw_ref, normed_ref, slope_ref, ga_ref, first_ref, last_ref, cat_ref, sums_ref
):
    frames, pixels, _ = own.shape
    width = first_ref.shape[1]

    def body(pair):
        rows = pl.ds(pl.multiple_of(2 * pair * pixels, 2 * pixels), 2 * pixels)
        for b in range(2):
            at = pl.multiple_of((2 * pair + b) * pixels, pixels)
            gather_taps(clip_ref, dil_ref, 2 * pair + b, own, nxt, prv, cat_ref, at, 0)
        grad_act = dot(cat_ref[rows], tw_ref[...]).astype(BF16)
        for b in range(2):
            f = 2 * pair + b
            one = grad_act[b * pixels : (b + 1) * pixels]
            ga_ref[f] = one
            first_ref[f] = one[:width]
            last_ref[f] = one[pixels - width :]
            gn = one.astype(F32) * slope_ref[f].astype(F32)
            sums_ref[f] = column_sums(gn, gn * normed_ref[f].astype(F32))

    loop(frames // 2, body)


def temporal_grad_kernel(act_ref, cat_ref, out_ref):
    frames, pixels, channels = act_ref.shape
    out_ref[...] = dot_rows(act_ref[...].reshape(frames * pixels, channels), cat_ref[...])


def norm_back(inv, means, normed, slope, grad_act):
    gn = grad_act.astype(F32) * slope.astype(F32)
    return inv * (gn - means[0:1] - normed.astype(F32) * means[1:2])


def norm_back_kernel(width, n, m, entries, group_size, normed_ref, slope_ref, ga_ref, *refs):
    parts, grad_parts = refs[:n], refs[n : n + m]
    g_ref, moved_ref = refs[n + m :]
    _, pixels, channels = normed_ref.shape

    def body(f):
        _, inv = mean_and_inv(parts, f, entries, group_size)
        means = frame_stats(grad_parts, f, entries, group_size)
        wide = norm_back(inv, means, normed_ref[f], slope_ref[f], ga_ref[f])
        grad = wide.astype(BF16)
        g_ref[f] = grad
        here = pl.ds(pl.multiple_of(f * pixels, pixels), pixels)
        moved_ref[here, :channels] = from_right(wide, width).astype(BF16)
        moved_ref[here, channels : 2 * channels] = grad
        moved_ref[here, 2 * channels :] = from_left(wide, width).astype(BF16)

    loop(normed_ref.shape[0], body)


def weight_part_kernel(xt_ref, moved_ref, out_ref):
    out_ref[...] = dot(xt_ref[...], moved_ref[:, : out_ref.shape[1]])


def weight_grad_kernel(xt_ref, moved_ref, part_ref, temporal_ref, send_ref, keep_ref, acc_ref):
    channels = temporal_ref.shape[0]
    done = part_ref.shape[1]
    acc_ref[: 3 * channels, done:] = dot(xt_ref[...], moved_ref[:, done:])
    acc_ref[: 3 * channels, :done] = part_ref[...]
    acc_ref[3 * channels :, :] = temporal_ref[...]

    chips, depth, block, _ = keep_ref.shape
    half = chips * depth * block
    core = lax.axis_index("tm") & 1

    def hand_out(kept, sent):
        for p in range(chips):
            for z in range(depth):
                at = (p * depth + z) * block
                keep_ref[p, z] = acc_ref[kept + at : kept + at + block]
                send_ref[p, z] = acc_ref[sent + at : sent + at + block].astype(BF16)

    pl.when(core == 0)(functools.partial(hand_out, 0, half))
    pl.when(core == 1)(functools.partial(hand_out, half, 0))


def conv_back_kernel(n, m, entries, group_size, g_ref, near_above, near_below, ga_above, ga_below, cot_ref, w_ref, *refs):
    parts, grad_parts = refs[:n], refs[n : n + m]
    out_ref, lhs_ref = refs[n + m :]
    frames, rows, width, channels = cot_ref.shape
    pixels = rows * width
    place, size = lax.axis_index("space"), lax.axis_size("space")

    def body(pair):
        for b in range(2):
            f = 2 * pair + b
            _, inv = mean_and_inv(parts, f, entries, group_size)
            means = frame_stats(grad_parts, f, entries, group_size)
            above = norm_back(inv, means, near_above[f, 0], near_above[f, 1], ga_above[f])
            below = norm_back(inv, means, near_below[f, 0], near_below[f, 1], ga_below[f])
            above = jnp.where(place > 0, above, 0.0).astype(BF16)
            below = jnp.where(place < size - 1, below, 0.0).astype(BF16)
            put_windows(above, g_ref[f], below, lhs_ref, b * pixels, (2, 1, 0))
        lhs = lhs_ref[...]
        z = [dot(lhs, w_ref[j]) for j in range(3)]
        out = z[1] + from_right(z[0], width) + from_left(z[2], width)
        for b in range(2):
            one = out[b * pixels : (b + 1) * pixels].reshape(rows, width, channels)
            out_ref[2 * pair + b] = (one + cot_ref[2 * pair + b].astype(F32)).astype(BF16)

    loop(frames // 2, body)


def out_kernel(clip_ref, dil_ref, own, nxt, prv, tw_ref, x_ref, out_ref, cat_ref):
    frames, rows, width, channels = x_ref.shape
    pixels = rows * width

    def body(pair):
        for b in range(2):
            gather_taps(clip_ref, dil_ref, 2 * pair + b, own, nxt, prv, cat_ref, b * pixels, 2)
        temporal_out = dot(cat_ref[...], tw_ref[...]).astype(BF16).astype(F32)
        for b in range(2):
            one = temporal_out[b * pixels : (b + 1) * pixels].reshape(rows, width, channels)
            out_ref[2 * pair + b] = (x_ref[2 * pair + b].astype(F32) + one).astype(BF16)

    loop(frames // 2, body)


def core_sum_kernel(keep_ref, got_ref, own_ref, *send_refs):
    chip = lax.axis_index("tm") >> 1
    own_ref[...] = keep_ref[chip] + got_ref[chip].astype(F32)
    for s, ref in enumerate(send_refs, 1):
        ref[...] = (keep_ref[chip ^ s] + got_ref[chip ^ s].astype(F32)).astype(BF16)


def sum_kernel(count, own_ref, *refs):
    total = own_ref[...]
    for ref in refs[:count]:
        total = total + ref[...].astype(F32)
    refs[count][...] = total.astype(BF16)


def sum_split_kernel(count, own_ref, *refs):
    got, (mine_ref, *send_refs) = refs[:count], refs[count:]
    deep = lax.axis_index("space")

    def block(k):
        total = own_ref[k]
        for ref in got:
            total = total + ref[k].astype(F32)
        return total

    mine_ref[...] = block(deep)
    for s, ref in enumerate(send_refs, 1):
        ref[...] = block(deep ^ s).astype(BF16)


def place_kernel(axis, shift, *refs):
    me = lax.axis_index(axis) >> shift
    for s, ref in enumerate(refs[:-1]):
        refs[-1][me ^ s] = ref[...]


def finish_kernel(mine_ref, got_ref, spatial_ref, temporal_ref):
    chips, depth, block, _ = mine_ref.shape
    channels = spatial_ref.shape[-1]

    def write(pair):
        for c in range(2):
            for p in range(chips):
                for z in range(depth):
                    row = ((c * chips + p) * depth + z) * block
                    values = pair[c][p, z].astype(F32)
                    i, at = row // channels, row % channels
                    for k in range(3):
                        lanes = values[:, k * channels : (k + 1) * channels]
                        if i < 3:
                            spatial_ref[i, k, at : at + block] = lanes
                        else:
                            temporal_ref[k, at : at + block] = lanes

    core = lax.axis_index("tm") & 1
    pl.when(core == 0)(functools.partial(write, (mine_ref, got_ref)))
    pl.when(core == 1)(functools.partial(write, (got_ref, mine_ref)))


def neighbours(axis, low, high):
    size = lax.axis_size(axis)
    up = [(i, i + 1) for i in range(size - 1)]
    down = [(j, i) for i, j in up]
    return lax.ppermute(high, axis, up), lax.ppermute(low, axis, down)


def spread_sums(part, axis):
    size = lax.axis_size(axis)
    step, got = 1, None
    while step < size:
        if got is not None:
            part = part + got
        got = lax.ppermute(part, axis, [(i, i ^ step) for i in range(size)])
        step *= 2
    return [part, got]


def per_device(frames_in, cotangent, spatial, temporal, norm_gain, norm_shift, clip_frames, dilation):
    frames, rows, width, channels = frames_in.shape
    pixels = rows * width
    n, tm = lax.axis_size("space"), lax.axis_size("tm")
    chips = tm // 2
    group_size = channels // GROUPS
    entries = float(rows * n * width * group_size)
    gain, shift = norm_gain[None], norm_shift[None]
    big = frames * pixels * channels
    shape = jax.ShapeDtypeStruct
    per_px = (frames, pixels, channels)
    windows = pltpu.VMEM((2 * pixels, 3 * channels), BF16)

    cot = cotangent.reshape(per_px)
    cot_prev, cot_next = neighbours("tm", cot, cot)
    above, below = neighbours("space", frames_in[:, :1], frames_in[:, rows - 1 :])

    back_weights, back_taps = call(
        turn_weights_kernel, "turn_weights", [spatial, temporal],
        [shape((3, 3 * channels, channels), BF16), shape((3 * channels, channels), BF16)], 0, big,
    )
    above, back_weights, back_taps = lax.optimization_barrier((above, back_weights, back_taps))
    conv_out, sums = call(
        conv_kernel, "conv_forward", [frames_in, above, below, spatial],
        [shape(per_px, F32), shape((frames, 2, channels), F32)],
        18 * big * channels, 8 * big, [windows], 18,
    )
    parts = spread_sums(sums, "space")
    x_turned = call(
        turn_kernel, "turned", [frames_in, above, below], shape((3 * channels, frames * pixels), BF16),
        0, 8 * big, [pltpu.VMEM((pixels, 3 * channels), BF16)],
    )
    x_turned, *parts = lax.optimization_barrier((x_turned, *parts))
    edge = shape((frames, 2, width, channels), BF16)
    act, normed, slope, near_first, near_last = call(
        functools.partial(act_kernel, len(parts), entries, group_size), "activation",
        [clip_frames, *parts, conv_out, gain, shift],
        [shape(per_px, BF16)] * 3 + [edge] * 2, 10 * big, 10 * big,
    )
    near_above, near_below = neighbours("space", near_first, near_last)

    edge = shape((frames, width, channels), BF16)
    grad_act, ga_first, ga_last, cot_cat, grad_sums = call(
        grad_act_kernel, "grad_activation",
        [clip_frames, dilation, cot, cot_next, cot_prev, back_taps, normed, slope],
        [
            shape(per_px, BF16), edge, edge, shape((frames * pixels, 3 * channels), BF16),
            shape((frames, 2, channels), F32),
        ],
        6 * big * channels, 16 * big,
    )
    ga_above, ga_below = neighbours("space", ga_first, ga_last)
    grad_parts = spread_sums(grad_sums, "space")
    grad_parts[0], act_sent = lax.optimization_barrier((grad_parts[0], act))
    act_prev, act_next = neighbours("tm", act_sent, act_sent)
    temporal_part = call(
        temporal_grad_kernel, "temporal_grad", [act, cot_cat],
        shape((channels, 3 * channels), F32), 6 * big * channels, 8 * big,
    )
    grad_parts[0], near_above, near_below = lax.optimization_barrier((grad_parts[0], near_above, near_below))
    lanes = 3 * channels
    grad_conv, moved = call(
        functools.partial(norm_back_kernel, width, len(parts), len(grad_parts), entries, group_size), "norm_backward",
        [normed, slope, grad_act, *parts, *grad_parts],
        [shape(per_px, BF16), shape((frames * pixels, lanes), BF16)],
        0, 12 * big,
    )
    part = call(
        weight_part_kernel, "weight_part", [x_turned, moved], shape((lanes, 2 * channels), F32),
        12 * big * channels, 8 * big,
    )
    moved, ga_above, ga_below = lax.optimization_barrier((moved, ga_above, ga_below))
    block = 2 * channels // (chips * n)
    send, keep = call(
        weight_grad_kernel, "weight_grad", [x_turned, moved, part, temporal_part],
        [shape((chips, n, block, lanes), BF16), shape((chips, n, block, lanes), F32)],
        6 * big * channels, 8 * big, [pltpu.VMEM((4 * channels, lanes), F32)], 20,
    )

    def other_chip(s):
        return [(i, i ^ (2 * s)) for i in range(tm)]

    def other_plane(s):
        return [(i, i ^ s) for i in range(n)]

    other_core = [(i, i ^ 1) for i in range(tm)]
    got = lax.ppermute(send, "tm", other_core)
    own, *sends = call(
        core_sum_kernel, "core_sum", [keep, got],
        [shape((n, block, lanes), F32)] + [shape((n, block, lanes), BF16)] * (chips - 1), 0, 4 * big,
    )
    gots = [lax.ppermute(x, "tm", other_chip(s)) for s, x in enumerate(sends, 1)]

    in_grad = call(
        functools.partial(conv_back_kernel, len(parts), len(grad_parts), entries, group_size), "conv_backward",
        [grad_conv, near_above, near_below, ga_above, ga_below, cotangent, back_weights, *parts, *grad_parts],
        shape(frames_in.shape, BF16), 18 * big * channels, 8 * big, [windows], 20,
    )
    own, in_grad = lax.optimization_barrier((own, in_grad))

    own, *sends = call(
        functools.partial(sum_split_kernel, chips - 1), "plane_sum", [own, *gots],
        [shape((block, lanes), F32)] + [shape((block, lanes), BF16)] * (n - 1), 0, big,
    )
    gots = [lax.ppermute(x, "space", other_plane(s)) for s, x in enumerate(sends, 1)]
    own = call(
        functools.partial(sum_kernel, n - 1), "line_sum", [own, *gots], shape((block, lanes), BF16), 0, big
    )
    gots = [lax.ppermute(own, "space", other_plane(s)) for s in range(1, n)]
    own = call(
        functools.partial(place_kernel, "space", 0), "line_place", [own, *gots], shape((n, block, lanes), BF16), 0, big
    )
    gots = [lax.ppermute(own, "tm", other_chip(s)) for s in range(1, chips)]

    out_frames = call(
        out_kernel, "temporal_forward",
        [clip_frames, dilation, act, act_next, act_prev, temporal.reshape(3 * channels, channels), frames_in],
        shape(frames_in.shape, BF16), 6 * big * channels, 10 * big, [windows],
    )
    own, out_frames = lax.optimization_barrier((own, out_frames))

    own = call(
        functools.partial(place_kernel, "tm", 1), "plane_place", [own, *gots], shape((chips, n, block, lanes), BF16), 0, big
    )
    got = lax.ppermute(own, "tm", other_core)
    spatial_grad, temporal_grad = call(
        finish_kernel, "finish", [own, got], [shape(spatial.shape, F32), shape(temporal.shape, F32)], 0, 4 * big
    )
    return (out_frames, in_grad, spatial_grad, temporal_grad)


def solution(mesh):
    tiles = P("tm", "space", None, None)
    return jax.shard_map(
        per_device,
        mesh=mesh,
        in_specs=(tiles, tiles, P(), P(), P(), P(), P(), P()),
        out_specs=(tiles, tiles, P(), P()),
        check_vma=False,
    )
```

```python
import functools

import jax
import jax.numpy as jnp
from jax import lax
from jax.experimental import pallas as pl
from jax.experimental.pallas import tpu as pltpu
from jax.sharding import PartitionSpec as P

GROUPS = 32
NORM_EPS = 1e-05
BF16 = jnp.bfloat16
F32 = jnp.float32
MIB = 2**20


def call(kernel, name, operands, out_shape, flops=0, moved=0, scratch=(), grant=14):
    vmem = pl.BlockSpec(memory_space=pltpu.VMEM)
    smem = pl.BlockSpec(memory_space=pltpu.SMEM)
    return pl.pallas_call(
        kernel,
        in_specs=[smem if x.dtype == jnp.int32 else vmem for x in operands],
        out_specs=jax.tree.map(lambda _: vmem, out_shape),
        out_shape=out_shape,
        scratch_shapes=list(scratch),
        compiler_params=pltpu.CompilerParams(vmem_limit_bytes=grant * MIB),
        cost_estimate=pl.CostEstimate(flops=int(flops), bytes_accessed=int(moved), transcendentals=0),
        name=name,
    )(*operands)


def dot(a, b):
    return jnp.dot(a, b, preferred_element_type=F32)


def dot_rows(a, b):
    return lax.dot_general(a, b, (((0,), (0,)), ((), ())), preferred_element_type=F32)


def group_total(row, group_size):
    channels = row.shape[-1]
    lane = lax.broadcasted_iota(jnp.int32, row.shape, 1)
    step = 1
    while step < group_size:
        up = pltpu.roll(row, channels - step, axis=1)
        down = pltpu.roll(row, step, axis=1)
        row = row + jnp.where((lane & step) == 0, up, down)
        step *= 2
    return row


def frame_stats(part_refs, f, entries, group_size):
    total = part_refs[0][f]
    for ref in part_refs[1:]:
        total = total + ref[f]
    return group_total(total, group_size) / entries


def mean_and_inv(part_refs, f, entries, group_size):
    both = frame_stats(part_refs, f, entries, group_size)
    mean = both[0:1]
    inv = lax.rsqrt(both[1:2] - mean * mean + NORM_EPS)
    return mean, inv


def column_sums(first, second):
    return jnp.concatenate(
        [jnp.sum(first, axis=0, keepdims=True), jnp.sum(second, axis=0, keepdims=True)], axis=0
    )


def put_windows(above, mid, below, lhs_ref, at, order):
    width, (pixels, channels) = above.shape[0], mid.shape
    first, mid_at, last = (slice(k * channels, (k + 1) * channels) for k in order)
    lhs_ref[at : at + width, first] = above
    lhs_ref[at + width : at + pixels, first] = mid[: pixels - width]
    lhs_ref[at : at + pixels, mid_at] = mid
    lhs_ref[at : at + pixels - width, last] = mid[width:]
    lhs_ref[at + pixels - width : at + pixels, last] = below


def from_left(y, width):
    col = lax.broadcasted_iota(jnp.int32, y.shape, 0) & (width - 1)
    return jnp.where(col == 0, 0.0, pltpu.roll(y, 1, axis=0))


def from_right(y, width):
    col = lax.broadcasted_iota(jnp.int32, y.shape, 0) & (width - 1)
    return jnp.where(col == width - 1, 0.0, pltpu.roll(y, y.shape[0] - 1, axis=0))


def slot_sources(clip_ref, dil_ref, local, frames):
    slot = lax.axis_index("tm") * frames + local
    start1 = clip_ref[0]
    filled = start1 + clip_ref[1]
    in_first = slot < start1
    d = jnp.where(in_first, dil_ref[0], dil_ref[1])
    low = jnp.where(in_first, 0, start1)
    high = jnp.where(in_first, start1, filled)
    used = slot < filled
    later, earlier = local + d, local - d
    later_live = used & (slot + d < high)
    earlier_live = used & (slot - d >= low)
    later_which = jnp.where(later_live, jnp.where(later < frames, 1, 2), 0)
    earlier_which = jnp.where(earlier_live, jnp.where(earlier >= 0, 1, 2), 0)
    return (later, later_which), (earlier, earlier_which), used


def gather_taps(clip_ref, dil_ref, local, own, nxt, prv, corner, cat_ref, at, up_slot):
    frames, pixels, channels = own.shape
    later, earlier, used = slot_sources(clip_ref, dil_ref, local, frames)
    me, half = lax.axis_index("tm"), frames // 2

    def put(slot, ref, index):
        cat_ref[pl.ds(at, pixels), slot * channels : (slot + 1) * channels] = ref[index]

    def clear(slot):
        cat_ref[pl.ds(at, pixels), slot * channels : (slot + 1) * channels] = jnp.zeros((pixels, channels), BF16)

    for slot, (index, which), other, shift, turn in (
        (up_slot, later, nxt, -frames, 3),
        (2 - up_slot, earlier, prv, frames, 4),
    ):
        beyond = which == 2
        there = jnp.clip(index + shift, 0, frames - 1)
        pl.when(which == 0)(functools.partial(clear, slot))
        pl.when(which == 1)(functools.partial(put, slot, own, jnp.clip(index, 0, frames - 1)))
        if corner:
            by_corner = beyond & (me == turn)
            low, high = by_corner & (there < half), by_corner & (there >= half)
            pl.when(low)(functools.partial(put, slot, corner[0], jnp.minimum(there, half - 1)))
            pl.when(high)(functools.partial(put, slot, corner[1], jnp.maximum(there - half, 0)))
            beyond = beyond & (me != turn)
        pl.when(beyond)(functools.partial(put, slot, other, there))
    pl.when(used)(functools.partial(put, 1, own, local))
    pl.when(jnp.logical_not(used))(functools.partial(clear, 1))


def loop(count, body):
    def step(k, carry):
        body(k)
        return carry

    lax.fori_loop(0, count, step, 0)


def conv_kernel(x_ref, above_ref, below_ref, w_ref, out_ref, sums_ref, lhs_ref):
    frames, rows, width, channels = x_ref.shape
    pixels = rows * width

    def body(pair):
        for b in range(2):
            f = 2 * pair + b
            mid = x_ref[f].reshape(pixels, channels)
            put_windows(above_ref[f, 0], mid, below_ref[f, 0], lhs_ref, b * pixels, (0, 1, 2))
        lhs = lhs_ref[...]
        y = [dot(lhs, w_ref[:, j].reshape(3 * channels, channels)) for j in range(3)]
        out = y[1] + from_left(y[0], width) + from_right(y[2], width)
        for b in range(2):
            one = out[b * pixels : (b + 1) * pixels]
            out_ref[2 * pair + b] = one
            sums_ref[2 * pair + b] = column_sums(one, one * one)

    loop(frames // 2, body)


def edge_kernel(n, entries, group_size, *refs):
    parts, (conv_ref, first_ref, last_ref) = refs[:n], refs[n:]
    frames, pixels, _ = conv_ref.shape
    width = first_ref.shape[1]

    def body(f):
        mean, inv = mean_and_inv(parts, f, entries, group_size)
        first_ref[f] = ((conv_ref[f, :width] - mean) * inv).astype(BF16)
        last_ref[f] = ((conv_ref[f, pixels - width :] - mean) * inv).astype(BF16)

    loop(frames, body)


def silu_parts(normed, half_gain, half_shift):
    h = normed * half_gain + half_shift
    t = jnp.tanh(h)
    rise = 1.0 + t
    return h, rise, rise * (1.0 + h * (1.0 - t)) * half_gain


def act_kernel(n, entries, group_size, clip_ref, *refs):
    parts, refs = refs[:n], refs[n:]
    conv_ref, gain_ref, shift_ref, act_ref, normed_ref, slope_ref = refs
    frames = conv_ref.shape[0]
    first = lax.axis_index("tm") * frames
    filled = clip_ref[0] + clip_ref[1]
    half_gain, half_shift = 0.5 * gain_ref[...], 0.5 * shift_ref[...]

    def body(f):
        mean, inv = mean_and_inv(parts, f, entries, group_size)
        normed = (conv_ref[f] - mean) * inv
        h, rise, slope = silu_parts(normed, half_gain, half_shift)
        act_ref[f] = jnp.where(first + f < filled, h * rise, 0.0).astype(BF16)
        normed_ref[f] = normed.astype(BF16)
        slope_ref[f] = slope.astype(BF16)

    loop(frames, body)


def turn_kernel(x_ref, above_ref, below_ref, xt_ref, lhs_ref):
    frames, rows, width, channels = x_ref.shape
    pixels = rows * width

    def body(f):
        mid = x_ref[f].reshape(pixels, channels)
        put_windows(above_ref[f, 0], mid, below_ref[f, 0], lhs_ref, 0, (0, 1, 2))
        lanes = pl.ds(pl.multiple_of(f * pixels, pixels), pixels)
        for i in range(3):
            block = slice(i * channels, (i + 1) * channels)
            xt_ref[block, lanes] = lhs_ref[:, block].T

    loop(frames, body)


def turn_weights_kernel(spatial_ref, temporal_ref, back_ref, out_ref):
    channels = spatial_ref.shape[-1]
    for i in range(3):
        rows = slice(i * channels, (i + 1) * channels)
        out_ref[rows] = temporal_ref[i].T
        for j in range(3):
            back_ref[j, rows] = spatial_ref[i, j].T


def grad_act_kernel(corners, clip_ref, dil_ref, own, nxt, prv, *refs):
    corner, refs = refs[:corners], refs[corners:]
    tw_ref, normed_ref, slope_ref, ga_ref, first_ref, last_ref, cat_ref, sums_ref = refs
    frames, pixels, _ = own.shape
    width = first_ref.shape[1]

    def body(pair):
        rows = pl.ds(pl.multiple_of(2 * pair * pixels, 2 * pixels), 2 * pixels)
        for b in range(2):
            at = pl.multiple_of((2 * pair + b) * pixels, pixels)
            gather_taps(clip_ref, dil_ref, 2 * pair + b, own, nxt, prv, corner, cat_ref, at, 0)
        grad_act = dot(cat_ref[rows], tw_ref[...]).astype(BF16)
        for b in range(2):
            f = 2 * pair + b
            one = grad_act[b * pixels : (b + 1) * pixels]
            ga_ref[f] = one
            first_ref[f] = one[:width]
            last_ref[f] = one[pixels - width :]
            gn = one.astype(F32) * slope_ref[f].astype(F32)
            sums_ref[f] = column_sums(gn, gn * normed_ref[f].astype(F32))

    loop(frames // 2, body)


def temporal_grad_kernel(act_ref, cat_ref, out_ref):
    frames, pixels, channels = act_ref.shape
    out_ref[...] = dot_rows(act_ref[...].reshape(frames * pixels, channels), cat_ref[...])


def norm_back(inv, means, normed, slope, grad_act):
    gn = grad_act.astype(F32) * slope.astype(F32)
    return inv * (gn - means[0:1] - normed.astype(F32) * means[1:2])


def norm_back_kernel(width, n, m, entries, group_size, normed_ref, slope_ref, ga_ref, *refs):
    parts, grad_parts = refs[:n], refs[n : n + m]
    g_ref, moved_ref = refs[n + m :]
    _, pixels, channels = normed_ref.shape

    def body(f):
        _, inv = mean_and_inv(parts, f, entries, group_size)
        means = frame_stats(grad_parts, f, entries, group_size)
        wide = norm_back(inv, means, normed_ref[f], slope_ref[f], ga_ref[f])
        grad = wide.astype(BF16)
        g_ref[f] = grad
        here = pl.ds(pl.multiple_of(f * pixels, pixels), pixels)
        moved_ref[here, :channels] = from_right(wide, width).astype(BF16)
        moved_ref[here, channels : 2 * channels] = grad
        moved_ref[here, 2 * channels :] = from_left(wide, width).astype(BF16)

    loop(normed_ref.shape[0], body)


def weight_part_kernel(xt_ref, moved_ref, out_ref):
    out_ref[...] = dot(xt_ref[...], moved_ref[:, : out_ref.shape[1]])


def weight_grad_kernel(xt_ref, moved_ref, part_ref, temporal_ref, send_ref, keep_ref, acc_ref):
    channels = temporal_ref.shape[0]
    done = part_ref.shape[1]
    acc_ref[: 3 * channels, done:] = dot(xt_ref[...], moved_ref[:, done:])
    acc_ref[: 3 * channels, :done] = part_ref[...]
    acc_ref[3 * channels :, :] = temporal_ref[...]

    chips, depth, block, _ = keep_ref.shape
    half = chips * depth * block
    core = lax.axis_index("tm") & 1

    def hand_out(kept, sent):
        for p in range(chips):
            for z in range(depth):
                at = (p * depth + z) * block
                keep_ref[p, z] = acc_ref[kept + at : kept + at + block]
                send_ref[p, z] = acc_ref[sent + at : sent + at + block].astype(BF16)

    pl.when(core == 0)(functools.partial(hand_out, 0, half))
    pl.when(core == 1)(functools.partial(hand_out, half, 0))


def conv_back_kernel(
    n, m, entries, group_size, g_ref, near_above, near_below, ga_above, ga_below, gain_ref, shift_ref, cot_ref, w_ref, *refs
):
    parts, grad_parts = refs[:n], refs[n : n + m]
    out_ref, lhs_ref = refs[n + m :]
    frames, rows, width, channels = cot_ref.shape
    pixels = rows * width
    place, size = lax.axis_index("space"), lax.axis_size("space")
    half_gain, half_shift = 0.5 * gain_ref[...], 0.5 * shift_ref[...]

    def edge(inv, means, normed, grad_act, there):
        _, _, slope = silu_parts(normed.astype(F32), half_gain, half_shift)
        return jnp.where(there, norm_back(inv, means, normed, slope, grad_act), 0.0).astype(BF16)

    def body(pair):
        for b in range(2):
            f = 2 * pair + b
            _, inv = mean_and_inv(parts, f, entries, group_size)
            means = frame_stats(grad_parts, f, entries, group_size)
            above = edge(inv, means, near_above[f], ga_above[f], place > 0)
            below = edge(inv, means, near_below[f], ga_below[f], place < size - 1)
            put_windows(above, g_ref[f], below, lhs_ref, b * pixels, (2, 1, 0))
        lhs = lhs_ref[...]
        z = [dot(lhs, w_ref[j]) for j in range(3)]
        out = z[1] + from_right(z[0], width) + from_left(z[2], width)
        for b in range(2):
            one = out[b * pixels : (b + 1) * pixels].reshape(rows, width, channels)
            out_ref[2 * pair + b] = (one + cot_ref[2 * pair + b].astype(F32)).astype(BF16)

    loop(frames // 2, body)


def out_kernel(corners, clip_ref, dil_ref, own, nxt, prv, *refs):
    corner, (tw_ref, x_ref, out_ref, cat_ref) = refs[:corners], refs[corners:]
    frames, rows, width, channels = x_ref.shape
    pixels = rows * width

    def body(pair):
        for b in range(2):
            gather_taps(clip_ref, dil_ref, 2 * pair + b, own, nxt, prv, corner, cat_ref, b * pixels, 2)
        temporal_out = dot(cat_ref[...], tw_ref[...]).astype(BF16).astype(F32)
        for b in range(2):
            one = temporal_out[b * pixels : (b + 1) * pixels].reshape(rows, width, channels)
            out_ref[2 * pair + b] = (x_ref[2 * pair + b].astype(F32) + one).astype(BF16)

    loop(frames // 2, body)


def core_sum_kernel(keep_ref, got_ref, own_ref, *send_refs):
    chip = lax.axis_index("tm") >> 1
    own_ref[...] = keep_ref[chip] + got_ref[chip].astype(F32)
    for s, ref in enumerate(send_refs, 1):
        ref[...] = (keep_ref[chip ^ s] + got_ref[chip ^ s].astype(F32)).astype(BF16)


def sum_split_kernel(count, bit, own_ref, *refs):
    got, (keep_ref, send_ref) = refs[:count], refs[count:]
    mine = (lax.axis_index("space") >> bit) & 1

    def block(k):
        total = own_ref[k]
        for ref in got:
            total = total + ref[k].astype(F32)
        return total

    for k in range(keep_ref.shape[0]):
        keep_ref[k] = block(2 * k + mine)
        send_ref[k] = block(2 * k + 1 - mine).astype(BF16)


def sum_kernel(own_ref, got_ref, out_ref):
    out_ref[...] = (own_ref[...] + got_ref[...].astype(F32)).astype(BF16)


def weave_kernel(bit, mine_ref, got_ref, out_ref):
    mine = (lax.axis_index("space") >> bit) & 1
    for k in range(mine_ref.shape[0]):
        out_ref[2 * k + mine] = mine_ref[k]
        out_ref[2 * k + 1 - mine] = got_ref[k]


def place_kernel(axis, shift, *refs):
    me = lax.axis_index(axis) >> shift
    for s, ref in enumerate(refs[:-1]):
        refs[-1][me ^ s] = ref[...]


def finish_kernel(mine_ref, got_ref, spatial_ref, temporal_ref):
    chips, depth, block, _ = mine_ref.shape
    channels = spatial_ref.shape[-1]

    def write(pair):
        for c in range(2):
            for p in range(chips):
                for z in range(depth):
                    row = ((c * chips + p) * depth + z) * block
                    values = pair[c][p, z].astype(F32)
                    i, at = row // channels, row % channels
                    for k in range(3):
                        lanes = values[:, k * channels : (k + 1) * channels]
                        if i < 3:
                            spatial_ref[i, k, at : at + block] = lanes
                        else:
                            temporal_ref[k, at : at + block] = lanes

    core = lax.axis_index("tm") & 1
    pl.when(core == 0)(functools.partial(write, (mine_ref, got_ref)))
    pl.when(core == 1)(functools.partial(write, (got_ref, mine_ref)))


def neighbours(axis, low, high, but=None):
    size = lax.axis_size(axis)
    up = [(i, i + 1) for i in range(size - 1) if i != but]
    down = [(j, i) for i, j in up]
    return lax.ppermute(high, axis, up), lax.ppermute(low, axis, down)


def spread_sums(part, axis):
    size = lax.axis_size(axis)
    step, got = 1, None
    while step < size:
        if got is not None:
            part = part + got
        got = lax.ppermute(part, axis, [(i, i ^ step) for i in range(size)])
        step *= 2
    return [part, got]


def per_device(frames_in, cotangent, spatial, temporal, norm_gain, norm_shift, clip_frames, dilation):
    frames, rows, width, channels = frames_in.shape
    pixels = rows * width
    n, tm = lax.axis_size("space"), lax.axis_size("tm")
    chips = tm // 2
    group_size = channels // GROUPS
    entries = float(rows * n * width * group_size)
    gain, shift = norm_gain[None], norm_shift[None]
    big = frames * pixels * channels
    shape = jax.ShapeDtypeStruct
    per_px = (frames, pixels, channels)
    windows = pltpu.VMEM((2 * pixels, 3 * channels), BF16)

    cot = cotangent.reshape(per_px)
    by_corner = tm == 8
    but = 3 if by_corner else None
    cot_prev, cot_next = neighbours("tm", cot, cot, but)
    above, below = neighbours("space", frames_in[:, :1], frames_in[:, rows - 1 :])
    back_weights, back_taps = call(
        turn_weights_kernel, "turn_weights", [spatial, temporal],
        [shape((3, 3 * channels, channels), BF16), shape((3 * channels, channels), BF16)], 0, big,
    )
    if by_corner:
        above, below, cot_late = lax.optimization_barrier((above, below, cot))
        cot_low, cot_high = cot_late[: frames // 2], cot_late[frames // 2 :]
        cot_relayed = lax.ppermute(cot_high, "tm", [(3, 7), (4, 0)])
    conv_out, sums = call(
        conv_kernel, "conv_forward", [frames_in, above, below, spatial],
        [shape(per_px, F32), shape((frames, 2, channels), F32)],
        18 * big * channels, 8 * big, [windows], 18,
    )
    cot_corner = []
    if by_corner:
        sums, cot_low = lax.optimization_barrier((sums, cot_low))
        cot_corner.append(lax.ppermute(cot_low, "tm", [(3, 4), (4, 3)]))
    parts = spread_sums(sums, "space")
    if by_corner:
        parts[0], cot_relayed = lax.optimization_barrier((parts[0], cot_relayed))
        cot_corner.append(lax.ppermute(cot_relayed, "tm", [(7, 4), (0, 3)]))
    x_turned = call(
        turn_kernel, "turned", [frames_in, above, below], shape((3 * channels, frames * pixels), BF16),
        0, 8 * big, [pltpu.VMEM((pixels, 3 * channels), BF16)],
    )
    x_turned, *parts = lax.optimization_barrier((x_turned, *parts))
    edge = shape((frames, width, channels), BF16)
    near_first, near_last = call(
        functools.partial(edge_kernel, len(parts), entries, group_size), "edges", [*parts, conv_out], [edge] * 2, 0, big,
    )
    near_first, near_last, cot_prev, cot_next = lax.optimization_barrier((near_first, near_last, cot_prev, cot_next))
    near_above, near_below = neighbours("space", near_first, near_last)
    act, normed, slope = call(
        functools.partial(act_kernel, len(parts), entries, group_size), "activation",
        [clip_frames, *parts, conv_out, gain, shift], [shape(per_px, BF16)] * 3, 0, big,
    )
    normed, near_above, near_below = lax.optimization_barrier((normed, near_above, near_below))

    grad_act, ga_first, ga_last, cot_cat, grad_sums = call(
        functools.partial(grad_act_kernel, len(cot_corner)), "grad_activation",
        [clip_frames, dilation, cot, cot_next, cot_prev, *cot_corner, back_taps, normed, slope],
        [
            shape(per_px, BF16), edge, edge, shape((frames * pixels, 3 * channels), BF16),
            shape((frames, 2, channels), F32),
        ],
        6 * big * channels, 16 * big,
    )
    ga_above, ga_below = neighbours("space", ga_first, ga_last)
    grad_sums, act_sent = lax.optimization_barrier((grad_sums, act))
    act_prev, act_next = neighbours("tm", act_sent, act_sent, but)
    grad_parts = spread_sums(grad_sums, "space")
    if by_corner:
        grad_parts[0], act_late = lax.optimization_barrier((grad_parts[0], act))
        act_relayed = lax.ppermute(act_late[frames // 2 :], "tm", [(3, 7), (4, 0)])
    temporal_part = call(
        temporal_grad_kernel, "temporal_grad", [act, cot_cat],
        shape((channels, 3 * channels), F32), 6 * big * channels, 8 * big,
    )
    lanes = 3 * channels
    grad_conv, moved = call(
        functools.partial(norm_back_kernel, width, len(parts), len(grad_parts), entries, group_size), "norm_backward",
        [normed, slope, grad_act, *parts, *grad_parts],
        [shape(per_px, BF16), shape((frames * pixels, lanes), BF16)],
        0, 12 * big,
    )
    part = call(
        weight_part_kernel, "weight_part", [x_turned, moved], shape((lanes, 2 * channels), F32),
        12 * big * channels, 8 * big,
    )
    moved, ga_above, ga_below = lax.optimization_barrier((moved, ga_above, ga_below))
    block = 2 * channels // (chips * n)
    send, keep = call(
        weight_grad_kernel, "weight_grad", [x_turned, moved, part, temporal_part],
        [shape((chips, n, block, lanes), BF16), shape((chips, n, block, lanes), F32)],
        6 * big * channels, 8 * big, [pltpu.VMEM((4 * channels, lanes), F32)], 20,
    )

    def other_chip(s):
        return [(i, i ^ (2 * s)) for i in range(tm)]

    def other_plane(s):
        return [(i, i ^ s) for i in range(n)]

    other_core = [(i, i ^ 1) for i in range(tm)]
    got = lax.ppermute(send, "tm", other_core)
    own, *sends = call(
        core_sum_kernel, "core_sum", [keep, got],
        [shape((n, block, lanes), F32)] + [shape((n, block, lanes), BF16)] * (chips - 1), 0, 4 * big,
    )
    gots = [lax.ppermute(x, "tm", other_chip(s)) for s, x in enumerate(sends, 1)]

    in_grad = call(
        functools.partial(conv_back_kernel, len(parts), len(grad_parts), entries, group_size), "conv_backward",
        [grad_conv, near_above, near_below, ga_above, ga_below, gain, shift, cotangent, back_weights, *parts, *grad_parts],
        shape(frames_in.shape, BF16), 18 * big * channels, 8 * big, [windows], 20,
    )
    own, in_grad, act_prev, act_next = lax.optimization_barrier((own, in_grad, act_prev, act_next))
    if by_corner:
        own, act_relayed = lax.optimization_barrier((own, act_relayed))

    act_corner = []
    bits = range(n.bit_length() - 1)
    for bit in bits:
        m = n >> bit
        own, send = call(
            functools.partial(sum_split_kernel, len(gots), bit), "plane_sum" if bit == 0 else "line_sum", [own, *gots],
            [shape((m // 2, block, lanes), F32), shape((m // 2, block, lanes), BF16)], 0, big,
        )
        if by_corner and bit == 0:
            own, low, high = lax.optimization_barrier((own, act_sent, act_relayed))
            act_corner = [
                lax.ppermute(low[: frames // 2], "tm", [(3, 4), (4, 3)]),
                lax.ppermute(high, "tm", [(7, 4), (0, 3)]),
            ]
        gots = [lax.ppermute(send, "space", other_plane(1 << bit))]
    own = call(sum_kernel, "line_total", [own, *gots], shape((1, block, lanes), BF16), 0, big)
    for bit in reversed(bits):
        got = lax.ppermute(own, "space", other_plane(1 << bit))
        own = call(
            functools.partial(weave_kernel, bit), "line_weave", [own, got],
            shape((n >> bit, block, lanes), BF16), 0, big,
        )
    gots = [lax.ppermute(own, "tm", other_chip(s)) for s in range(1, chips)]

    out_frames = call(
        functools.partial(out_kernel, len(act_corner)), "temporal_forward",
        [clip_frames, dilation, act, act_next, act_prev, *act_corner, temporal.reshape(3 * channels, channels), frames_in],
        shape(frames_in.shape, BF16), 6 * big * channels, 10 * big, [windows],
    )
    own, out_frames = lax.optimization_barrier((own, out_frames))

    own = call(
        functools.partial(place_kernel, "tm", 1), "plane_place", [own, *gots], shape((chips, n, block, lanes), BF16), 0, big
    )
    got = lax.ppermute(own, "tm", other_core)
    spatial_grad, temporal_grad = call(
        finish_kernel, "finish", [own, got], [shape(spatial.shape, F32), shape(temporal.shape, F32)], 0, 4 * big
    )
    return (out_frames, in_grad, spatial_grad, temporal_grad)


def solution(mesh):
    tiles = P("tm", "space", None, None)
    return jax.shard_map(
        per_device,
        mesh=mesh,
        in_specs=(tiles, tiles, P(), P(), P(), P(), P(), P()),
        out_specs=(tiles, tiles, P(), P()),
        check_vma=False,
    )
```

```python
import functools

import jax
import jax.numpy as jnp
from jax import lax
from jax.experimental import pallas as pl
from jax.experimental.pallas import tpu as pltpu
from jax.sharding import PartitionSpec as P

GROUPS = 32
NORM_EPS = 1e-05
BF16 = jnp.bfloat16
F32 = jnp.float32
MIB = 2**20


def call(kernel, name, operands, out_shape, flops=0, moved=0, scratch=(), grant=14):
    vmem = pl.BlockSpec(memory_space=pltpu.VMEM)
    smem = pl.BlockSpec(memory_space=pltpu.SMEM)
    return pl.pallas_call(
        kernel,
        in_specs=[smem if x.dtype == jnp.int32 else vmem for x in operands],
        out_specs=jax.tree.map(lambda _: vmem, out_shape),
        out_shape=out_shape,
        scratch_shapes=list(scratch),
        compiler_params=pltpu.CompilerParams(vmem_limit_bytes=grant * MIB),
        cost_estimate=pl.CostEstimate(flops=int(flops), bytes_accessed=int(moved), transcendentals=0),
        name=name,
    )(*operands)


def dot(a, b):
    return jnp.dot(a, b, preferred_element_type=F32)


def dot_rows(a, b):
    return lax.dot_general(a, b, (((0,), (0,)), ((), ())), preferred_element_type=F32)


def group_total(row, group_size):
    channels = row.shape[-1]
    lane = lax.broadcasted_iota(jnp.int32, row.shape, 1)
    step = 1
    while step < group_size:
        up = pltpu.roll(row, channels - step, axis=1)
        down = pltpu.roll(row, step, axis=1)
        row = row + jnp.where((lane & step) == 0, up, down)
        step *= 2
    return row


def frame_stats(part_refs, f, entries, group_size):
    total = part_refs[0][f]
    for ref in part_refs[1:]:
        total = total + ref[f]
    return group_total(total, group_size) / entries


def mean_and_inv(part_refs, f, entries, group_size):
    both = frame_stats(part_refs, f, entries, group_size)
    mean = both[0:1]
    inv = lax.rsqrt(both[1:2] - mean * mean + NORM_EPS)
    return mean, inv


def column_sums(first, second):
    return jnp.concatenate(
        [jnp.sum(first, axis=0, keepdims=True), jnp.sum(second, axis=0, keepdims=True)], axis=0
    )


def put_windows(above, mid, below, lhs_ref, at, order):
    width, (pixels, channels) = above.shape[0], mid.shape
    first, mid_at, last = (slice(k * channels, (k + 1) * channels) for k in order)
    lhs_ref[at : at + width, first] = above
    lhs_ref[at + width : at + pixels, first] = mid[: pixels - width]
    lhs_ref[at : at + pixels, mid_at] = mid
    lhs_ref[at : at + pixels - width, last] = mid[width:]
    lhs_ref[at + pixels - width : at + pixels, last] = below


def from_left(y, width):
    col = lax.broadcasted_iota(jnp.int32, y.shape, 0) & (width - 1)
    return jnp.where(col == 0, 0.0, pltpu.roll(y, 1, axis=0))


def from_right(y, width):
    col = lax.broadcasted_iota(jnp.int32, y.shape, 0) & (width - 1)
    return jnp.where(col == width - 1, 0.0, pltpu.roll(y, y.shape[0] - 1, axis=0))


def slot_sources(clip_ref, dil_ref, local, frames):
    slot = lax.axis_index("tm") * frames + local
    start1 = clip_ref[0]
    filled = start1 + clip_ref[1]
    in_first = slot < start1
    d = jnp.where(in_first, dil_ref[0], dil_ref[1])
    low = jnp.where(in_first, 0, start1)
    high = jnp.where(in_first, start1, filled)
    used = slot < filled
    later, earlier = local + d, local - d
    later_live = used & (slot + d < high)
    earlier_live = used & (slot - d >= low)
    later_which = jnp.where(later_live, jnp.where(later < frames, 1, 2), 0)
    earlier_which = jnp.where(earlier_live, jnp.where(earlier >= 0, 1, 2), 0)
    return (later, later_which), (earlier, earlier_which), used


def gather_taps(clip_ref, dil_ref, local, own, nxt, prv, corner, cat_ref, at, up_slot):
    frames, pixels, channels = own.shape
    later, earlier, used = slot_sources(clip_ref, dil_ref, local, frames)
    me, half = lax.axis_index("tm"), frames // 2

    def put(slot, ref, index):
        cat_ref[pl.ds(at, pixels), slot * channels : (slot + 1) * channels] = ref[index]

    def clear(slot):
        cat_ref[pl.ds(at, pixels), slot * channels : (slot + 1) * channels] = jnp.zeros((pixels, channels), BF16)

    for slot, (index, which), other, shift, turn in (
        (up_slot, later, nxt, -frames, 3),
        (2 - up_slot, earlier, prv, frames, 4),
    ):
        beyond = which == 2
        there = jnp.clip(index + shift, 0, frames - 1)
        pl.when(which == 0)(functools.partial(clear, slot))
        pl.when(which == 1)(functools.partial(put, slot, own, jnp.clip(index, 0, frames - 1)))
        if corner:
            by_corner = beyond & (me == turn)
            low, high = by_corner & (there < half), by_corner & (there >= half)
            pl.when(low)(functools.partial(put, slot, corner[0], jnp.minimum(there, half - 1)))
            pl.when(high)(functools.partial(put, slot, corner[1], jnp.maximum(there - half, 0)))
            beyond = beyond & (me != turn)
        pl.when(beyond)(functools.partial(put, slot, other, there))
    pl.when(used)(functools.partial(put, 1, own, local))
    pl.when(jnp.logical_not(used))(functools.partial(clear, 1))


def loop(count, body):
    def step(k, carry):
        body(k)
        return carry

    lax.fori_loop(0, count, step, 0)


def conv_kernel(x_ref, above_ref, below_ref, w_ref, out_ref, sums_ref, lhs_ref):
    frames, rows, width, channels = x_ref.shape
    pixels = rows * width

    def body(pair):
        for b in range(2):
            f = 2 * pair + b
            mid = x_ref[f].reshape(pixels, channels)
            put_windows(above_ref[f, 0], mid, below_ref[f, 0], lhs_ref, b * pixels, (0, 1, 2))
        lhs = lhs_ref[...]
        y = [dot(lhs, w_ref[:, j].reshape(3 * channels, channels)) for j in range(3)]
        out = y[1] + from_left(y[0], width) + from_right(y[2], width)
        for b in range(2):
            one = out[b * pixels : (b + 1) * pixels]
            out_ref[2 * pair + b] = one
            sums_ref[2 * pair + b] = column_sums(one, one * one)

    loop(frames // 2, body)


def silu_parts(normed, half_gain, half_shift):
    h = normed * half_gain + half_shift
    t = jnp.tanh(h)
    rise = 1.0 + t
    return h, rise, rise * (1.0 + h * (1.0 - t)) * half_gain


def act_kernel(n, entries, group_size, clip_ref, *refs):
    parts, refs = refs[:n], refs[n:]
    conv_ref, gain_ref, shift_ref, act_ref, normed_ref, slope_ref = refs
    frames = conv_ref.shape[0]
    first = lax.axis_index("tm") * frames
    filled = clip_ref[0] + clip_ref[1]
    half_gain, half_shift = 0.5 * gain_ref[...], 0.5 * shift_ref[...]

    def body(f):
        mean, inv = mean_and_inv(parts, f, entries, group_size)
        normed = (conv_ref[f] - mean) * inv
        h, rise, slope = silu_parts(normed, half_gain, half_shift)
        act_ref[f] = jnp.where(first + f < filled, h * rise, 0.0).astype(BF16)
        normed_ref[f] = normed.astype(BF16)
        slope_ref[f] = slope.astype(BF16)

    loop(frames, body)


def turn_kernel(x_ref, above_ref, below_ref, xt_ref, lhs_ref):
    frames, rows, width, channels = x_ref.shape
    pixels = rows * width

    def body(f):
        mid = x_ref[f].reshape(pixels, channels)
        put_windows(above_ref[f, 0], mid, below_ref[f, 0], lhs_ref, 0, (0, 1, 2))
        lanes = pl.ds(pl.multiple_of(f * pixels, pixels), pixels)
        for i in range(3):
            block = slice(i * channels, (i + 1) * channels)
            xt_ref[block, lanes] = lhs_ref[:, block].T

    loop(frames, body)


def turn_weights_kernel(spatial_ref, temporal_ref, back_ref, out_ref):
    channels = spatial_ref.shape[-1]
    for i in range(3):
        rows = slice(i * channels, (i + 1) * channels)
        out_ref[rows] = temporal_ref[i].T
        for j in range(3):
            back_ref[j, rows] = spatial_ref[i, j].T


def grad_act_kernel(clip_ref, dil_ref, own, nxt, prv, tw_ref, normed_ref, slope_ref, ga_ref, cat_ref, sums_ref):
    frames, pixels, _ = own.shape

    def body(pair):
        rows = pl.ds(pl.multiple_of(2 * pair * pixels, 2 * pixels), 2 * pixels)
        for b in range(2):
            at = pl.multiple_of((2 * pair + b) * pixels, pixels)
            gather_taps(clip_ref, dil_ref, 2 * pair + b, own, nxt, prv, (), cat_ref, at, 0)
        grad_act = dot(cat_ref[rows], tw_ref[...]).astype(BF16)
        for b in range(2):
            f = 2 * pair + b
            one = grad_act[b * pixels : (b + 1) * pixels]
            ga_ref[f] = one
            gn = one.astype(F32) * slope_ref[f].astype(F32)
            sums_ref[f] = column_sums(gn, gn * normed_ref[f].astype(F32))

    loop(frames // 2, body)


def temporal_grad_kernel(act_ref, cat_ref, out_ref):
    frames, pixels, channels = act_ref.shape
    out_ref[...] = dot_rows(act_ref[...].reshape(frames * pixels, channels), cat_ref[...])


def norm_back_kernel(n, m, entries, group_size, normed_ref, slope_ref, ga_ref, *refs):
    parts, grad_parts = refs[:n], refs[n : n + m]
    g_ref, first_ref, last_ref, moved_ref = refs[n + m :]
    _, pixels, channels = normed_ref.shape
    width = first_ref.shape[2]

    def body(f):
        _, inv = mean_and_inv(parts, f, entries, group_size)
        means = frame_stats(grad_parts, f, entries, group_size)
        gn = ga_ref[f].astype(F32) * slope_ref[f].astype(F32)
        wide = inv * (gn - means[0:1] - normed_ref[f].astype(F32) * means[1:2])
        grad = wide.astype(BF16)
        g_ref[f] = grad
        first_ref[f, 0] = grad[:width]
        last_ref[f, 0] = grad[pixels - width :]
        here = pl.ds(pl.multiple_of(f * pixels, pixels), pixels)
        moved_ref[here, :channels] = from_right(wide, width).astype(BF16)
        moved_ref[here, channels : 2 * channels] = grad
        moved_ref[here, 2 * channels :] = from_left(wide, width).astype(BF16)

    loop(normed_ref.shape[0], body)


def weight_grad_kernel(xt_ref, moved_ref, temporal_ref, out_ref):
    channels = temporal_ref.shape[0]
    for j in range(3):
        lanes = slice(j * channels, (j + 1) * channels)
        out_ref[: 3 * channels, lanes] = dot(xt_ref[...], moved_ref[:, lanes])
    out_ref[3 * channels :, :] = temporal_ref[...]


def hand_out_kernel(acc_ref, send_ref, keep_ref):
    chips, depth, block, _ = keep_ref.shape
    half = chips * depth * block
    core = lax.axis_index("tm") & 1

    def hand_out(kept, sent):
        for p in range(chips):
            for z in range(depth):
                at = (p * depth + z) * block
                keep_ref[p, z] = acc_ref[kept + at : kept + at + block]
                send_ref[p, z] = acc_ref[sent + at : sent + at + block].astype(BF16)

    pl.when(core == 0)(functools.partial(hand_out, 0, half))
    pl.when(core == 1)(functools.partial(hand_out, half, 0))


def conv_back_kernel(g_ref, above_ref, below_ref, cot_ref, w_ref, out_ref, lhs_ref):
    frames, rows, width, channels = cot_ref.shape
    pixels = rows * width

    def body(pair):
        for b in range(2):
            f = 2 * pair + b
            put_windows(above_ref[f, 0], g_ref[f], below_ref[f, 0], lhs_ref, b * pixels, (2, 1, 0))
        lhs = lhs_ref[...]
        z = [dot(lhs, w_ref[j]) for j in range(3)]
        out = z[1] + from_right(z[0], width) + from_left(z[2], width)
        for b in range(2):
            one = out[b * pixels : (b + 1) * pixels].reshape(rows, width, channels)
            out_ref[2 * pair + b] = (one + cot_ref[2 * pair + b].astype(F32)).astype(BF16)

    loop(frames // 2, body)


def out_kernel(corners, clip_ref, dil_ref, own, nxt, prv, *refs):
    corner, (tw_ref, x_ref, out_ref, cat_ref) = refs[:corners], refs[corners:]
    frames, rows, width, channels = x_ref.shape
    pixels = rows * width

    def body(pair):
        for b in range(2):
            gather_taps(clip_ref, dil_ref, 2 * pair + b, own, nxt, prv, corner, cat_ref, b * pixels, 2)
        temporal_out = dot(cat_ref[...], tw_ref[...]).astype(BF16).astype(F32)
        for b in range(2):
            one = temporal_out[b * pixels : (b + 1) * pixels].reshape(rows, width, channels)
            out_ref[2 * pair + b] = (x_ref[2 * pair + b].astype(F32) + one).astype(BF16)

    loop(frames // 2, body)


def core_sum_kernel(keep_ref, got_ref, own_ref, *send_refs):
    chip = lax.axis_index("tm") >> 1
    own_ref[...] = keep_ref[chip] + got_ref[chip].astype(F32)
    for s, ref in enumerate(send_refs, 1):
        ref[...] = (keep_ref[chip ^ s] + got_ref[chip ^ s].astype(F32)).astype(BF16)


def sum_kernel(count, own_ref, *refs):
    total = own_ref[...]
    for ref in refs[:count]:
        total = total + ref[...].astype(F32)
    refs[count][...] = total.astype(BF16)


def sum_split_kernel(count, own_ref, *refs):
    got, (mine_ref, *send_refs) = refs[:count], refs[count:]
    deep = lax.axis_index("space")

    def block(k):
        total = own_ref[k]
        for ref in got:
            total = total + ref[k].astype(F32)
        return total

    mine_ref[...] = block(deep)
    for s, ref in enumerate(send_refs, 1):
        ref[...] = block(deep ^ s).astype(BF16)


def finish_kernel(chips, got_ref, spatial_ref, temporal_ref):
    devices, block, _ = got_ref.shape
    depth = devices // (2 * chips)
    channels = spatial_ref.shape[-1]
    for d in range(devices):
        member, z = d // depth, d % depth
        row = (((member % 2) * chips + member // 2) * depth + z) * block
        values = got_ref[d].astype(F32)
        i, at = row // channels, row % channels
        for k in range(3):
            lanes = values[:, k * channels : (k + 1) * channels]
            if i < 3:
                spatial_ref[i, k, at : at + block] = lanes
            else:
                temporal_ref[k, at : at + block] = lanes


def neighbours(axis, low, high, but=None):
    size = lax.axis_size(axis)
    up = [(i, i + 1) for i in range(size - 1) if i != but]
    down = [(j, i) for i, j in up]
    return lax.ppermute(high, axis, up), lax.ppermute(low, axis, down)


def spread_sums(part, axis):
    size = lax.axis_size(axis)
    step, got = 1, None
    while step < size:
        if got is not None:
            part = part + got
        got = lax.ppermute(part, axis, [(i, i ^ step) for i in range(size)])
        step *= 2
    return [part, got]


def per_device(frames_in, cotangent, spatial, temporal, norm_gain, norm_shift, clip_frames, dilation):
    frames, rows, width, channels = frames_in.shape
    pixels = rows * width
    n, tm = lax.axis_size("space"), lax.axis_size("tm")
    chips = tm // 2
    group_size = channels // GROUPS
    entries = float(rows * n * width * group_size)
    gain, shift = norm_gain[None], norm_shift[None]
    big = frames * pixels * channels
    shape = jax.ShapeDtypeStruct
    per_px = (frames, pixels, channels)
    windows = pltpu.VMEM((2 * pixels, 3 * channels), BF16)

    cot = cotangent.reshape(per_px)
    cot_prev, cot_next = neighbours("tm", cot, cot)
    above, below = neighbours("space", frames_in[:, :1], frames_in[:, rows - 1 :])
    back_weights, back_taps = call(
        turn_weights_kernel, "turn_weights", [spatial, temporal],
        [shape((3, 3 * channels, channels), BF16), shape((3 * channels, channels), BF16)], 0, big,
    )
    conv_out, sums = call(
        conv_kernel, "conv_forward", [frames_in, above, below, spatial],
        [shape(per_px, F32), shape((frames, 2, channels), F32)],
        18 * big * channels, 8 * big, [windows], 18,
    )
    parts = spread_sums(sums, "space")
    x_turned = call(
        turn_kernel, "turned", [frames_in, above, below], shape((3 * channels, frames * pixels), BF16),
        0, 8 * big, [pltpu.VMEM((pixels, 3 * channels), BF16)],
    )
    x_turned, *parts = lax.optimization_barrier((x_turned, *parts))
    act, normed, slope = call(
        functools.partial(act_kernel, len(parts), entries, group_size), "activation",
        [clip_frames, *parts, conv_out, gain, shift], [shape(per_px, BF16)] * 3, 10 * big, 10 * big,
    )
    grad_act, cot_cat, grad_sums = call(
        grad_act_kernel, "grad_activation",
        [clip_frames, dilation, cot, cot_next, cot_prev, back_taps, normed, slope],
        [shape(per_px, BF16), shape((frames * pixels, 3 * channels), BF16), shape((frames, 2, channels), F32)],
        6 * big * channels, 16 * big,
    )
    by_corner = tm == 8
    grad_sums, act_sent = lax.optimization_barrier((grad_sums, act))
    act_prev, act_next = neighbours("tm", act_sent, act_sent, 3 if by_corner else None)
    grad_parts = spread_sums(grad_sums, "space")
    temporal_part = call(
        temporal_grad_kernel, "temporal_grad", [act, cot_cat],
        shape((channels, 3 * channels), F32), 6 * big * channels, 8 * big,
    )
    act_corner = []
    if by_corner:
        grad_parts[0], act_late = lax.optimization_barrier((grad_parts[0], act))
        act_relayed = lax.ppermute(act_late[frames // 2 :], "tm", [(3, 7), (4, 0)])
    lanes = 3 * channels
    grad_conv, first_rows, last_rows, moved = call(
        functools.partial(norm_back_kernel, len(parts), len(grad_parts), entries, group_size), "norm_backward",
        [normed, slope, grad_act, *parts, *grad_parts],
        [shape(per_px, BF16)] + [shape((frames, 1, width, channels), BF16)] * 2
        + [shape((frames * pixels, lanes), BF16)],
        0, 12 * big,
    )
    grad_above, grad_below = neighbours("space", first_rows, last_rows)
    sums = call(
        weight_grad_kernel, "weight_grad", [x_turned, moved, temporal_part], shape((4 * channels, lanes), F32),
        18 * big * channels, 12 * big,
    )
    sums, grad_above, grad_below = lax.optimization_barrier((sums, grad_above, grad_below))
    block = 2 * channels // (chips * n)
    send, keep = call(
        hand_out_kernel, "hand_out", [sums],
        [shape((chips, n, block, lanes), BF16), shape((chips, n, block, lanes), F32)], 0, big,
    )
    if by_corner:
        keep, act_late, act_relayed = lax.optimization_barrier((keep, act, act_relayed))
        act_corner.append(lax.ppermute(act_late[: frames // 2], "tm", [(3, 4), (4, 3)]))
        act_corner.append(lax.ppermute(act_relayed, "tm", [(7, 4), (0, 3)]))

    def other_chip(s):
        return [(i, i ^ (2 * s)) for i in range(tm)]

    def other_plane(s):
        return [(i, i ^ s) for i in range(n)]

    other_core = [(i, i ^ 1) for i in range(tm)]
    got = lax.ppermute(send, "tm", other_core)
    own, *sends = call(
        core_sum_kernel, "core_sum", [keep, got],
        [shape((n, block, lanes), F32)] + [shape((n, block, lanes), BF16)] * (chips - 1), 0, 4 * big,
    )
    gots = [lax.ppermute(x, "tm", other_chip(s)) for s, x in enumerate(sends, 1)]

    in_grad = call(
        conv_back_kernel, "conv_backward", [grad_conv, grad_above, grad_below, cotangent, back_weights],
        shape(frames_in.shape, BF16), 18 * big * channels, 8 * big, [windows], 20,
    )
    own, in_grad, act_prev, act_next = lax.optimization_barrier((own, in_grad, act_prev, act_next))

    own, *sends = call(
        functools.partial(sum_split_kernel, chips - 1), "plane_sum", [own, *gots],
        [shape((block, lanes), F32)] + [shape((block, lanes), BF16)] * (n - 1), 0, big,
    )
    gots = [lax.ppermute(x, "space", other_plane(s)) for s, x in enumerate(sends, 1)]
    own = call(
        functools.partial(sum_kernel, n - 1), "line_sum", [own, *gots], shape((block, lanes), BF16), 0, big
    )
    own, *act_corner = lax.optimization_barrier((own, *act_corner))
    everyone = lax.all_gather(own, ("tm", "space"))

    out_frames = call(
        functools.partial(out_kernel, len(act_corner)), "temporal_forward",
        [clip_frames, dilation, act, act_next, act_prev, *act_corner, temporal.reshape(3 * channels, channels), frames_in],
        shape(frames_in.shape, BF16), 6 * big * channels, 10 * big, [windows],
    )
    spatial_grad, temporal_grad = call(
        functools.partial(finish_kernel, chips), "finish", [everyone],
        [shape(spatial.shape, F32), shape(temporal.shape, F32)], 0, 4 * big,
    )
    return (out_frames, in_grad, spatial_grad, temporal_grad)


def solution(mesh):
    tiles = P("tm", "space", None, None)
    return jax.shard_map(
        per_device,
        mesh=mesh,
        in_specs=(tiles, tiles, P(), P(), P(), P(), P(), P()),
        out_specs=(tiles, tiles, P(), P()),
        check_vma=False,
    )
```

```python
import functools

import jax
import jax.numpy as jnp
from jax import lax
from jax.experimental import pallas as pl
from jax.experimental.pallas import tpu as pltpu
from jax.sharding import PartitionSpec as P

GROUPS = 32
NORM_EPS = 1e-05
BF16 = jnp.bfloat16
F32 = jnp.float32
MIB = 2**20


def call(kernel, name, operands, out_shape, flops=0, moved=0, scratch=(), grant=14):
    vmem = pl.BlockSpec(memory_space=pltpu.VMEM)
    smem = pl.BlockSpec(memory_space=pltpu.SMEM)
    return pl.pallas_call(
        kernel,
        in_specs=[smem if x.dtype == jnp.int32 else vmem for x in operands],
        out_specs=jax.tree.map(lambda _: vmem, out_shape),
        out_shape=out_shape,
        scratch_shapes=list(scratch),
        compiler_params=pltpu.CompilerParams(vmem_limit_bytes=grant * MIB),
        cost_estimate=pl.CostEstimate(flops=int(flops), bytes_accessed=int(moved), transcendentals=0),
        name=name,
    )(*operands)


def dot(a, b):
    return jnp.dot(a, b, preferred_element_type=F32)


def dot_rows(a, b):
    return lax.dot_general(a, b, (((0,), (0,)), ((), ())), preferred_element_type=F32)


def group_total(row, group_size):
    channels = row.shape[-1]
    lane = lax.broadcasted_iota(jnp.int32, row.shape, 1)
    step = 1
    while step < group_size:
        up = pltpu.roll(row, channels - step, axis=1)
        down = pltpu.roll(row, step, axis=1)
        row = row + jnp.where((lane & step) == 0, up, down)
        step *= 2
    return row


def frame_stats(part_refs, f, entries, group_size):
    total = part_refs[0][f]
    for ref in part_refs[1:]:
        total = total + ref[f]
    return group_total(total, group_size) / entries


def mean_and_inv(part_refs, f, entries, group_size):
    both = frame_stats(part_refs, f, entries, group_size)
    mean = both[0:1]
    inv = lax.rsqrt(both[1:2] - mean * mean + NORM_EPS)
    return mean, inv


def column_sums(first, second):
    return jnp.concatenate(
        [jnp.sum(first, axis=0, keepdims=True), jnp.sum(second, axis=0, keepdims=True)], axis=0
    )


def put_windows(above, mid, below, lhs_ref, at, order):
    width, (pixels, channels) = above.shape[0], mid.shape
    first, mid_at, last = (slice(k * channels, (k + 1) * channels) for k in order)
    lhs_ref[at : at + width, first] = above
    lhs_ref[at + width : at + pixels, first] = mid[: pixels - width]
    lhs_ref[at : at + pixels, mid_at] = mid
    lhs_ref[at : at + pixels - width, last] = mid[width:]
    lhs_ref[at + pixels - width : at + pixels, last] = below


def from_left(y, width):
    col = lax.broadcasted_iota(jnp.int32, y.shape, 0) & (width - 1)
    return jnp.where(col == 0, 0.0, pltpu.roll(y, 1, axis=0))


def from_right(y, width):
    col = lax.broadcasted_iota(jnp.int32, y.shape, 0) & (width - 1)
    return jnp.where(col == width - 1, 0.0, pltpu.roll(y, y.shape[0] - 1, axis=0))


def slot_sources(clip_ref, dil_ref, local, frames):
    slot = lax.axis_index("tm") * frames + local
    start1 = clip_ref[0]
    filled = start1 + clip_ref[1]
    in_first = slot < start1
    d = jnp.where(in_first, dil_ref[0], dil_ref[1])
    low = jnp.where(in_first, 0, start1)
    high = jnp.where(in_first, start1, filled)
    used = slot < filled
    later, earlier = local + d, local - d
    later_live = used & (slot + d < high)
    earlier_live = used & (slot - d >= low)
    later_which = jnp.where(later_live, jnp.where(later < frames, 1, 2), 0)
    earlier_which = jnp.where(earlier_live, jnp.where(earlier >= 0, 1, 2), 0)
    return (later, later_which), (earlier, earlier_which), used


def gather_taps(clip_ref, dil_ref, local, own, nxt, prv, corner, cat_ref, at, up_slot):
    frames, pixels, channels = own.shape
    later, earlier, used = slot_sources(clip_ref, dil_ref, local, frames)
    me, half = lax.axis_index("tm"), frames // 2

    def put(slot, ref, index):
        cat_ref[pl.ds(at, pixels), slot * channels : (slot + 1) * channels] = ref[index]

    def clear(slot):
        cat_ref[pl.ds(at, pixels), slot * channels : (slot + 1) * channels] = jnp.zeros((pixels, channels), BF16)

    for slot, (index, which), other, shift, turn in (
        (up_slot, later, nxt, -frames, 3),
        (2 - up_slot, earlier, prv, frames, 4),
    ):
        beyond = which == 2
        there = jnp.clip(index + shift, 0, frames - 1)
        pl.when(which == 0)(functools.partial(clear, slot))
        pl.when(which == 1)(functools.partial(put, slot, own, jnp.clip(index, 0, frames - 1)))
        if corner:
            by_corner = beyond & (me == turn)
            low, high = by_corner & (there < half), by_corner & (there >= half)
            pl.when(low)(functools.partial(put, slot, corner[0], jnp.minimum(there, half - 1)))
            pl.when(high)(functools.partial(put, slot, corner[1], jnp.maximum(there - half, 0)))
            beyond = beyond & (me != turn)
        pl.when(beyond)(functools.partial(put, slot, other, there))
    pl.when(used)(functools.partial(put, 1, own, local))
    pl.when(jnp.logical_not(used))(functools.partial(clear, 1))


def loop(count, body):
    def step(k, carry):
        body(k)
        return carry

    lax.fori_loop(0, count, step, 0)


def conv_kernel(x_ref, above_ref, below_ref, w_ref, out_ref, sums_ref, lhs_ref):
    frames, rows, width, channels = x_ref.shape
    pixels = rows * width

    def body(pair):
        for b in range(2):
            f = 2 * pair + b
            mid = x_ref[f].reshape(pixels, channels)
            put_windows(above_ref[f, 0], mid, below_ref[f, 0], lhs_ref, b * pixels, (0, 1, 2))
        lhs = lhs_ref[...]
        y = [dot(lhs, w_ref[:, j].reshape(3 * channels, channels)) for j in range(3)]
        out = y[1] + from_left(y[0], width) + from_right(y[2], width)
        for b in range(2):
            one = out[b * pixels : (b + 1) * pixels]
            out_ref[2 * pair + b] = one
            sums_ref[2 * pair + b] = column_sums(one, one * one)

    loop(frames // 2, body)


def silu_parts(normed, half_gain, half_shift):
    h = normed * half_gain + half_shift
    t = jnp.tanh(h)
    rise = 1.0 + t
    return h, rise, rise * (1.0 + h * (1.0 - t)) * half_gain


def act_kernel(n, entries, group_size, clip_ref, *refs):
    parts, refs = refs[:n], refs[n:]
    conv_ref, gain_ref, shift_ref, act_ref, normed_ref, slope_ref = refs
    frames = conv_ref.shape[0]
    first = lax.axis_index("tm") * frames
    filled = clip_ref[0] + clip_ref[1]
    half_gain, half_shift = 0.5 * gain_ref[...], 0.5 * shift_ref[...]

    def body(f):
        mean, inv = mean_and_inv(parts, f, entries, group_size)
        normed = (conv_ref[f] - mean) * inv
        h, rise, slope = silu_parts(normed, half_gain, half_shift)
        act_ref[f] = jnp.where(first + f < filled, h * rise, 0.0).astype(BF16)
        normed_ref[f] = normed.astype(BF16)
        slope_ref[f] = slope.astype(BF16)

    loop(frames, body)


def turn_kernel(x_ref, above_ref, below_ref, xt_ref, lhs_ref):
    frames, rows, width, channels = x_ref.shape
    pixels = rows * width

    def body(f):
        mid = x_ref[f].reshape(pixels, channels)
        put_windows(above_ref[f, 0], mid, below_ref[f, 0], lhs_ref, 0, (0, 1, 2))
        lanes = pl.ds(pl.multiple_of(f * pixels, pixels), pixels)
        for i in range(3):
            block = slice(i * channels, (i + 1) * channels)
            xt_ref[block, lanes] = lhs_ref[:, block].T

    loop(frames, body)


def turn_weights_kernel(spatial_ref, temporal_ref, back_ref, out_ref):
    channels = spatial_ref.shape[-1]
    for i in range(3):
        rows = slice(i * channels, (i + 1) * channels)
        out_ref[rows] = temporal_ref[i].T
        for j in range(3):
            back_ref[j, rows] = spatial_ref[i, j].T


def grad_act_kernel(corners, clip_ref, dil_ref, own, nxt, prv, *refs):
    corner, (tw_ref, normed_ref, slope_ref, ga_ref, cat_ref, sums_ref) = refs[:corners], refs[corners:]
    frames, pixels, _ = own.shape

    def body(pair):
        rows = pl.ds(pl.multiple_of(2 * pair * pixels, 2 * pixels), 2 * pixels)
        for b in range(2):
            at = pl.multiple_of((2 * pair + b) * pixels, pixels)
            gather_taps(clip_ref, dil_ref, 2 * pair + b, own, nxt, prv, corner, cat_ref, at, 0)
        grad_act = dot(cat_ref[rows], tw_ref[...]).astype(BF16)
        for b in range(2):
            f = 2 * pair + b
            one = grad_act[b * pixels : (b + 1) * pixels]
            ga_ref[f] = one
            gn = one.astype(F32) * slope_ref[f].astype(F32)
            sums_ref[f] = column_sums(gn, gn * normed_ref[f].astype(F32))

    loop(frames // 2, body)


def temporal_grad_kernel(act_ref, cat_ref, out_ref):
    frames, pixels, channels = act_ref.shape
    out_ref[...] = dot_rows(act_ref[...].reshape(frames * pixels, channels), cat_ref[...])


def norm_back_kernel(n, m, entries, group_size, normed_ref, slope_ref, ga_ref, *refs):
    parts, grad_parts = refs[:n], refs[n : n + m]
    g_ref, first_ref, last_ref, moved_ref = refs[n + m :]
    _, pixels, channels = normed_ref.shape
    width = first_ref.shape[2]

    def body(f):
        _, inv = mean_and_inv(parts, f, entries, group_size)
        means = frame_stats(grad_parts, f, entries, group_size)
        gn = ga_ref[f].astype(F32) * slope_ref[f].astype(F32)
        wide = inv * (gn - means[0:1] - normed_ref[f].astype(F32) * means[1:2])
        grad = wide.astype(BF16)
        g_ref[f] = grad
        first_ref[f, 0] = grad[:width]
        last_ref[f, 0] = grad[pixels - width :]
        here = pl.ds(pl.multiple_of(f * pixels, pixels), pixels)
        moved_ref[here, :channels] = from_right(wide, width).astype(BF16)
        moved_ref[here, channels : 2 * channels] = grad
        moved_ref[here, 2 * channels :] = from_left(wide, width).astype(BF16)

    loop(normed_ref.shape[0], body)


def weight_grad_kernel(xt_ref, moved_ref, temporal_ref, out_ref):
    channels = temporal_ref.shape[0]
    for j in range(3):
        lanes = slice(j * channels, (j + 1) * channels)
        out_ref[: 3 * channels, lanes] = dot(xt_ref[...], moved_ref[:, lanes])
    out_ref[3 * channels :, :] = temporal_ref[...]


def hand_out_kernel(acc_ref, send_ref, keep_ref):
    chips, depth, block, _ = keep_ref.shape
    half = chips * depth * block
    core = lax.axis_index("tm") & 1

    def hand_out(kept, sent):
        for p in range(chips):
            for z in range(depth):
                at = (p * depth + z) * block
                keep_ref[p, z] = acc_ref[kept + at : kept + at + block]
                send_ref[p, z] = acc_ref[sent + at : sent + at + block].astype(BF16)

    pl.when(core == 0)(functools.partial(hand_out, 0, half))
    pl.when(core == 1)(functools.partial(hand_out, half, 0))


def conv_back_kernel(g_ref, above_ref, below_ref, cot_ref, w_ref, out_ref, lhs_ref):
    frames, rows, width, channels = cot_ref.shape
    pixels = rows * width

    def body(pair):
        for b in range(2):
            f = 2 * pair + b
            put_windows(above_ref[f, 0], g_ref[f], below_ref[f, 0], lhs_ref, b * pixels, (2, 1, 0))
        lhs = lhs_ref[...]
        z = [dot(lhs, w_ref[j]) for j in range(3)]
        out = z[1] + from_right(z[0], width) + from_left(z[2], width)
        for b in range(2):
            one = out[b * pixels : (b + 1) * pixels].reshape(rows, width, channels)
            out_ref[2 * pair + b] = (one + cot_ref[2 * pair + b].astype(F32)).astype(BF16)

    loop(frames // 2, body)


def out_kernel(clip_ref, dil_ref, own, nxt, prv, tw_ref, x_ref, out_ref, cat_ref):
    frames, rows, width, channels = x_ref.shape
    pixels = rows * width

    def body(pair):
        for b in range(2):
            gather_taps(clip_ref, dil_ref, 2 * pair + b, own, nxt, prv, (), cat_ref, b * pixels, 2)
        temporal_out = dot(cat_ref[...], tw_ref[...]).astype(BF16).astype(F32)
        for b in range(2):
            one = temporal_out[b * pixels : (b + 1) * pixels].reshape(rows, width, channels)
            out_ref[2 * pair + b] = (x_ref[2 * pair + b].astype(F32) + one).astype(BF16)

    loop(frames // 2, body)


def core_sum_kernel(keep_ref, got_ref, own_ref, *send_refs):
    chip = lax.axis_index("tm") >> 1
    own_ref[...] = keep_ref[chip] + got_ref[chip].astype(F32)
    for s, ref in enumerate(send_refs, 1):
        ref[...] = (keep_ref[chip ^ s] + got_ref[chip ^ s].astype(F32)).astype(BF16)


def sum_kernel(count, own_ref, *refs):
    total = own_ref[...]
    for ref in refs[:count]:
        total = total + ref[...].astype(F32)
    refs[count][...] = total.astype(BF16)


def sum_split_kernel(count, own_ref, *refs):
    got, (mine_ref, *send_refs) = refs[:count], refs[count:]
    deep = lax.axis_index("space")

    def block(k):
        total = own_ref[k]
        for ref in got:
            total = total + ref[k].astype(F32)
        return total

    mine_ref[...] = block(deep)
    for s, ref in enumerate(send_refs, 1):
        ref[...] = block(deep ^ s).astype(BF16)


def place_kernel(axis, shift, *refs):
    me = lax.axis_index(axis) >> shift
    for s, ref in enumerate(refs[:-1]):
        refs[-1][me ^ s] = ref[...]


def finish_kernel(mine_ref, got_ref, spatial_ref, temporal_ref):
    chips, depth, block, _ = mine_ref.shape
    channels = spatial_ref.shape[-1]

    def write(pair):
        for c in range(2):
            for p in range(chips):
                for z in range(depth):
                    row = ((c * chips + p) * depth + z) * block
                    values = pair[c][p, z].astype(F32)
                    i, at = row // channels, row % channels
                    for k in range(3):
                        lanes = values[:, k * channels : (k + 1) * channels]
                        if i < 3:
                            spatial_ref[i, k, at : at + block] = lanes
                        else:
                            temporal_ref[k, at : at + block] = lanes

    core = lax.axis_index("tm") & 1
    pl.when(core == 0)(functools.partial(write, (mine_ref, got_ref)))
    pl.when(core == 1)(functools.partial(write, (got_ref, mine_ref)))


def neighbours(axis, low, high, but=None):
    size = lax.axis_size(axis)
    up = [(i, i + 1) for i in range(size - 1) if i != but]
    down = [(j, i) for i, j in up]
    return lax.ppermute(high, axis, up), lax.ppermute(low, axis, down)


def spread_sums(part, axis):
    size = lax.axis_size(axis)
    step, got = 1, None
    while step < size:
        if got is not None:
            part = part + got
        got = lax.ppermute(part, axis, [(i, i ^ step) for i in range(size)])
        step *= 2
    return [part, got]


def per_device(frames_in, cotangent, spatial, temporal, norm_gain, norm_shift, clip_frames, dilation):
    frames, rows, width, channels = frames_in.shape
    pixels = rows * width
    n, tm = lax.axis_size("space"), lax.axis_size("tm")
    chips = tm // 2
    group_size = channels // GROUPS
    entries = float(rows * n * width * group_size)
    gain, shift = norm_gain[None], norm_shift[None]
    big = frames * pixels * channels
    shape = jax.ShapeDtypeStruct
    per_px = (frames, pixels, channels)
    windows = pltpu.VMEM((2 * pixels, 3 * channels), BF16)

    cot = cotangent.reshape(per_px)
    by_corner = tm == 8
    cot_prev, cot_next = neighbours("tm", cot, cot, 3 if by_corner else None)
    cot_corner = []
    if by_corner:
        relayed = lax.ppermute(cot, "tm", [(3, 7), (4, 0)])
    above, below = neighbours("space", frames_in[:, :1], frames_in[:, rows - 1 :])
    back_weights, back_taps = call(
        turn_weights_kernel, "turn_weights", [spatial, temporal],
        [shape((3, 3 * channels, channels), BF16), shape((3 * channels, channels), BF16)], 0, big,
    )
    conv_out, sums = call(
        conv_kernel, "conv_forward", [frames_in, above, below, spatial],
        [shape(per_px, F32), shape((frames, 2, channels), F32)],
        18 * big * channels, 8 * big, [windows], 18,
    )
    if by_corner:
        sums, straight = lax.optimization_barrier((sums, cot))
        cot_corner.append(lax.ppermute(straight[: frames // 2], "tm", [(3, 4), (4, 3)]))
    parts = spread_sums(sums, "space")
    if by_corner:
        parts[0], relayed = lax.optimization_barrier((parts[0], relayed))
        cot_corner.append(lax.ppermute(relayed[frames // 2 :], "tm", [(7, 4), (0, 3)]))
    x_turned = call(
        turn_kernel, "turned", [frames_in, above, below], shape((3 * channels, frames * pixels), BF16),
        0, 8 * big, [pltpu.VMEM((pixels, 3 * channels), BF16)],
    )
    x_turned, *parts = lax.optimization_barrier((x_turned, *parts))
    act, normed, slope = call(
        functools.partial(act_kernel, len(parts), entries, group_size), "activation",
        [clip_frames, *parts, conv_out, gain, shift], [shape(per_px, BF16)] * 3, 10 * big, 10 * big,
    )
    act_prev, act_next = neighbours("tm", act, act)

    grad_act, cot_cat, grad_sums = call(
        functools.partial(grad_act_kernel, len(cot_corner)), "grad_activation",
        [clip_frames, dilation, cot, cot_next, cot_prev, *cot_corner, back_taps, normed, slope],
        [shape(per_px, BF16), shape((frames * pixels, 3 * channels), BF16), shape((frames, 2, channels), F32)],
        6 * big * channels, 16 * big,
    )
    grad_parts = spread_sums(grad_sums, "space")
    temporal_part = call(
        temporal_grad_kernel, "temporal_grad", [act, cot_cat],
        shape((channels, 3 * channels), F32), 6 * big * channels, 8 * big,
    )
    lanes = 3 * channels
    grad_conv, first_rows, last_rows, moved = call(
        functools.partial(norm_back_kernel, len(parts), len(grad_parts), entries, group_size), "norm_backward",
        [normed, slope, grad_act, *parts, *grad_parts],
        [shape(per_px, BF16)] + [shape((frames, 1, width, channels), BF16)] * 2
        + [shape((frames * pixels, lanes), BF16)],
        0, 12 * big,
    )
    grad_above, grad_below = neighbours("space", first_rows, last_rows)
    sums = call(
        weight_grad_kernel, "weight_grad", [x_turned, moved, temporal_part], shape((4 * channels, lanes), F32),
        18 * big * channels, 12 * big,
    )
    sums, grad_above, grad_below = lax.optimization_barrier((sums, grad_above, grad_below))
    block = 2 * channels // (chips * n)
    send, keep = call(
        hand_out_kernel, "hand_out", [sums],
        [shape((chips, n, block, lanes), BF16), shape((chips, n, block, lanes), F32)], 0, big,
    )
    def other_chip(s):
        return [(i, i ^ (2 * s)) for i in range(tm)]

    def other_plane(s):
        return [(i, i ^ s) for i in range(n)]

    other_core = [(i, i ^ 1) for i in range(tm)]
    got = lax.ppermute(send, "tm", other_core)
    own, *sends = call(
        core_sum_kernel, "core_sum", [keep, got],
        [shape((n, block, lanes), F32)] + [shape((n, block, lanes), BF16)] * (chips - 1), 0, 4 * big,
    )
    gots = [lax.ppermute(x, "tm", other_chip(s)) for s, x in enumerate(sends, 1)]

    in_grad = call(
        conv_back_kernel, "conv_backward", [grad_conv, grad_above, grad_below, cotangent, back_weights],
        shape(frames_in.shape, BF16), 18 * big * channels, 8 * big, [windows], 20,
    )
    own, in_grad, act_prev, act_next = lax.optimization_barrier((own, in_grad, act_prev, act_next))

    own, *sends = call(
        functools.partial(sum_split_kernel, chips - 1), "plane_sum", [own, *gots],
        [shape((block, lanes), F32)] + [shape((block, lanes), BF16)] * (n - 1), 0, big,
    )
    gots = [lax.ppermute(x, "space", other_plane(s)) for s, x in enumerate(sends, 1)]
    own = call(
        functools.partial(sum_kernel, n - 1), "line_sum", [own, *gots], shape((block, lanes), BF16), 0, big
    )
    gots = [lax.ppermute(own, "space", other_plane(s)) for s in range(1, n)]
    own = call(
        functools.partial(place_kernel, "space", 0), "line_place", [own, *gots], shape((n, block, lanes), BF16), 0, big
    )
    gots = [lax.ppermute(own, "tm", other_chip(s)) for s in range(1, chips)]

    out_frames = call(
        out_kernel, "temporal_forward",
        [clip_frames, dilation, act, act_next, act_prev, temporal.reshape(3 * channels, channels), frames_in],
        shape(frames_in.shape, BF16), 6 * big * channels, 10 * big, [windows],
    )
    own, out_frames = lax.optimization_barrier((own, out_frames))

    own = call(
        functools.partial(place_kernel, "tm", 1), "plane_place", [own, *gots], shape((chips, n, block, lanes), BF16), 0, big
    )
    got = lax.ppermute(own, "tm", other_core)
    spatial_grad, temporal_grad = call(
        finish_kernel, "finish", [own, got], [shape(spatial.shape, F32), shape(temporal.shape, F32)], 0, 4 * big
    )
    return (out_frames, in_grad, spatial_grad, temporal_grad)


def solution(mesh):
    tiles = P("tm", "space", None, None)
    return jax.shard_map(
        per_device,
        mesh=mesh,
        in_specs=(tiles, tiles, P(), P(), P(), P(), P(), P()),
        out_specs=(tiles, tiles, P(), P()),
        check_vma=False,
    )
```

```python
import functools

import jax
import jax.numpy as jnp
from jax import lax
from jax.experimental import pallas as pl
from jax.experimental.pallas import tpu as pltpu
from jax.sharding import PartitionSpec as P

GROUPS = 32
NORM_EPS = 1e-05
BF16 = jnp.bfloat16
F32 = jnp.float32
MIB = 2**20


def call(kernel, name, operands, out_shape, flops=0, moved=0, scratch=(), grant=14):
    vmem = pl.BlockSpec(memory_space=pltpu.VMEM)
    smem = pl.BlockSpec(memory_space=pltpu.SMEM)
    return pl.pallas_call(
        kernel,
        in_specs=[smem if x.dtype == jnp.int32 else vmem for x in operands],
        out_specs=jax.tree.map(lambda _: vmem, out_shape),
        out_shape=out_shape,
        scratch_shapes=list(scratch),
        compiler_params=pltpu.CompilerParams(vmem_limit_bytes=grant * MIB),
        cost_estimate=pl.CostEstimate(flops=int(flops), bytes_accessed=int(moved), transcendentals=0),
        name=name,
    )(*operands)


def dot(a, b):
    return jnp.dot(a, b, preferred_element_type=F32)


def dot_rows(a, b):
    return lax.dot_general(a, b, (((0,), (0,)), ((), ())), preferred_element_type=F32)


def group_total(row, group_size):
    channels = row.shape[-1]
    lane = lax.broadcasted_iota(jnp.int32, row.shape, 1)
    step = 1
    while step < group_size:
        up = pltpu.roll(row, channels - step, axis=1)
        down = pltpu.roll(row, step, axis=1)
        row = row + jnp.where((lane & step) == 0, up, down)
        step *= 2
    return row


def frame_stats(part_refs, f, entries, group_size):
    total = part_refs[0][f]
    for ref in part_refs[1:]:
        total = total + ref[f]
    return group_total(total, group_size) / entries


def mean_and_inv(part_refs, f, entries, group_size):
    both = frame_stats(part_refs, f, entries, group_size)
    mean = both[0:1]
    inv = lax.rsqrt(both[1:2] - mean * mean + NORM_EPS)
    return mean, inv


def column_sums(first, second):
    return jnp.concatenate(
        [jnp.sum(first, axis=0, keepdims=True), jnp.sum(second, axis=0, keepdims=True)], axis=0
    )


def put_windows(above, mid, below, lhs_ref, at, order):
    width, (pixels, channels) = above.shape[0], mid.shape
    first, mid_at, last = (slice(k * channels, (k + 1) * channels) for k in order)
    lhs_ref[at : at + width, first] = above
    lhs_ref[at + width : at + pixels, first] = mid[: pixels - width]
    lhs_ref[at : at + pixels, mid_at] = mid
    lhs_ref[at : at + pixels - width, last] = mid[width:]
    lhs_ref[at + pixels - width : at + pixels, last] = below


def from_left(y, width):
    col = lax.broadcasted_iota(jnp.int32, y.shape, 0) & (width - 1)
    return jnp.where(col == 0, 0.0, pltpu.roll(y, 1, axis=0))


def from_right(y, width):
    col = lax.broadcasted_iota(jnp.int32, y.shape, 0) & (width - 1)
    return jnp.where(col == width - 1, 0.0, pltpu.roll(y, y.shape[0] - 1, axis=0))


def slot_sources(clip_ref, dil_ref, local, frames):
    slot = lax.axis_index("tm") * frames + local
    start1 = clip_ref[0]
    filled = start1 + clip_ref[1]
    in_first = slot < start1
    d = jnp.where(in_first, dil_ref[0], dil_ref[1])
    low = jnp.where(in_first, 0, start1)
    high = jnp.where(in_first, start1, filled)
    used = slot < filled
    later, earlier = local + d, local - d
    later_live = used & (slot + d < high)
    earlier_live = used & (slot - d >= low)
    later_which = jnp.where(later_live, jnp.where(later < frames, 1, 2), 0)
    earlier_which = jnp.where(earlier_live, jnp.where(earlier >= 0, 1, 2), 0)
    return (later, later_which), (earlier, earlier_which), used


def gather_taps(clip_ref, dil_ref, local, own, nxt, prv, corner, cat_ref, at, up_slot):
    frames, pixels, channels = own.shape
    later, earlier, used = slot_sources(clip_ref, dil_ref, local, frames)
    me, half = lax.axis_index("tm"), frames // 2

    def put(slot, ref, index):
        cat_ref[pl.ds(at, pixels), slot * channels : (slot + 1) * channels] = ref[index]

    def clear(slot):
        cat_ref[pl.ds(at, pixels), slot * channels : (slot + 1) * channels] = jnp.zeros((pixels, channels), BF16)

    for slot, (index, which), other, shift, turn in (
        (up_slot, later, nxt, -frames, 3),
        (2 - up_slot, earlier, prv, frames, 4),
    ):
        beyond = which == 2
        there = jnp.clip(index + shift, 0, frames - 1)
        pl.when(which == 0)(functools.partial(clear, slot))
        pl.when(which == 1)(functools.partial(put, slot, own, jnp.clip(index, 0, frames - 1)))
        if corner:
            by_corner = beyond & (me == turn)
            low, high = by_corner & (there < half), by_corner & (there >= half)
            pl.when(low)(functools.partial(put, slot, corner[0], jnp.minimum(there, half - 1)))
            pl.when(high)(functools.partial(put, slot, corner[1], jnp.maximum(there - half, 0)))
            beyond = beyond & (me != turn)
        pl.when(beyond)(functools.partial(put, slot, other, there))
    pl.when(used)(functools.partial(put, 1, own, local))
    pl.when(jnp.logical_not(used))(functools.partial(clear, 1))


def loop(count, body):
    def step(k, carry):
        body(k)
        return carry

    lax.fori_loop(0, count, step, 0)


def conv_kernel(x_ref, above_ref, below_ref, w_ref, out_ref, sums_ref, lhs_ref):
    frames, rows, width, channels = x_ref.shape
    pixels = rows * width

    def body(pair):
        for b in range(2):
            f = 2 * pair + b
            mid = x_ref[f].reshape(pixels, channels)
            put_windows(above_ref[f, 0], mid, below_ref[f, 0], lhs_ref, b * pixels, (0, 1, 2))
        lhs = lhs_ref[...]
        y = [dot(lhs, w_ref[:, j].reshape(3 * channels, channels)) for j in range(3)]
        out = y[1] + from_left(y[0], width) + from_right(y[2], width)
        for b in range(2):
            one = out[b * pixels : (b + 1) * pixels]
            out_ref[2 * pair + b] = one
            sums_ref[2 * pair + b] = column_sums(one, one * one)

    loop(frames // 2, body)


def silu_parts(normed, half_gain, half_shift):
    h = normed * half_gain + half_shift
    t = jnp.tanh(h)
    rise = 1.0 + t
    return h, rise, rise * (1.0 + h * (1.0 - t)) * half_gain


def act_kernel(n, entries, group_size, clip_ref, *refs):
    parts, refs = refs[:n], refs[n:]
    conv_ref, gain_ref, shift_ref, act_ref, normed_ref, slope_ref = refs
    frames = conv_ref.shape[0]
    first = lax.axis_index("tm") * frames
    filled = clip_ref[0] + clip_ref[1]
    half_gain, half_shift = 0.5 * gain_ref[...], 0.5 * shift_ref[...]

    def body(f):
        mean, inv = mean_and_inv(parts, f, entries, group_size)
        normed = (conv_ref[f] - mean) * inv
        h, rise, slope = silu_parts(normed, half_gain, half_shift)
        act_ref[f] = jnp.where(first + f < filled, h * rise, 0.0).astype(BF16)
        normed_ref[f] = normed.astype(BF16)
        slope_ref[f] = slope.astype(BF16)

    loop(frames, body)


def turn_kernel(x_ref, above_ref, below_ref, xt_ref, lhs_ref):
    frames, rows, width, channels = x_ref.shape
    pixels = rows * width

    def body(f):
        mid = x_ref[f].reshape(pixels, channels)
        put_windows(above_ref[f, 0], mid, below_ref[f, 0], lhs_ref, 0, (0, 1, 2))
        lanes = pl.ds(pl.multiple_of(f * pixels, pixels), pixels)
        for i in range(3):
            block = slice(i * channels, (i + 1) * channels)
            xt_ref[block, lanes] = lhs_ref[:, block].T

    loop(frames, body)


def turn_weights_kernel(spatial_ref, temporal_ref, back_ref, out_ref):
    channels = spatial_ref.shape[-1]
    for i in range(3):
        rows = slice(i * channels, (i + 1) * channels)
        out_ref[rows] = temporal_ref[i].T
        for j in range(3):
            back_ref[j, rows] = spatial_ref[i, j].T


def grad_act_kernel(corners, clip_ref, dil_ref, own, nxt, prv, *refs):
    corner, (tw_ref, normed_ref, slope_ref, ga_ref, cat_ref, sums_ref) = refs[:corners], refs[corners:]
    frames, pixels, _ = own.shape

    def body(pair):
        rows = pl.ds(pl.multiple_of(2 * pair * pixels, 2 * pixels), 2 * pixels)
        for b in range(2):
            at = pl.multiple_of((2 * pair + b) * pixels, pixels)
            gather_taps(clip_ref, dil_ref, 2 * pair + b, own, nxt, prv, corner, cat_ref, at, 0)
        grad_act = dot(cat_ref[rows], tw_ref[...]).astype(BF16)
        for b in range(2):
            f = 2 * pair + b
            one = grad_act[b * pixels : (b + 1) * pixels]
            ga_ref[f] = one
            gn = one.astype(F32) * slope_ref[f].astype(F32)
            sums_ref[f] = column_sums(gn, gn * normed_ref[f].astype(F32))

    loop(frames // 2, body)


def temporal_grad_kernel(act_ref, cat_ref, out_ref):
    frames, pixels, channels = act_ref.shape
    out_ref[...] = dot_rows(act_ref[...].reshape(frames * pixels, channels), cat_ref[...])


def norm_back_kernel(n, m, entries, group_size, normed_ref, slope_ref, ga_ref, *refs):
    parts, grad_parts = refs[:n], refs[n : n + m]
    g_ref, first_ref, last_ref, moved_ref = refs[n + m :]
    _, pixels, channels = normed_ref.shape
    width = first_ref.shape[2]

    def body(f):
        _, inv = mean_and_inv(parts, f, entries, group_size)
        means = frame_stats(grad_parts, f, entries, group_size)
        gn = ga_ref[f].astype(F32) * slope_ref[f].astype(F32)
        wide = inv * (gn - means[0:1] - normed_ref[f].astype(F32) * means[1:2])
        grad = wide.astype(BF16)
        g_ref[f] = grad
        first_ref[f, 0] = grad[:width]
        last_ref[f, 0] = grad[pixels - width :]
        here = pl.ds(pl.multiple_of(f * pixels, pixels), pixels)
        moved_ref[here, :channels] = from_right(wide, width).astype(BF16)
        moved_ref[here, channels : 2 * channels] = grad
        moved_ref[here, 2 * channels :] = from_left(wide, width).astype(BF16)

    loop(normed_ref.shape[0], body)


def weight_grad_kernel(xt_ref, moved_ref, temporal_ref, out_ref):
    channels = temporal_ref.shape[0]
    for j in range(3):
        lanes = slice(j * channels, (j + 1) * channels)
        out_ref[: 3 * channels, lanes] = dot(xt_ref[...], moved_ref[:, lanes])
    out_ref[3 * channels :, :] = temporal_ref[...]


def hand_out_kernel(acc_ref, send_ref, keep_ref):
    chips, depth, block, _ = keep_ref.shape
    half = chips * depth * block
    core = lax.axis_index("tm") & 1

    def hand_out(kept, sent):
        for p in range(chips):
            for z in range(depth):
                at = (p * depth + z) * block
                keep_ref[p, z] = acc_ref[kept + at : kept + at + block]
                send_ref[p, z] = acc_ref[sent + at : sent + at + block].astype(BF16)

    pl.when(core == 0)(functools.partial(hand_out, 0, half))
    pl.when(core == 1)(functools.partial(hand_out, half, 0))


def conv_back_kernel(g_ref, above_ref, below_ref, cot_ref, w_ref, out_ref, lhs_ref):
    frames, rows, width, channels = cot_ref.shape
    pixels = rows * width

    def body(pair):
        for b in range(2):
            f = 2 * pair + b
            put_windows(above_ref[f, 0], g_ref[f], below_ref[f, 0], lhs_ref, b * pixels, (2, 1, 0))
        lhs = lhs_ref[...]
        z = [dot(lhs, w_ref[j]) for j in range(3)]
        out = z[1] + from_right(z[0], width) + from_left(z[2], width)
        for b in range(2):
            one = out[b * pixels : (b + 1) * pixels].reshape(rows, width, channels)
            out_ref[2 * pair + b] = (one + cot_ref[2 * pair + b].astype(F32)).astype(BF16)

    loop(frames // 2, body)


def out_kernel(clip_ref, dil_ref, own, nxt, prv, tw_ref, x_ref, out_ref, cat_ref):
    frames, rows, width, channels = x_ref.shape
    pixels = rows * width

    def body(pair):
        for b in range(2):
            gather_taps(clip_ref, dil_ref, 2 * pair + b, own, nxt, prv, (), cat_ref, b * pixels, 2)
        temporal_out = dot(cat_ref[...], tw_ref[...]).astype(BF16).astype(F32)
        for b in range(2):
            one = temporal_out[b * pixels : (b + 1) * pixels].reshape(rows, width, channels)
            out_ref[2 * pair + b] = (x_ref[2 * pair + b].astype(F32) + one).astype(BF16)

    loop(frames // 2, body)


def core_sum_kernel(keep_ref, got_ref, own_ref, *send_refs):
    chip = lax.axis_index("tm") >> 1
    own_ref[...] = keep_ref[chip] + got_ref[chip].astype(F32)
    for s, ref in enumerate(send_refs, 1):
        ref[...] = (keep_ref[chip ^ s] + got_ref[chip ^ s].astype(F32)).astype(BF16)


def sum_kernel(count, own_ref, *refs):
    total = own_ref[...]
    for ref in refs[:count]:
        total = total + ref[...].astype(F32)
    refs[count][...] = total.astype(BF16)


def sum_split_kernel(count, own_ref, *refs):
    got, (mine_ref, *send_refs) = refs[:count], refs[count:]
    deep = lax.axis_index("space")

    def block(k):
        total = own_ref[k]
        for ref in got:
            total = total + ref[k].astype(F32)
        return total

    mine_ref[...] = block(deep)
    for s, ref in enumerate(send_refs, 1):
        ref[...] = block(deep ^ s).astype(BF16)


def place_kernel(axis, shift, *refs):
    me = lax.axis_index(axis) >> shift
    for s, ref in enumerate(refs[:-1]):
        refs[-1][me ^ s] = ref[...]


def finish_kernel(mine_ref, got_ref, spatial_ref, temporal_ref):
    chips, depth, block, _ = mine_ref.shape
    channels = spatial_ref.shape[-1]

    def write(pair):
        for c in range(2):
            for p in range(chips):
                for z in range(depth):
                    row = ((c * chips + p) * depth + z) * block
                    values = pair[c][p, z].astype(F32)
                    i, at = row // channels, row % channels
                    for k in range(3):
                        lanes = values[:, k * channels : (k + 1) * channels]
                        if i < 3:
                            spatial_ref[i, k, at : at + block] = lanes
                        else:
                            temporal_ref[k, at : at + block] = lanes

    core = lax.axis_index("tm") & 1
    pl.when(core == 0)(functools.partial(write, (mine_ref, got_ref)))
    pl.when(core == 1)(functools.partial(write, (got_ref, mine_ref)))


def neighbours(axis, low, high, but=None):
    size = lax.axis_size(axis)
    up = [(i, i + 1) for i in range(size - 1) if i != but]
    down = [(j, i) for i, j in up]
    return lax.ppermute(high, axis, up), lax.ppermute(low, axis, down)


def spread_sums(part, axis):
    size = lax.axis_size(axis)
    step, got = 1, None
    while step < size:
        if got is not None:
            part = part + got
        got = lax.ppermute(part, axis, [(i, i ^ step) for i in range(size)])
        step *= 2
    return [part, got]


def per_device(frames_in, cotangent, spatial, temporal, norm_gain, norm_shift, clip_frames, dilation):
    frames, rows, width, channels = frames_in.shape
    pixels = rows * width
    n, tm = lax.axis_size("space"), lax.axis_size("tm")
    chips = tm // 2
    group_size = channels // GROUPS
    entries = float(rows * n * width * group_size)
    gain, shift = norm_gain[None], norm_shift[None]
    big = frames * pixels * channels
    shape = jax.ShapeDtypeStruct
    per_px = (frames, pixels, channels)
    windows = pltpu.VMEM((2 * pixels, 3 * channels), BF16)

    cot = cotangent.reshape(per_px)
    by_corner = tm == 8
    cot_prev, cot_next = neighbours("tm", cot, cot, 3 if by_corner else None)
    cot_corner = []
    if by_corner:
        relayed = lax.ppermute(cot, "tm", [(3, 7), (4, 0)])
    above, below = neighbours("space", frames_in[:, :1], frames_in[:, rows - 1 :])
    back_weights, back_taps = call(
        turn_weights_kernel, "turn_weights", [spatial, temporal],
        [shape((3, 3 * channels, channels), BF16), shape((3 * channels, channels), BF16)], 0, big,
    )
    conv_out, sums = call(
        conv_kernel, "conv_forward", [frames_in, above, below, spatial],
        [shape(per_px, F32), shape((frames, 2, channels), F32)],
        100 * big * channels, 8 * big, [windows], 18,
    )
    if by_corner:
        sums, straight = lax.optimization_barrier((sums, cot))
        cot_corner.append(lax.ppermute(straight[: frames // 2], "tm", [(3, 4), (4, 3)]))
    parts = spread_sums(sums, "space")
    if by_corner:
        parts[0], relayed = lax.optimization_barrier((parts[0], relayed))
        cot_corner.append(lax.ppermute(relayed[frames // 2 :], "tm", [(7, 4), (0, 3)]))
    x_turned = call(
        turn_kernel, "turned", [frames_in, above, below], shape((3 * channels, frames * pixels), BF16),
        0, 8 * big, [pltpu.VMEM((pixels, 3 * channels), BF16)],
    )
    x_turned, *parts = lax.optimization_barrier((x_turned, *parts))
    act, normed, slope = call(
        functools.partial(act_kernel, len(parts), entries, group_size), "activation",
        [clip_frames, *parts, conv_out, gain, shift], [shape(per_px, BF16)] * 3, 10 * big, 10 * big,
    )
    act_prev, act_next = neighbours("tm", act, act)

    grad_act, cot_cat, grad_sums = call(
        functools.partial(grad_act_kernel, len(cot_corner)), "grad_activation",
        [clip_frames, dilation, cot, cot_next, cot_prev, *cot_corner, back_taps, normed, slope],
        [shape(per_px, BF16), shape((frames * pixels, 3 * channels), BF16), shape((frames, 2, channels), F32)],
        6 * big * channels, 16 * big,
    )
    grad_parts = spread_sums(grad_sums, "space")
    temporal_part = call(
        temporal_grad_kernel, "temporal_grad", [act, cot_cat],
        shape((channels, 3 * channels), F32), 6 * big * channels, 8 * big,
    )
    lanes = 3 * channels
    grad_conv, first_rows, last_rows, moved = call(
        functools.partial(norm_back_kernel, len(parts), len(grad_parts), entries, group_size), "norm_backward",
        [normed, slope, grad_act, *parts, *grad_parts],
        [shape(per_px, BF16)] + [shape((frames, 1, width, channels), BF16)] * 2
        + [shape((frames * pixels, lanes), BF16)],
        0, 12 * big,
    )
    grad_above, grad_below = neighbours("space", first_rows, last_rows)
    sums = call(
        weight_grad_kernel, "weight_grad", [x_turned, moved, temporal_part], shape((4 * channels, lanes), F32),
        18 * big * channels, 12 * big,
    )
    sums, grad_above, grad_below = lax.optimization_barrier((sums, grad_above, grad_below))
    block = 2 * channels // (chips * n)
    send, keep = call(
        hand_out_kernel, "hand_out", [sums],
        [shape((chips, n, block, lanes), BF16), shape((chips, n, block, lanes), F32)], 0, big,
    )
    def other_chip(s):
        return [(i, i ^ (2 * s)) for i in range(tm)]

    def other_plane(s):
        return [(i, i ^ s) for i in range(n)]

    other_core = [(i, i ^ 1) for i in range(tm)]
    got = lax.ppermute(send, "tm", other_core)
    own, *sends = call(
        core_sum_kernel, "core_sum", [keep, got],
        [shape((n, block, lanes), F32)] + [shape((n, block, lanes), BF16)] * (chips - 1), 0, 4 * big,
    )
    gots = [lax.ppermute(x, "tm", other_chip(s)) for s, x in enumerate(sends, 1)]

    in_grad = call(
        conv_back_kernel, "conv_backward", [grad_conv, grad_above, grad_below, cotangent, back_weights],
        shape(frames_in.shape, BF16), 18 * big * channels, 8 * big, [windows], 20,
    )
    own, in_grad, act_prev, act_next = lax.optimization_barrier((own, in_grad, act_prev, act_next))

    own, *sends = call(
        functools.partial(sum_split_kernel, chips - 1), "plane_sum", [own, *gots],
        [shape((block, lanes), F32)] + [shape((block, lanes), BF16)] * (n - 1), 0, big,
    )
    gots = [lax.ppermute(x, "space", other_plane(s)) for s, x in enumerate(sends, 1)]
    own = call(
        functools.partial(sum_kernel, n - 1), "line_sum", [own, *gots], shape((block, lanes), BF16), 0, big
    )
    gots = [lax.ppermute(own, "space", other_plane(s)) for s in range(1, n)]
    own = call(
        functools.partial(place_kernel, "space", 0), "line_place", [own, *gots], shape((n, block, lanes), BF16), 0, big
    )
    gots = [lax.ppermute(own, "tm", other_chip(s)) for s in range(1, chips)]

    out_frames = call(
        out_kernel, "temporal_forward",
        [clip_frames, dilation, act, act_next, act_prev, temporal.reshape(3 * channels, channels), frames_in],
        shape(frames_in.shape, BF16), 6 * big * channels, 10 * big, [windows],
    )
    own, out_frames = lax.optimization_barrier((own, out_frames))

    own = call(
        functools.partial(place_kernel, "tm", 1), "plane_place", [own, *gots], shape((chips, n, block, lanes), BF16), 0, big
    )
    got = lax.ppermute(own, "tm", other_core)
    spatial_grad, temporal_grad = call(
        finish_kernel, "finish", [own, got], [shape(spatial.shape, F32), shape(temporal.shape, F32)], 0, 4 * big
    )
    return (out_frames, in_grad, spatial_grad, temporal_grad)


def solution(mesh):
    tiles = P("tm", "space", None, None)
    return jax.shard_map(
        per_device,
        mesh=mesh,
        in_specs=(tiles, tiles, P(), P(), P(), P(), P(), P()),
        out_specs=(tiles, tiles, P(), P()),
        check_vma=False,
    )
```

```python
import functools

import jax
import jax.numpy as jnp
from jax import lax
from jax.experimental import pallas as pl
from jax.experimental.pallas import tpu as pltpu
from jax.sharding import PartitionSpec as P

GROUPS = 32
NORM_EPS = 1e-05
BF16 = jnp.bfloat16
F32 = jnp.float32
MIB = 2**20


def call(kernel, name, operands, out_shape, flops=0, moved=0, scratch=(), grant=14):
    vmem = pl.BlockSpec(memory_space=pltpu.VMEM)
    smem = pl.BlockSpec(memory_space=pltpu.SMEM)
    return pl.pallas_call(
        kernel,
        in_specs=[smem if x.dtype == jnp.int32 else vmem for x in operands],
        out_specs=jax.tree.map(lambda _: vmem, out_shape),
        out_shape=out_shape,
        scratch_shapes=list(scratch),
        compiler_params=pltpu.CompilerParams(vmem_limit_bytes=grant * MIB),
        cost_estimate=pl.CostEstimate(flops=int(flops), bytes_accessed=int(moved), transcendentals=0),
        name=name,
    )(*operands)


def dot(a, b):
    return jnp.dot(a, b, preferred_element_type=F32)


def dot_rows(a, b):
    return lax.dot_general(a, b, (((0,), (0,)), ((), ())), preferred_element_type=F32)


def group_total(row, group_size):
    channels = row.shape[-1]
    lane = lax.broadcasted_iota(jnp.int32, row.shape, 1)
    step = 1
    while step < group_size:
        up = pltpu.roll(row, channels - step, axis=1)
        down = pltpu.roll(row, step, axis=1)
        row = row + jnp.where((lane & step) == 0, up, down)
        step *= 2
    return row


def frame_stats(part_refs, f, entries, group_size):
    total = part_refs[0][f]
    for ref in part_refs[1:]:
        total = total + ref[f]
    return group_total(total, group_size) / entries


def mean_and_inv(part_refs, f, entries, group_size):
    both = frame_stats(part_refs, f, entries, group_size)
    mean = both[0:1]
    inv = lax.rsqrt(both[1:2] - mean * mean + NORM_EPS)
    return mean, inv


def column_sums(first, second):
    return jnp.concatenate(
        [jnp.sum(first, axis=0, keepdims=True), jnp.sum(second, axis=0, keepdims=True)], axis=0
    )


def put_windows(above, mid, below, lhs_ref, at, order):
    width, (pixels, channels) = above.shape[0], mid.shape
    first, mid_at, last = (slice(k * channels, (k + 1) * channels) for k in order)
    lhs_ref[at : at + width, first] = above
    lhs_ref[at + width : at + pixels, first] = mid[: pixels - width]
    lhs_ref[at : at + pixels, mid_at] = mid
    lhs_ref[at : at + pixels - width, last] = mid[width:]
    lhs_ref[at + pixels - width : at + pixels, last] = below


def from_left(y, width):
    col = lax.broadcasted_iota(jnp.int32, y.shape, 0) & (width - 1)
    return jnp.where(col == 0, 0.0, pltpu.roll(y, 1, axis=0))


def from_right(y, width):
    col = lax.broadcasted_iota(jnp.int32, y.shape, 0) & (width - 1)
    return jnp.where(col == width - 1, 0.0, pltpu.roll(y, y.shape[0] - 1, axis=0))


def slot_sources(clip_ref, dil_ref, local, frames):
    slot = lax.axis_index("tm") * frames + local
    start1 = clip_ref[0]
    filled = start1 + clip_ref[1]
    in_first = slot < start1
    d = jnp.where(in_first, dil_ref[0], dil_ref[1])
    low = jnp.where(in_first, 0, start1)
    high = jnp.where(in_first, start1, filled)
    used = slot < filled
    later, earlier = local + d, local - d
    later_live = used & (slot + d < high)
    earlier_live = used & (slot - d >= low)
    later_which = jnp.where(later_live, jnp.where(later < frames, 1, 2), 0)
    earlier_which = jnp.where(earlier_live, jnp.where(earlier >= 0, 1, 2), 0)
    return (later, later_which), (earlier, earlier_which), used


def gather_taps(clip_ref, dil_ref, local, own, nxt, prv, corner, cat_ref, at, up_slot):
    frames, pixels, channels = own.shape
    later, earlier, used = slot_sources(clip_ref, dil_ref, local, frames)
    me, half = lax.axis_index("tm"), frames // 2

    def put(slot, ref, index):
        cat_ref[pl.ds(at, pixels), slot * channels : (slot + 1) * channels] = ref[index]

    def clear(slot):
        cat_ref[pl.ds(at, pixels), slot * channels : (slot + 1) * channels] = jnp.zeros((pixels, channels), BF16)

    for slot, (index, which), other, shift, turn in (
        (up_slot, later, nxt, -frames, 3),
        (2 - up_slot, earlier, prv, frames, 4),
    ):
        beyond = which == 2
        there = jnp.clip(index + shift, 0, frames - 1)
        pl.when(which == 0)(functools.partial(clear, slot))
        pl.when(which == 1)(functools.partial(put, slot, own, jnp.clip(index, 0, frames - 1)))
        if corner:
            by_corner = beyond & (me == turn)
            low, high = by_corner & (there < half), by_corner & (there >= half)
            pl.when(low)(functools.partial(put, slot, corner[0], jnp.minimum(there, half - 1)))
            pl.when(high)(functools.partial(put, slot, corner[1], jnp.maximum(there - half, 0)))
            beyond = beyond & (me != turn)
        pl.when(beyond)(functools.partial(put, slot, other, there))
    pl.when(used)(functools.partial(put, 1, own, local))
    pl.when(jnp.logical_not(used))(functools.partial(clear, 1))


def loop(count, body):
    def step(k, carry):
        body(k)
        return carry

    lax.fori_loop(0, count, step, 0)


def conv_kernel(x_ref, above_ref, below_ref, w_ref, out_ref, sums_ref, lhs_ref):
    frames, rows, width, channels = x_ref.shape
    pixels = rows * width

    def body(pair):
        for b in range(2):
            f = 2 * pair + b
            mid = x_ref[f].reshape(pixels, channels)
            put_windows(above_ref[f, 0], mid, below_ref[f, 0], lhs_ref, b * pixels, (0, 1, 2))
        lhs = lhs_ref[...]
        y = [dot(lhs, w_ref[:, j].reshape(3 * channels, channels)) for j in range(3)]
        out = y[1] + from_left(y[0], width) + from_right(y[2], width)
        for b in range(2):
            one = out[b * pixels : (b + 1) * pixels]
            out_ref[2 * pair + b] = one
            sums_ref[2 * pair + b] = column_sums(one, one * one)

    loop(frames // 2, body)


def silu_parts(normed, half_gain, half_shift):
    h = normed * half_gain + half_shift
    t = jnp.tanh(h)
    rise = 1.0 + t
    return h, rise, rise * (1.0 + h * (1.0 - t)) * half_gain


def act_kernel(n, entries, group_size, clip_ref, *refs):
    parts, refs = refs[:n], refs[n:]
    conv_ref, gain_ref, shift_ref, act_ref, normed_ref, slope_ref = refs
    frames = conv_ref.shape[0]
    first = lax.axis_index("tm") * frames
    filled = clip_ref[0] + clip_ref[1]
    half_gain, half_shift = 0.5 * gain_ref[...], 0.5 * shift_ref[...]

    def body(f):
        mean, inv = mean_and_inv(parts, f, entries, group_size)
        normed = (conv_ref[f] - mean) * inv
        h, rise, slope = silu_parts(normed, half_gain, half_shift)
        act_ref[f] = jnp.where(first + f < filled, h * rise, 0.0).astype(BF16)
        normed_ref[f] = normed.astype(BF16)
        slope_ref[f] = slope.astype(BF16)

    loop(frames, body)


def turn_kernel(x_ref, above_ref, below_ref, xt_ref, lhs_ref):
    frames, rows, width, channels = x_ref.shape
    pixels = rows * width

    def body(f):
        mid = x_ref[f].reshape(pixels, channels)
        put_windows(above_ref[f, 0], mid, below_ref[f, 0], lhs_ref, 0, (0, 1, 2))
        lanes = pl.ds(pl.multiple_of(f * pixels, pixels), pixels)
        for i in range(3):
            block = slice(i * channels, (i + 1) * channels)
            xt_ref[block, lanes] = lhs_ref[:, block].T

    loop(frames, body)


def turn_weights_kernel(spatial_ref, temporal_ref, back_ref, out_ref):
    channels = spatial_ref.shape[-1]
    for i in range(3):
        rows = slice(i * channels, (i + 1) * channels)
        out_ref[rows] = temporal_ref[i].T
        for j in range(3):
            back_ref[j, rows] = spatial_ref[i, j].T


def grad_act_kernel(corners, clip_ref, dil_ref, own, nxt, prv, *refs):
    corner, (tw_ref, normed_ref, slope_ref, ga_ref, cat_ref, sums_ref) = refs[:corners], refs[corners:]
    frames, pixels, _ = own.shape

    def body(pair):
        rows = pl.ds(pl.multiple_of(2 * pair * pixels, 2 * pixels), 2 * pixels)
        for b in range(2):
            at = pl.multiple_of((2 * pair + b) * pixels, pixels)
            gather_taps(clip_ref, dil_ref, 2 * pair + b, own, nxt, prv, corner, cat_ref, at, 0)
        grad_act = dot(cat_ref[rows], tw_ref[...]).astype(BF16)
        for b in range(2):
            f = 2 * pair + b
            one = grad_act[b * pixels : (b + 1) * pixels]
            ga_ref[f] = one
            gn = one.astype(F32) * slope_ref[f].astype(F32)
            sums_ref[f] = column_sums(gn, gn * normed_ref[f].astype(F32))

    loop(frames // 2, body)


def temporal_grad_kernel(act_ref, cat_ref, out_ref):
    frames, pixels, channels = act_ref.shape
    out_ref[...] = dot_rows(act_ref[...].reshape(frames * pixels, channels), cat_ref[...])


def norm_back_kernel(n, m, entries, group_size, normed_ref, slope_ref, ga_ref, *refs):
    parts, grad_parts = refs[:n], refs[n : n + m]
    g_ref, first_ref, last_ref, moved_ref = refs[n + m :]
    _, pixels, channels = normed_ref.shape
    width = first_ref.shape[2]

    def body(f):
        _, inv = mean_and_inv(parts, f, entries, group_size)
        means = frame_stats(grad_parts, f, entries, group_size)
        gn = ga_ref[f].astype(F32) * slope_ref[f].astype(F32)
        wide = inv * (gn - means[0:1] - normed_ref[f].astype(F32) * means[1:2])
        grad = wide.astype(BF16)
        g_ref[f] = grad
        first_ref[f, 0] = grad[:width]
        last_ref[f, 0] = grad[pixels - width :]
        here = pl.ds(pl.multiple_of(f * pixels, pixels), pixels)
        moved_ref[here, :channels] = from_right(wide, width).astype(BF16)
        moved_ref[here, channels : 2 * channels] = grad
        moved_ref[here, 2 * channels :] = from_left(wide, width).astype(BF16)

    loop(normed_ref.shape[0], body)


def weight_grad_kernel(xt_ref, moved_ref, temporal_ref, out_ref):
    channels = temporal_ref.shape[0]
    for j in range(3):
        lanes = slice(j * channels, (j + 1) * channels)
        out_ref[: 3 * channels, lanes] = dot(xt_ref[...], moved_ref[:, lanes])
    out_ref[3 * channels :, :] = temporal_ref[...]


def hand_out_kernel(acc_ref, send_ref, keep_ref):
    chips, depth, block, _ = keep_ref.shape
    half = chips * depth * block
    core = lax.axis_index("tm") & 1

    def hand_out(kept, sent):
        for p in range(chips):
            for z in range(depth):
                at = (p * depth + z) * block
                keep_ref[p, z] = acc_ref[kept + at : kept + at + block]
                send_ref[p, z] = acc_ref[sent + at : sent + at + block].astype(BF16)

    pl.when(core == 0)(functools.partial(hand_out, 0, half))
    pl.when(core == 1)(functools.partial(hand_out, half, 0))


def conv_back_kernel(g_ref, above_ref, below_ref, cot_ref, w_ref, out_ref, lhs_ref):
    frames, rows, width, channels = cot_ref.shape
    pixels = rows * width

    def body(pair):
        for b in range(2):
            f = 2 * pair + b
            put_windows(above_ref[f, 0], g_ref[f], below_ref[f, 0], lhs_ref, b * pixels, (2, 1, 0))
        lhs = lhs_ref[...]
        z = [dot(lhs, w_ref[j]) for j in range(3)]
        out = z[1] + from_right(z[0], width) + from_left(z[2], width)
        for b in range(2):
            one = out[b * pixels : (b + 1) * pixels].reshape(rows, width, channels)
            out_ref[2 * pair + b] = (one + cot_ref[2 * pair + b].astype(F32)).astype(BF16)

    loop(frames // 2, body)


def out_kernel(clip_ref, dil_ref, own, nxt, prv, tw_ref, x_ref, out_ref, cat_ref):
    frames, rows, width, channels = x_ref.shape
    pixels = rows * width

    def body(pair):
        for b in range(2):
            gather_taps(clip_ref, dil_ref, 2 * pair + b, own, nxt, prv, (), cat_ref, b * pixels, 2)
        temporal_out = dot(cat_ref[...], tw_ref[...]).astype(BF16).astype(F32)
        for b in range(2):
            one = temporal_out[b * pixels : (b + 1) * pixels].reshape(rows, width, channels)
            out_ref[2 * pair + b] = (x_ref[2 * pair + b].astype(F32) + one).astype(BF16)

    loop(frames // 2, body)


def core_sum_kernel(keep_ref, got_ref, own_ref, *send_refs):
    chip = lax.axis_index("tm") >> 1
    own_ref[...] = keep_ref[chip] + got_ref[chip].astype(F32)
    for s, ref in enumerate(send_refs, 1):
        ref[...] = (keep_ref[chip ^ s] + got_ref[chip ^ s].astype(F32)).astype(BF16)


def sum_kernel(count, own_ref, *refs):
    total = own_ref[...]
    for ref in refs[:count]:
        total = total + ref[...].astype(F32)
    refs[count][...] = total.astype(BF16)


def sum_split_kernel(count, own_ref, *refs):
    got, (mine_ref, *send_refs) = refs[:count], refs[count:]
    deep = lax.axis_index("space")

    def block(k):
        total = own_ref[k]
        for ref in got:
            total = total + ref[k].astype(F32)
        return total

    mine_ref[...] = block(deep)
    for s, ref in enumerate(send_refs, 1):
        ref[...] = block(deep ^ s).astype(BF16)


def place_kernel(axis, shift, *refs):
    me = lax.axis_index(axis) >> shift
    for s, ref in enumerate(refs[:-1]):
        refs[-1][me ^ s] = ref[...]


def finish_kernel(mine_ref, got_ref, spatial_ref, temporal_ref):
    chips, depth, block, _ = mine_ref.shape
    channels = spatial_ref.shape[-1]

    def write(pair):
        for c in range(2):
            for p in range(chips):
                for z in range(depth):
                    row = ((c * chips + p) * depth + z) * block
                    values = pair[c][p, z].astype(F32)
                    i, at = row // channels, row % channels
                    for k in range(3):
                        lanes = values[:, k * channels : (k + 1) * channels]
                        if i < 3:
                            spatial_ref[i, k, at : at + block] = lanes
                        else:
                            temporal_ref[k, at : at + block] = lanes

    core = lax.axis_index("tm") & 1
    pl.when(core == 0)(functools.partial(write, (mine_ref, got_ref)))
    pl.when(core == 1)(functools.partial(write, (got_ref, mine_ref)))


def neighbours(axis, low, high, but=None):
    size = lax.axis_size(axis)
    up = [(i, i + 1) for i in range(size - 1) if i != but]
    down = [(j, i) for i, j in up]
    return lax.ppermute(high, axis, up), lax.ppermute(low, axis, down)


def spread_parts(part, axis):
    size = lax.axis_size(axis)
    return [part] + [lax.ppermute(part, axis, [(i, i ^ s) for i in range(size)]) for s in range(1, size)]


def spread_sums(part, axis):
    size = lax.axis_size(axis)
    step, got = 1, None
    while step < size:
        if got is not None:
            part = part + got
        got = lax.ppermute(part, axis, [(i, i ^ step) for i in range(size)])
        step *= 2
    return [part, got]


def per_device(frames_in, cotangent, spatial, temporal, norm_gain, norm_shift, clip_frames, dilation):
    frames, rows, width, channels = frames_in.shape
    pixels = rows * width
    n, tm = lax.axis_size("space"), lax.axis_size("tm")
    chips = tm // 2
    group_size = channels // GROUPS
    entries = float(rows * n * width * group_size)
    gain, shift = norm_gain[None], norm_shift[None]
    big = frames * pixels * channels
    shape = jax.ShapeDtypeStruct
    per_px = (frames, pixels, channels)
    windows = pltpu.VMEM((2 * pixels, 3 * channels), BF16)

    cot = cotangent.reshape(per_px)
    by_corner = tm == 8
    first, last = frames_in[:, :1], frames_in[:, rows - 1 :]
    first, last, near = lax.optimization_barrier((first, last, cot))
    cot_prev, cot_next = neighbours("tm", near, near, 3 if by_corner else None)
    cot_corner = []
    if by_corner:
        straight, relayed = cot[: frames // 2], cot[frames // 2 :]
        relayed = lax.ppermute(relayed, "tm", [(3, 7), (4, 0)])
    above, below = neighbours("space", first, last)
    back_weights, back_taps = call(
        turn_weights_kernel, "turn_weights", [spatial, temporal],
        [shape((3, 3 * channels, channels), BF16), shape((3 * channels, channels), BF16)], 0, big,
    )
    conv_out, sums = call(
        conv_kernel, "conv_forward", [frames_in, above, below, spatial],
        [shape(per_px, F32), shape((frames, 2, channels), F32)],
        100 * big * channels, 8 * big, [windows], 18,
    )
    if by_corner:
        sums, straight = lax.optimization_barrier((sums, straight))
        cot_corner.append(lax.ppermute(straight, "tm", [(3, 4), (4, 3)]))
    parts = spread_sums(sums, "space")
    if by_corner:
        parts[0], relayed = lax.optimization_barrier((parts[0], relayed))
        cot_corner.append(lax.ppermute(relayed, "tm", [(7, 4), (0, 3)]))
    x_turned = call(
        turn_kernel, "turned", [frames_in, above, below], shape((3 * channels, frames * pixels), BF16),
        0, 8 * big, [pltpu.VMEM((pixels, 3 * channels), BF16)],
    )
    x_turned, *parts = lax.optimization_barrier((x_turned, *parts))
    act, normed, slope = call(
        functools.partial(act_kernel, len(parts), entries, group_size), "activation",
        [clip_frames, *parts, conv_out, gain, shift], [shape(per_px, BF16)] * 3, 10 * big, 10 * big,
    )
    act_prev, act_next = neighbours("tm", act, act)

    grad_act, cot_cat, grad_sums = call(
        functools.partial(grad_act_kernel, len(cot_corner)), "grad_activation",
        [clip_frames, dilation, cot, cot_next, cot_prev, *cot_corner, back_taps, normed, slope],
        [shape(per_px, BF16), shape((frames * pixels, 3 * channels), BF16), shape((frames, 2, channels), F32)],
        6 * big * channels, 16 * big,
    )
    grad_parts = spread_parts(grad_sums, "space")
    temporal_part = call(
        temporal_grad_kernel, "temporal_grad", [act, cot_cat],
        shape((channels, 3 * channels), F32), 6 * big * channels, 8 * big,
    )
    lanes = 3 * channels
    grad_conv, first_rows, last_rows, moved = call(
        functools.partial(norm_back_kernel, len(parts), len(grad_parts), entries, group_size), "norm_backward",
        [normed, slope, grad_act, *parts, *grad_parts],
        [shape(per_px, BF16)] + [shape((frames, 1, width, channels), BF16)] * 2
        + [shape((frames * pixels, lanes), BF16)],
        0, 12 * big,
    )
    grad_above, grad_below = neighbours("space", first_rows, last_rows)
    sums = call(
        weight_grad_kernel, "weight_grad", [x_turned, moved, temporal_part], shape((4 * channels, lanes), F32),
        18 * big * channels, 12 * big,
    )
    sums, grad_above, grad_below = lax.optimization_barrier((sums, grad_above, grad_below))
    block = 2 * channels // (chips * n)
    send, keep = call(
        hand_out_kernel, "hand_out", [sums],
        [shape((chips, n, block, lanes), BF16), shape((chips, n, block, lanes), F32)], 0, big,
    )
    def other_chip(s):
        return [(i, i ^ (2 * s)) for i in range(tm)]

    def other_plane(s):
        return [(i, i ^ s) for i in range(n)]

    other_core = [(i, i ^ 1) for i in range(tm)]
    got = lax.ppermute(send, "tm", other_core)
    own, *sends = call(
        core_sum_kernel, "core_sum", [keep, got],
        [shape((n, block, lanes), F32)] + [shape((n, block, lanes), BF16)] * (chips - 1), 0, 4 * big,
    )
    gots = [lax.ppermute(x, "tm", other_chip(s)) for s, x in enumerate(sends, 1)]

    in_grad = call(
        conv_back_kernel, "conv_backward", [grad_conv, grad_above, grad_below, cotangent, back_weights],
        shape(frames_in.shape, BF16), 18 * big * channels, 8 * big, [windows], 20,
    )
    own, in_grad, act_prev, act_next = lax.optimization_barrier((own, in_grad, act_prev, act_next))

    own, *sends = call(
        functools.partial(sum_split_kernel, chips - 1), "plane_sum", [own, *gots],
        [shape((block, lanes), F32)] + [shape((block, lanes), BF16)] * (n - 1), 0, big,
    )
    gots = [lax.ppermute(x, "space", other_plane(s)) for s, x in enumerate(sends, 1)]
    out_frames = call(
        out_kernel, "temporal_forward",
        [clip_frames, dilation, act, act_next, act_prev, temporal.reshape(3 * channels, channels), frames_in],
        shape(frames_in.shape, BF16), 6 * big * channels, 10 * big, [windows],
    )
    own, out_frames = lax.optimization_barrier((own, out_frames))
    own = call(
        functools.partial(sum_kernel, n - 1), "line_sum", [own, *gots], shape((block, lanes), BF16), 0, big
    )
    gots = [lax.ppermute(own, "space", other_plane(s)) for s in range(1, n)]
    own = call(
        functools.partial(place_kernel, "space", 0), "line_place", [own, *gots], shape((n, block, lanes), BF16), 0, big
    )
    gots = [lax.ppermute(own, "tm", other_chip(s)) for s in range(1, chips)]


    own = call(
        functools.partial(place_kernel, "tm", 1), "plane_place", [own, *gots], shape((chips, n, block, lanes), BF16), 0, big
    )
    got = lax.ppermute(own, "tm", other_core)
    spatial_grad, temporal_grad = call(
        finish_kernel, "finish", [own, got], [shape(spatial.shape, F32), shape(temporal.shape, F32)], 0, 4 * big
    )
    return (out_frames, in_grad, spatial_grad, temporal_grad)


def solution(mesh):
    tiles = P("tm", "space", None, None)
    return jax.shard_map(
        per_device,
        mesh=mesh,
        in_specs=(tiles, tiles, P(), P(), P(), P(), P(), P()),
        out_specs=(tiles, tiles, P(), P()),
        check_vma=False,
    )
```

```python
import functools

import jax
import jax.numpy as jnp
from jax import lax
from jax.experimental import pallas as pl
from jax.experimental.pallas import tpu as pltpu
from jax.sharding import PartitionSpec as P

GROUPS = 32
NORM_EPS = 1e-05
BF16 = jnp.bfloat16
F32 = jnp.float32
MIB = 2**20


def call(kernel, name, operands, out_shape, flops=0, moved=0, scratch=(), grant=14):
    vmem = pl.BlockSpec(memory_space=pltpu.VMEM)
    smem = pl.BlockSpec(memory_space=pltpu.SMEM)
    return pl.pallas_call(
        kernel,
        in_specs=[smem if x.dtype == jnp.int32 else vmem for x in operands],
        out_specs=jax.tree.map(lambda _: vmem, out_shape),
        out_shape=out_shape,
        scratch_shapes=list(scratch),
        compiler_params=pltpu.CompilerParams(vmem_limit_bytes=grant * MIB),
        cost_estimate=pl.CostEstimate(flops=int(flops), bytes_accessed=int(moved), transcendentals=0),
        name=name,
    )(*operands)


def dot(a, b):
    return jnp.dot(a, b, preferred_element_type=F32)


def dot_rows(a, b):
    return lax.dot_general(a, b, (((0,), (0,)), ((), ())), preferred_element_type=F32)


def group_total(row, group_size):
    channels = row.shape[-1]
    lane = lax.broadcasted_iota(jnp.int32, row.shape, 1)
    step = 1
    while step < group_size:
        up = pltpu.roll(row, channels - step, axis=1)
        down = pltpu.roll(row, step, axis=1)
        row = row + jnp.where((lane & step) == 0, up, down)
        step *= 2
    return row


def frame_stats(part_refs, f, entries, group_size):
    total = part_refs[0][f]
    for ref in part_refs[1:]:
        total = total + ref[f]
    return group_total(total, group_size) / entries


def mean_and_inv(part_refs, f, entries, group_size):
    both = frame_stats(part_refs, f, entries, group_size)
    mean = both[0:1]
    inv = lax.rsqrt(both[1:2] - mean * mean + NORM_EPS)
    return mean, inv


def column_sums(first, second):
    return jnp.concatenate(
        [jnp.sum(first, axis=0, keepdims=True), jnp.sum(second, axis=0, keepdims=True)], axis=0
    )


def put_windows(above, mid, below, lhs_ref, at, order):
    width, (pixels, channels) = above.shape[0], mid.shape
    first, mid_at, last = (slice(k * channels, (k + 1) * channels) for k in order)
    lhs_ref[at : at + width, first] = above
    lhs_ref[at + width : at + pixels, first] = mid[: pixels - width]
    lhs_ref[at : at + pixels, mid_at] = mid
    lhs_ref[at : at + pixels - width, last] = mid[width:]
    lhs_ref[at + pixels - width : at + pixels, last] = below


def from_left(y, width):
    col = lax.broadcasted_iota(jnp.int32, y.shape, 0) & (width - 1)
    return jnp.where(col == 0, 0.0, pltpu.roll(y, 1, axis=0))


def from_right(y, width):
    col = lax.broadcasted_iota(jnp.int32, y.shape, 0) & (width - 1)
    return jnp.where(col == width - 1, 0.0, pltpu.roll(y, y.shape[0] - 1, axis=0))


def slot_sources(clip_ref, dil_ref, local, frames):
    slot = lax.axis_index("tm") * frames + local
    start1 = clip_ref[0]
    filled = start1 + clip_ref[1]
    in_first = slot < start1
    d = jnp.where(in_first, dil_ref[0], dil_ref[1])
    low = jnp.where(in_first, 0, start1)
    high = jnp.where(in_first, start1, filled)
    used = slot < filled
    later, earlier = local + d, local - d
    later_live = used & (slot + d < high)
    earlier_live = used & (slot - d >= low)
    later_which = jnp.where(later_live, jnp.where(later < frames, 1, 2), 0)
    earlier_which = jnp.where(earlier_live, jnp.where(earlier >= 0, 1, 2), 0)
    return (later, later_which), (earlier, earlier_which), used


def gather_taps(clip_ref, dil_ref, local, own, nxt, prv, corner, cat_ref, at, up_slot):
    frames, pixels, channels = own.shape
    later, earlier, used = slot_sources(clip_ref, dil_ref, local, frames)
    me = lax.axis_index("tm")

    def put(slot, ref, index):
        cat_ref[pl.ds(at, pixels), slot * channels : (slot + 1) * channels] = ref[index]

    def clear(slot):
        cat_ref[pl.ds(at, pixels), slot * channels : (slot + 1) * channels] = jnp.zeros((pixels, channels), BF16)

    def put_from(slot, pieces, wanted, index):
        start = 0
        for ref in pieces:
            count = ref.shape[0]
            here = wanted & (index >= start) & (index < start + count)
            pl.when(here)(functools.partial(put, slot, ref, jnp.clip(index - start, 0, count - 1)))
            start += count

    for slot, (index, which), other, shift, turn in (
        (up_slot, later, nxt, -frames, 3),
        (2 - up_slot, earlier, prv, frames, 4),
    ):
        pl.when(which == 0)(functools.partial(clear, slot))
        pl.when(which == 1)(functools.partial(put, slot, own, jnp.clip(index, 0, frames - 1)))
        there = jnp.clip(index + shift, 0, frames - 1)
        beyond = which == 2
        if corner:
            put_from(slot, corner, beyond & (me == turn), there)
            beyond = beyond & (me != turn)
        put_from(slot, other, beyond, there)
    pl.when(used)(functools.partial(put, 1, own, local))
    pl.when(jnp.logical_not(used))(functools.partial(clear, 1))


def loop(count, body):
    def step(k, carry):
        body(k)
        return carry

    lax.fori_loop(0, count, step, 0)


def conv_kernel(x_ref, above_ref, below_ref, w_ref, out_ref, sums_ref, lhs_ref):
    frames, rows, width, channels = x_ref.shape
    pixels = rows * width

    def body(pair):
        for b in range(2):
            f = 2 * pair + b
            mid = x_ref[f].reshape(pixels, channels)
            put_windows(above_ref[f, 0], mid, below_ref[f, 0], lhs_ref, b * pixels, (0, 1, 2))
        lhs = lhs_ref[...]
        y = [dot(lhs, w_ref[:, j].reshape(3 * channels, channels)) for j in range(3)]
        out = y[1] + from_left(y[0], width) + from_right(y[2], width)
        for b in range(2):
            one = out[b * pixels : (b + 1) * pixels]
            out_ref[2 * pair + b] = one
            sums_ref[2 * pair + b] = column_sums(one, one * one)

    loop(frames // 2, body)


def silu_parts(normed, half_gain, half_shift):
    h = normed * half_gain + half_shift
    t = jnp.tanh(h)
    rise = 1.0 + t
    return h, rise, rise * (1.0 + h * (1.0 - t)) * half_gain


def act_kernel(n, entries, group_size, clip_ref, *refs):
    parts, refs = refs[:n], refs[n:]
    conv_ref, gain_ref, shift_ref, act_ref, early_ref, late_ref, normed_ref, slope_ref = refs
    frames, ahead = conv_ref.shape[0], early_ref.shape[0]
    first = lax.axis_index("tm") * frames
    filled = clip_ref[0] + clip_ref[1]
    half_gain, half_shift = 0.5 * gain_ref[...], 0.5 * shift_ref[...]

    def body(f):
        mean, inv = mean_and_inv(parts, f, entries, group_size)
        normed = (conv_ref[f] - mean) * inv
        h, rise, slope = silu_parts(normed, half_gain, half_shift)
        act = jnp.where(first + f < filled, h * rise, 0.0).astype(BF16)
        act_ref[f] = act

        @pl.when(f < ahead)
        def _():
            early_ref[jnp.minimum(f, ahead - 1)] = act

        @pl.when(f >= ahead)
        def _():
            late_ref[jnp.maximum(f - ahead, 0)] = act

        normed_ref[f] = normed.astype(BF16)
        slope_ref[f] = slope.astype(BF16)

    loop(frames, body)


def turn_kernel(x_ref, above_ref, below_ref, xt_ref, lhs_ref):
    frames, rows, width, channels = x_ref.shape
    pixels = rows * width

    def body(f):
        mid = x_ref[f].reshape(pixels, channels)
        put_windows(above_ref[f, 0], mid, below_ref[f, 0], lhs_ref, 0, (0, 1, 2))
        lanes = pl.ds(pl.multiple_of(f * pixels, pixels), pixels)
        for i in range(3):
            block = slice(i * channels, (i + 1) * channels)
            xt_ref[block, lanes] = lhs_ref[:, block].T

    loop(frames, body)


def turn_weights_kernel(spatial_ref, temporal_ref, back_ref, out_ref):
    channels = spatial_ref.shape[-1]
    for i in range(3):
        rows = slice(i * channels, (i + 1) * channels)
        out_ref[rows] = temporal_ref[i].T
        for j in range(3):
            back_ref[j, rows] = spatial_ref[i, j].T


def grad_act_kernel(corners, clip_ref, dil_ref, own, nxt, prv, *refs):
    corner, (tw_ref, normed_ref, slope_ref, ga_ref, cat_ref, sums_ref) = refs[:corners], refs[corners:]
    frames, pixels, _ = own.shape

    def body(pair):
        rows = pl.ds(pl.multiple_of(2 * pair * pixels, 2 * pixels), 2 * pixels)
        for b in range(2):
            at = pl.multiple_of((2 * pair + b) * pixels, pixels)
            gather_taps(clip_ref, dil_ref, 2 * pair + b, own, (nxt,), (prv,), corner, cat_ref, at, 0)
        grad_act = dot(cat_ref[rows], tw_ref[...]).astype(BF16)
        for b in range(2):
            f = 2 * pair + b
            one = grad_act[b * pixels : (b + 1) * pixels]
            ga_ref[f] = one
            gn = one.astype(F32) * slope_ref[f].astype(F32)
            sums_ref[f] = column_sums(gn, gn * normed_ref[f].astype(F32))

    loop(frames // 2, body)


def temporal_grad_kernel(act_ref, cat_ref, out_ref):
    frames, pixels, channels = act_ref.shape
    out_ref[...] = dot_rows(act_ref[...].reshape(frames * pixels, channels), cat_ref[...])


def norm_back_kernel(n, m, entries, group_size, normed_ref, slope_ref, ga_ref, *refs):
    parts, grad_parts = refs[:n], refs[n : n + m]
    g_ref, first_ref, last_ref, moved_ref = refs[n + m :]
    _, pixels, channels = normed_ref.shape
    width = first_ref.shape[2]

    def body(f):
        _, inv = mean_and_inv(parts, f, entries, group_size)
        means = frame_stats(grad_parts, f, entries, group_size)
        gn = ga_ref[f].astype(F32) * slope_ref[f].astype(F32)
        wide = inv * (gn - means[0:1] - normed_ref[f].astype(F32) * means[1:2])
        grad = wide.astype(BF16)
        g_ref[f] = grad
        first_ref[f, 0] = grad[:width]
        last_ref[f, 0] = grad[pixels - width :]
        here = pl.ds(pl.multiple_of(f * pixels, pixels), pixels)
        moved_ref[here, :channels] = from_right(wide, width).astype(BF16)
        moved_ref[here, channels : 2 * channels] = grad
        moved_ref[here, 2 * channels :] = from_left(wide, width).astype(BF16)

    loop(normed_ref.shape[0], body)


def weight_grad_kernel(xt_ref, moved_ref, temporal_ref, out_ref):
    channels = temporal_ref.shape[0]
    for j in range(3):
        lanes = slice(j * channels, (j + 1) * channels)
        out_ref[: 3 * channels, lanes] = dot(xt_ref[...], moved_ref[:, lanes])
    out_ref[3 * channels :, :] = temporal_ref[...]


def hand_out_kernel(acc_ref, send_ref, keep_ref):
    chips, depth, block, _ = keep_ref.shape
    half = chips * depth * block
    core = lax.axis_index("tm") & 1

    def hand_out(kept, sent):
        for p in range(chips):
            for z in range(depth):
                at = (p * depth + z) * block
                keep_ref[p, z] = acc_ref[kept + at : kept + at + block]
                send_ref[p, z] = acc_ref[sent + at : sent + at + block].astype(BF16)

    pl.when(core == 0)(functools.partial(hand_out, 0, half))
    pl.when(core == 1)(functools.partial(hand_out, half, 0))


def conv_back_kernel(g_ref, above_ref, below_ref, cot_ref, w_ref, out_ref, lhs_ref):
    frames, rows, width, channels = cot_ref.shape
    pixels = rows * width

    def body(pair):
        for b in range(2):
            f = 2 * pair + b
            put_windows(above_ref[f, 0], g_ref[f], below_ref[f, 0], lhs_ref, b * pixels, (2, 1, 0))
        lhs = lhs_ref[...]
        z = [dot(lhs, w_ref[j]) for j in range(3)]
        out = z[1] + from_right(z[0], width) + from_left(z[2], width)
        for b in range(2):
            one = out[b * pixels : (b + 1) * pixels].reshape(rows, width, channels)
            out_ref[2 * pair + b] = (one + cot_ref[2 * pair + b].astype(F32)).astype(BF16)

    loop(frames // 2, body)


def out_kernel(clip_ref, dil_ref, own, nxt_a, nxt_b, prv_a, prv_b, tw_ref, x_ref, out_ref, cat_ref):
    frames, rows, width, channels = x_ref.shape
    pixels = rows * width

    def body(pair):
        for b in range(2):
            gather_taps(clip_ref, dil_ref, 2 * pair + b, own, (nxt_a, nxt_b), (prv_a, prv_b), (), cat_ref, b * pixels, 2)
        temporal_out = dot(cat_ref[...], tw_ref[...]).astype(BF16).astype(F32)
        for b in range(2):
            one = temporal_out[b * pixels : (b + 1) * pixels].reshape(rows, width, channels)
            out_ref[2 * pair + b] = (x_ref[2 * pair + b].astype(F32) + one).astype(BF16)

    loop(frames // 2, body)


def core_sum_kernel(keep_ref, got_ref, own_ref, *send_refs):
    chip = lax.axis_index("tm") >> 1
    own_ref[...] = keep_ref[chip] + got_ref[chip].astype(F32)
    for s, ref in enumerate(send_refs, 1):
        ref[...] = (keep_ref[chip ^ s] + got_ref[chip ^ s].astype(F32)).astype(BF16)


def sum_kernel(count, own_ref, *refs):
    total = own_ref[...]
    for ref in refs[:count]:
        total = total + ref[...].astype(F32)
    refs[count][...] = total.astype(BF16)


def sum_split_kernel(count, own_ref, *refs):
    got, (mine_ref, *send_refs) = refs[:count], refs[count:]
    deep = lax.axis_index("space")

    def block(k):
        total = own_ref[k]
        for ref in got:
            total = total + ref[k].astype(F32)
        return total

    mine_ref[...] = block(deep)
    for s, ref in enumerate(send_refs, 1):
        ref[...] = block(deep ^ s).astype(BF16)


def place_kernel(axis, shift, *refs):
    me = lax.axis_index(axis) >> shift
    for s, ref in enumerate(refs[:-1]):
        refs[-1][me ^ s] = ref[...]


def finish_kernel(mine_ref, got_ref, spatial_ref, temporal_ref):
    chips, depth, block, _ = mine_ref.shape
    channels = spatial_ref.shape[-1]

    def write(pair):
        for c in range(2):
            for p in range(chips):
                for z in range(depth):
                    row = ((c * chips + p) * depth + z) * block
                    values = pair[c][p, z].astype(F32)
                    i, at = row // channels, row % channels
                    for k in range(3):
                        lanes = values[:, k * channels : (k + 1) * channels]
                        if i < 3:
                            spatial_ref[i, k, at : at + block] = lanes
                        else:
                            temporal_ref[k, at : at + block] = lanes

    core = lax.axis_index("tm") & 1
    pl.when(core == 0)(functools.partial(write, (mine_ref, got_ref)))
    pl.when(core == 1)(functools.partial(write, (got_ref, mine_ref)))


def neighbours(axis, low, high, but=None):
    size = lax.axis_size(axis)
    up = [(i, i + 1) for i in range(size - 1) if i != but]
    down = [(j, i) for i, j in up]
    return lax.ppermute(high, axis, up), lax.ppermute(low, axis, down)


def spread_parts(part, axis):
    size = lax.axis_size(axis)
    return [part] + [lax.ppermute(part, axis, [(i, i ^ s) for i in range(size)]) for s in range(1, size)]


def spread_sums(part, axis):
    size = lax.axis_size(axis)
    step, got = 1, None
    while step < size:
        if got is not None:
            part = part + got
        got = lax.ppermute(part, axis, [(i, i ^ step) for i in range(size)])
        step *= 2
    return [part, got]


def per_device(frames_in, cotangent, spatial, temporal, norm_gain, norm_shift, clip_frames, dilation):
    frames, rows, width, channels = frames_in.shape
    pixels = rows * width
    n, tm = lax.axis_size("space"), lax.axis_size("tm")
    chips = tm // 2
    group_size = channels // GROUPS
    entries = float(rows * n * width * group_size)
    gain, shift = norm_gain[None], norm_shift[None]
    big = frames * pixels * channels
    shape = jax.ShapeDtypeStruct
    per_px = (frames, pixels, channels)
    windows = pltpu.VMEM((2 * pixels, 3 * channels), BF16)

    cot = cotangent.reshape(per_px)
    by_corner = tm == 8
    first, last = frames_in[:, :1], frames_in[:, rows - 1 :]
    first, last, near = lax.optimization_barrier((first, last, cot))
    cot_prev, cot_next = neighbours("tm", near, near, 3 if by_corner else None)
    cot_corner = []
    if by_corner:
        straight, relayed = cot[: frames // 2], cot[frames // 2 :]
        relayed = lax.ppermute(relayed, "tm", [(3, 7), (4, 0)])
    above, below = neighbours("space", first, last)
    back_weights, back_taps = call(
        turn_weights_kernel, "turn_weights", [spatial, temporal],
        [shape((3, 3 * channels, channels), BF16), shape((3 * channels, channels), BF16)], 0, big,
    )
    conv_out, sums = call(
        conv_kernel, "conv_forward", [frames_in, above, below, spatial],
        [shape(per_px, F32), shape((frames, 2, channels), F32)],
        100 * big * channels, 8 * big, [windows], 18,
    )
    if by_corner:
        sums, straight = lax.optimization_barrier((sums, straight))
        cot_corner.append(lax.ppermute(straight, "tm", [(3, 4), (4, 3)]))
    parts = spread_sums(sums, "space")
    if by_corner:
        parts[0], relayed = lax.optimization_barrier((parts[0], relayed))
        cot_corner.append(lax.ppermute(relayed, "tm", [(7, 4), (0, 3)]))
    x_turned = call(
        turn_kernel, "turned", [frames_in, above, below], shape((3 * channels, frames * pixels), BF16),
        0, 8 * big, [pltpu.VMEM((pixels, 3 * channels), BF16)],
    )
    x_turned, *parts = lax.optimization_barrier((x_turned, *parts))
    ahead = (3 * frames) // 4
    act, act_early, act_late, normed, slope = call(
        functools.partial(act_kernel, len(parts), entries, group_size), "activation",
        [clip_frames, *parts, conv_out, gain, shift], [shape((k, pixels, channels), BF16) for k in (frames, ahead, frames - ahead, frames, frames)], 10 * big, 10 * big,
    )
    act_prev, act_next = neighbours("tm", act_early, act_early)

    grad_act, cot_cat, grad_sums = call(
        functools.partial(grad_act_kernel, len(cot_corner)), "grad_activation",
        [clip_frames, dilation, cot, cot_next, cot_prev, *cot_corner, back_taps, normed, slope],
        [shape(per_px, BF16), shape((frames * pixels, 3 * channels), BF16), shape((frames, 2, channels), F32)],
        6 * big * channels, 16 * big,
    )
    grad_parts = spread_parts(grad_sums, "space")
    temporal_part = call(
        temporal_grad_kernel, "temporal_grad", [act, cot_cat],
        shape((channels, 3 * channels), F32), 6 * big * channels, 8 * big,
    )
    lanes = 3 * channels
    grad_conv, first_rows, last_rows, moved = call(
        functools.partial(norm_back_kernel, len(parts), len(grad_parts), entries, group_size), "norm_backward",
        [normed, slope, grad_act, *parts, *grad_parts],
        [shape(per_px, BF16)] + [shape((frames, 1, width, channels), BF16)] * 2
        + [shape((frames * pixels, lanes), BF16)],
        0, 12 * big,
    )
    grad_above, grad_below = neighbours("space", first_rows, last_rows)
    sums = call(
        weight_grad_kernel, "weight_grad", [x_turned, moved, temporal_part], shape((4 * channels, lanes), F32),
        18 * big * channels, 12 * big,
    )
    sums, grad_above, grad_below = lax.optimization_barrier((sums, grad_above, grad_below))
    block = 2 * channels // (chips * n)
    send, keep = call(
        hand_out_kernel, "hand_out", [sums],
        [shape((chips, n, block, lanes), BF16), shape((chips, n, block, lanes), F32)], 0, big,
    )
    def other_chip(s):
        return [(i, i ^ (2 * s)) for i in range(tm)]

    def other_plane(s):
        return [(i, i ^ s) for i in range(n)]

    other_core = [(i, i ^ 1) for i in range(tm)]
    got = lax.ppermute(send, "tm", other_core)
    own, *sends = call(
        core_sum_kernel, "core_sum", [keep, got],
        [shape((n, block, lanes), F32)] + [shape((n, block, lanes), BF16)] * (chips - 1), 0, 4 * big,
    )
    gots = [lax.ppermute(x, "tm", other_chip(s)) for s, x in enumerate(sends, 1)]

    in_grad = call(
        conv_back_kernel, "conv_backward", [grad_conv, grad_above, grad_below, cotangent, back_weights],
        shape(frames_in.shape, BF16), 18 * big * channels, 8 * big, [windows], 20,
    )
    own, in_grad, act_prev, act_next = lax.optimization_barrier((own, in_grad, act_prev, act_next))

    own, *sends = call(
        functools.partial(sum_split_kernel, chips - 1), "plane_sum", [own, *gots],
        [shape((block, lanes), F32)] + [shape((block, lanes), BF16)] * (n - 1), 0, big,
    )
    gots = [lax.ppermute(x, "space", other_plane(s)) for s, x in enumerate(sends, 1)]
    gots[0], act_late = lax.optimization_barrier((gots[0], act_late))
    late_prev, late_next = neighbours("tm", act_late, act_late)
    own = call(
        functools.partial(sum_kernel, n - 1), "line_sum", [own, *gots], shape((block, lanes), BF16), 0, big
    )
    gots = [lax.ppermute(own, "space", other_plane(s)) for s in range(1, n)]
    own = call(
        functools.partial(place_kernel, "space", 0), "line_place", [own, *gots], shape((n, block, lanes), BF16), 0, big
    )
    gots = [lax.ppermute(own, "tm", other_chip(s)) for s in range(1, chips)]


    out_frames = call(
        out_kernel, "temporal_forward",
        [clip_frames, dilation, act, act_next, late_next, act_prev, late_prev, temporal.reshape(3 * channels, channels), frames_in],
        shape(frames_in.shape, BF16), 6 * big * channels, 10 * big, [windows],
    )
    own, out_frames = lax.optimization_barrier((own, out_frames))
    own = call(
        functools.partial(place_kernel, "tm", 1), "plane_place", [own, *gots], shape((chips, n, block, lanes), BF16), 0, big
    )
    got = lax.ppermute(own, "tm", other_core)
    spatial_grad, temporal_grad = call(
        finish_kernel, "finish", [own, got], [shape(spatial.shape, F32), shape(temporal.shape, F32)], 0, 4 * big
    )
    return (out_frames, in_grad, spatial_grad, temporal_grad)


def solution(mesh):
    tiles = P("tm", "space", None, None)
    return jax.shard_map(
        per_device,
        mesh=mesh,
        in_specs=(tiles, tiles, P(), P(), P(), P(), P(), P()),
        out_specs=(tiles, tiles, P(), P()),
        check_vma=False,
    )
```

```python
import functools

import jax
import jax.numpy as jnp
from jax import lax
from jax.experimental import pallas as pl
from jax.experimental.pallas import tpu as pltpu
from jax.sharding import PartitionSpec as P

GROUPS = 32
NORM_EPS = 1e-05
BF16 = jnp.bfloat16
F32 = jnp.float32
MIB = 2**20


def call(kernel, name, operands, out_shape, flops=0, moved=0, scratch=(), grant=14):
    vmem = pl.BlockSpec(memory_space=pltpu.VMEM)
    smem = pl.BlockSpec(memory_space=pltpu.SMEM)
    return pl.pallas_call(
        kernel,
        in_specs=[smem if x.dtype == jnp.int32 else vmem for x in operands],
        out_specs=jax.tree.map(lambda _: vmem, out_shape),
        out_shape=out_shape,
        scratch_shapes=list(scratch),
        compiler_params=pltpu.CompilerParams(vmem_limit_bytes=grant * MIB),
        cost_estimate=pl.CostEstimate(flops=int(flops), bytes_accessed=int(moved), transcendentals=0),
        name=name,
    )(*operands)


def dot(a, b):
    return jnp.dot(a, b, preferred_element_type=F32)


def dot_rows(a, b):
    return lax.dot_general(a, b, (((0,), (0,)), ((), ())), preferred_element_type=F32)


def group_total(row, group_size):
    channels = row.shape[-1]
    lane = lax.broadcasted_iota(jnp.int32, row.shape, 1)
    step = 1
    while step < group_size:
        up = pltpu.roll(row, channels - step, axis=1)
        down = pltpu.roll(row, step, axis=1)
        row = row + jnp.where((lane & step) == 0, up, down)
        step *= 2
    return row


def frame_stats(part_refs, f, entries, group_size):
    total = part_refs[0][f]
    for ref in part_refs[1:]:
        total = total + ref[f]
    return group_total(total, group_size) / entries


def mean_and_inv(part_refs, f, entries, group_size):
    both = frame_stats(part_refs, f, entries, group_size)
    mean = both[0:1]
    inv = lax.rsqrt(both[1:2] - mean * mean + NORM_EPS)
    return mean, inv


def column_sums(first, second):
    return jnp.concatenate(
        [jnp.sum(first, axis=0, keepdims=True), jnp.sum(second, axis=0, keepdims=True)], axis=0
    )


def put_windows(above, mid, below, lhs_ref, at, order):
    width, (pixels, channels) = above.shape[0], mid.shape
    first, mid_at, last = (slice(k * channels, (k + 1) * channels) for k in order)
    lhs_ref[at : at + width, first] = above
    lhs_ref[at + width : at + pixels, first] = mid[: pixels - width]
    lhs_ref[at : at + pixels, mid_at] = mid
    lhs_ref[at : at + pixels - width, last] = mid[width:]
    lhs_ref[at + pixels - width : at + pixels, last] = below


def from_left(y, width):
    col = lax.broadcasted_iota(jnp.int32, y.shape, 0) & (width - 1)
    return jnp.where(col == 0, 0.0, pltpu.roll(y, 1, axis=0))


def from_right(y, width):
    col = lax.broadcasted_iota(jnp.int32, y.shape, 0) & (width - 1)
    return jnp.where(col == width - 1, 0.0, pltpu.roll(y, y.shape[0] - 1, axis=0))


def slot_sources(clip_ref, dil_ref, local, frames):
    slot = lax.axis_index("tm") * frames + local
    start1 = clip_ref[0]
    filled = start1 + clip_ref[1]
    in_first = slot < start1
    d = jnp.where(in_first, dil_ref[0], dil_ref[1])
    low = jnp.where(in_first, 0, start1)
    high = jnp.where(in_first, start1, filled)
    used = slot < filled
    later, earlier = local + d, local - d
    later_live = used & (slot + d < high)
    earlier_live = used & (slot - d >= low)
    later_which = jnp.where(later_live, jnp.where(later < frames, 1, 2), 0)
    earlier_which = jnp.where(earlier_live, jnp.where(earlier >= 0, 1, 2), 0)
    return (later, later_which), (earlier, earlier_which), used


def gather_taps(clip_ref, dil_ref, local, own, nxt, prv, corner, cat_ref, at, up_slot):
    frames, pixels, channels = own.shape
    later, earlier, used = slot_sources(clip_ref, dil_ref, local, frames)
    me = lax.axis_index("tm")

    def put(slot, ref, index):
        cat_ref[pl.ds(at, pixels), slot * channels : (slot + 1) * channels] = ref[index]

    def clear(slot):
        cat_ref[pl.ds(at, pixels), slot * channels : (slot + 1) * channels] = jnp.zeros((pixels, channels), BF16)

    def put_from(slot, pieces, wanted, index):
        start = 0
        for ref in pieces:
            count = ref.shape[0]
            here = wanted & (index >= start) & (index < start + count)
            pl.when(here)(functools.partial(put, slot, ref, jnp.clip(index - start, 0, count - 1)))
            start += count

    for slot, (index, which), other, shift, turn in (
        (up_slot, later, nxt, -frames, 3),
        (2 - up_slot, earlier, prv, frames, 4),
    ):
        pl.when(which == 0)(functools.partial(clear, slot))
        pl.when(which == 1)(functools.partial(put, slot, own, jnp.clip(index, 0, frames - 1)))
        there = jnp.clip(index + shift, 0, frames - 1)
        beyond = which == 2
        if corner:
            put_from(slot, corner, beyond & (me == turn), there)
            beyond = beyond & (me != turn)
        put_from(slot, other, beyond, there)
    pl.when(used)(functools.partial(put, 1, own, local))
    pl.when(jnp.logical_not(used))(functools.partial(clear, 1))


def loop(count, body):
    def step(k, carry):
        body(k)
        return carry

    lax.fori_loop(0, count, step, 0)


def conv_kernel(x_ref, above_ref, below_ref, w_ref, out_ref, sums_ref, lhs_ref):
    frames, rows, width, channels = x_ref.shape
    pixels = rows * width

    def body(pair):
        for b in range(2):
            f = 2 * pair + b
            mid = x_ref[f].reshape(pixels, channels)
            put_windows(above_ref[f, 0], mid, below_ref[f, 0], lhs_ref, b * pixels, (0, 1, 2))
        lhs = lhs_ref[...]
        y = [dot(lhs, w_ref[:, j].reshape(3 * channels, channels)) for j in range(3)]
        out = y[1] + from_left(y[0], width) + from_right(y[2], width)
        for b in range(2):
            one = out[b * pixels : (b + 1) * pixels]
            out_ref[2 * pair + b] = one
            sums_ref[2 * pair + b] = column_sums(one, one * one)

    loop(frames // 2, body)


def silu_parts(normed, half_gain, half_shift):
    h = normed * half_gain + half_shift
    t = jnp.tanh(h)
    rise = 1.0 + t
    return h, rise, rise * (1.0 + h * (1.0 - t)) * half_gain


def act_kernel(n, entries, group_size, clip_ref, *refs):
    parts, refs = refs[:n], refs[n:]
    conv_ref, gain_ref, shift_ref, act_ref, early_ref, late_ref, normed_ref, slope_ref = refs
    frames, ahead = conv_ref.shape[0], early_ref.shape[0]
    first = lax.axis_index("tm") * frames
    filled = clip_ref[0] + clip_ref[1]
    half_gain, half_shift = 0.5 * gain_ref[...], 0.5 * shift_ref[...]

    def body(f):
        mean, inv = mean_and_inv(parts, f, entries, group_size)
        normed = (conv_ref[f] - mean) * inv
        h, rise, slope = silu_parts(normed, half_gain, half_shift)
        act = jnp.where(first + f < filled, h * rise, 0.0).astype(BF16)
        act_ref[f] = act

        @pl.when(f < ahead)
        def _():
            early_ref[jnp.minimum(f, ahead - 1)] = act

        @pl.when(f >= ahead)
        def _():
            late_ref[jnp.maximum(f - ahead, 0)] = act

        normed_ref[f] = normed.astype(BF16)
        slope_ref[f] = slope.astype(BF16)

    loop(frames, body)


def turn_kernel(x_ref, above_ref, below_ref, xt_ref, lhs_ref):
    frames, rows, width, channels = x_ref.shape
    pixels = rows * width

    def body(f):
        mid = x_ref[f].reshape(pixels, channels)
        put_windows(above_ref[f, 0], mid, below_ref[f, 0], lhs_ref, 0, (0, 1, 2))
        lanes = pl.ds(pl.multiple_of(f * pixels, pixels), pixels)
        for i in range(3):
            block = slice(i * channels, (i + 1) * channels)
            xt_ref[block, lanes] = lhs_ref[:, block].T

    loop(frames, body)


def turn_weights_kernel(spatial_ref, temporal_ref, back_ref, out_ref):
    channels = spatial_ref.shape[-1]
    for i in range(3):
        rows = slice(i * channels, (i + 1) * channels)
        out_ref[rows] = temporal_ref[i].T
        for j in range(3):
            back_ref[j, rows] = spatial_ref[i, j].T


def grad_act_kernel(corners, clip_ref, dil_ref, own, nxt, prv, *refs):
    corner, (tw_ref, normed_ref, slope_ref, ga_ref, cat_ref, sums_ref) = refs[:corners], refs[corners:]
    frames, pixels, _ = own.shape

    def body(pair):
        rows = pl.ds(pl.multiple_of(2 * pair * pixels, 2 * pixels), 2 * pixels)
        for b in range(2):
            at = pl.multiple_of((2 * pair + b) * pixels, pixels)
            gather_taps(clip_ref, dil_ref, 2 * pair + b, own, (nxt,), (prv,), corner, cat_ref, at, 0)
        grad_act = dot(cat_ref[rows], tw_ref[...]).astype(BF16)
        for b in range(2):
            f = 2 * pair + b
            one = grad_act[b * pixels : (b + 1) * pixels]
            ga_ref[f] = one
            gn = one.astype(F32) * slope_ref[f].astype(F32)
            sums_ref[f] = column_sums(gn, gn * normed_ref[f].astype(F32))

    loop(frames // 2, body)


def temporal_grad_kernel(act_ref, cat_ref, out_ref):
    frames, pixels, channels = act_ref.shape
    out_ref[...] = dot_rows(act_ref[...].reshape(frames * pixels, channels), cat_ref[...])


def norm_back_kernel(n, m, entries, group_size, normed_ref, slope_ref, ga_ref, *refs):
    parts, grad_parts = refs[:n], refs[n : n + m]
    g_ref, first_ref, last_ref, moved_ref = refs[n + m :]
    _, pixels, channels = normed_ref.shape
    width = first_ref.shape[2]

    def body(f):
        _, inv = mean_and_inv(parts, f, entries, group_size)
        means = frame_stats(grad_parts, f, entries, group_size)
        gn = ga_ref[f].astype(F32) * slope_ref[f].astype(F32)
        wide = inv * (gn - means[0:1] - normed_ref[f].astype(F32) * means[1:2])
        grad = wide.astype(BF16)
        g_ref[f] = grad
        first_ref[f, 0] = grad[:width]
        last_ref[f, 0] = grad[pixels - width :]
        here = pl.ds(pl.multiple_of(f * pixels, pixels), pixels)
        moved_ref[here, :channels] = from_right(wide, width).astype(BF16)
        moved_ref[here, channels : 2 * channels] = grad
        moved_ref[here, 2 * channels :] = from_left(wide, width).astype(BF16)

    loop(normed_ref.shape[0], body)


def weight_grad_kernel(xt_ref, moved_ref, temporal_ref, out_ref):
    channels = temporal_ref.shape[0]
    for j in range(3):
        lanes = slice(j * channels, (j + 1) * channels)
        out_ref[: 3 * channels, lanes] = dot(xt_ref[...], moved_ref[:, lanes])
    out_ref[3 * channels :, :] = temporal_ref[...]


def hand_out_kernel(acc_ref, send_ref, keep_ref):
    chips, depth, block, _ = keep_ref.shape
    half = chips * depth * block
    core = lax.axis_index("tm") & 1

    def hand_out(kept, sent):
        for p in range(chips):
            for z in range(depth):
                at = (p * depth + z) * block
                keep_ref[p, z] = acc_ref[kept + at : kept + at + block]
                send_ref[p, z] = acc_ref[sent + at : sent + at + block].astype(BF16)

    pl.when(core == 0)(functools.partial(hand_out, 0, half))
    pl.when(core == 1)(functools.partial(hand_out, half, 0))


def conv_back_kernel(g_ref, above_ref, below_ref, cot_ref, w_ref, out_ref, lhs_ref):
    frames, rows, width, channels = cot_ref.shape
    pixels = rows * width

    def body(pair):
        for b in range(2):
            f = 2 * pair + b
            put_windows(above_ref[f, 0], g_ref[f], below_ref[f, 0], lhs_ref, b * pixels, (2, 1, 0))
        lhs = lhs_ref[...]
        z = [dot(lhs, w_ref[j]) for j in range(3)]
        out = z[1] + from_right(z[0], width) + from_left(z[2], width)
        for b in range(2):
            one = out[b * pixels : (b + 1) * pixels].reshape(rows, width, channels)
            out_ref[2 * pair + b] = (one + cot_ref[2 * pair + b].astype(F32)).astype(BF16)

    loop(frames // 2, body)


def out_kernel(clip_ref, dil_ref, own, nxt_a, nxt_b, prv_a, prv_b, tw_ref, x_ref, out_ref, cat_ref):
    frames, rows, width, channels = x_ref.shape
    pixels = rows * width

    def body(pair):
        for b in range(2):
            gather_taps(clip_ref, dil_ref, 2 * pair + b, own, (nxt_a, nxt_b), (prv_a, prv_b), (), cat_ref, b * pixels, 2)
        temporal_out = dot(cat_ref[...], tw_ref[...]).astype(BF16).astype(F32)
        for b in range(2):
            one = temporal_out[b * pixels : (b + 1) * pixels].reshape(rows, width, channels)
            out_ref[2 * pair + b] = (x_ref[2 * pair + b].astype(F32) + one).astype(BF16)

    loop(frames // 2, body)


def core_sum_kernel(keep_ref, got_ref, own_ref, *send_refs):
    chip = lax.axis_index("tm") >> 1
    own_ref[...] = keep_ref[chip] + got_ref[chip].astype(F32)
    for s, ref in enumerate(send_refs, 1):
        ref[...] = (keep_ref[chip ^ s] + got_ref[chip ^ s].astype(F32)).astype(BF16)


def sum_kernel(count, own_ref, *refs):
    total = own_ref[...]
    for ref in refs[:count]:
        total = total + ref[...].astype(F32)
    refs[count][...] = total.astype(BF16)


def sum_split_kernel(count, own_ref, *refs):
    got, (mine_ref, *send_refs) = refs[:count], refs[count:]
    deep = lax.axis_index("space")

    def block(k):
        total = own_ref[k]
        for ref in got:
            total = total + ref[k].astype(F32)
        return total

    mine_ref[...] = block(deep)
    for s, ref in enumerate(send_refs, 1):
        ref[...] = block(deep ^ s).astype(BF16)


def place_kernel(axis, shift, *refs):
    me = lax.axis_index(axis) >> shift
    for s, ref in enumerate(refs[:-1]):
        refs[-1][me ^ s] = ref[...]


def finish_kernel(mine_ref, got_ref, spatial_ref, temporal_ref):
    chips, depth, block, _ = mine_ref.shape
    channels = spatial_ref.shape[-1]

    def write(pair):
        for c in range(2):
            for p in range(chips):
                for z in range(depth):
                    row = ((c * chips + p) * depth + z) * block
                    values = pair[c][p, z].astype(F32)
                    i, at = row // channels, row % channels
                    for k in range(3):
                        lanes = values[:, k * channels : (k + 1) * channels]
                        if i < 3:
                            spatial_ref[i, k, at : at + block] = lanes
                        else:
                            temporal_ref[k, at : at + block] = lanes

    core = lax.axis_index("tm") & 1
    pl.when(core == 0)(functools.partial(write, (mine_ref, got_ref)))
    pl.when(core == 1)(functools.partial(write, (got_ref, mine_ref)))


def neighbours(axis, low, high, but=None):
    size = lax.axis_size(axis)
    up = [(i, i + 1) for i in range(size - 1) if i != but]
    down = [(j, i) for i, j in up]
    return lax.ppermute(high, axis, up), lax.ppermute(low, axis, down)


def spread_parts(part, axis):
    size = lax.axis_size(axis)
    return [part] + [lax.ppermute(part, axis, [(i, i ^ s) for i in range(size)]) for s in range(1, size)]


def spread_sums(part, axis):
    size = lax.axis_size(axis)
    step, got = 1, None
    while step < size:
        if got is not None:
            part = part + got
        got = lax.ppermute(part, axis, [(i, i ^ step) for i in range(size)])
        step *= 2
    return [part, got]


def per_device(frames_in, cotangent, spatial, temporal, norm_gain, norm_shift, clip_frames, dilation):
    frames, rows, width, channels = frames_in.shape
    pixels = rows * width
    n, tm = lax.axis_size("space"), lax.axis_size("tm")
    chips = tm // 2
    group_size = channels // GROUPS
    entries = float(rows * n * width * group_size)
    gain, shift = norm_gain[None], norm_shift[None]
    big = frames * pixels * channels
    shape = jax.ShapeDtypeStruct
    per_px = (frames, pixels, channels)
    windows = pltpu.VMEM((2 * pixels, 3 * channels), BF16)

    cot = cotangent.reshape(per_px)
    by_corner = tm == 8
    first, last = frames_in[:, :1], frames_in[:, rows - 1 :]
    first, last, near = lax.optimization_barrier((first, last, cot))
    cot_prev, cot_next = neighbours("tm", near, near, 3 if by_corner else None)
    cot_corner = []
    if by_corner:
        straight, relayed = cot[: frames // 2], cot[frames // 2 :]
        relayed = lax.ppermute(relayed, "tm", [(3, 7), (4, 0)])
    above, below = neighbours("space", first, last)
    back_weights, back_taps = call(
        turn_weights_kernel, "turn_weights", [spatial, temporal],
        [shape((3, 3 * channels, channels), BF16), shape((3 * channels, channels), BF16)], 0, big,
    )
    conv_out, sums = call(
        conv_kernel, "conv_forward", [frames_in, above, below, spatial],
        [shape(per_px, F32), shape((frames, 2, channels), F32)],
        100 * big * channels, 8 * big, [windows], 18,
    )
    if by_corner:
        sums, straight = lax.optimization_barrier((sums, straight))
        cot_corner.append(lax.ppermute(straight, "tm", [(3, 4), (4, 3)]))
    parts = spread_sums(sums, "space")
    if by_corner:
        parts[0], relayed = lax.optimization_barrier((parts[0], relayed))
        cot_corner.append(lax.ppermute(relayed, "tm", [(7, 4), (0, 3)]))
    x_turned = call(
        turn_kernel, "turned", [frames_in, above, below], shape((3 * channels, frames * pixels), BF16),
        0, 8 * big, [pltpu.VMEM((pixels, 3 * channels), BF16)],
    )
    x_turned, *parts = lax.optimization_barrier((x_turned, *parts))
    ahead = (3 * frames) // 4
    act, act_early, act_late, normed, slope = call(
        functools.partial(act_kernel, len(parts), entries, group_size), "activation",
        [clip_frames, *parts, conv_out, gain, shift], [shape((k, pixels, channels), BF16) for k in (frames, ahead, frames - ahead, frames, frames)], 10 * big, 10 * big,
    )
    act_prev, act_next = neighbours("tm", act_early, act_early)

    grad_act, cot_cat, grad_sums = call(
        functools.partial(grad_act_kernel, len(cot_corner)), "grad_activation",
        [clip_frames, dilation, cot, cot_next, cot_prev, *cot_corner, back_taps, normed, slope],
        [shape(per_px, BF16), shape((frames * pixels, 3 * channels), BF16), shape((frames, 2, channels), F32)],
        6 * big * channels, 16 * big,
    )
    grad_parts = spread_parts(grad_sums, "space")
    temporal_part = call(
        temporal_grad_kernel, "temporal_grad", [act, cot_cat],
        shape((channels, 3 * channels), F32), 6 * big * channels, 8 * big,
    )
    lanes = 3 * channels
    grad_conv, first_rows, last_rows, moved = call(
        functools.partial(norm_back_kernel, len(parts), len(grad_parts), entries, group_size), "norm_backward",
        [normed, slope, grad_act, *parts, *grad_parts],
        [shape(per_px, BF16)] + [shape((frames, 1, width, channels), BF16)] * 2
        + [shape((frames * pixels, lanes), BF16)],
        0, 12 * big,
    )
    grad_above, grad_below = neighbours("space", first_rows, last_rows)
    sums = call(
        weight_grad_kernel, "weight_grad", [x_turned, moved, temporal_part], shape((4 * channels, lanes), F32),
        18 * big * channels, 12 * big,
    )
    sums, grad_above, grad_below = lax.optimization_barrier((sums, grad_above, grad_below))
    block = 2 * channels // (chips * n)
    send, keep = call(
        hand_out_kernel, "hand_out", [sums],
        [shape((chips, n, block, lanes), BF16), shape((chips, n, block, lanes), F32)], 0, big,
    )
    def other_chip(s):
        return [(i, i ^ (2 * s)) for i in range(tm)]

    def other_plane(s):
        return [(i, i ^ s) for i in range(n)]

    other_core = [(i, i ^ 1) for i in range(tm)]
    got = lax.ppermute(send, "tm", other_core)
    own, *sends = call(
        core_sum_kernel, "core_sum", [keep, got],
        [shape((n, block, lanes), F32)] + [shape((n, block, lanes), BF16)] * (chips - 1), 0, 4 * big,
    )
    gots = [lax.ppermute(x, "tm", other_chip(s)) for s, x in enumerate(sends, 1)]

    in_grad = call(
        conv_back_kernel, "conv_backward", [grad_conv, grad_above, grad_below, cotangent, back_weights],
        shape(frames_in.shape, BF16), 18 * big * channels, 8 * big, [windows], 20,
    )
    own, in_grad, act_prev, act_next = lax.optimization_barrier((own, in_grad, act_prev, act_next))

    own, *sends = call(
        functools.partial(sum_split_kernel, chips - 1), "plane_sum", [own, *gots],
        [shape((block, lanes), F32)] + [shape((block, lanes), BF16)] * (n - 1), 0, big,
    )
    gots = [lax.ppermute(x, "space", other_plane(s)) for s, x in enumerate(sends, 1)]
    own, act_late = lax.optimization_barrier((own, act_late))
    late_prev, late_next = neighbours("tm", act_late, act_late)
    own = call(
        functools.partial(sum_kernel, n - 1), "line_sum", [own, *gots], shape((block, lanes), BF16), 0, big
    )
    gots = [lax.ppermute(own, "space", other_plane(s)) for s in range(1, n)]
    own = call(
        functools.partial(place_kernel, "space", 0), "line_place", [own, *gots], shape((n, block, lanes), BF16), 0, big
    )
    gots = [lax.ppermute(own, "tm", other_chip(s)) for s in range(1, chips)]


    out_frames = call(
        out_kernel, "temporal_forward",
        [clip_frames, dilation, act, act_next, late_next, act_prev, late_prev, temporal.reshape(3 * channels, channels), frames_in],
        shape(frames_in.shape, BF16), 6 * big * channels, 10 * big, [windows],
    )
    own, out_frames = lax.optimization_barrier((own, out_frames))
    own = call(
        functools.partial(place_kernel, "tm", 1), "plane_place", [own, *gots], shape((chips, n, block, lanes), BF16), 0, big
    )
    got = lax.ppermute(own, "tm", other_core)
    spatial_grad, temporal_grad = call(
        finish_kernel, "finish", [own, got], [shape(spatial.shape, F32), shape(temporal.shape, F32)], 0, 4 * big
    )
    return (out_frames, in_grad, spatial_grad, temporal_grad)


def solution(mesh):
    tiles = P("tm", "space", None, None)
    return jax.shard_map(
        per_device,
        mesh=mesh,
        in_specs=(tiles, tiles, P(), P(), P(), P(), P(), P()),
        out_specs=(tiles, tiles, P(), P()),
        check_vma=False,
    )
```

```python
import functools

import jax
import jax.numpy as jnp
from jax import lax
from jax.experimental import pallas as pl
from jax.experimental.pallas import tpu as pltpu
from jax.sharding import PartitionSpec as P

GROUPS = 32
NORM_EPS = 1e-05
BF16 = jnp.bfloat16
F32 = jnp.float32
MIB = 2**20


def call(kernel, name, operands, out_shape, flops=0, moved=0, scratch=(), grant=14):
    vmem = pl.BlockSpec(memory_space=pltpu.VMEM)
    smem = pl.BlockSpec(memory_space=pltpu.SMEM)
    return pl.pallas_call(
        kernel,
        in_specs=[smem if x.dtype == jnp.int32 else vmem for x in operands],
        out_specs=jax.tree.map(lambda _: vmem, out_shape),
        out_shape=out_shape,
        scratch_shapes=list(scratch),
        compiler_params=pltpu.CompilerParams(vmem_limit_bytes=grant * MIB),
        cost_estimate=pl.CostEstimate(flops=int(flops), bytes_accessed=int(moved), transcendentals=0),
        name=name,
    )(*operands)


def dot(a, b):
    return jnp.dot(a, b, preferred_element_type=F32)


def dot_rows(a, b):
    return lax.dot_general(a, b, (((0,), (0,)), ((), ())), preferred_element_type=F32)


def group_total(row, group_size):
    channels = row.shape[-1]
    lane = lax.broadcasted_iota(jnp.int32, row.shape, 1)
    step = 1
    while step < group_size:
        up = pltpu.roll(row, channels - step, axis=1)
        down = pltpu.roll(row, step, axis=1)
        row = row + jnp.where((lane & step) == 0, up, down)
        step *= 2
    return row


def frame_stats(part_refs, f, entries, group_size):
    total = part_refs[0][f]
    for ref in part_refs[1:]:
        total = total + ref[f]
    return group_total(total, group_size) / entries


def mean_and_inv(part_refs, f, entries, group_size):
    both = frame_stats(part_refs, f, entries, group_size)
    mean = both[0:1]
    inv = lax.rsqrt(both[1:2] - mean * mean + NORM_EPS)
    return mean, inv


def column_sums(first, second):
    return jnp.concatenate(
        [jnp.sum(first, axis=0, keepdims=True), jnp.sum(second, axis=0, keepdims=True)], axis=0
    )


def put_windows(above, mid, below, lhs_ref, at, order):
    width, (pixels, channels) = above.shape[0], mid.shape
    first, mid_at, last = (slice(k * channels, (k + 1) * channels) for k in order)
    lhs_ref[at : at + width, first] = above
    lhs_ref[at + width : at + pixels, first] = mid[: pixels - width]
    lhs_ref[at : at + pixels, mid_at] = mid
    lhs_ref[at : at + pixels - width, last] = mid[width:]
    lhs_ref[at + pixels - width : at + pixels, last] = below


def from_left(y, width):
    col = lax.broadcasted_iota(jnp.int32, y.shape, 0) & (width - 1)
    return jnp.where(col == 0, 0.0, pltpu.roll(y, 1, axis=0))


def from_right(y, width):
    col = lax.broadcasted_iota(jnp.int32, y.shape, 0) & (width - 1)
    return jnp.where(col == width - 1, 0.0, pltpu.roll(y, y.shape[0] - 1, axis=0))


def slot_sources(clip_ref, dil_ref, local, frames):
    slot = lax.axis_index("tm") * frames + local
    start1 = clip_ref[0]
    filled = start1 + clip_ref[1]
    in_first = slot < start1
    d = jnp.where(in_first, dil_ref[0], dil_ref[1])
    low = jnp.where(in_first, 0, start1)
    high = jnp.where(in_first, start1, filled)
    used = slot < filled
    later, earlier = local + d, local - d
    later_live = used & (slot + d < high)
    earlier_live = used & (slot - d >= low)
    later_which = jnp.where(later_live, jnp.where(later < frames, 1, 2), 0)
    earlier_which = jnp.where(earlier_live, jnp.where(earlier >= 0, 1, 2), 0)
    return (later, later_which), (earlier, earlier_which), used


def gather_taps(clip_ref, dil_ref, local, own, nxt, prv, corner, cat_ref, at, up_slot):
    frames, pixels, channels = own.shape
    later, earlier, used = slot_sources(clip_ref, dil_ref, local, frames)
    me = lax.axis_index("tm")

    def put(slot, ref, index):
        cat_ref[pl.ds(at, pixels), slot * channels : (slot + 1) * channels] = ref[index]

    def clear(slot):
        cat_ref[pl.ds(at, pixels), slot * channels : (slot + 1) * channels] = jnp.zeros((pixels, channels), BF16)

    def put_from(slot, pieces, wanted, index):
        start = 0
        for ref in pieces:
            count = ref.shape[0]
            here = wanted & (index >= start) & (index < start + count)
            pl.when(here)(functools.partial(put, slot, ref, jnp.clip(index - start, 0, count - 1)))
            start += count

    for slot, (index, which), other, shift, turn in (
        (up_slot, later, nxt, -frames, 3),
        (2 - up_slot, earlier, prv, frames, 4),
    ):
        pl.when(which == 0)(functools.partial(clear, slot))
        pl.when(which == 1)(functools.partial(put, slot, own, jnp.clip(index, 0, frames - 1)))
        there = jnp.clip(index + shift, 0, frames - 1)
        beyond = which == 2
        if corner:
            put_from(slot, corner, beyond & (me == turn), there)
            beyond = beyond & (me != turn)
        put_from(slot, other, beyond, there)
    pl.when(used)(functools.partial(put, 1, own, local))
    pl.when(jnp.logical_not(used))(functools.partial(clear, 1))


def loop(count, body):
    def step(k, carry):
        body(k)
        return carry

    lax.fori_loop(0, count, step, 0)


def conv_kernel(x_ref, above_ref, below_ref, w_ref, out_ref, sums_ref, lhs_ref):
    frames, rows, width, channels = x_ref.shape
    pixels = rows * width

    def body(pair):
        for b in range(2):
            f = 2 * pair + b
            mid = x_ref[f].reshape(pixels, channels)
            put_windows(above_ref[f, 0], mid, below_ref[f, 0], lhs_ref, b * pixels, (0, 1, 2))
        lhs = lhs_ref[...]
        y = [dot(lhs, w_ref[:, j].reshape(3 * channels, channels)) for j in range(3)]
        out = y[1] + from_left(y[0], width) + from_right(y[2], width)
        for b in range(2):
            one = out[b * pixels : (b + 1) * pixels]
            out_ref[2 * pair + b] = one
            sums_ref[2 * pair + b] = column_sums(one, one * one)

    loop(frames // 2, body)


def silu_parts(normed, half_gain, half_shift):
    h = normed * half_gain + half_shift
    t = jnp.tanh(h)
    rise = 1.0 + t
    return h, rise, rise * (1.0 + h * (1.0 - t)) * half_gain


def act_kernel(n, entries, group_size, clip_ref, *refs):
    parts, refs = refs[:n], refs[n:]
    conv_ref, gain_ref, shift_ref, act_ref, early_ref, late_ref, normed_ref, slope_ref = refs
    frames, ahead = conv_ref.shape[0], early_ref.shape[0]
    first = lax.axis_index("tm") * frames
    filled = clip_ref[0] + clip_ref[1]
    half_gain, half_shift = 0.5 * gain_ref[...], 0.5 * shift_ref[...]

    def body(f):
        mean, inv = mean_and_inv(parts, f, entries, group_size)
        normed = (conv_ref[f] - mean) * inv
        h, rise, slope = silu_parts(normed, half_gain, half_shift)
        act = jnp.where(first + f < filled, h * rise, 0.0).astype(BF16)
        act_ref[f] = act

        @pl.when(f < ahead)
        def _():
            early_ref[jnp.minimum(f, ahead - 1)] = act

        @pl.when(f >= ahead)
        def _():
            late_ref[jnp.maximum(f - ahead, 0)] = act

        normed_ref[f] = normed.astype(BF16)
        slope_ref[f] = slope.astype(BF16)

    loop(frames, body)


def turn_kernel(x_ref, above_ref, below_ref, xt_ref, lhs_ref):
    frames, rows, width, channels = x_ref.shape
    pixels = rows * width

    def body(f):
        mid = x_ref[f].reshape(pixels, channels)
        put_windows(above_ref[f, 0], mid, below_ref[f, 0], lhs_ref, 0, (0, 1, 2))
        lanes = pl.ds(pl.multiple_of(f * pixels, pixels), pixels)
        for i in range(3):
            block = slice(i * channels, (i + 1) * channels)
            xt_ref[block, lanes] = lhs_ref[:, block].T

    loop(frames, body)


def turn_weights_kernel(spatial_ref, temporal_ref, back_ref, out_ref):
    channels = spatial_ref.shape[-1]
    for i in range(3):
        rows = slice(i * channels, (i + 1) * channels)
        out_ref[rows] = temporal_ref[i].T
        for j in range(3):
            back_ref[j, rows] = spatial_ref[i, j].T


def grad_act_kernel(corners, clip_ref, dil_ref, own, nxt, prv, *refs):
    corner, (tw_ref, normed_ref, slope_ref, ga_ref, cat_ref, sums_ref) = refs[:corners], refs[corners:]
    frames, pixels, _ = own.shape

    def body(pair):
        rows = pl.ds(pl.multiple_of(2 * pair * pixels, 2 * pixels), 2 * pixels)
        for b in range(2):
            at = pl.multiple_of((2 * pair + b) * pixels, pixels)
            gather_taps(clip_ref, dil_ref, 2 * pair + b, own, (nxt,), (prv,), corner, cat_ref, at, 0)
        grad_act = dot(cat_ref[rows], tw_ref[...]).astype(BF16)
        for b in range(2):
            f = 2 * pair + b
            one = grad_act[b * pixels : (b + 1) * pixels]
            ga_ref[f] = one
            gn = one.astype(F32) * slope_ref[f].astype(F32)
            sums_ref[f] = column_sums(gn, gn * normed_ref[f].astype(F32))

    loop(frames // 2, body)


def temporal_grad_kernel(act_ref, cat_ref, out_ref):
    frames, pixels, channels = act_ref.shape
    out_ref[...] = dot_rows(act_ref[...].reshape(frames * pixels, channels), cat_ref[...])


def norm_back_kernel(n, m, entries, group_size, normed_ref, slope_ref, ga_ref, *refs):
    parts, grad_parts = refs[:n], refs[n : n + m]
    g_ref, first_ref, last_ref, moved_ref = refs[n + m :]
    _, pixels, channels = normed_ref.shape
    width = first_ref.shape[2]

    def body(f):
        _, inv = mean_and_inv(parts, f, entries, group_size)
        means = frame_stats(grad_parts, f, entries, group_size)
        gn = ga_ref[f].astype(F32) * slope_ref[f].astype(F32)
        wide = inv * (gn - means[0:1] - normed_ref[f].astype(F32) * means[1:2])
        grad = wide.astype(BF16)
        g_ref[f] = grad
        first_ref[f, 0] = grad[:width]
        last_ref[f, 0] = grad[pixels - width :]
        here = pl.ds(pl.multiple_of(f * pixels, pixels), pixels)
        moved_ref[here, :channels] = from_right(wide, width).astype(BF16)
        moved_ref[here, channels : 2 * channels] = grad
        moved_ref[here, 2 * channels :] = from_left(wide, width).astype(BF16)

    loop(normed_ref.shape[0], body)


def weight_grad_kernel(xt_ref, moved_ref, temporal_ref, out_ref):
    channels = temporal_ref.shape[0]
    for j in range(3):
        lanes = slice(j * channels, (j + 1) * channels)
        out_ref[: 3 * channels, lanes] = dot(xt_ref[...], moved_ref[:, lanes])
    out_ref[3 * channels :, :] = temporal_ref[...]


def hand_out_kernel(acc_ref, send_ref, keep_ref):
    chips, depth, block, _ = keep_ref.shape
    half = chips * depth * block
    core = lax.axis_index("tm") & 1

    def hand_out(kept, sent):
        for p in range(chips):
            for z in range(depth):
                at = (p * depth + z) * block
                keep_ref[p, z] = acc_ref[kept + at : kept + at + block]
                send_ref[p, z] = acc_ref[sent + at : sent + at + block].astype(BF16)

    pl.when(core == 0)(functools.partial(hand_out, 0, half))
    pl.when(core == 1)(functools.partial(hand_out, half, 0))


def conv_back_kernel(g_ref, above_ref, below_ref, cot_ref, w_ref, out_ref, lhs_ref):
    frames, rows, width, channels = cot_ref.shape
    pixels = rows * width

    def body(pair):
        for b in range(2):
            f = 2 * pair + b
            put_windows(above_ref[f, 0], g_ref[f], below_ref[f, 0], lhs_ref, b * pixels, (2, 1, 0))
        lhs = lhs_ref[...]
        z = [dot(lhs, w_ref[j]) for j in range(3)]
        out = z[1] + from_right(z[0], width) + from_left(z[2], width)
        for b in range(2):
            one = out[b * pixels : (b + 1) * pixels].reshape(rows, width, channels)
            out_ref[2 * pair + b] = (one + cot_ref[2 * pair + b].astype(F32)).astype(BF16)

    loop(frames // 2, body)


def out_kernel(clip_ref, dil_ref, own, nxt_a, nxt_b, prv_a, prv_b, tw_ref, x_ref, out_ref, cat_ref):
    frames, rows, width, channels = x_ref.shape
    pixels = rows * width

    def body(pair):
        for b in range(2):
            gather_taps(clip_ref, dil_ref, 2 * pair + b, own, (nxt_a, nxt_b), (prv_a, prv_b), (), cat_ref, b * pixels, 2)
        temporal_out = dot(cat_ref[...], tw_ref[...]).astype(BF16).astype(F32)
        for b in range(2):
            one = temporal_out[b * pixels : (b + 1) * pixels].reshape(rows, width, channels)
            out_ref[2 * pair + b] = (x_ref[2 * pair + b].astype(F32) + one).astype(BF16)

    loop(frames // 2, body)


def core_sum_kernel(keep_ref, got_ref, own_ref, *send_refs):
    chip = lax.axis_index("tm") >> 1
    own_ref[...] = keep_ref[chip] + got_ref[chip].astype(F32)
    for s, ref in enumerate(send_refs, 1):
        ref[...] = (keep_ref[chip ^ s] + got_ref[chip ^ s].astype(F32)).astype(BF16)


def sum_kernel(count, own_ref, *refs):
    total = own_ref[...]
    for ref in refs[:count]:
        total = total + ref[...].astype(F32)
    refs[count][...] = total.astype(BF16)


def sum_split_kernel(count, own_ref, *refs):
    got, (mine_ref, *send_refs) = refs[:count], refs[count:]
    deep = lax.axis_index("space")

    def block(k):
        total = own_ref[k]
        for ref in got:
            total = total + ref[k].astype(F32)
        return total

    mine_ref[...] = block(deep)
    for s, ref in enumerate(send_refs, 1):
        ref[...] = block(deep ^ s).astype(BF16)


def place_kernel(axis, shift, *refs):
    me = lax.axis_index(axis) >> shift
    for s, ref in enumerate(refs[:-1]):
        refs[-1][me ^ s] = ref[...]


def finish_kernel(mine_ref, got_ref, spatial_ref, temporal_ref):
    chips, depth, block, _ = mine_ref.shape
    channels = spatial_ref.shape[-1]

    def write(pair):
        for c in range(2):
            for p in range(chips):
                for z in range(depth):
                    row = ((c * chips + p) * depth + z) * block
                    values = pair[c][p, z].astype(F32)
                    i, at = row // channels, row % channels
                    for k in range(3):
                        lanes = values[:, k * channels : (k + 1) * channels]
                        if i < 3:
                            spatial_ref[i, k, at : at + block] = lanes
                        else:
                            temporal_ref[k, at : at + block] = lanes

    core = lax.axis_index("tm") & 1
    pl.when(core == 0)(functools.partial(write, (mine_ref, got_ref)))
    pl.when(core == 1)(functools.partial(write, (got_ref, mine_ref)))


def neighbours(axis, low, high, but=None):
    size = lax.axis_size(axis)
    up = [(i, i + 1) for i in range(size - 1) if i != but]
    down = [(j, i) for i, j in up]
    return lax.ppermute(high, axis, up), lax.ppermute(low, axis, down)


def spread_parts(part, axis):
    size = lax.axis_size(axis)
    return [part] + [lax.ppermute(part, axis, [(i, i ^ s) for i in range(size)]) for s in range(1, size)]


def spread_sums(part, axis):
    size = lax.axis_size(axis)
    step, got = 1, None
    while step < size:
        if got is not None:
            part = part + got
        got = lax.ppermute(part, axis, [(i, i ^ step) for i in range(size)])
        step *= 2
    return [part, got]


def per_device(frames_in, cotangent, spatial, temporal, norm_gain, norm_shift, clip_frames, dilation):
    frames, rows, width, channels = frames_in.shape
    pixels = rows * width
    n, tm = lax.axis_size("space"), lax.axis_size("tm")
    chips = tm // 2
    group_size = channels // GROUPS
    entries = float(rows * n * width * group_size)
    gain, shift = norm_gain[None], norm_shift[None]
    big = frames * pixels * channels
    shape = jax.ShapeDtypeStruct
    per_px = (frames, pixels, channels)
    windows = pltpu.VMEM((2 * pixels, 3 * channels), BF16)

    cot = cotangent.reshape(per_px)
    by_corner = tm == 8
    first, last = frames_in[:, :1], frames_in[:, rows - 1 :]
    first, last, near = lax.optimization_barrier((first, last, cot))
    cot_prev, cot_next = neighbours("tm", near, near, 3 if by_corner else None)
    above, below = neighbours("space", first, last)
    cot_corner = []
    if by_corner:
        above, below, late = lax.optimization_barrier((above, below, cot))
        straight, relayed = late[: frames // 2], late[frames // 2 :]
        relayed = lax.ppermute(relayed, "tm", [(3, 7), (4, 0)])
    back_weights, back_taps = call(
        turn_weights_kernel, "turn_weights", [spatial, temporal],
        [shape((3, 3 * channels, channels), BF16), shape((3 * channels, channels), BF16)], 0, big,
    )
    conv_out, sums = call(
        conv_kernel, "conv_forward", [frames_in, above, below, spatial],
        [shape(per_px, F32), shape((frames, 2, channels), F32)],
        100 * big * channels, 8 * big, [windows], 18,
    )
    if by_corner:
        sums, straight = lax.optimization_barrier((sums, straight))
        cot_corner.append(lax.ppermute(straight, "tm", [(3, 4), (4, 3)]))
    parts = spread_sums(sums, "space")
    x_turned = call(
        turn_kernel, "turned", [frames_in, above, below], shape((3 * channels, frames * pixels), BF16),
        0, 8 * big, [pltpu.VMEM((pixels, 3 * channels), BF16)],
    )
    if by_corner:
        parts[1], relayed = lax.optimization_barrier((parts[1], relayed))
        cot_corner.append(lax.ppermute(relayed, "tm", [(7, 4), (0, 3)]))
    x_turned, *parts = lax.optimization_barrier((x_turned, *parts))
    ahead = (3 * frames) // 4
    act, act_early, act_late, normed, slope = call(
        functools.partial(act_kernel, len(parts), entries, group_size), "activation",
        [clip_frames, *parts, conv_out, gain, shift], [shape((k, pixels, channels), BF16) for k in (frames, ahead, frames - ahead, frames, frames)], 10 * big, 10 * big,
    )
    act_prev, act_next = neighbours("tm", act_early, act_early)

    grad_act, cot_cat, grad_sums = call(
        functools.partial(grad_act_kernel, len(cot_corner)), "grad_activation",
        [clip_frames, dilation, cot, cot_next, cot_prev, *cot_corner, back_taps, normed, slope],
        [shape(per_px, BF16), shape((frames * pixels, 3 * channels), BF16), shape((frames, 2, channels), F32)],
        6 * big * channels, 16 * big,
    )
    grad_parts = spread_parts(grad_sums, "space")
    temporal_part = call(
        temporal_grad_kernel, "temporal_grad", [act, cot_cat],
        shape((channels, 3 * channels), F32), 6 * big * channels, 8 * big,
    )
    lanes = 3 * channels
    grad_conv, first_rows, last_rows, moved = call(
        functools.partial(norm_back_kernel, len(parts), len(grad_parts), entries, group_size), "norm_backward",
        [normed, slope, grad_act, *parts, *grad_parts],
        [shape(per_px, BF16)] + [shape((frames, 1, width, channels), BF16)] * 2
        + [shape((frames * pixels, lanes), BF16)],
        0, 12 * big,
    )
    grad_above, grad_below = neighbours("space", first_rows, last_rows)
    sums = call(
        weight_grad_kernel, "weight_grad", [x_turned, moved, temporal_part], shape((4 * channels, lanes), F32),
        18 * big * channels, 12 * big,
    )
    sums, grad_above, grad_below = lax.optimization_barrier((sums, grad_above, grad_below))
    block = 2 * channels // (chips * n)
    send, keep = call(
        hand_out_kernel, "hand_out", [sums],
        [shape((chips, n, block, lanes), BF16), shape((chips, n, block, lanes), F32)], 0, big,
    )
    def other_chip(s):
        return [(i, i ^ (2 * s)) for i in range(tm)]

    def other_plane(s):
        return [(i, i ^ s) for i in range(n)]

    other_core = [(i, i ^ 1) for i in range(tm)]
    got = lax.ppermute(send, "tm", other_core)
    own, *sends = call(
        core_sum_kernel, "core_sum", [keep, got],
        [shape((n, block, lanes), F32)] + [shape((n, block, lanes), BF16)] * (chips - 1), 0, 4 * big,
    )
    gots = [lax.ppermute(x, "tm", other_chip(s)) for s, x in enumerate(sends, 1)]

    in_grad = call(
        conv_back_kernel, "conv_backward", [grad_conv, grad_above, grad_below, cotangent, back_weights],
        shape(frames_in.shape, BF16), 18 * big * channels, 8 * big, [windows], 20,
    )
    own, in_grad, act_prev, act_next = lax.optimization_barrier((own, in_grad, act_prev, act_next))

    own, *sends = call(
        functools.partial(sum_split_kernel, chips - 1), "plane_sum", [own, *gots],
        [shape((block, lanes), F32)] + [shape((block, lanes), BF16)] * (n - 1), 0, big,
    )
    gots = [lax.ppermute(x, "space", other_plane(s)) for s, x in enumerate(sends, 1)]
    own, act_late = lax.optimization_barrier((own, act_late))
    late_prev, late_next = neighbours("tm", act_late, act_late)
    own = call(
        functools.partial(sum_kernel, n - 1), "line_sum", [own, *gots], shape((block, lanes), BF16), 0, big
    )
    gots = [lax.ppermute(own, "space", other_plane(s)) for s in range(1, n)]
    own = call(
        functools.partial(place_kernel, "space", 0), "line_place", [own, *gots], shape((n, block, lanes), BF16), 0, big
    )
    gots = [lax.ppermute(own, "tm", other_chip(s)) for s in range(1, chips)]


    out_frames = call(
        out_kernel, "temporal_forward",
        [clip_frames, dilation, act, act_next, late_next, act_prev, late_prev, temporal.reshape(3 * channels, channels), frames_in],
        shape(frames_in.shape, BF16), 6 * big * channels, 10 * big, [windows],
    )
    own, out_frames = lax.optimization_barrier((own, out_frames))
    own = call(
        functools.partial(place_kernel, "tm", 1), "plane_place", [own, *gots], shape((chips, n, block, lanes), BF16), 0, big
    )
    got = lax.ppermute(own, "tm", other_core)
    spatial_grad, temporal_grad = call(
        finish_kernel, "finish", [own, got], [shape(spatial.shape, F32), shape(temporal.shape, F32)], 0, 4 * big
    )
    return (out_frames, in_grad, spatial_grad, temporal_grad)


def solution(mesh):
    tiles = P("tm", "space", None, None)
    return jax.shard_map(
        per_device,
        mesh=mesh,
        in_specs=(tiles, tiles, P(), P(), P(), P(), P(), P()),
        out_specs=(tiles, tiles, P(), P()),
        check_vma=False,
    )
```

```python
import functools

import jax
import jax.numpy as jnp
from jax import lax
from jax.experimental import pallas as pl
from jax.experimental.pallas import tpu as pltpu
from jax.sharding import PartitionSpec as P

GROUPS = 32
NORM_EPS = 1e-05
BF16 = jnp.bfloat16
F32 = jnp.float32
MIB = 2**20


def call(kernel, name, operands, out_shape, flops=0, moved=0, scratch=(), grant=14):
    vmem = pl.BlockSpec(memory_space=pltpu.VMEM)
    smem = pl.BlockSpec(memory_space=pltpu.SMEM)
    return pl.pallas_call(
        kernel,
        in_specs=[smem if x.dtype == jnp.int32 else vmem for x in operands],
        out_specs=jax.tree.map(lambda _: vmem, out_shape),
        out_shape=out_shape,
        scratch_shapes=list(scratch),
        compiler_params=pltpu.CompilerParams(vmem_limit_bytes=grant * MIB),
        cost_estimate=pl.CostEstimate(flops=int(flops), bytes_accessed=int(moved), transcendentals=0),
        name=name,
    )(*operands)


def dot(a, b):
    return jnp.dot(a, b, preferred_element_type=F32)


def dot_rows(a, b):
    return lax.dot_general(a, b, (((0,), (0,)), ((), ())), preferred_element_type=F32)


def group_total(row, group_size):
    channels = row.shape[-1]
    lane = lax.broadcasted_iota(jnp.int32, row.shape, 1)
    step = 1
    while step < group_size:
        up = pltpu.roll(row, channels - step, axis=1)
        down = pltpu.roll(row, step, axis=1)
        row = row + jnp.where((lane & step) == 0, up, down)
        step *= 2
    return row


def group_means(part_refs, entries, group_size):
    total = part_refs[0][...]
    for ref in part_refs[1:]:
        total = total + ref[...]
    frames, _, channels = total.shape
    means = group_total(total.reshape(2 * frames, channels), group_size) / entries
    means = means.reshape(frames, 2, channels)
    return means[:, 0], means[:, 1]


def mean_and_inv(part_refs, entries, group_size):
    mean, square = group_means(part_refs, entries, group_size)
    return mean, lax.rsqrt(square - mean * mean + NORM_EPS)


def column_sums(first, second):
    return jnp.concatenate(
        [jnp.sum(first, axis=0, keepdims=True), jnp.sum(second, axis=0, keepdims=True)], axis=0
    )


def put_windows(above, mid, below, lhs_ref, at, order):
    width, (pixels, channels) = above.shape[0], mid.shape
    first, mid_at, last = (slice(k * channels, (k + 1) * channels) for k in order)
    lhs_ref[at : at + width, first] = above
    lhs_ref[at + width : at + pixels, first] = mid[: pixels - width]
    lhs_ref[at : at + pixels, mid_at] = mid
    lhs_ref[at : at + pixels - width, last] = mid[width:]
    lhs_ref[at + pixels - width : at + pixels, last] = below


def from_left(y, width):
    col = lax.broadcasted_iota(jnp.int32, y.shape, 0) & (width - 1)
    return jnp.where(col == 0, 0.0, pltpu.roll(y, 1, axis=0))


def from_right(y, width):
    col = lax.broadcasted_iota(jnp.int32, y.shape, 0) & (width - 1)
    return jnp.where(col == width - 1, 0.0, pltpu.roll(y, y.shape[0] - 1, axis=0))


def slot_sources(clip_ref, dil_ref, local, frames):
    slot = lax.axis_index("tm") * frames + local
    start1 = clip_ref[0]
    filled = start1 + clip_ref[1]
    in_first = slot < start1
    d = jnp.where(in_first, dil_ref[0], dil_ref[1])
    low = jnp.where(in_first, 0, start1)
    high = jnp.where(in_first, start1, filled)
    used = slot < filled
    later, earlier = local + d, local - d
    later_live = used & (slot + d < high)
    earlier_live = used & (slot - d >= low)
    later_which = jnp.where(later_live, jnp.where(later < frames, 1, 2), 0)
    earlier_which = jnp.where(earlier_live, jnp.where(earlier >= 0, 1, 2), 0)
    return (later, later_which), (earlier, earlier_which), used


def gather_taps(clip_ref, dil_ref, local, own, nxt, prv, corner, cat_ref, at, up_slot):
    frames, pixels, channels = own.shape
    later, earlier, used = slot_sources(clip_ref, dil_ref, local, frames)
    me = lax.axis_index("tm")

    def put(slot, ref, index):
        cat_ref[pl.ds(at, pixels), slot * channels : (slot + 1) * channels] = ref[index]

    def clear(slot):
        cat_ref[pl.ds(at, pixels), slot * channels : (slot + 1) * channels] = jnp.zeros((pixels, channels), BF16)

    def put_from(slot, pieces, wanted, index):
        start = 0
        for ref in pieces:
            count = ref.shape[0]
            here = wanted & (index >= start) & (index < start + count)
            pl.when(here)(functools.partial(put, slot, ref, jnp.clip(index - start, 0, count - 1)))
            start += count

    for slot, (index, which), other, shift, turn in (
        (up_slot, later, nxt, -frames, 3),
        (2 - up_slot, earlier, prv, frames, 4),
    ):
        pl.when(which == 0)(functools.partial(clear, slot))
        pl.when(which == 1)(functools.partial(put, slot, own, jnp.clip(index, 0, frames - 1)))
        there = jnp.clip(index + shift, 0, frames - 1)
        beyond = which == 2
        if corner:
            put_from(slot, corner, beyond & (me == turn), there)
            beyond = beyond & (me != turn)
        put_from(slot, other, beyond, there)
    pl.when(used)(functools.partial(put, 1, own, local))
    pl.when(jnp.logical_not(used))(functools.partial(clear, 1))


def loop(count, body):
    def step(k, carry):
        body(k)
        return carry

    lax.fori_loop(0, count, step, 0)


def conv_kernel(x_ref, above_ref, below_ref, w_ref, out_ref, sums_ref, lhs_ref):
    frames, rows, width, channels = x_ref.shape
    pixels = rows * width

    def body(pair):
        for b in range(2):
            f = 2 * pair + b
            mid = x_ref[f].reshape(pixels, channels)
            put_windows(above_ref[f, 0], mid, below_ref[f, 0], lhs_ref, b * pixels, (0, 1, 2))
        lhs = lhs_ref[...]
        y = [dot(lhs, w_ref[:, j].reshape(3 * channels, channels)) for j in range(3)]
        out = y[1] + from_left(y[0], width) + from_right(y[2], width)
        for b in range(2):
            one = out[b * pixels : (b + 1) * pixels]
            out_ref[2 * pair + b] = one
            sums_ref[2 * pair + b] = column_sums(one, one * one)

    loop(frames // 2, body)


def silu_parts(normed, half_gain, half_shift):
    h = normed * half_gain + half_shift
    t = jnp.tanh(h)
    rise = 1.0 + t
    return h, rise, rise * (1.0 + h * (1.0 - t)) * half_gain


def act_kernel(n, entries, group_size, clip_ref, *refs):
    parts, refs = refs[:n], refs[n:]
    conv_ref, gain_ref, shift_ref, act_ref, early_ref, late_ref, normed_ref, slope_ref, mean_ref, inv_ref = refs
    frames, ahead = conv_ref.shape[0], early_ref.shape[0]
    first = lax.axis_index("tm") * frames
    filled = clip_ref[0] + clip_ref[1]
    half_gain, half_shift = 0.5 * gain_ref[...], 0.5 * shift_ref[...]
    mean_ref[...], inv_ref[...] = mean_and_inv(parts, entries, group_size)

    def body(f):
        normed = (conv_ref[f] - mean_ref[pl.ds(f, 1)]) * inv_ref[pl.ds(f, 1)]
        h, rise, slope = silu_parts(normed, half_gain, half_shift)
        act = jnp.where(first + f < filled, h * rise, 0.0).astype(BF16)
        act_ref[f] = act

        @pl.when(f < ahead)
        def _():
            early_ref[jnp.minimum(f, ahead - 1)] = act

        @pl.when(f >= ahead)
        def _():
            late_ref[jnp.maximum(f - ahead, 0)] = act

        normed_ref[f] = normed.astype(BF16)
        slope_ref[f] = slope.astype(BF16)

    loop(frames, body)


def turn_kernel(x_ref, above_ref, below_ref, xt_ref, lhs_ref):
    frames, rows, width, channels = x_ref.shape
    pixels = rows * width

    def body(f):
        mid = x_ref[f].reshape(pixels, channels)
        put_windows(above_ref[f, 0], mid, below_ref[f, 0], lhs_ref, 0, (0, 1, 2))
        lanes = pl.ds(pl.multiple_of(f * pixels, pixels), pixels)
        for i in range(3):
            block = slice(i * channels, (i + 1) * channels)
            xt_ref[block, lanes] = lhs_ref[:, block].T

    loop(frames, body)


def turn_weights_kernel(spatial_ref, temporal_ref, back_ref, out_ref):
    channels = spatial_ref.shape[-1]
    for i in range(3):
        rows = slice(i * channels, (i + 1) * channels)
        out_ref[rows] = temporal_ref[i].T
        for j in range(3):
            back_ref[j, rows] = spatial_ref[i, j].T


def grad_act_kernel(corners, clip_ref, dil_ref, own, nxt, prv, *refs):
    corner, (tw_ref, normed_ref, slope_ref, ga_ref, cat_ref, sums_ref) = refs[:corners], refs[corners:]
    frames, pixels, _ = own.shape

    def body(pair):
        rows = pl.ds(pl.multiple_of(2 * pair * pixels, 2 * pixels), 2 * pixels)
        for b in range(2):
            at = pl.multiple_of((2 * pair + b) * pixels, pixels)
            gather_taps(clip_ref, dil_ref, 2 * pair + b, own, (nxt,), (prv,), corner, cat_ref, at, 0)
        grad_act = dot(cat_ref[rows], tw_ref[...]).astype(BF16)
        for b in range(2):
            f = 2 * pair + b
            one = grad_act[b * pixels : (b + 1) * pixels]
            ga_ref[f] = one
            gn = one.astype(F32) * slope_ref[f].astype(F32)
            sums_ref[f] = column_sums(gn, gn * normed_ref[f].astype(F32))

    loop(frames // 2, body)


def temporal_grad_kernel(act_ref, cat_ref, out_ref):
    frames, pixels, channels = act_ref.shape
    out_ref[...] = dot_rows(act_ref[...].reshape(frames * pixels, channels), cat_ref[...])


def norm_back_kernel(n, m, entries, group_size, normed_ref, slope_ref, ga_ref, *refs):
    parts, grad_parts = refs[:n], refs[n : n + m]
    g_ref, first_ref, last_ref, moved_ref, inv_ref, first_mean_ref, second_mean_ref = refs[n + m :]
    _, pixels, channels = normed_ref.shape
    width = first_ref.shape[2]

    _, inv_ref[...] = mean_and_inv(parts, entries, group_size)
    first_mean_ref[...], second_mean_ref[...] = group_means(grad_parts, entries, group_size)

    def body(f):
        row = pl.ds(f, 1)
        gn = ga_ref[f].astype(F32) * slope_ref[f].astype(F32)
        wide = inv_ref[row] * (gn - first_mean_ref[row] - normed_ref[f].astype(F32) * second_mean_ref[row])
        grad = wide.astype(BF16)
        g_ref[f] = grad
        first_ref[f, 0] = grad[:width]
        last_ref[f, 0] = grad[pixels - width :]
        here = pl.ds(pl.multiple_of(f * pixels, pixels), pixels)
        moved_ref[here, :channels] = from_right(wide, width).astype(BF16)
        moved_ref[here, channels : 2 * channels] = grad
        moved_ref[here, 2 * channels :] = from_left(wide, width).astype(BF16)

    loop(normed_ref.shape[0], body)


def weight_grad_kernel(xt_ref, moved_ref, temporal_ref, out_ref):
    channels = temporal_ref.shape[0]
    for j in range(3):
        lanes = slice(j * channels, (j + 1) * channels)
        out_ref[: 3 * channels, lanes] = dot(xt_ref[...], moved_ref[:, lanes])
    out_ref[3 * channels :, :] = temporal_ref[...]


def hand_out_kernel(acc_ref, send_ref, keep_ref):
    chips, depth, block, _ = keep_ref.shape
    half = chips * depth * block
    core = lax.axis_index("tm") & 1

    def hand_out(kept, sent):
        for p in range(chips):
            for z in range(depth):
                at = (p * depth + z) * block
                keep_ref[p, z] = acc_ref[kept + at : kept + at + block]
                send_ref[p, z] = acc_ref[sent + at : sent + at + block].astype(BF16)

    pl.when(core == 0)(functools.partial(hand_out, 0, half))
    pl.when(core == 1)(functools.partial(hand_out, half, 0))


def conv_back_kernel(g_ref, above_ref, below_ref, cot_ref, w_ref, out_ref, lhs_ref):
    frames, rows, width, channels = cot_ref.shape
    pixels = rows * width

    def body(pair):
        for b in range(2):
            f = 2 * pair + b
            put_windows(above_ref[f, 0], g_ref[f], below_ref[f, 0], lhs_ref, b * pixels, (2, 1, 0))
        lhs = lhs_ref[...]
        z = [dot(lhs, w_ref[j]) for j in range(3)]
        out = z[1] + from_right(z[0], width) + from_left(z[2], width)
        for b in range(2):
            one = out[b * pixels : (b + 1) * pixels].reshape(rows, width, channels)
            out_ref[2 * pair + b] = (one + cot_ref[2 * pair + b].astype(F32)).astype(BF16)

    loop(frames // 2, body)


def out_kernel(clip_ref, dil_ref, own, nxt_a, nxt_b, prv_a, prv_b, tw_ref, x_ref, out_ref, cat_ref):
    frames, rows, width, channels = x_ref.shape
    pixels = rows * width

    def body(pair):
        for b in range(2):
            gather_taps(clip_ref, dil_ref, 2 * pair + b, own, (nxt_a, nxt_b), (prv_a, prv_b), (), cat_ref, b * pixels, 2)
        temporal_out = dot(cat_ref[...], tw_ref[...]).astype(BF16).astype(F32)
        for b in range(2):
            one = temporal_out[b * pixels : (b + 1) * pixels].reshape(rows, width, channels)
            out_ref[2 * pair + b] = (x_ref[2 * pair + b].astype(F32) + one).astype(BF16)

    loop(frames // 2, body)


def core_sum_kernel(keep_ref, got_ref, own_ref, *send_refs):
    chip = lax.axis_index("tm") >> 1
    own_ref[...] = keep_ref[chip] + got_ref[chip].astype(F32)
    for s, ref in enumerate(send_refs, 1):
        ref[...] = (keep_ref[chip ^ s] + got_ref[chip ^ s].astype(F32)).astype(BF16)


def sum_kernel(count, own_ref, *refs):
    total = own_ref[...]
    for ref in refs[:count]:
        total = total + ref[...].astype(F32)
    refs[count][...] = total.astype(BF16)


def sum_split_kernel(count, own_ref, *refs):
    got, (mine_ref, *send_refs) = refs[:count], refs[count:]
    deep = lax.axis_index("space")

    def block(k):
        total = own_ref[k]
        for ref in got:
            total = total + ref[k].astype(F32)
        return total

    mine_ref[...] = block(deep)
    for s, ref in enumerate(send_refs, 1):
        ref[...] = block(deep ^ s).astype(BF16)


def place_kernel(axis, shift, *refs):
    me = lax.axis_index(axis) >> shift
    for s, ref in enumerate(refs[:-1]):
        refs[-1][me ^ s] = ref[...]


def finish_kernel(mine_ref, got_ref, spatial_ref, temporal_ref):
    chips, depth, block, _ = mine_ref.shape
    channels = spatial_ref.shape[-1]

    def write(pair):
        for c in range(2):
            for p in range(chips):
                for z in range(depth):
                    row = ((c * chips + p) * depth + z) * block
                    values = pair[c][p, z].astype(F32)
                    i, at = row // channels, row % channels
                    for k in range(3):
                        lanes = values[:, k * channels : (k + 1) * channels]
                        if i < 3:
                            spatial_ref[i, k, at : at + block] = lanes
                        else:
                            temporal_ref[k, at : at + block] = lanes

    core = lax.axis_index("tm") & 1
    pl.when(core == 0)(functools.partial(write, (mine_ref, got_ref)))
    pl.when(core == 1)(functools.partial(write, (got_ref, mine_ref)))


def neighbours(axis, low, high, but=None):
    size = lax.axis_size(axis)
    up = [(i, i + 1) for i in range(size - 1) if i != but]
    down = [(j, i) for i, j in up]
    return lax.ppermute(high, axis, up), lax.ppermute(low, axis, down)


def spread_parts(part, axis):
    size = lax.axis_size(axis)
    return [part] + [lax.ppermute(part, axis, [(i, i ^ s) for i in range(size)]) for s in range(1, size)]


def spread_sums(part, axis):
    size = lax.axis_size(axis)
    step, got = 1, None
    while step < size:
        if got is not None:
            part = part + got
        got = lax.ppermute(part, axis, [(i, i ^ step) for i in range(size)])
        step *= 2
    return [part, got]


def per_device(frames_in, cotangent, spatial, temporal, norm_gain, norm_shift, clip_frames, dilation):
    frames, rows, width, channels = frames_in.shape
    pixels = rows * width
    n, tm = lax.axis_size("space"), lax.axis_size("tm")
    chips = tm // 2
    group_size = channels // GROUPS
    entries = float(rows * n * width * group_size)
    gain, shift = norm_gain[None], norm_shift[None]
    big = frames * pixels * channels
    shape = jax.ShapeDtypeStruct
    per_px = (frames, pixels, channels)
    windows = pltpu.VMEM((2 * pixels, 3 * channels), BF16)

    cot = cotangent.reshape(per_px)
    by_corner = tm == 8
    first, last = frames_in[:, :1], frames_in[:, rows - 1 :]
    first, last, near = lax.optimization_barrier((first, last, cot))
    cot_prev, cot_next = neighbours("tm", near, near, 3 if by_corner else None)
    cot_corner = []
    if by_corner:
        straight, relayed = cot[: frames // 2], cot[frames // 2 :]
        relayed = lax.ppermute(relayed, "tm", [(3, 7), (4, 0)])
    above, below = neighbours("space", first, last)
    back_weights, back_taps = call(
        turn_weights_kernel, "turn_weights", [spatial, temporal],
        [shape((3, 3 * channels, channels), BF16), shape((3 * channels, channels), BF16)], 0, big,
    )
    conv_out, sums = call(
        conv_kernel, "conv_forward", [frames_in, above, below, spatial],
        [shape(per_px, F32), shape((frames, 2, channels), F32)],
        100 * big * channels, 8 * big, [windows], 18,
    )
    if by_corner:
        sums, straight = lax.optimization_barrier((sums, straight))
        cot_corner.append(lax.ppermute(straight, "tm", [(3, 4), (4, 3)]))
    parts = spread_sums(sums, "space")
    if by_corner:
        parts[0], relayed = lax.optimization_barrier((parts[0], relayed))
        cot_corner.append(lax.ppermute(relayed, "tm", [(7, 4), (0, 3)]))
    x_turned = call(
        turn_kernel, "turned", [frames_in, above, below], shape((3 * channels, frames * pixels), BF16),
        0, 8 * big, [pltpu.VMEM((pixels, 3 * channels), BF16)],
    )
    x_turned, *parts = lax.optimization_barrier((x_turned, *parts))
    ahead = (3 * frames) // 4
    row = pltpu.VMEM((frames, channels), F32)
    act, act_early, act_late, normed, slope = call(
        functools.partial(act_kernel, len(parts), entries, group_size), "activation",
        [clip_frames, *parts, conv_out, gain, shift], [shape((k, pixels, channels), BF16) for k in (frames, ahead, frames - ahead, frames, frames)], 10 * big, 10 * big, [row] * 2,
    )
    act_prev, act_next = neighbours("tm", act_early, act_early)

    grad_act, cot_cat, grad_sums = call(
        functools.partial(grad_act_kernel, len(cot_corner)), "grad_activation",
        [clip_frames, dilation, cot, cot_next, cot_prev, *cot_corner, back_taps, normed, slope],
        [shape(per_px, BF16), shape((frames * pixels, 3 * channels), BF16), shape((frames, 2, channels), F32)],
        6 * big * channels, 16 * big,
    )
    grad_parts = spread_parts(grad_sums, "space")
    temporal_part = call(
        temporal_grad_kernel, "temporal_grad", [act, cot_cat],
        shape((channels, 3 * channels), F32), 6 * big * channels, 8 * big,
    )
    lanes = 3 * channels
    grad_conv, first_rows, last_rows, moved = call(
        functools.partial(norm_back_kernel, len(parts), len(grad_parts), entries, group_size), "norm_backward",
        [normed, slope, grad_act, *parts, *grad_parts],
        [shape(per_px, BF16)] + [shape((frames, 1, width, channels), BF16)] * 2
        + [shape((frames * pixels, lanes), BF16)],
        0, 12 * big, [row] * 3,
    )
    grad_above, grad_below = neighbours("space", first_rows, last_rows)
    sums = call(
        weight_grad_kernel, "weight_grad", [x_turned, moved, temporal_part], shape((4 * channels, lanes), F32),
        18 * big * channels, 12 * big,
    )
    sums, grad_above, grad_below = lax.optimization_barrier((sums, grad_above, grad_below))
    block = 2 * channels // (chips * n)
    send, keep = call(
        hand_out_kernel, "hand_out", [sums],
        [shape((chips, n, block, lanes), BF16), shape((chips, n, block, lanes), F32)], 0, big,
    )
    def other_chip(s):
        return [(i, i ^ (2 * s)) for i in range(tm)]

    def other_plane(s):
        return [(i, i ^ s) for i in range(n)]

    other_core = [(i, i ^ 1) for i in range(tm)]
    got = lax.ppermute(send, "tm", other_core)
    own, *sends = call(
        core_sum_kernel, "core_sum", [keep, got],
        [shape((n, block, lanes), F32)] + [shape((n, block, lanes), BF16)] * (chips - 1), 0, 4 * big,
    )
    gots = [lax.ppermute(x, "tm", other_chip(s)) for s, x in enumerate(sends, 1)]

    in_grad = call(
        conv_back_kernel, "conv_backward", [grad_conv, grad_above, grad_below, cotangent, back_weights],
        shape(frames_in.shape, BF16), 18 * big * channels, 8 * big, [windows], 20,
    )
    own, in_grad, act_prev, act_next = lax.optimization_barrier((own, in_grad, act_prev, act_next))

    own, *sends = call(
        functools.partial(sum_split_kernel, chips - 1), "plane_sum", [own, *gots],
        [shape((block, lanes), F32)] + [shape((block, lanes), BF16)] * (n - 1), 0, big,
    )
    gots = [lax.ppermute(x, "space", other_plane(s)) for s, x in enumerate(sends, 1)]
    own, act_late = lax.optimization_barrier((own, act_late))
    late_prev, late_next = neighbours("tm", act_late, act_late)
    own = call(
        functools.partial(sum_kernel, n - 1), "line_sum", [own, *gots], shape((block, lanes), BF16), 0, big
    )
    gots = [lax.ppermute(own, "space", other_plane(s)) for s in range(1, n)]
    own = call(
        functools.partial(place_kernel, "space", 0), "line_place", [own, *gots], shape((n, block, lanes), BF16), 0, big
    )
    gots = [lax.ppermute(own, "tm", other_chip(s)) for s in range(1, chips)]


    out_frames = call(
        out_kernel, "temporal_forward",
        [clip_frames, dilation, act, act_next, late_next, act_prev, late_prev, temporal.reshape(3 * channels, channels), frames_in],
        shape(frames_in.shape, BF16), 6 * big * channels, 10 * big, [windows],
    )
    own, out_frames = lax.optimization_barrier((own, out_frames))
    own = call(
        functools.partial(place_kernel, "tm", 1), "plane_place", [own, *gots], shape((chips, n, block, lanes), BF16), 0, big
    )
    got = lax.ppermute(own, "tm", other_core)
    spatial_grad, temporal_grad = call(
        finish_kernel, "finish", [own, got], [shape(spatial.shape, F32), shape(temporal.shape, F32)], 0, 4 * big
    )
    return (out_frames, in_grad, spatial_grad, temporal_grad)


def solution(mesh):
    tiles = P("tm", "space", None, None)
    return jax.shard_map(
        per_device,
        mesh=mesh,
        in_specs=(tiles, tiles, P(), P(), P(), P(), P(), P()),
        out_specs=(tiles, tiles, P(), P()),
        check_vma=False,
    )
```

```python
import functools

import jax
import jax.numpy as jnp
from jax import lax
from jax.experimental import pallas as pl
from jax.experimental.pallas import tpu as pltpu
from jax.sharding import PartitionSpec as P

GROUPS = 32
NORM_EPS = 1e-05
BF16 = jnp.bfloat16
F32 = jnp.float32
MIB = 2**20


def call(kernel, name, operands, out_shape, flops=0, moved=0, scratch=(), grant=14):
    vmem = pl.BlockSpec(memory_space=pltpu.VMEM)
    smem = pl.BlockSpec(memory_space=pltpu.SMEM)
    return pl.pallas_call(
        kernel,
        in_specs=[smem if x.dtype == jnp.int32 else vmem for x in operands],
        out_specs=jax.tree.map(lambda _: vmem, out_shape),
        out_shape=out_shape,
        scratch_shapes=list(scratch),
        compiler_params=pltpu.CompilerParams(vmem_limit_bytes=grant * MIB),
        cost_estimate=pl.CostEstimate(flops=int(flops), bytes_accessed=int(moved), transcendentals=0),
        name=name,
    )(*operands)


def dot(a, b):
    return jnp.dot(a, b, preferred_element_type=F32)


def dot_rows(a, b):
    return lax.dot_general(a, b, (((0,), (0,)), ((), ())), preferred_element_type=F32)


def group_total(row, group_size):
    channels = row.shape[-1]
    lane = lax.broadcasted_iota(jnp.int32, row.shape, 1)
    step = 1
    while step < group_size:
        up = pltpu.roll(row, channels - step, axis=1)
        down = pltpu.roll(row, step, axis=1)
        row = row + jnp.where((lane & step) == 0, up, down)
        step *= 2
    return row


def group_means(part_refs, entries, group_size):
    total = part_refs[0][...]
    for ref in part_refs[1:]:
        total = total + ref[...]
    frames, _, channels = total.shape
    means = group_total(total.reshape(2 * frames, channels), group_size) / entries
    means = means.reshape(frames, 2, channels)
    return means[:, 0], means[:, 1]


def mean_and_inv(part_refs, entries, group_size):
    mean, square = group_means(part_refs, entries, group_size)
    return mean, lax.rsqrt(square - mean * mean + NORM_EPS)


def column_sums(first, second):
    return jnp.concatenate(
        [jnp.sum(first, axis=0, keepdims=True), jnp.sum(second, axis=0, keepdims=True)], axis=0
    )


def put_windows(above, mid, below, lhs_ref, at, order):
    width, (pixels, channels) = above.shape[0], mid.shape
    first, mid_at, last = (slice(k * channels, (k + 1) * channels) for k in order)
    lhs_ref[at : at + width, first] = above
    lhs_ref[at + width : at + pixels, first] = mid[: pixels - width]
    lhs_ref[at : at + pixels, mid_at] = mid
    lhs_ref[at : at + pixels - width, last] = mid[width:]
    lhs_ref[at + pixels - width : at + pixels, last] = below


def from_left(y, width):
    col = lax.broadcasted_iota(jnp.int32, y.shape, 0) & (width - 1)
    return jnp.where(col == 0, 0.0, pltpu.roll(y, 1, axis=0))


def from_right(y, width):
    col = lax.broadcasted_iota(jnp.int32, y.shape, 0) & (width - 1)
    return jnp.where(col == width - 1, 0.0, pltpu.roll(y, y.shape[0] - 1, axis=0))


def slot_sources(clip_ref, dil_ref, local, frames):
    slot = lax.axis_index("tm") * frames + local
    start1 = clip_ref[0]
    filled = start1 + clip_ref[1]
    in_first = slot < start1
    d = jnp.where(in_first, dil_ref[0], dil_ref[1])
    low = jnp.where(in_first, 0, start1)
    high = jnp.where(in_first, start1, filled)
    used = slot < filled
    later, earlier = local + d, local - d
    later_live = used & (slot + d < high)
    earlier_live = used & (slot - d >= low)
    later_which = jnp.where(later_live, jnp.where(later < frames, 1, 2), 0)
    earlier_which = jnp.where(earlier_live, jnp.where(earlier >= 0, 1, 2), 0)
    return (later, later_which), (earlier, earlier_which), used


def gather_taps(clip_ref, dil_ref, local, own, nxt, prv, corner, cat_ref, at, up_slot):
    frames, pixels, channels = own.shape
    later, earlier, used = slot_sources(clip_ref, dil_ref, local, frames)
    me = lax.axis_index("tm")

    def put(slot, ref, index):
        cat_ref[pl.ds(at, pixels), slot * channels : (slot + 1) * channels] = ref[index]

    def clear(slot):
        cat_ref[pl.ds(at, pixels), slot * channels : (slot + 1) * channels] = jnp.zeros((pixels, channels), BF16)

    def put_from(slot, pieces, wanted, index):
        start = 0
        for ref in pieces:
            count = ref.shape[0]
            here = wanted & (index >= start) & (index < start + count)
            pl.when(here)(functools.partial(put, slot, ref, jnp.clip(index - start, 0, count - 1)))
            start += count

    for slot, (index, which), other, shift, turn in (
        (up_slot, later, nxt, -frames, 3),
        (2 - up_slot, earlier, prv, frames, 4),
    ):
        pl.when(which == 0)(functools.partial(clear, slot))
        pl.when(which == 1)(functools.partial(put, slot, own, jnp.clip(index, 0, frames - 1)))
        there = jnp.clip(index + shift, 0, frames - 1)
        beyond = which == 2
        if corner:
            put_from(slot, corner, beyond & (me == turn), there)
            beyond = beyond & (me != turn)
        put_from(slot, other, beyond, there)
    pl.when(used)(functools.partial(put, 1, own, local))
    pl.when(jnp.logical_not(used))(functools.partial(clear, 1))


def loop(count, body):
    def step(k, carry):
        body(k)
        return carry

    lax.fori_loop(0, count, step, 0)


def conv_kernel(x_ref, above_ref, below_ref, w_ref, out_ref, sums_ref, lhs_ref):
    frames, rows, width, channels = x_ref.shape
    pixels = rows * width

    def body(pair):
        for b in range(2):
            f = 2 * pair + b
            mid = x_ref[f].reshape(pixels, channels)
            put_windows(above_ref[f, 0], mid, below_ref[f, 0], lhs_ref, b * pixels, (0, 1, 2))
        lhs = lhs_ref[...]
        y = [dot(lhs, w_ref[:, j].reshape(3 * channels, channels)) for j in range(3)]
        out = y[1] + from_left(y[0], width) + from_right(y[2], width)
        for b in range(2):
            one = out[b * pixels : (b + 1) * pixels]
            out_ref[2 * pair + b] = one
            sums_ref[2 * pair + b] = column_sums(one, one * one)

    loop(frames // 2, body)


def silu_parts(normed, half_gain, half_shift):
    h = normed * half_gain + half_shift
    t = jnp.tanh(h)
    rise = 1.0 + t
    return h, rise, rise * (1.0 + h * (1.0 - t)) * half_gain


def act_kernel(n, entries, group_size, clip_ref, *refs):
    parts, refs = refs[:n], refs[n:]
    conv_ref, gain_ref, shift_ref, act_ref, early_ref, late_ref, normed_ref, slope_ref, mean_ref, inv_ref = refs
    frames, ahead = conv_ref.shape[0], early_ref.shape[0]
    first = lax.axis_index("tm") * frames
    filled = clip_ref[0] + clip_ref[1]
    half_gain, half_shift = 0.5 * gain_ref[...], 0.5 * shift_ref[...]
    mean_ref[...], inv_ref[...] = mean_and_inv(parts, entries, group_size)

    def body(f):
        normed = (conv_ref[f] - mean_ref[pl.ds(f, 1)]) * inv_ref[pl.ds(f, 1)]
        h, rise, slope = silu_parts(normed, half_gain, half_shift)
        act = jnp.where(first + f < filled, h * rise, 0.0).astype(BF16)
        act_ref[f] = act

        @pl.when(f < ahead)
        def _():
            early_ref[jnp.minimum(f, ahead - 1)] = act

        @pl.when(f >= ahead)
        def _():
            late_ref[jnp.maximum(f - ahead, 0)] = act

        normed_ref[f] = normed.astype(BF16)
        slope_ref[f] = slope.astype(BF16)

    loop(frames, body)


def turn_kernel(x_ref, above_ref, below_ref, xt_ref, lhs_ref):
    frames, rows, width, channels = x_ref.shape
    pixels = rows * width

    def body(f):
        mid = x_ref[f].reshape(pixels, channels)
        put_windows(above_ref[f, 0], mid, below_ref[f, 0], lhs_ref, 0, (0, 1, 2))
        lanes = pl.ds(pl.multiple_of(f * pixels, pixels), pixels)
        for i in range(3):
            block = slice(i * channels, (i + 1) * channels)
            xt_ref[block, lanes] = lhs_ref[:, block].T

    loop(frames, body)


def turn_weights_kernel(spatial_ref, temporal_ref, back_ref, out_ref):
    channels = spatial_ref.shape[-1]
    for i in range(3):
        rows = slice(i * channels, (i + 1) * channels)
        out_ref[rows] = temporal_ref[i].T
        for j in range(3):
            back_ref[j, rows] = spatial_ref[i, j].T


def grad_act_kernel(corners, clip_ref, dil_ref, own, nxt, prv, *refs):
    corner, (tw_ref, normed_ref, slope_ref, ga_ref, cat_ref, sums_ref) = refs[:corners], refs[corners:]
    frames, pixels, _ = own.shape

    def body(pair):
        rows = pl.ds(pl.multiple_of(2 * pair * pixels, 2 * pixels), 2 * pixels)
        for b in range(2):
            at = pl.multiple_of((2 * pair + b) * pixels, pixels)
            gather_taps(clip_ref, dil_ref, 2 * pair + b, own, (nxt,), (prv,), corner, cat_ref, at, 0)
        grad_act = dot(cat_ref[rows], tw_ref[...]).astype(BF16)
        for b in range(2):
            f = 2 * pair + b
            one = grad_act[b * pixels : (b + 1) * pixels]
            ga_ref[f] = one
            gn = one.astype(F32) * slope_ref[f].astype(F32)
            sums_ref[f] = column_sums(gn, gn * normed_ref[f].astype(F32))

    loop(frames // 2, body)


def temporal_grad_kernel(act_ref, cat_ref, out_ref):
    frames, pixels, channels = act_ref.shape
    out_ref[...] = dot_rows(act_ref[...].reshape(frames * pixels, channels), cat_ref[...])


def norm_back_kernel(n, m, entries, group_size, normed_ref, slope_ref, ga_ref, *refs):
    parts, grad_parts = refs[:n], refs[n : n + m]
    g_ref, first_ref, last_ref, moved_ref, inv_ref, first_mean_ref, second_mean_ref = refs[n + m :]
    _, pixels, channels = normed_ref.shape
    width = first_ref.shape[2]

    _, inv_ref[...] = mean_and_inv(parts, entries, group_size)
    first_mean_ref[...], second_mean_ref[...] = group_means(grad_parts, entries, group_size)

    def body(f):
        row = pl.ds(f, 1)
        gn = ga_ref[f].astype(F32) * slope_ref[f].astype(F32)
        wide = inv_ref[row] * (gn - first_mean_ref[row] - normed_ref[f].astype(F32) * second_mean_ref[row])
        grad = wide.astype(BF16)
        g_ref[f] = grad
        first_ref[f, 0] = grad[:width]
        last_ref[f, 0] = grad[pixels - width :]
        here = pl.ds(pl.multiple_of(f * pixels, pixels), pixels)
        moved_ref[here, :channels] = from_right(wide, width).astype(BF16)
        moved_ref[here, channels : 2 * channels] = grad
        moved_ref[here, 2 * channels :] = from_left(wide, width).astype(BF16)

    loop(normed_ref.shape[0], body)


def weight_grad_kernel(xt_ref, moved_ref, temporal_ref, out_ref):
    channels = temporal_ref.shape[0]
    for j in range(3):
        lanes = slice(j * channels, (j + 1) * channels)
        out_ref[: 3 * channels, lanes] = dot(xt_ref[...], moved_ref[:, lanes])
    out_ref[3 * channels :, :] = temporal_ref[...]


def hand_out_kernel(acc_ref, send_ref, keep_ref):
    chips, depth, block, _ = keep_ref.shape
    half = chips * depth * block
    core = lax.axis_index("tm") & 1

    def hand_out(kept, sent):
        for p in range(chips):
            for z in range(depth):
                at = (p * depth + z) * block
                keep_ref[p, z] = acc_ref[kept + at : kept + at + block]
                send_ref[p, z] = acc_ref[sent + at : sent + at + block].astype(BF16)

    pl.when(core == 0)(functools.partial(hand_out, 0, half))
    pl.when(core == 1)(functools.partial(hand_out, half, 0))


def conv_back_kernel(g_ref, above_ref, below_ref, cot_ref, w_ref, out_ref, lhs_ref):
    frames, rows, width, channels = cot_ref.shape
    pixels = rows * width

    def body(pair):
        for b in range(2):
            f = 2 * pair + b
            put_windows(above_ref[f, 0], g_ref[f], below_ref[f, 0], lhs_ref, b * pixels, (2, 1, 0))
        lhs = lhs_ref[...]
        z = [dot(lhs, w_ref[j]) for j in range(3)]
        out = z[1] + from_right(z[0], width) + from_left(z[2], width)
        for b in range(2):
            one = out[b * pixels : (b + 1) * pixels].reshape(rows, width, channels)
            out_ref[2 * pair + b] = (one + cot_ref[2 * pair + b].astype(F32)).astype(BF16)

    loop(frames // 2, body)


def out_kernel(clip_ref, dil_ref, own, nxt_a, nxt_b, prv_a, prv_b, tw_ref, x_ref, out_ref, cat_ref):
    frames, rows, width, channels = x_ref.shape
    pixels = rows * width

    def body(pair):
        for b in range(2):
            gather_taps(clip_ref, dil_ref, 2 * pair + b, own, (nxt_a, nxt_b), (prv_a, prv_b), (), cat_ref, b * pixels, 2)
        temporal_out = dot(cat_ref[...], tw_ref[...]).astype(BF16).astype(F32)
        for b in range(2):
            one = temporal_out[b * pixels : (b + 1) * pixels].reshape(rows, width, channels)
            out_ref[2 * pair + b] = (x_ref[2 * pair + b].astype(F32) + one).astype(BF16)

    loop(frames // 2, body)


def core_sum_kernel(keep_ref, got_ref, own_ref, *send_refs):
    chip = lax.axis_index("tm") >> 1
    own_ref[...] = keep_ref[chip] + got_ref[chip].astype(F32)
    for s, ref in enumerate(send_refs, 1):
        ref[...] = (keep_ref[chip ^ s] + got_ref[chip ^ s].astype(F32)).astype(BF16)


def sum_kernel(count, own_ref, *refs):
    total = own_ref[...]
    for ref in refs[:count]:
        total = total + ref[...].astype(F32)
    refs[count][...] = total.astype(BF16)


def sum_split_kernel(count, own_ref, *refs):
    got, (mine_ref, *send_refs) = refs[:count], refs[count:]
    deep = lax.axis_index("space")

    def block(k):
        total = own_ref[k]
        for ref in got:
            total = total + ref[k].astype(F32)
        return total

    mine_ref[...] = block(deep)
    for s, ref in enumerate(send_refs, 1):
        ref[...] = block(deep ^ s).astype(BF16)


def place_kernel(axis, shift, *refs):
    me = lax.axis_index(axis) >> shift
    for s, ref in enumerate(refs[:-1]):
        refs[-1][me ^ s] = ref[...]


def finish_kernel(mine_ref, got_ref, spatial_ref, temporal_ref):
    chips, depth, block, _ = mine_ref.shape
    channels = spatial_ref.shape[-1]

    def write(pair):
        for c in range(2):
            for p in range(chips):
                for z in range(depth):
                    row = ((c * chips + p) * depth + z) * block
                    values = pair[c][p, z].astype(F32)
                    i, at = row // channels, row % channels
                    for k in range(3):
                        lanes = values[:, k * channels : (k + 1) * channels]
                        if i < 3:
                            spatial_ref[i, k, at : at + block] = lanes
                        else:
                            temporal_ref[k, at : at + block] = lanes

    core = lax.axis_index("tm") & 1
    pl.when(core == 0)(functools.partial(write, (mine_ref, got_ref)))
    pl.when(core == 1)(functools.partial(write, (got_ref, mine_ref)))


def neighbours(axis, low, high, but=None):
    size = lax.axis_size(axis)
    up = [(i, i + 1) for i in range(size - 1) if i != but]
    down = [(j, i) for i, j in up]
    return lax.ppermute(high, axis, up), lax.ppermute(low, axis, down)


def spread_parts(part, axis):
    size = lax.axis_size(axis)
    return [part] + [lax.ppermute(part, axis, [(i, i ^ s) for i in range(size)]) for s in range(1, size)]


def spread_sums(part, axis):
    size = lax.axis_size(axis)
    step, got = 1, None
    while step < size:
        if got is not None:
            part = part + got
        got = lax.ppermute(part, axis, [(i, i ^ step) for i in range(size)])
        step *= 2
    return [part, got]


def per_device(frames_in, cotangent, spatial, temporal, norm_gain, norm_shift, clip_frames, dilation):
    frames, rows, width, channels = frames_in.shape
    pixels = rows * width
    n, tm = lax.axis_size("space"), lax.axis_size("tm")
    chips = tm // 2
    group_size = channels // GROUPS
    entries = float(rows * n * width * group_size)
    gain, shift = norm_gain[None], norm_shift[None]
    big = frames * pixels * channels
    shape = jax.ShapeDtypeStruct
    per_px = (frames, pixels, channels)
    windows = pltpu.VMEM((2 * pixels, 3 * channels), BF16)

    cot = cotangent.reshape(per_px)
    by_corner = tm == 8
    first, last = frames_in[:, :1], frames_in[:, rows - 1 :]
    first, last, near = lax.optimization_barrier((first, last, cot))
    cot_prev, cot_next = neighbours("tm", near, near, 3 if by_corner else None)
    cot_corner = []
    if by_corner:
        straight, relayed = cot[: frames // 2], cot[frames // 2 :]
        relayed = lax.ppermute(relayed, "tm", [(3, 7), (4, 0)])
    above, below = neighbours("space", first, last)
    back_weights, back_taps = call(
        turn_weights_kernel, "turn_weights", [spatial, temporal],
        [shape((3, 3 * channels, channels), BF16), shape((3 * channels, channels), BF16)], 0, big,
    )
    conv_out, sums = call(
        conv_kernel, "conv_forward", [frames_in, above, below, spatial],
        [shape(per_px, F32), shape((frames, 2, channels), F32)],
        100 * big * channels, 8 * big, [windows], 18,
    )
    if by_corner:
        sums, straight = lax.optimization_barrier((sums, straight))
        cot_corner.append(lax.ppermute(straight, "tm", [(3, 4), (4, 3)]))
    parts = spread_sums(sums, "space")
    if by_corner:
        parts[0], relayed = lax.optimization_barrier((parts[0], relayed))
        cot_corner.append(lax.ppermute(relayed, "tm", [(7, 4), (0, 3)]))
    x_turned = call(
        turn_kernel, "turned", [frames_in, above, below], shape((3 * channels, frames * pixels), BF16),
        0, 8 * big, [pltpu.VMEM((pixels, 3 * channels), BF16)],
    )
    x_turned, *parts = lax.optimization_barrier((x_turned, *parts))
    ahead = (3 * frames) // 4
    row = pltpu.VMEM((frames, channels), F32)
    act, act_early, act_late, normed, slope = call(
        functools.partial(act_kernel, len(parts), entries, group_size), "activation",
        [clip_frames, *parts, conv_out, gain, shift], [shape((k, pixels, channels), BF16) for k in (frames, ahead, frames - ahead, frames, frames)], 10 * big, 10 * big, [row] * 2,
    )
    act_early, *cot_corner = lax.optimization_barrier((act_early, *cot_corner))
    act_prev, act_next = neighbours("tm", act_early, act_early)

    grad_act, cot_cat, grad_sums = call(
        functools.partial(grad_act_kernel, len(cot_corner)), "grad_activation",
        [clip_frames, dilation, cot, cot_next, cot_prev, *cot_corner, back_taps, normed, slope],
        [shape(per_px, BF16), shape((frames * pixels, 3 * channels), BF16), shape((frames, 2, channels), F32)],
        6 * big * channels, 16 * big,
    )
    grad_parts = spread_parts(grad_sums, "space")
    temporal_part = call(
        temporal_grad_kernel, "temporal_grad", [act, cot_cat],
        shape((channels, 3 * channels), F32), 6 * big * channels, 8 * big,
    )
    lanes = 3 * channels
    grad_conv, first_rows, last_rows, moved = call(
        functools.partial(norm_back_kernel, len(parts), len(grad_parts), entries, group_size), "norm_backward",
        [normed, slope, grad_act, *parts, *grad_parts],
        [shape(per_px, BF16)] + [shape((frames, 1, width, channels), BF16)] * 2
        + [shape((frames * pixels, lanes), BF16)],
        0, 12 * big, [row] * 3,
    )
    grad_above, grad_below = neighbours("space", first_rows, last_rows)
    sums = call(
        weight_grad_kernel, "weight_grad", [x_turned, moved, temporal_part], shape((4 * channels, lanes), F32),
        18 * big * channels, 12 * big,
    )
    sums, grad_above, grad_below = lax.optimization_barrier((sums, grad_above, grad_below))
    block = 2 * channels // (chips * n)
    send, keep = call(
        hand_out_kernel, "hand_out", [sums],
        [shape((chips, n, block, lanes), BF16), shape((chips, n, block, lanes), F32)], 0, big,
    )
    def other_chip(s):
        return [(i, i ^ (2 * s)) for i in range(tm)]

    def other_plane(s):
        return [(i, i ^ s) for i in range(n)]

    other_core = [(i, i ^ 1) for i in range(tm)]
    got = lax.ppermute(send, "tm", other_core)
    own, *sends = call(
        core_sum_kernel, "core_sum", [keep, got],
        [shape((n, block, lanes), F32)] + [shape((n, block, lanes), BF16)] * (chips - 1), 0, 4 * big,
    )
    gots = [lax.ppermute(x, "tm", other_chip(s)) for s, x in enumerate(sends, 1)]

    in_grad = call(
        conv_back_kernel, "conv_backward", [grad_conv, grad_above, grad_below, cotangent, back_weights],
        shape(frames_in.shape, BF16), 18 * big * channels, 8 * big, [windows], 20,
    )
    own, in_grad, act_prev, act_next = lax.optimization_barrier((own, in_grad, act_prev, act_next))

    own, *sends = call(
        functools.partial(sum_split_kernel, chips - 1), "plane_sum", [own, *gots],
        [shape((block, lanes), F32)] + [shape((block, lanes), BF16)] * (n - 1), 0, big,
    )
    gots = [lax.ppermute(x, "space", other_plane(s)) for s, x in enumerate(sends, 1)]
    own, act_late = lax.optimization_barrier((own, act_late))
    late_prev, late_next = neighbours("tm", act_late, act_late)
    own = call(
        functools.partial(sum_kernel, n - 1), "line_sum", [own, *gots], shape((block, lanes), BF16), 0, big
    )
    gots = [lax.ppermute(own, "space", other_plane(s)) for s in range(1, n)]
    own = call(
        functools.partial(place_kernel, "space", 0), "line_place", [own, *gots], shape((n, block, lanes), BF16), 0, big
    )
    gots = [lax.ppermute(own, "tm", other_chip(s)) for s in range(1, chips)]


    out_frames = call(
        out_kernel, "temporal_forward",
        [clip_frames, dilation, act, act_next, late_next, act_prev, late_prev, temporal.reshape(3 * channels, channels), frames_in],
        shape(frames_in.shape, BF16), 6 * big * channels, 10 * big, [windows],
    )
    own, out_frames = lax.optimization_barrier((own, out_frames))
    own = call(
        functools.partial(place_kernel, "tm", 1), "plane_place", [own, *gots], shape((chips, n, block, lanes), BF16), 0, big
    )
    got = lax.ppermute(own, "tm", other_core)
    spatial_grad, temporal_grad = call(
        finish_kernel, "finish", [own, got], [shape(spatial.shape, F32), shape(temporal.shape, F32)], 0, 4 * big
    )
    return (out_frames, in_grad, spatial_grad, temporal_grad)


def solution(mesh):
    tiles = P("tm", "space", None, None)
    return jax.shard_map(
        per_device,
        mesh=mesh,
        in_specs=(tiles, tiles, P(), P(), P(), P(), P(), P()),
        out_specs=(tiles, tiles, P(), P()),
        check_vma=False,
    )
```

```python
import functools

import jax
import jax.numpy as jnp
from jax import lax
from jax.experimental import pallas as pl
from jax.experimental.pallas import tpu as pltpu
from jax.sharding import PartitionSpec as P

GROUPS = 32
NORM_EPS = 1e-05
BF16 = jnp.bfloat16
F32 = jnp.float32
MIB = 2**20


def call(kernel, name, operands, out_shape, flops=0, moved=0, scratch=(), grant=14):
    vmem = pl.BlockSpec(memory_space=pltpu.VMEM)
    smem = pl.BlockSpec(memory_space=pltpu.SMEM)
    return pl.pallas_call(
        kernel,
        in_specs=[smem if x.dtype == jnp.int32 else vmem for x in operands],
        out_specs=jax.tree.map(lambda _: vmem, out_shape),
        out_shape=out_shape,
        scratch_shapes=list(scratch),
        compiler_params=pltpu.CompilerParams(vmem_limit_bytes=grant * MIB),
        cost_estimate=pl.CostEstimate(flops=int(flops), bytes_accessed=int(moved), transcendentals=0),
        name=name,
    )(*operands)


def dot(a, b):
    return jnp.dot(a, b, preferred_element_type=F32)


def dot_rows(a, b):
    return lax.dot_general(a, b, (((0,), (0,)), ((), ())), preferred_element_type=F32)


def group_total(row, group_size):
    channels = row.shape[-1]
    lane = lax.broadcasted_iota(jnp.int32, row.shape, 1)
    step = 1
    while step < group_size:
        up = pltpu.roll(row, channels - step, axis=1)
        down = pltpu.roll(row, step, axis=1)
        row = row + jnp.where((lane & step) == 0, up, down)
        step *= 2
    return row


def group_means(part_refs, entries, group_size):
    total = part_refs[0][...]
    for ref in part_refs[1:]:
        total = total + ref[...]
    frames, _, channels = total.shape
    means = group_total(total.reshape(2 * frames, channels), group_size) / entries
    means = means.reshape(frames, 2, channels)
    return means[:, 0], means[:, 1]


def mean_and_inv(part_refs, entries, group_size):
    mean, square = group_means(part_refs, entries, group_size)
    return mean, lax.rsqrt(square - mean * mean + NORM_EPS)


def column_sums(first, second):
    return jnp.concatenate(
        [jnp.sum(first, axis=0, keepdims=True), jnp.sum(second, axis=0, keepdims=True)], axis=0
    )


def put_windows(above, mid, below, lhs_ref, at, order):
    width, (pixels, channels) = above.shape[0], mid.shape
    first, mid_at, last = (slice(k * channels, (k + 1) * channels) for k in order)
    lhs_ref[at : at + width, first] = above
    lhs_ref[at + width : at + pixels, first] = mid[: pixels - width]
    lhs_ref[at : at + pixels, mid_at] = mid
    lhs_ref[at : at + pixels - width, last] = mid[width:]
    lhs_ref[at + pixels - width : at + pixels, last] = below


def from_left(y, width):
    col = lax.broadcasted_iota(jnp.int32, y.shape, 0) & (width - 1)
    return jnp.where(col == 0, 0.0, pltpu.roll(y, 1, axis=0))


def from_right(y, width):
    col = lax.broadcasted_iota(jnp.int32, y.shape, 0) & (width - 1)
    return jnp.where(col == width - 1, 0.0, pltpu.roll(y, y.shape[0] - 1, axis=0))


def slot_sources(clip_ref, dil_ref, local, frames):
    slot = lax.axis_index("tm") * frames + local
    start1 = clip_ref[0]
    filled = start1 + clip_ref[1]
    in_first = slot < start1
    d = jnp.where(in_first, dil_ref[0], dil_ref[1])
    low = jnp.where(in_first, 0, start1)
    high = jnp.where(in_first, start1, filled)
    used = slot < filled
    later, earlier = local + d, local - d
    later_live = used & (slot + d < high)
    earlier_live = used & (slot - d >= low)
    later_which = jnp.where(later_live, jnp.where(later < frames, 1, 2), 0)
    earlier_which = jnp.where(earlier_live, jnp.where(earlier >= 0, 1, 2), 0)
    return (later, later_which), (earlier, earlier_which), used


def gather_taps(clip_ref, dil_ref, local, own, nxt, prv, corner, cat_ref, at, up_slot):
    frames, pixels, channels = own.shape
    later, earlier, used = slot_sources(clip_ref, dil_ref, local, frames)
    me = lax.axis_index("tm")

    def put(slot, ref, index):
        cat_ref[pl.ds(at, pixels), slot * channels : (slot + 1) * channels] = ref[index]

    def clear(slot):
        cat_ref[pl.ds(at, pixels), slot * channels : (slot + 1) * channels] = jnp.zeros((pixels, channels), BF16)

    def put_from(slot, pieces, wanted, index):
        start = 0
        for ref in pieces:
            count = ref.shape[0]
            here = wanted & (index >= start) & (index < start + count)
            pl.when(here)(functools.partial(put, slot, ref, jnp.clip(index - start, 0, count - 1)))
            start += count

    for slot, (index, which), other, shift, turn in (
        (up_slot, later, nxt, -frames, 3),
        (2 - up_slot, earlier, prv, frames, 4),
    ):
        pl.when(which == 0)(functools.partial(clear, slot))
        pl.when(which == 1)(functools.partial(put, slot, own, jnp.clip(index, 0, frames - 1)))
        there = jnp.clip(index + shift, 0, frames - 1)
        beyond = which == 2
        if corner:
            put_from(slot, corner, beyond & (me == turn), there)
            beyond = beyond & (me != turn)
        put_from(slot, other, beyond, there)
    pl.when(used)(functools.partial(put, 1, own, local))
    pl.when(jnp.logical_not(used))(functools.partial(clear, 1))


def loop(count, body):
    def step(k, carry):
        body(k)
        return carry

    lax.fori_loop(0, count, step, 0)


def conv_kernel(x_ref, above_ref, below_ref, w_ref, out_ref, sums_ref, lhs_ref):
    frames, rows, width, channels = x_ref.shape
    pixels = rows * width

    def body(pair):
        for b in range(2):
            f = 2 * pair + b
            mid = x_ref[f].reshape(pixels, channels)
            put_windows(above_ref[f, 0], mid, below_ref[f, 0], lhs_ref, b * pixels, (0, 1, 2))
        lhs = lhs_ref[...]
        y = [dot(lhs, w_ref[:, j].reshape(3 * channels, channels)) for j in range(3)]
        out = y[1] + from_left(y[0], width) + from_right(y[2], width)
        for b in range(2):
            one = out[b * pixels : (b + 1) * pixels]
            out_ref[2 * pair + b] = one
            sums_ref[2 * pair + b] = column_sums(one, one * one)

    loop(frames // 2, body)


def silu_parts(normed, half_gain, half_shift):
    h = normed * half_gain + half_shift
    t = jnp.tanh(h)
    rise = 1.0 + t
    return h, rise, rise * (1.0 + h * (1.0 - t)) * half_gain


def act_kernel(n, entries, group_size, clip_ref, *refs):
    parts, refs = refs[:n], refs[n:]
    conv_ref, gain_ref, shift_ref, act_ref, early_ref, late_ref, normed_ref, slope_ref, mean_ref, inv_ref = refs
    frames, ahead = conv_ref.shape[0], early_ref.shape[0]
    first = lax.axis_index("tm") * frames
    filled = clip_ref[0] + clip_ref[1]
    half_gain, half_shift = 0.5 * gain_ref[...], 0.5 * shift_ref[...]
    mean_ref[...], inv_ref[...] = mean_and_inv(parts, entries, group_size)

    def body(f):
        normed = (conv_ref[f] - mean_ref[pl.ds(f, 1)]) * inv_ref[pl.ds(f, 1)]
        h, rise, slope = silu_parts(normed, half_gain, half_shift)
        act = jnp.where(first + f < filled, h * rise, 0.0).astype(BF16)
        act_ref[f] = act

        @pl.when(f < ahead)
        def _():
            early_ref[jnp.minimum(f, ahead - 1)] = act

        @pl.when(f >= ahead)
        def _():
            late_ref[jnp.maximum(f - ahead, 0)] = act

        normed_ref[f] = normed.astype(BF16)
        slope_ref[f] = slope.astype(BF16)

    loop(frames, body)


def turn_kernel(x_ref, above_ref, below_ref, xt_ref, lhs_ref):
    frames, rows, width, channels = x_ref.shape
    pixels = rows * width

    def body(f):
        mid = x_ref[f].reshape(pixels, channels)
        put_windows(above_ref[f, 0], mid, below_ref[f, 0], lhs_ref, 0, (0, 1, 2))
        lanes = pl.ds(pl.multiple_of(f * pixels, pixels), pixels)
        for i in range(3):
            block = slice(i * channels, (i + 1) * channels)
            xt_ref[block, lanes] = lhs_ref[:, block].T

    loop(frames, body)


def turn_weights_kernel(spatial_ref, temporal_ref, back_ref, out_ref):
    channels = spatial_ref.shape[-1]
    for i in range(3):
        rows = slice(i * channels, (i + 1) * channels)
        out_ref[rows] = temporal_ref[i].T
        for j in range(3):
            back_ref[j, rows] = spatial_ref[i, j].T


def grad_act_kernel(corners, clip_ref, dil_ref, own, nxt, prv, *refs):
    corner, (tw_ref, normed_ref, slope_ref, ga_ref, cat_ref, sums_ref) = refs[:corners], refs[corners:]
    frames, pixels, _ = own.shape

    def body(pair):
        rows = pl.ds(pl.multiple_of(2 * pair * pixels, 2 * pixels), 2 * pixels)
        for b in range(2):
            at = pl.multiple_of((2 * pair + b) * pixels, pixels)
            gather_taps(clip_ref, dil_ref, 2 * pair + b, own, (nxt,), (prv,), corner, cat_ref, at, 0)
        grad_act = dot(cat_ref[rows], tw_ref[...]).astype(BF16)
        for b in range(2):
            f = 2 * pair + b
            one = grad_act[b * pixels : (b + 1) * pixels]
            ga_ref[f] = one
            gn = one.astype(F32) * slope_ref[f].astype(F32)
            sums_ref[f] = column_sums(gn, gn * normed_ref[f].astype(F32))

    loop(frames // 2, body)


def temporal_grad_kernel(act_ref, cat_ref, out_ref):
    frames, pixels, channels = act_ref.shape
    out_ref[...] = dot_rows(act_ref[...].reshape(frames * pixels, channels), cat_ref[...])


def norm_back_kernel(n, m, entries, group_size, normed_ref, slope_ref, ga_ref, *refs):
    parts, grad_parts = refs[:n], refs[n : n + m]
    g_ref, first_ref, last_ref, moved_ref, inv_ref, first_mean_ref, second_mean_ref = refs[n + m :]
    _, pixels, channels = normed_ref.shape
    width = first_ref.shape[2]

    _, inv_ref[...] = mean_and_inv(parts, entries, group_size)
    first_mean_ref[...], second_mean_ref[...] = group_means(grad_parts, entries, group_size)

    def body(f):
        row = pl.ds(f, 1)
        gn = ga_ref[f].astype(F32) * slope_ref[f].astype(F32)
        wide = inv_ref[row] * (gn - first_mean_ref[row] - normed_ref[f].astype(F32) * second_mean_ref[row])
        grad = wide.astype(BF16)
        g_ref[f] = grad
        first_ref[f, 0] = grad[:width]
        last_ref[f, 0] = grad[pixels - width :]
        here = pl.ds(pl.multiple_of(f * pixels, pixels), pixels)
        moved_ref[here, :channels] = from_right(wide, width).astype(BF16)
        moved_ref[here, channels : 2 * channels] = grad
        moved_ref[here, 2 * channels :] = from_left(wide, width).astype(BF16)

    loop(normed_ref.shape[0], body)


def weight_grad_kernel(xt_ref, moved_ref, temporal_ref, out_ref):
    channels = temporal_ref.shape[0]
    for j in range(3):
        lanes = slice(j * channels, (j + 1) * channels)
        out_ref[: 3 * channels, lanes] = dot(xt_ref[...], moved_ref[:, lanes])
    out_ref[3 * channels :, :] = temporal_ref[...]


def hand_out_kernel(acc_ref, send_ref, keep_ref):
    chips, depth, block, _ = keep_ref.shape
    half = chips * depth * block
    core = lax.axis_index("tm") & 1

    def hand_out(kept, sent):
        for p in range(chips):
            for z in range(depth):
                at = (p * depth + z) * block
                keep_ref[p, z] = acc_ref[kept + at : kept + at + block]
                send_ref[p, z] = acc_ref[sent + at : sent + at + block].astype(BF16)

    pl.when(core == 0)(functools.partial(hand_out, 0, half))
    pl.when(core == 1)(functools.partial(hand_out, half, 0))


def conv_back_kernel(g_ref, above_ref, below_ref, cot_ref, w_ref, out_ref, lhs_ref):
    frames, rows, width, channels = cot_ref.shape
    pixels = rows * width

    def body(pair):
        for b in range(2):
            f = 2 * pair + b
            put_windows(above_ref[f, 0], g_ref[f], below_ref[f, 0], lhs_ref, b * pixels, (2, 1, 0))
        lhs = lhs_ref[...]
        z = [dot(lhs, w_ref[j]) for j in range(3)]
        out = z[1] + from_right(z[0], width) + from_left(z[2], width)
        for b in range(2):
            one = out[b * pixels : (b + 1) * pixels].reshape(rows, width, channels)
            out_ref[2 * pair + b] = (one + cot_ref[2 * pair + b].astype(F32)).astype(BF16)

    loop(frames // 2, body)


def out_kernel(clip_ref, dil_ref, own, nxt_a, nxt_b, prv_a, prv_b, tw_ref, x_ref, out_ref, cat_ref):
    frames, rows, width, channels = x_ref.shape
    pixels = rows * width

    def body(pair):
        for b in range(2):
            gather_taps(clip_ref, dil_ref, 2 * pair + b, own, (nxt_a, nxt_b), (prv_a, prv_b), (), cat_ref, b * pixels, 2)
        temporal_out = dot(cat_ref[...], tw_ref[...]).astype(BF16).astype(F32)
        for b in range(2):
            one = temporal_out[b * pixels : (b + 1) * pixels].reshape(rows, width, channels)
            out_ref[2 * pair + b] = (x_ref[2 * pair + b].astype(F32) + one).astype(BF16)

    loop(frames // 2, body)


def core_sum_kernel(keep_ref, got_ref, own_ref, *send_refs):
    chip = lax.axis_index("tm") >> 1
    own_ref[...] = keep_ref[chip] + got_ref[chip].astype(F32)
    for s, ref in enumerate(send_refs, 1):
        ref[...] = (keep_ref[chip ^ s] + got_ref[chip ^ s].astype(F32)).astype(BF16)


def sum_kernel(count, own_ref, *refs):
    total = own_ref[...]
    for ref in refs[:count]:
        total = total + ref[...].astype(F32)
    refs[count][...] = total.astype(BF16)


def sum_split_kernel(count, own_ref, *refs):
    got, (mine_ref, *send_refs) = refs[:count], refs[count:]
    deep = lax.axis_index("space")

    def block(k):
        total = own_ref[k]
        for ref in got:
            total = total + ref[k].astype(F32)
        return total

    mine_ref[...] = block(deep)
    for s, ref in enumerate(send_refs, 1):
        ref[...] = block(deep ^ s).astype(BF16)


def place_kernel(axis, shift, *refs):
    me = lax.axis_index(axis) >> shift
    for s, ref in enumerate(refs[:-1]):
        refs[-1][me ^ s] = ref[...]


def finish_kernel(mine_ref, got_ref, spatial_ref, temporal_ref):
    chips, depth, block, _ = mine_ref.shape
    channels = spatial_ref.shape[-1]

    def write(pair):
        for c in range(2):
            for p in range(chips):
                for z in range(depth):
                    row = ((c * chips + p) * depth + z) * block
                    values = pair[c][p, z].astype(F32)
                    i, at = row // channels, row % channels
                    for k in range(3):
                        lanes = values[:, k * channels : (k + 1) * channels]
                        if i < 3:
                            spatial_ref[i, k, at : at + block] = lanes
                        else:
                            temporal_ref[k, at : at + block] = lanes

    core = lax.axis_index("tm") & 1
    pl.when(core == 0)(functools.partial(write, (mine_ref, got_ref)))
    pl.when(core == 1)(functools.partial(write, (got_ref, mine_ref)))


def neighbours(axis, low, high, but=None):
    size = lax.axis_size(axis)
    up = [(i, i + 1) for i in range(size - 1) if i != but]
    down = [(j, i) for i, j in up]
    return lax.ppermute(high, axis, up), lax.ppermute(low, axis, down)


def spread_parts(part, axis):
    size = lax.axis_size(axis)
    return [part] + [lax.ppermute(part, axis, [(i, i ^ s) for i in range(size)]) for s in range(1, size)]


def spread_sums(part, axis):
    size = lax.axis_size(axis)
    step, got = 1, None
    while step < size:
        if got is not None:
            part = part + got
        got = lax.ppermute(part, axis, [(i, i ^ step) for i in range(size)])
        step *= 2
    return [part, got]


def per_device(frames_in, cotangent, spatial, temporal, norm_gain, norm_shift, clip_frames, dilation):
    frames, rows, width, channels = frames_in.shape
    pixels = rows * width
    n, tm = lax.axis_size("space"), lax.axis_size("tm")
    chips = tm // 2
    group_size = channels // GROUPS
    entries = float(rows * n * width * group_size)
    gain, shift = norm_gain[None], norm_shift[None]
    big = frames * pixels * channels
    shape = jax.ShapeDtypeStruct
    per_px = (frames, pixels, channels)
    windows = pltpu.VMEM((2 * pixels, 3 * channels), BF16)

    cot = cotangent.reshape(per_px)
    by_corner = tm == 8
    first, last = frames_in[:, :1], frames_in[:, rows - 1 :]
    first, last, near = lax.optimization_barrier((first, last, cot))
    cot_prev, cot_next = neighbours("tm", near, near, 3 if by_corner else None)
    cot_corner = []
    if by_corner:
        straight, relayed = cot[: frames // 2], cot[frames // 2 :]
        relayed = lax.ppermute(relayed, "tm", [(3, 7), (4, 0)])
    above, below = neighbours("space", first, last)
    back_weights, back_taps = call(
        turn_weights_kernel, "turn_weights", [spatial, temporal],
        [shape((3, 3 * channels, channels), BF16), shape((3 * channels, channels), BF16)], 0, big,
    )
    conv_out, sums = call(
        conv_kernel, "conv_forward", [frames_in, above, below, spatial],
        [shape(per_px, F32), shape((frames, 2, channels), F32)],
        100 * big * channels, 8 * big, [windows], 18,
    )
    if by_corner:
        sums, straight = lax.optimization_barrier((sums, straight))
        cot_corner.append(lax.ppermute(straight, "tm", [(3, 4), (4, 3)]))
    parts = spread_sums(sums, "space")
    if by_corner:
        _, relayed = lax.optimization_barrier((sums, relayed))
        cot_corner.append(lax.ppermute(relayed, "tm", [(7, 4), (0, 3)]))
    x_turned = call(
        turn_kernel, "turned", [frames_in, above, below], shape((3 * channels, frames * pixels), BF16),
        0, 8 * big, [pltpu.VMEM((pixels, 3 * channels), BF16)],
    )
    x_turned, *parts = lax.optimization_barrier((x_turned, *parts))
    ahead = (3 * frames) // 4
    row = pltpu.VMEM((frames, channels), F32)
    act, act_early, act_late, normed, slope = call(
        functools.partial(act_kernel, len(parts), entries, group_size), "activation",
        [clip_frames, *parts, conv_out, gain, shift], [shape((k, pixels, channels), BF16) for k in (frames, ahead, frames - ahead, frames, frames)], 10 * big, 10 * big, [row] * 2,
    )
    act_prev, act_next = neighbours("tm", act_early, act_early)

    grad_act, cot_cat, grad_sums = call(
        functools.partial(grad_act_kernel, len(cot_corner)), "grad_activation",
        [clip_frames, dilation, cot, cot_next, cot_prev, *cot_corner, back_taps, normed, slope],
        [shape(per_px, BF16), shape((frames * pixels, 3 * channels), BF16), shape((frames, 2, channels), F32)],
        6 * big * channels, 16 * big,
    )
    grad_parts = spread_parts(grad_sums, "space")
    temporal_part = call(
        temporal_grad_kernel, "temporal_grad", [act, cot_cat],
        shape((channels, 3 * channels), F32), 6 * big * channels, 8 * big,
    )
    lanes = 3 * channels
    grad_conv, first_rows, last_rows, moved = call(
        functools.partial(norm_back_kernel, len(parts), len(grad_parts), entries, group_size), "norm_backward",
        [normed, slope, grad_act, *parts, *grad_parts],
        [shape(per_px, BF16)] + [shape((frames, 1, width, channels), BF16)] * 2
        + [shape((frames * pixels, lanes), BF16)],
        0, 12 * big, [row] * 3,
    )
    grad_above, grad_below = neighbours("space", first_rows, last_rows)
    sums = call(
        weight_grad_kernel, "weight_grad", [x_turned, moved, temporal_part], shape((4 * channels, lanes), F32),
        18 * big * channels, 12 * big,
    )
    sums, grad_above, grad_below = lax.optimization_barrier((sums, grad_above, grad_below))
    block = 2 * channels // (chips * n)
    send, keep = call(
        hand_out_kernel, "hand_out", [sums],
        [shape((chips, n, block, lanes), BF16), shape((chips, n, block, lanes), F32)], 0, big,
    )
    def other_chip(s):
        return [(i, i ^ (2 * s)) for i in range(tm)]

    def other_plane(s):
        return [(i, i ^ s) for i in range(n)]

    other_core = [(i, i ^ 1) for i in range(tm)]
    got = lax.ppermute(send, "tm", other_core)
    own, *sends = call(
        core_sum_kernel, "core_sum", [keep, got],
        [shape((n, block, lanes), F32)] + [shape((n, block, lanes), BF16)] * (chips - 1), 0, 4 * big,
    )
    gots = [lax.ppermute(x, "tm", other_chip(s)) for s, x in enumerate(sends, 1)]

    in_grad = call(
        conv_back_kernel, "conv_backward", [grad_conv, grad_above, grad_below, cotangent, back_weights],
        shape(frames_in.shape, BF16), 18 * big * channels, 8 * big, [windows], 20,
    )
    own, in_grad, act_prev, act_next = lax.optimization_barrier((own, in_grad, act_prev, act_next))

    own, *sends = call(
        functools.partial(sum_split_kernel, chips - 1), "plane_sum", [own, *gots],
        [shape((block, lanes), F32)] + [shape((block, lanes), BF16)] * (n - 1), 0, big,
    )
    gots = [lax.ppermute(x, "space", other_plane(s)) for s, x in enumerate(sends, 1)]
    own, act_late = lax.optimization_barrier((own, act_late))
    late_prev, late_next = neighbours("tm", act_late, act_late)
    own = call(
        functools.partial(sum_kernel, n - 1), "line_sum", [own, *gots], shape((block, lanes), BF16), 0, big
    )
    gots = [lax.ppermute(own, "space", other_plane(s)) for s in range(1, n)]
    own = call(
        functools.partial(place_kernel, "space", 0), "line_place", [own, *gots], shape((n, block, lanes), BF16), 0, big
    )
    gots = [lax.ppermute(own, "tm", other_chip(s)) for s in range(1, chips)]


    out_frames = call(
        out_kernel, "temporal_forward",
        [clip_frames, dilation, act, act_next, late_next, act_prev, late_prev, temporal.reshape(3 * channels, channels), frames_in],
        shape(frames_in.shape, BF16), 6 * big * channels, 10 * big, [windows],
    )
    own, out_frames = lax.optimization_barrier((own, out_frames))
    own = call(
        functools.partial(place_kernel, "tm", 1), "plane_place", [own, *gots], shape((chips, n, block, lanes), BF16), 0, big
    )
    got = lax.ppermute(own, "tm", other_core)
    spatial_grad, temporal_grad = call(
        finish_kernel, "finish", [own, got], [shape(spatial.shape, F32), shape(temporal.shape, F32)], 0, 4 * big
    )
    return (out_frames, in_grad, spatial_grad, temporal_grad)


def solution(mesh):
    tiles = P("tm", "space", None, None)
    return jax.shard_map(
        per_device,
        mesh=mesh,
        in_specs=(tiles, tiles, P(), P(), P(), P(), P(), P()),
        out_specs=(tiles, tiles, P(), P()),
        check_vma=False,
    )
```
